32 devices in a mesh: uly: 8 (over y, x, core), blk: 4 (over z).
Axes of the slice: x: 2, y: 2, z: 4, core: 2. Of those that a mesh axis runs over, the one named last changes fastest.
Arguments:
- hidden_in: bfloat16 [4096, 2048], P(('uly', 'blk')), may hold values from -6 to 6
- out_grad: bfloat16 [4096, 2048], P(('uly', 'blk')), may hold values from -6 to 6
- attn_gain: bfloat16 [2048], P(('uly', 'blk')), may hold values from 0.5 to 1.5
- query_weight: bfloat16 [2048, 2048], P(('uly', 'blk')), may hold values from -0.125 to 0.125
- key_weight: bfloat16 [2048, 2048], P(('uly', 'blk')), may hold values from -0.125 to 0.125
- value_weight: bfloat16 [2048, 2048], P(('uly', 'blk')), may hold values from -0.125 to 0.125
- out_weight: bfloat16 [2048, 2048], P(('uly', 'blk')), may hold values from -1.5 to 1.5
- query_gain: bfloat16 [2048], P(('uly', 'blk')), may hold values from 0.5 to 1.5
- key_gain: bfloat16 [2048], P(('uly', 'blk')), may hold values from 0.5 to 1.5
- ffn_gain: bfloat16 [2048], P(('uly', 'blk')), may hold values from 0.5 to 1.5
- router_weight: bfloat16 [2048, 64], P(('uly', 'blk')), may hold values from -0.0625 to 0.0625
- expert_weights: bfloat16 [64, 3, 2048, 1024], P('uly', None, None, 'blk'), may hold values from -4 to 4
- routes: int32 [4096, 8], P(('uly', 'blk')), may hold values from 0 to 63, all different within a row; in each aligned block of 128 rows (0 to 127, 128 to 255, ...) at most 17 rows name the same one
- doc_starts: int32 [5], replicated, may hold values from 0 to 3378, as said below
Outputs:
- output: bfloat16 [4096, 2048], P(('uly', 'blk'))
- hidden_grad: float32 [4096, 2048], P(('uly', 'blk'))
- attn_gain_grad: float32 [2048], P(('uly', 'blk'))
- query_weight_grad: float32 [2048, 2048], P(('uly', 'blk'))
- key_weight_grad: float32 [2048, 2048], P(('uly', 'blk'))
- value_weight_grad: float32 [2048, 2048], P(('uly', 'blk'))
- out_weight_grad: float32 [2048, 2048], P(('uly', 'blk'))
- query_gain_grad: float32 [2048], P(('uly', 'blk'))
- key_gain_grad: float32 [2048], P(('uly', 'blk'))
- ffn_gain_grad: float32 [2048], P(('uly', 'blk'))
- router_weight_grad: float32 [2048, 64], P(('uly', 'blk'))
- expert_weights_grad: float32 [64, 3, 2048, 1024], P('uly', None, None, 'blk')
The draws below stay inside these ranges and needn't reach their ends.
Inputs may be any that keep to these rules, and one draw needn't show every extreme that they name: `routes`: each row names 8 different experts; at most 17 of the rows of one device name the same expert. `doc_starts`: increasing, the first 0.
All inputs are finite; a program needn't handle non-finite values.
Results may differ from the reference program's by a relative error of at most 0.02.
Values may be sent and summed in bfloat16 or wider, within the bound.
A program may use at most 512 MiB of HBM per device.

```python
import math
import jax
import jax.numpy as jnp
import numpy as np
from jax import lax

D = 2048
HEADS = 16
HEAD_DIM = 128
EXPERTS = 64
FF = 1024
TOPK = 8
DOCS = 5
TOK_DEV = 128
CAP = 17
TOKENS = 4096


def draw_expert_weights(key, part):
    key = jax.random.fold_in(key, 11)
    base = jax.random.truncated_normal(key, -4.0, 4.0, (EXPERTS, 3, D, FF), jnp.float32)
    scaling = jnp.array([D ** (-0.5), D ** (-0.5), 0.25], jnp.float32)
    return (base * scaling[None, :, None, None]).astype(jnp.bfloat16)


def draw_doc_starts(key, part):
    key = jax.random.fold_in(key, 7)
    jitter = TOKENS // 40
    spaced = jnp.arange(1, DOCS).astype(jnp.int32) * TOKENS // DOCS
    offsets = jax.random.randint(key, (DOCS - 1,), -jitter, jitter + 1).astype(jnp.int32)
    last_slot = jnp.arange(DOCS - 1).astype(jnp.int32) == DOCS - 2
    offsets = jnp.where(last_slot, jnp.int32(jitter), offsets).astype(jnp.int32)
    rest = spaced + offsets
    return jnp.concatenate([jnp.zeros((1,), jnp.int32), rest]).astype(jnp.int32)


def steps_of(rng, shape, cuts, least, largest):
    def one(dim, parts):
        heights = jax.random.uniform(jax.random.fold_in(jax.random.fold_in(rng, 6), dim), (parts,), jnp.float32, least / len(cuts), largest / len(cuts))
        return jnp.repeat(jnp.exp(heights), shape[dim] // parts).reshape((-1,) + (1,) * (len(shape) - dim - 1))

    factor_of = one(*cuts[0])
    for cut in cuts[1:]:
        factor_of = factor_of * one(*cut)
    return factor_of


def assign_block(stream_key, own, number, rows, number_of, top, reach, slope):
    sequence = jax.random.permutation(stream_key, number_of)
    packed, ordinary = portions_of(number_of, rows * top, reach, slope, True), portions_of(number_of, rows * top, reach, slope, False)
    places = jnp.arange(number_of)

    def named(sizes, offset_by):
        used = int((sizes > 0).sum())
        fixed = max(1, used // 4)
        shifted = fixed + (places - fixed + offset_by * (used - fixed)) % max(1, number_of - fixed)
        return jnp.zeros((number_of,), jnp.int32).at[sequence[jnp.where(places < fixed, places, shifted)]].set(jnp.asarray(sizes, jnp.int32))

    sizes = jnp.where(number % 4 == 0, named(packed, number // 4), named(ordinary, number - number // 4 - 1))
    mixed = jax.random.permutation(jax.random.fold_in(own, 3), number_of)
    giver, receiver = mixed[0:number_of // 2 * 2:2], mixed[1:number_of // 2 * 2:2]
    slack = jnp.minimum(sizes[giver] - 1, reach - sizes[receiver]) // 2
    slack = jnp.where((giver == sequence[0]) | (receiver == sequence[0]) | (sizes[receiver] == 0), 0, jnp.maximum(slack, 0))
    shifted = jax.random.randint(jax.random.fold_in(own, 4), (number_of // 2,), 0, 1 << 20) % (slack + 1)
    sizes = sizes.at[giver].add(-shifted).at[receiver].add(shifted)
    items = jnp.searchsorted(jnp.cumsum(sizes), jnp.arange(rows * top), side="right").astype(jnp.int32)
    table = items.reshape(top, rows).T
    table = table[jax.random.permutation(jax.random.fold_in(own, 1), rows)]
    offset_by = jax.random.randint(jax.random.fold_in(own, 2), (rows, 1), 0, top)
    return jnp.take_along_axis(table, (jnp.arange(top)[None, :] + offset_by) % top, axis=1)


def portions_of(amount, total, limit, skew, full):
    loads = [(1 << 20) // math.isqrt(grade ** skew) + 1 for grade in range(1, amount + 1)]
    largest = limit if full else min(limit, max(-(-total // amount), total * loads[0] // sum(loads)))
    least = 1 if total - largest >= amount - 1 else 0
    given, spare = [largest] + [least] * (amount - 1), total - largest - least * (amount - 1)
    while spare > 0:
        candidates = [i for i in range(1, amount) if given[i] < largest] or [i for i in range(1, amount) if given[i] < limit]
        mass, remaining = sum([loads[i] for i in candidates]), spare
        for i in candidates:
            addition = min(limit - given[i], max(1, remaining * loads[i] // mass), spare)
            given[i] = given[i] + addition
            spare = spare - addition
    return np.array(given)


def bell_draw(own_key, shape, spread, reach, pieces=(), dtype=jnp.bfloat16):
    values = spread * jax.random.normal(own_key, shape, jnp.float32)
    if pieces:
        values = values * steps_of(own_key, shape, pieces, -0.22, 0.18)
    return jnp.clip(values, -reach, reach).astype(dtype)


def setup_inputs(seed: int = 0) -> dict:
    splits = jax.random.split(jax.random.key(seed), 15)
    hidden_in = bell_draw(splits[0], (TOKENS, D), 1.0, 6.0, ((0, 32),))
    out_grad = bell_draw(splits[1], (TOKENS, D), 1.0, 6.0, ((0, 32),))
    attn_gain = jnp.clip(1.0 + 0.1 * jax.random.normal(splits[2], (D,), jnp.float32), 0.5, 1.5).astype(jnp.bfloat16)
    query_weight = bell_draw(splits[3], (D, D), D ** -0.5, 0.125, ((0, 32),))
    key_weight = bell_draw(splits[4], (D, D), D ** -0.5, 0.125, ((0, 32),))
    value_weight = bell_draw(splits[5], (D, D), D ** -0.5, 0.125, ((0, 32),))
    out_weight = bell_draw(splits[6], (D, D), (max(D // 128, 1)) ** -0.5, 1.5, ((0, 32),))
    query_gain = jnp.clip(1.0 + 0.1 * jax.random.normal(splits[7], (D,), jnp.float32), 0.5, 1.5).astype(jnp.bfloat16)
    key_gain = jnp.clip(1.0 + 0.1 * jax.random.normal(splits[8], (D,), jnp.float32), 0.5, 1.5).astype(jnp.bfloat16)
    ffn_gain = jnp.clip(1.0 + 0.1 * jax.random.normal(splits[9], (D,), jnp.float32), 0.5, 1.5).astype(jnp.bfloat16)
    router_weight = bell_draw(splits[10], (D, EXPERTS), (4 * D) ** -0.5, 0.0625, ((0, 32),))
    expert_weights = draw_expert_weights(jax.random.fold_in(splits[14], 71), 0)
    routes_keys = jax.random.split(jax.random.fold_in(splits[12], 1), TOKENS // TOK_DEV)
    routes_turns = jax.random.permutation(jax.random.fold_in(splits[12], 3), TOKENS // TOK_DEV)
    routes = jax.vmap(lambda own, number: assign_block(jax.random.fold_in(splits[12], 2), own, number, TOK_DEV, EXPERTS, TOPK, CAP, 1))(routes_keys, routes_turns).reshape((TOKENS, TOPK))
    doc_starts = draw_doc_starts(jax.random.fold_in(splits[14], 71), 0)
    return {"hidden_in": hidden_in, "out_grad": out_grad, "attn_gain": attn_gain, "query_weight": query_weight, "key_weight": key_weight, "value_weight": value_weight, "out_weight": out_weight, "query_gain": query_gain, "key_gain": key_gain, "ffn_gain": ffn_gain, "router_weight": router_weight, "expert_weights": expert_weights, "routes": routes, "doc_starts": doc_starts}


EPS = 1e-05
THETA = 10000.0
NEG = -1e+30
HIGH = lax.Precision.HIGHEST

@jax.custom_vjp
def low(v):
    return lax.optimization_barrier(v.astype(jnp.bfloat16)).astype(jnp.float32)

@jax.custom_vjp
def low_back(v):
    return v

def low_keep(v):
    return (low(v), None)

def low_pass(kept, grad):
    return (grad,)

def back_keep(v):
    return (v, None)

def back_low(kept, grad):
    return (low(grad),)
low.defvjp(low_keep, low_pass)
low_back.defvjp(back_keep, back_low)

def rms(values, gain_row):
    return values * lax.rsqrt(lax.optimization_barrier(jnp.mean(values * values, axis=-1, keepdims=True)) + EPS) * gain_row

def tables(count):
    halfway = HEAD_DIM // 2
    frequency = THETA ** (-(jnp.arange(halfway).astype(jnp.float32) * 2.0 / HEAD_DIM))
    angles = jnp.arange(count).astype(jnp.float32)[:, None] * frequency[None, :]
    cosine = jnp.concatenate([jnp.cos(angles), jnp.cos(angles)], axis=1)[:, None, :]
    sine_table = jnp.concatenate([jnp.sin(angles), jnp.sin(angles)], axis=1)[:, None, :]
    return (cosine, sine_table)

def rotary(values, cosine, sine_table):
    halfway = values.shape[-1] // 2
    turned = jnp.concatenate([-values[..., halfway:], values[..., :halfway]], axis=-1)
    return values * cosine + turned * sine_table

def one_head(query_rows, key_rows, value_rows, allowed):
    scores = low_back(jnp.dot(query_rows, key_rows.T, precision=HIGH) * HEAD_DIM ** (-0.5))
    scores = jnp.where(allowed, scores, NEG)
    row_max = lax.optimization_barrier(jnp.max(scores, axis=1, keepdims=True))
    weights = jnp.exp(scores - row_max)
    weights = weights / lax.optimization_barrier(jnp.sum(weights, axis=1, keepdims=True))
    return jnp.dot(low(weights), value_rows, precision=HIGH)

def layer(hidden, attn_gain, query_weight, key_weight, value_weight, out_weight, query_gain, key_gain, ffn_gain, router_weight, expert_weights, chosen, allowed, cosine, sine_table):
    normed = low(rms(hidden, attn_gain))
    query = low_back(jnp.dot(normed, query_weight, precision=HIGH))
    keyed = low_back(jnp.dot(normed, key_weight, precision=HIGH))
    valued = low_back(low(jnp.dot(normed, value_weight, precision=HIGH)))
    query = rms(query, query_gain).reshape(TOKENS, HEADS, HEAD_DIM)
    keyed = rms(keyed, key_gain).reshape(TOKENS, HEADS, HEAD_DIM)
    query = low_back(low(rotary(query, cosine, sine_table)))
    keyed = low_back(low(rotary(keyed, cosine, sine_table)))
    valued = valued.reshape(TOKENS, HEADS, HEAD_DIM)

    def head_step(head_parts):
        return one_head(head_parts[0], head_parts[1], head_parts[2], allowed)
    mixed = lax.map(jax.checkpoint(head_step), (query.transpose(1, 0, 2), keyed.transpose(1, 0, 2), valued.transpose(1, 0, 2)))
    mixed = low_back(low(mixed.transpose(1, 0, 2).reshape(TOKENS, D)))
    residual = hidden + low_back(jnp.dot(mixed, out_weight, precision=HIGH))
    second = low(rms(residual, ffn_gain))
    logits = low_back(jnp.dot(second, router_weight, precision=HIGH))
    probabilities = jax.nn.softmax(logits, axis=-1)
    gate_values = probabilities * chosen

    def expert_step(moe_total, expert_pair):
        weights, gate_column = expert_pair
        entry_rows = low_back(second)
        gate_pre = low_back(jnp.dot(entry_rows, weights[0], precision=HIGH))
        up_value = low_back(jnp.dot(entry_rows, weights[1], precision=HIGH))
        inner_low = low(jax.nn.silu(gate_pre) * up_value)
        result = low_back(low(jnp.dot(inner_low, weights[2].T, precision=HIGH)))
        return (moe_total + gate_column[:, None] * result, None)
    moe_total, unused = lax.scan(jax.checkpoint(expert_step), jnp.zeros((TOKENS, D), jnp.float32), (expert_weights, gate_values.T))
    return residual + moe_total

def reference(hidden_in, out_grad, attn_gain, query_weight, key_weight, value_weight, out_weight, query_gain, key_gain, ffn_gain, router_weight, expert_weights, routes, doc_starts):
    position = jnp.arange(TOKENS).astype(jnp.int32)
    document = lax.optimization_barrier(jnp.sum((doc_starts[None, :] <= position[:, None]).astype(jnp.int32), axis=1))
    allowed = (position[None, :] <= position[:, None]) & (document[None, :] == document[:, None])
    expert_iota = jnp.arange(EXPERTS).astype(jnp.int32)
    chosen = lax.optimization_barrier(jnp.sum((routes[:, :, None] == expert_iota[None, None, :]).astype(jnp.float32), axis=1))
    cosine, sine_table = tables(TOKENS)

    def forward(hidden, gain_attn, weight_query, weight_key, weight_value, weight_out, gain_query, gain_key, gain_ffn, weight_router, weight_experts):
        return layer(hidden, gain_attn, weight_query, weight_key, weight_value, weight_out, gain_query, gain_key, gain_ffn, weight_router, weight_experts, chosen, allowed, cosine, sine_table)
    output, pullback = jax.vjp(forward, hidden_in.astype(jnp.float32), attn_gain.astype(jnp.float32), query_weight.astype(jnp.float32), key_weight.astype(jnp.float32), value_weight.astype(jnp.float32), out_weight.astype(jnp.float32), query_gain.astype(jnp.float32), key_gain.astype(jnp.float32), ffn_gain.astype(jnp.float32), router_weight.astype(jnp.float32), expert_weights.astype(jnp.float32))
    gradients = pullback(out_grad.astype(jnp.float32))
    return (output.astype(jnp.bfloat16), gradients[0], gradients[1], gradients[2], gradients[3], gradients[4], gradients[5], gradients[6], gradients[7], gradients[8], gradients[9], gradients[10])
```

```python
import functools

import jax
import jax.numpy as jnp
from jax import lax
from jax.experimental import pallas as pl
from jax.experimental.pallas import tpu as pltpu
from jax.sharding import PartitionSpec as P

HEADS = 16
HEAD_DIM = 128
EXPERTS = 64
CAP = 17

EPS = 1e-05
THETA = 10000.0
NEG = -1e30
FIRST_DIM = (((0,), (0,)), ((), ()))
LAST_DIM = (((1,), (1,)), ((), ()))
ALL = ("uly", "blk")
F32 = jnp.float32
BF16 = jnp.bfloat16
VMEM_BYTES = 56 * 1024 * 1024


def dot(a, b, dims=(((1,), (0,)), ((), ()))):
    return lax.dot_general(a, b, dims, preferred_element_type=F32)


def rotary_tables(position):
    halfway = HEAD_DIM // 2
    frequency = THETA ** (-(jnp.arange(halfway).astype(F32) * 2.0 / HEAD_DIM))
    angles = position.astype(F32)[:, None] * frequency[None, :]
    cosine = jnp.concatenate([jnp.cos(angles), jnp.cos(angles)], axis=1)
    sine = jnp.concatenate([jnp.sin(angles), jnp.sin(angles)], axis=1)
    return cosine, sine


def rotate_forward(values, cosine, sine):
    halfway = values.shape[-1] // 2
    turned = jnp.concatenate([-values[..., halfway:], values[..., :halfway]], axis=-1)
    return values * cosine + turned * sine


def rotate_backward(upstream, cosine, sine):
    halfway = upstream.shape[-1] // 2
    moved = upstream * sine
    turned = jnp.concatenate([moved[..., halfway:], -moved[..., :halfway]], axis=-1)
    return upstream * cosine + turned


def norm_scale(values):
    return lax.rsqrt(jnp.mean(values * values, axis=-1, keepdims=True) + EPS)


MESH = pl.DeviceIdType.MESH


def _send(src, dst, send_sem, recv_sem, to):
    copy = pltpu.make_async_remote_copy(
        src_ref=src, dst_ref=dst, send_sem=send_sem, recv_sem=recv_sem, device_id=to, device_id_type=MESH
    )
    copy.start()
    return copy


def _expect(ref, sem, here):
    pltpu.make_async_remote_copy(
        src_ref=ref, dst_ref=ref, send_sem=sem, recv_sem=sem, device_id=here, device_id_type=MESH
    ).wait_recv()


def _sent(ref, sem, here):
    pltpu.make_async_remote_copy(
        src_ref=ref, dst_ref=ref, send_sem=sem, recv_sem=sem, device_id=here, device_id_type=MESH
    ).wait_send()


def _greet(u, z, planes, line, depth):
    barrier = pltpu.get_barrier_semaphore()
    for bit in planes:
        pl.semaphore_signal(barrier, inc=1, device_id=(u ^ bit, z), device_id_type=MESH)
    if line:

        @pl.when(z > 0)
        def _():
            pl.semaphore_signal(barrier, inc=1, device_id=(u, z - 1), device_id_type=MESH)

        @pl.when(z < depth - 1)
        def _():
            pl.semaphore_signal(barrier, inc=1, device_id=(u, z + 1), device_id_type=MESH)

    ends = jnp.where((z == 0) | (z == depth - 1), 1, 2) if line else 0
    pl.semaphore_wait(barrier, len(planes) + ends)


def _line_order(z):
    second = jnp.where(z == 0, 1, z - 1)
    third = jnp.where(z == 0, 2, jnp.where(z == 3, 1, z + 1))
    fourth = jnp.where(z < 2, 3, 0)
    return (z, second, third, fourth)


def _gather_all_kernel(x_ref, o_ref, own_sem, z_send, z_recv, p_send, p_recv, c_send, c_recv):
    u, z = lax.axis_index("uly"), lax.axis_index("blk")
    depth = 4
    half = x_ref.shape[0] // 2
    halves = (pl.ds(0, half), pl.ds(half, half))
    here = (u, z)
    _greet(u, z, (1, 2, 4), True, depth)
    own = pltpu.make_async_copy(x_ref, o_ref.at[u * depth + z], own_sem)
    own.start()
    order = _line_order(z)

    def block(who, level):
        return o_ref.at[who * depth + level]

    def part(who, level, h):
        return o_ref.at[who * depth + level, halves[h]]

    first, then = (2, 4), (4, 2)

    def along(level, source, step):
        @pl.when((z > 0) & (level >= z))
        def _():
            step(source, 0, level, (u, z - 1))

        @pl.when((z < depth - 1) & (level <= z))
        def _():
            step(source, 1, level, (u, z + 1))

    def go(source, way, level, to):
        _send(source, block(u, level), z_send.at[way, level], z_recv.at[level], to)

    def gone(source, way, level, to):
        _sent(source, z_send.at[way, level], here)

    def across(level, source):
        for h in range(2):
            _send(
                source.at[halves[h]], part(u, level, h), p_send.at[level, h, 0], p_recv.at[level, h, 0], (u ^ first[h], z)
            )
        _send(source, block(u, level), c_send.at[level, 0], c_recv.at[level, 0], (u ^ 1, z))

    def onward(level, source):
        for h in range(2):
            _expect(part(u ^ first[h], level, h), p_recv.at[level, h, 0], here)
            to = (u ^ then[h], z)
            _send(source.at[halves[h]], part(u, level, h), p_send.at[level, h, 1], p_recv.at[level, h, 1], to)
            _send(
                part(u ^ first[h], level, h),
                part(u ^ first[h], level, h),
                p_send.at[level, h, 2],
                p_recv.at[level, h, 2],
                to,
            )

    def share(level):
        for h in range(2):
            _expect(part(u ^ then[h], level, h), p_recv.at[level, h, 1], here)
            _expect(part(u ^ 6, level, h), p_recv.at[level, h, 2], here)
        for i, bit in enumerate((2, 4, 6)):
            _send(block(u ^ bit, level), block(u ^ bit, level), c_send.at[level, i + 1], c_recv.at[level, i + 1], (u ^ 1, z))

    sources = [x_ref] + [block(u, order[i]) for i in range(1, 4)]
    along(z, x_ref, go)
    across(z, x_ref)
    for i in range(1, 4):
        _expect(block(u, order[i]), z_recv.at[order[i]], here)
        along(order[i], sources[i], go)
        across(order[i], sources[i])
        onward(order[i - 1], sources[i - 1])
        if i >= 2:
            share(order[i - 2])
    onward(order[3], sources[3])
    share(order[2])
    share(order[3])
    for i in range(4):
        level = order[i]
        along(level, sources[i], gone)
        for h in range(2):
            for k in range(3):
                _sent(part(u, level, h), p_send.at[level, h, k], here)
        for k, bit in enumerate((0, 2, 4, 6)):
            _sent(block(u, level), c_send.at[level, k], here)
            _expect(block(u ^ 1 ^ bit, level), c_recv.at[level, k], here)
    own.wait()


def gather_all(x, collective_id):
    U, Z = lax.axis_size("uly"), lax.axis_size("blk")
    if (U, Z) != (8, 4):
        return lax.all_gather(x, ALL, axis=0, tiled=True)
    T, D = x.shape
    dma = pltpu.SemaphoreType.DMA
    any_space = pl.BlockSpec(memory_space=pl.ANY)
    out = pl.pallas_call(
        _gather_all_kernel,
        out_shape=jax.ShapeDtypeStruct((U * Z, T, D), x.dtype),
        in_specs=[any_space],
        out_specs=any_space,
        scratch_shapes=[
            dma,
            dma((2, 4)),
            dma((4,)),
            dma((4, 2, 3)),
            dma((4, 2, 3)),
            dma((4, 4)),
            dma((4, 4)),
        ],
        compiler_params=pltpu.CompilerParams(collective_id=collective_id, has_side_effects=True),
        cost_estimate=pl.CostEstimate(flops=0, bytes_accessed=2 * U * Z * T * D * 2, transcendentals=0),
    )(x)
    return out.reshape(U * Z * T, D)


def _accumulate(target, source, rows):
    strip = 16

    def step(i, _):
        at = pl.ds(pl.multiple_of(i * strip, strip), strip)
        target[at, :] = target[at, :] + source[at, :]
        return 0

    lax.fori_loop(0, rows // strip, step, 0)


def _scatter_all_kernel(
    x_ref, o_ref, work, c_buf, p_buf, q_buf, z_buf, load_sem, c_send, c_recv, p_send, p_recv, q_send, q_recv, z_send, z_recv
):
    u, z = lax.axis_index("uly"), lax.axis_index("blk")
    depth = 4
    T = x_ref.shape[1]
    half = T // 2
    halves = (pl.ds(0, half), pl.ds(half, half))
    here = (u, z)
    order = tuple(reversed(_line_order(z)))
    _greet(u, z, (1, 2, 4), True, depth)
    chips = (0, 2, 4, 6)

    def sibling(i, bit):
        return x_ref.at[(u ^ bit ^ 1) * depth + order[i]]

    def load(i, k, bit):
        return pltpu.make_async_copy(x_ref.at[(u ^ bit) * depth + order[i]], work.at[i, k], load_sem.at[i, k])

    def core(i):
        for k, bit in enumerate(chips):
            _send(sibling(i, bit), c_buf.at[i, k], c_send.at[i, k], c_recv.at[i, k], (u ^ 1, z))
            load(i, k, bit).start()

    first, then = (4, 2), (2, 4)

    def add_core(i):
        for k in (3, 2, 1, 0):
            load(i, k, chips[k]).wait()
            _expect(c_buf.at[i, k], c_recv.at[i, k], here)
            _accumulate(work.at[i, k], c_buf.at[i, k], T)
        for h in range(2):
            to = (u ^ first[h], z)
            for j, bit in enumerate((first[h], 6)):
                k = chips.index(bit)
                _send(work.at[i, k, halves[h]], p_buf.at[i, h, j], p_send.at[i, h, j], p_recv.at[i, h, j], to)

    def add_first(i):
        for h in range(2):
            k = chips.index(then[h])
            _expect(p_buf.at[i, h, 1], p_recv.at[i, h, 1], here)
            _accumulate(work.at[i, k, halves[h]], p_buf.at[i, h, 1], half)
            _send(work.at[i, k, halves[h]], q_buf.at[i, h], q_send.at[i, h], q_recv.at[i, h], (u ^ then[h], z))
            _expect(p_buf.at[i, h, 0], p_recv.at[i, h, 0], here)
            _accumulate(work.at[i, 0, halves[h]], p_buf.at[i, h, 0], half)

    def add_then(i):
        for h in range(2):
            _expect(q_buf.at[i, h], q_recv.at[i, h], here)
            _accumulate(work.at[i, 0, halves[h]], q_buf.at[i, h], half)

    def line(i):
        level = order[i]

        @pl.when((level > z) & (z > 0))
        def _():
            _expect(z_buf.at[0, level], z_recv.at[0, level], here)
            _accumulate(work.at[i, 0], z_buf.at[0, level], T)

        @pl.when((level < z) & (z < depth - 1))
        def _():
            _expect(z_buf.at[1, level], z_recv.at[1, level], here)
            _accumulate(work.at[i, 0], z_buf.at[1, level], T)

        @pl.when(level > z)
        def _():
            _send(work.at[i, 0], z_buf.at[0, level], z_send.at[i], z_recv.at[0, level], (u, z + 1))

        @pl.when(level < z)
        def _():
            _send(work.at[i, 0], z_buf.at[1, level], z_send.at[i], z_recv.at[1, level], (u, z - 1))

    for i in range(4):
        core(i)
    for i in range(4):
        add_core(i)
        if i >= 1:
            add_first(i - 1)
        if i >= 2:
            add_then(i - 2)
            line(i - 2)
    add_first(3)
    add_then(2)
    line(2)
    add_then(3)

    @pl.when(z > 0)
    def _():
        _expect(z_buf.at[0, z], z_recv.at[0, z], here)
        _accumulate(work.at[3, 0], z_buf.at[0, z], T)

    @pl.when(z < depth - 1)
    def _():
        _expect(z_buf.at[1, z], z_recv.at[1, z], here)
        _accumulate(work.at[3, 0], z_buf.at[1, z], T)

    o_ref[...] = work[3, 0]
    for i in range(4):
        for k in range(4):
            _sent(c_buf.at[i, k], c_send.at[i, k], here)
        for h in range(2):
            for j in range(2):
                _sent(p_buf.at[i, h, j], p_send.at[i, h, j], here)
            _sent(q_buf.at[i, h], q_send.at[i, h], here)
        if i < 3:
            _sent(work.at[i, 0], z_send.at[i], here)


def scatter_all(x, collective_id):
    U, Z = lax.axis_size("uly"), lax.axis_size("blk")
    if (U, Z) != (8, 4):
        return lax.psum_scatter(x, ALL, scatter_dimension=0, tiled=True)
    N, D = x.shape
    T = N // (U * Z)
    half = T // 2
    dma = pltpu.SemaphoreType.DMA
    return pl.pallas_call(
        _scatter_all_kernel,
        out_shape=jax.ShapeDtypeStruct((T, D), x.dtype),
        in_specs=[pl.BlockSpec(memory_space=pl.ANY)],
        out_specs=pl.BlockSpec(memory_space=pltpu.VMEM),
        scratch_shapes=[
            pltpu.VMEM((4, 4, T, D), BF16),
            pltpu.VMEM((4, 4, T, D), BF16),
            pltpu.VMEM((4, 2, 2, half, D), BF16),
            pltpu.VMEM((4, 2, half, D), BF16),
            pltpu.VMEM((2, 4, T, D), BF16),
            dma((4, 4)),
            dma((4, 4)),
            dma((4, 4)),
            dma((4, 2, 2)),
            dma((4, 2, 2)),
            dma((4, 2)),
            dma((4, 2)),
            dma((4,)),
            dma((2, 4)),
        ],
        compiler_params=pltpu.CompilerParams(
            collective_id=collective_id, has_side_effects=True, vmem_limit_bytes=VMEM_BYTES
        ),
        cost_estimate=pl.CostEstimate(flops=N * D * 2, bytes_accessed=2 * N * D * 2, transcendentals=0),
    )(x.reshape(U * Z, T, D))


def _gather_small_kernel(*refs, count):
    xs, outs = refs[:count], refs[count : 2 * count]
    own_sem, z_send, z_recv, u_send, u_recv = refs[2 * count :]
    u, z = lax.axis_index("uly"), lax.axis_index("blk")
    here = (u, z)
    barrier = pltpu.get_barrier_semaphore()
    for k in range(1, 4):
        pl.semaphore_signal(barrier, inc=1, device_id=(u, z ^ k), device_id_type=MESH)
    for k in range(1, 8):
        pl.semaphore_signal(barrier, inc=1, device_id=(u ^ k, z), device_id_type=MESH)
    pl.semaphore_wait(barrier, 10)
    for a, (x, o) in enumerate(zip(xs, outs)):
        pltpu.make_async_copy(x, o.at[u, z], own_sem.at[a]).start()
        for k in range(1, 4):
            _send(x, o.at[u, z], z_send.at[a, k], z_recv.at[a, k], (u, z ^ k))
    for a, (x, o) in enumerate(zip(xs, outs)):
        pltpu.make_async_copy(x, o.at[u, z], own_sem.at[a]).wait()
        for k in range(1, 4):
            _expect(o.at[u, z ^ k], z_recv.at[a, k], here)
        for k in range(1, 8):
            _send(o.at[u], o.at[u], u_send.at[a, k], u_recv.at[a, k], (u ^ k, z))
    for a, (x, o) in enumerate(zip(xs, outs)):
        for k in range(1, 4):
            _sent(x, z_send.at[a, k], here)
        for k in range(1, 8):
            _sent(o.at[u], u_send.at[a, k], here)
            _expect(o.at[u ^ k], u_recv.at[a, k], here)


def gather_small(xs, collective_id):
    U, Z = lax.axis_size("uly"), lax.axis_size("blk")
    if (U, Z) != (8, 4):
        return [lax.all_gather(x, ALL).reshape((U, Z) + x.shape) for x in xs]
    dma = pltpu.SemaphoreType.DMA
    space = pl.BlockSpec(memory_space=pl.ANY)
    n = len(xs)
    return pl.pallas_call(
        functools.partial(_gather_small_kernel, count=n),
        out_shape=[jax.ShapeDtypeStruct((U, Z) + x.shape, x.dtype) for x in xs],
        in_specs=[space] * n,
        out_specs=[space] * n,
        scratch_shapes=[dma((n,)), dma((n, 4)), dma((n, 4)), dma((n, 8)), dma((n, 8))],
        compiler_params=pltpu.CompilerParams(collective_id=collective_id, has_side_effects=True),
    )(*xs)


def gather_uly(x):
    return lax.all_gather(x, "uly", axis=0, tiled=True)


def scatter_uly(x):
    return lax.psum_scatter(x, "uly", scatter_dimension=0, tiled=True)


def gather_blk(x):
    return lax.all_gather(x, "blk", axis=0, tiled=True)


def _row_limits(doc_ref, first, rows):
    position = first + lax.broadcasted_iota(jnp.int32, (rows, 1), 0)
    start = jnp.zeros_like(position)
    lowest = jnp.int32(0)
    for d in range(doc_ref.shape[0]):
        begin = doc_ref[d]
        start = jnp.where(begin <= position, jnp.maximum(start, begin), start)
        lowest = jnp.where(begin <= first, jnp.maximum(lowest, begin), lowest)
    return position, start, lowest


def _scores(query, key, position, start, key_first, scaling):
    raw = dot(query, key, LAST_DIM) * scaling
    key_position = key_first + lax.broadcasted_iota(jnp.int32, raw.shape, 1)
    return jnp.where((key_position <= position) & (key_position >= start), raw, NEG)


def _attend_kernel(index_ref, doc_ref, q_ref, k_ref, v_ref, o_ref, log_ref, *, chunk, scaling):
    rows = q_ref.shape[0]
    heads = q_ref.shape[1] // HEAD_DIM
    first = (pl.program_id(0) * index_ref[1] + index_ref[0]) * rows
    position, start, lowest = _row_limits(doc_ref, first, rows)

    def step(i, state):
        at = pl.multiple_of(i * chunk, chunk)
        new = []
        for h in range(heads):
            cols = pl.ds(h * HEAD_DIM, HEAD_DIM)
            top, total, out = state[h]
            scores = _scores(q_ref[:, cols], k_ref[pl.ds(at, chunk), cols], position, start, at, scaling)
            now = jnp.maximum(top, jnp.max(scores, axis=1, keepdims=True))
            weights = jnp.exp(scores - now)
            fade = jnp.exp(top - now)
            total = total * fade + jnp.sum(weights, axis=1, keepdims=True)
            out = out * fade + dot(weights.astype(BF16), v_ref[pl.ds(at, chunk), cols])
            new.append((now, total, out))
        return tuple(new)

    zero = (
        jnp.full((rows, 1), NEG, F32),
        jnp.zeros((rows, 1), F32),
        jnp.zeros((rows, HEAD_DIM), F32),
    )
    last = first + rows
    state = lax.fori_loop(lowest // chunk, (last + chunk - 1) // chunk, step, (zero,) * heads)
    for h in range(heads):
        cols = pl.ds(h * HEAD_DIM, HEAD_DIM)
        top, total, out = state[h]
        o_ref[:, cols] = out / total
        log_ref[:, cols] = jnp.broadcast_to(top + jnp.log(total), (rows, HEAD_DIM))


def _attend_back_kernel(
    index_ref, doc_ref, q_ref, g_ref, o_ref, log_ref, k_ref, v_ref, dq_ref, dk_ref, dv_ref, dk_sum, dv_sum, *, chunk, scaling
):
    rows = q_ref.shape[0]
    heads = q_ref.shape[1] // HEAD_DIM
    first = (pl.program_id(0) * index_ref[1] + index_ref[0]) * rows
    position, start, lowest = _row_limits(doc_ref, first, rows)

    @pl.when(pl.program_id(0) == 0)
    def _():
        dk_sum[...] = jnp.zeros_like(dk_sum)
        dv_sum[...] = jnp.zeros_like(dv_sum)

    deltas, logs = [], []
    for h in range(heads):
        cols = pl.ds(h * HEAD_DIM, HEAD_DIM)
        deltas.append(jnp.sum(g_ref[:, cols].astype(F32) * o_ref[:, cols], axis=1, keepdims=True))
        logs.append(log_ref[:, cols][:, :1])

    def step(i, state):
        at = pl.multiple_of(i * chunk, chunk)
        new = []
        for h in range(heads):
            cols = pl.ds(h * HEAD_DIM, HEAD_DIM)
            query, grad = q_ref[:, cols], g_ref[:, cols]
            key = k_ref[pl.ds(at, chunk), cols]
            scores = _scores(query, key, position, start, at, scaling)
            weights = jnp.exp(scores - logs[h])
            weight_grad = dot(grad, v_ref[pl.ds(at, chunk), cols], LAST_DIM)
            score_grad = (weights * (weight_grad - deltas[h])).astype(BF16)
            dv_sum[pl.ds(at, chunk), cols] += dot(weights.astype(BF16), grad, FIRST_DIM)
            dk_sum[pl.ds(at, chunk), cols] += dot(score_grad, query, FIRST_DIM)
            new.append(state[h] + dot(score_grad, key))
        return tuple(new)

    last = first + rows
    state = lax.fori_loop(
        lowest // chunk, (last + chunk - 1) // chunk, step, (jnp.zeros((rows, HEAD_DIM), F32),) * heads
    )
    for h in range(heads):
        dq_ref[:, pl.ds(h * HEAD_DIM, HEAD_DIM)] = (state[h] * scaling).astype(BF16)

    @pl.when(pl.program_id(0) == pl.num_programs(0) - 1)
    def _():
        dk_ref[...] = (dk_sum[...] * scaling).astype(BF16)
        dv_ref[...] = dv_sum[...].astype(BF16)


def _attention_specs(L, N, C, rows):
    block = pl.BlockSpec((rows, C), lambda i, *_: (i, 0))
    whole = pl.BlockSpec((N, C), lambda i, *_: (0, 0), pipeline_mode=pl.Buffered(1))
    return block, whole


def attention_forward(index, docs, query, key_all, value_all, rows, chunk):
    (L, C), N = query.shape, key_all.shape[0]
    block, whole = _attention_specs(L, N, C, rows)
    return pl.pallas_call(
        functools.partial(_attend_kernel, chunk=chunk, scaling=HEAD_DIM ** (-0.5)),
        out_shape=[jax.ShapeDtypeStruct((L, C), F32)] * 2,
        grid_spec=pltpu.PrefetchScalarGridSpec(
            num_scalar_prefetch=2, grid=(L // rows,), in_specs=[block, whole, whole], out_specs=[block, block]
        ),
        compiler_params=pltpu.CompilerParams(vmem_limit_bytes=VMEM_BYTES),
        cost_estimate=pl.CostEstimate(flops=4 * L * C * 1024, bytes_accessed=4 * N * C, transcendentals=L * 1024),
    )(index, docs, query, key_all, value_all)


def attention_backward(index, docs, query, grad, attended, logs, key_all, value_all, rows, chunk):
    (L, C), N = query.shape, key_all.shape[0]
    block, whole = _attention_specs(L, N, C, rows)
    return pl.pallas_call(
        functools.partial(_attend_back_kernel, chunk=chunk, scaling=HEAD_DIM ** (-0.5)),
        out_shape=[jax.ShapeDtypeStruct((L, C), BF16)] + [jax.ShapeDtypeStruct((N, C), BF16)] * 2,
        grid_spec=pltpu.PrefetchScalarGridSpec(
            num_scalar_prefetch=2,
            grid=(L // rows,),
            in_specs=[block, block, block, block, whole, whole],
            out_specs=[block, whole, whole],
            scratch_shapes=[pltpu.VMEM((N, C), F32)] * 2,
        ),
        compiler_params=pltpu.CompilerParams(vmem_limit_bytes=VMEM_BYTES),
        cost_estimate=pl.CostEstimate(flops=10 * L * C * 1024, bytes_accessed=8 * N * C, transcendentals=L * 1024),
    )(index, docs, query, grad, attended, logs, key_all, value_all)


def body(
    hidden_in,
    out_grad,
    attn_gain,
    query_weight,
    key_weight,
    value_weight,
    out_weight,
    query_gain,
    key_gain,
    ffn_gain,
    router_weight,
    expert_weights,
    routes,
    doc_starts,
):
    U = lax.axis_size("uly")
    Z = lax.axis_size("blk")
    u = lax.axis_index("uly")
    z = lax.axis_index("blk")
    T, D = hidden_in.shape
    EL = expert_weights.shape[0]
    C = D // U
    L = U * T
    N = U * Z * T
    RW = query_weight.shape[0]

    gain_rows = attn_gain.astype(F32)[:, None]
    own_weights = jnp.stack([query_weight, key_weight, value_weight], axis=1).astype(F32)
    scaled_rows = (own_weights * gain_rows[:, :, None]).astype(BF16).reshape(RW, 3, U, C)
    swapped = lax.all_to_all(scaled_rows, "uly", split_axis=2, concat_axis=0, tiled=True)
    swapped = swapped.reshape(U, RW, 3 * C)
    qkv_weight = lax.all_gather(swapped, "blk", axis=1, tiled=True).reshape(D, 3 * C)
    out_rows = gather_blk(out_weight)
    head_gains = gather_blk(jnp.stack([query_gain, key_gain], axis=1)).astype(F32)
    gain_query, gain_key = head_gains[:, 0], head_gains[:, 1]
    router_pack = jnp.pad(jnp.concatenate([router_weight, ffn_gain[:, None]], axis=1), ((0, 0), (0, 127 - EXPERTS)))
    packed, routes_all = gather_small([router_pack, routes.T], 3)
    packed = packed.reshape(D, 128)
    weight_router = packed[:, :EXPERTS]
    gain_ffn = packed[:, EXPERTS].astype(F32)
    upstream_all = lax.all_gather(out_grad, ALL, axis=0, tiled=True)
    routes_all = routes_all.transpose(0, 1, 3, 2).reshape(N, -1)

    hidden = hidden_in.astype(F32)
    first_scale = norm_scale(hidden)
    first_rows = gather_uly((hidden * first_scale).astype(BF16))
    qkv_pre = dot(first_rows, qkv_weight)
    query_pre, key_pre, value_pre = qkv_pre[:, :C], qkv_pre[:, C : 2 * C], qkv_pre[:, 2 * C :]
    squares = jnp.stack([jnp.sum(query_pre * query_pre, axis=1), jnp.sum(key_pre * key_pre, axis=1)])
    scales = lax.rsqrt(lax.psum(squares, "uly") / D + EPS)
    query_scale, key_scale = scales[0][:, None], scales[1][:, None]
    local = jnp.arange(L, dtype=jnp.int32)
    qpos = (local // T * Z + z) * T + local % T
    cosine, sine = rotary_tables(qpos)
    cosine, sine = cosine[:, None, :], sine[:, None, :]

    def rotated(pre, scale, gain):
        return rotate_forward((pre * scale * gain).reshape(L, C // HEAD_DIM, HEAD_DIM), cosine, sine).reshape(L, C).astype(BF16)

    query_rot = rotated(query_pre, query_scale, gain_query)
    key_rot = rotated(key_pre, key_scale, gain_key)
    key_values = lax.all_gather(jnp.stack([key_rot, value_pre.astype(BF16)]).reshape(2, U, T, C), "blk", axis=2, tiled=False)
    key_all, value_all = key_values[0].reshape(N, C), key_values[1].reshape(N, C)
    index = jnp.stack([z, jnp.int32(Z)]).astype(jnp.int32)
    chunk = min(512, N)
    attended, logs = attention_forward(index, doc_starts, query_rot, key_all, value_all, T, chunk)
    attended_low = attended.astype(BF16)
    residual = hidden + scatter_uly(dot(attended_low, out_rows).astype(BF16)).astype(F32)

    second_scale = norm_scale(residual)
    second_low = (residual * second_scale * gain_ffn).astype(BF16)
    probabilities = jax.nn.softmax(dot(second_low, weight_router), axis=-1)
    second_all = gather_all(second_low, 1)

    group = min(512, N)
    groups = N // group
    slots = -(-(group // T * CAP) // 8) * 8
    own_experts = u * EL + jnp.arange(EL, dtype=jnp.int32)
    chosen = jnp.any(routes_all[:, :, None] == own_experts[None, None, :], axis=1)
    logits_all = dot(second_all, weight_router)
    probs_all = jax.nn.softmax(logits_all, axis=-1)
    gate_all = jnp.where(chosen, lax.dynamic_slice_in_dim(probs_all, u * EL, EL, 1), 0.0)
    chosen_groups = chosen.reshape(groups, group, EL).astype(jnp.int32)
    slot = jnp.cumsum(chosen_groups, axis=1) - 1
    slot = jnp.where(chosen_groups > 0, slot, -1).transpose(0, 2, 1)
    pick = (slot[:, :, None, :] == jnp.arange(slots, dtype=jnp.int32)[None, None, :, None]).astype(BF16)
    second_groups = second_all.reshape(groups, group, D)
    upstream_groups = upstream_all.reshape(groups, group, D)
    rows = groups * slots

    def picked(x):
        r = jnp.einsum("gert,gtd->egrd", pick, x, preferred_element_type=F32)
        return r.astype(BF16).reshape(EL, rows, D)

    entry_rows = picked(second_groups)
    upstream_rows = picked(upstream_groups)
    gate_rows = jnp.einsum(
        "gert,gte->egr", pick.astype(F32), gate_all.reshape(groups, group, EL), precision=lax.Precision.HIGHEST
    ).reshape(EL, rows, 1)
    gate_pre = jnp.einsum("erd,edf->erf", entry_rows, expert_weights[:, 0], preferred_element_type=F32)
    up_value = jnp.einsum("erd,edf->erf", entry_rows, expert_weights[:, 1], preferred_element_type=F32)
    back = jnp.einsum("erd,edf->erf", upstream_rows, expert_weights[:, 2], preferred_element_type=F32)
    sigmoid_gate = jax.nn.sigmoid(gate_pre)
    inner = gate_pre * sigmoid_gate * up_value
    gate_grad_rows = jnp.sum(inner * back, axis=2)
    inner_grad = back * gate_rows
    gate_pre_grad = (inner_grad * up_value * sigmoid_gate * (1.0 + gate_pre * (1.0 - sigmoid_gate))).astype(BF16)
    up_grad = (inner_grad * gate_pre * sigmoid_gate).astype(BF16)
    inner_gated = (inner * gate_rows).astype(BF16)
    out_rows_e = jnp.einsum("erf,edf->erd", inner_gated, expert_weights[:, 2], preferred_element_type=F32)
    entry_grad_rows = jnp.einsum("erf,edf->erd", gate_pre_grad, expert_weights[:, 0], preferred_element_type=F32)
    entry_grad_rows += jnp.einsum("erf,edf->erd", up_grad, expert_weights[:, 1], preferred_element_type=F32)

    def spread(x):
        return jnp.einsum(
            "gert,egrd->gtd", pick, x.astype(BF16).reshape(EL, groups, slots, D), preferred_element_type=F32
        ).reshape(N, D)

    gate_grad_all = jnp.einsum(
        "gert,egr->gte", pick.astype(F32), gate_grad_rows.reshape(EL, groups, slots), precision=lax.Precision.HIGHEST
    ).reshape(N, EL)
    expert_iota = jnp.arange(EXPERTS, dtype=jnp.int32)
    place = (own_experts[:, None] == expert_iota[None, :]).astype(F32)
    gate_grad_wide = jnp.dot(gate_grad_all, place, precision=lax.Precision.HIGHEST)
    gate_grad_wide = jnp.pad(gate_grad_wide, ((0, 0), (0, 128 - EXPERTS)))
    entry_part = jnp.concatenate([spread(entry_grad_rows), gate_grad_wide], axis=1).astype(BF16)
    entry_sum = scatter_all(entry_part, 2).astype(F32)
    out_sum = scatter_all(spread(out_rows_e).astype(BF16), 5).astype(F32)
    output = (residual + out_sum).astype(BF16)
    expert_grads = jnp.stack(
        [
            jnp.einsum("erd,erf->edf", entry_rows, gate_pre_grad, preferred_element_type=F32),
            jnp.einsum("erd,erf->edf", entry_rows, up_grad, preferred_element_type=F32),
            jnp.einsum("erd,erf->edf", upstream_rows, inner_gated, preferred_element_type=F32),
        ],
        axis=1,
    )

    second_grad, prob_grad = entry_sum[:, :D], entry_sum[:, D : D + EXPERTS]
    logit_grad = (
        probabilities * (prob_grad - jnp.sum(probabilities * prob_grad, axis=1, keepdims=True))
    ).astype(BF16)
    logit_grad_all = gather_small([jnp.pad(logit_grad, ((0, 0), (0, 128 - EXPERTS)))], 4)[0].reshape(N, 128)[:, :EXPERTS]
    own_columns = lax.dynamic_slice_in_dim(second_all, (u * Z + z) * RW, RW, 1)
    router_grad = dot(own_columns, logit_grad_all, FIRST_DIM)
    second_grad = second_grad + dot(logit_grad, weight_router, LAST_DIM)
    upstream = out_grad.astype(F32)
    weighted = second_grad * gain_ffn
    inner_mean = jnp.mean(weighted * residual, axis=-1, keepdims=True)
    residual_grad = upstream + second_scale * weighted - residual * (second_scale**3) * inner_mean
    ffn_gain_part = jnp.sum(second_grad * residual * second_scale, axis=0)
    ffn_gain_grad = lax.psum_scatter(ffn_gain_part, ALL, scatter_dimension=0, tiled=True)

    residual_rows = gather_uly(residual_grad.astype(BF16))
    out_part = dot(attended_low, residual_rows, FIRST_DIM).astype(BF16)
    out_weight_grad = lax.psum_scatter(out_part, "blk", scatter_dimension=0, tiled=True).astype(F32)
    attended_grad = dot(residual_rows, out_rows, LAST_DIM).astype(BF16)
    dq, dk, dv = attention_backward(
        index, doc_starts, query_rot, attended_grad, attended, logs, key_all, value_all, T, chunk
    )
    kv_grads = lax.psum_scatter(
        jnp.stack([dk, dv]).reshape(2, U, Z, T, C), "blk", scatter_dimension=2, tiled=True
    ).reshape(2, L, C)

    def rotated_back(grad):
        return rotate_backward(grad.astype(F32).reshape(L, C // HEAD_DIM, HEAD_DIM), cosine, sine).reshape(L, C)

    query_up = rotated_back(dq.astype(BF16))
    key_up = rotated_back(kv_grads[0])
    inner_sums = lax.psum(
        jnp.stack([jnp.sum(query_up * gain_query * query_pre, axis=1), jnp.sum(key_up * gain_key * key_pre, axis=1)]),
        "uly",
    ) / D

    def pre_grad(up, gain, pre, scale, mean):
        return (scale * (up * gain) - pre * (scale**3) * mean[:, None]).astype(BF16)

    pre_grads = jnp.concatenate(
        [
            pre_grad(query_up, gain_query, query_pre, query_scale, inner_sums[0]),
            pre_grad(key_up, gain_key, key_pre, key_scale, inner_sums[1]),
            kv_grads[1],
        ],
        axis=1,
    )
    gain_parts = jnp.stack(
        [jnp.sum(query_up * query_pre * query_scale, axis=0), jnp.sum(key_up * key_pre * key_scale, axis=0)], axis=1
    )
    head_gain_grads = lax.psum_scatter(gain_parts, "blk", scatter_dimension=0, tiled=True)
    weight_part = dot(first_rows, pre_grads, FIRST_DIM).astype(BF16).reshape(U, Z * RW, 3 * C)
    weight_part = lax.psum_scatter(weight_part, "blk", scatter_dimension=1, tiled=True)
    weight_sum = lax.all_to_all(weight_part, "uly", split_axis=0, concat_axis=0, tiled=True)
    weight_sum = weight_sum.reshape(U, RW, 3, C).transpose(1, 2, 0, 3).reshape(RW, 3, D).astype(F32)
    attn_gain_grad = jnp.sum(own_weights * weight_sum, axis=(1, 2))
    weight_grads = weight_sum * gain_rows[:, :, None]
    first_part = dot(pre_grads, qkv_weight, LAST_DIM).astype(BF16)
    first_weighted = scatter_uly(first_part).astype(F32)
    first_mean = jnp.mean(first_weighted * hidden, axis=-1, keepdims=True)
    hidden_grad = residual_grad + first_scale * first_weighted - hidden * (first_scale**3) * first_mean
    return (
        output,
        hidden_grad,
        attn_gain_grad,
        weight_grads[:, 0],
        weight_grads[:, 1],
        weight_grads[:, 2],
        out_weight_grad,
        head_gain_grads[:, 0],
        head_gain_grads[:, 1],
        ffn_gain_grad,
        router_grad,
        expert_grads,
    )


def solution(mesh):
    rows = P(ALL, None)
    flat = P(ALL)
    experts = P("uly", None, None, "blk")
    return jax.shard_map(
        body,
        mesh=mesh,
        in_specs=(rows, rows, flat, rows, rows, rows, rows, flat, flat, flat, rows, experts, rows, P()),
        out_specs=(rows, rows, flat, rows, rows, rows, rows, flat, flat, flat, rows, experts),
        check_vma=False,
    )
```

```python
import functools

import jax
import jax.numpy as jnp
from jax import lax
from jax.experimental import pallas as pl
from jax.experimental.pallas import tpu as pltpu
from jax.sharding import PartitionSpec as P

HEADS = 16
HEAD_DIM = 128
EXPERTS = 64
CAP = 17

EPS = 1e-05
THETA = 10000.0
NEG = -1e30
FIRST_DIM = (((0,), (0,)), ((), ()))
LAST_DIM = (((1,), (1,)), ((), ()))
ALL = ("uly", "blk")
F32 = jnp.float32
BF16 = jnp.bfloat16
VMEM_BYTES = 56 * 1024 * 1024


def dot(a, b, dims=(((1,), (0,)), ((), ()))):
    return lax.dot_general(a, b, dims, preferred_element_type=F32)


def rotary_tables(position):
    halfway = HEAD_DIM // 2
    frequency = THETA ** (-(jnp.arange(halfway).astype(F32) * 2.0 / HEAD_DIM))
    angles = position.astype(F32)[:, None] * frequency[None, :]
    cosine = jnp.concatenate([jnp.cos(angles), jnp.cos(angles)], axis=1)
    sine = jnp.concatenate([jnp.sin(angles), jnp.sin(angles)], axis=1)
    return cosine, sine


def rotate_forward(values, cosine, sine):
    halfway = values.shape[-1] // 2
    turned = jnp.concatenate([-values[..., halfway:], values[..., :halfway]], axis=-1)
    return values * cosine + turned * sine


def rotate_backward(upstream, cosine, sine):
    halfway = upstream.shape[-1] // 2
    moved = upstream * sine
    turned = jnp.concatenate([moved[..., halfway:], -moved[..., :halfway]], axis=-1)
    return upstream * cosine + turned


def norm_scale(values):
    return lax.rsqrt(jnp.mean(values * values, axis=-1, keepdims=True) + EPS)


MESH = pl.DeviceIdType.MESH
DMA = pltpu.SemaphoreType.DMA
ANY_SPACE = pl.BlockSpec(memory_space=pl.ANY)
IN_VMEM = pl.BlockSpec(memory_space=pltpu.VMEM)
DEPTH = 4
CHIPS = (0, 2, 4, 6)
FIRST, THEN = (2, 4), (4, 2)


def _send(src, dst, send_sem, recv_sem, to):
    pltpu.make_async_remote_copy(
        src_ref=src, dst_ref=dst, send_sem=send_sem, recv_sem=recv_sem, device_id=to, device_id_type=MESH
    ).start()


def _expect(ref, sem, here):
    pltpu.make_async_remote_copy(
        src_ref=ref, dst_ref=ref, send_sem=sem, recv_sem=sem, device_id=here, device_id_type=MESH
    ).wait_recv()


def _sent(ref, sem, here):
    pltpu.make_async_remote_copy(
        src_ref=ref, dst_ref=ref, send_sem=sem, recv_sem=sem, device_id=here, device_id_type=MESH
    ).wait_send()


def _greet(u, z, planes, line=False, others=(), maybe=None):
    barrier = pltpu.get_barrier_semaphore()
    for bit in planes:
        pl.semaphore_signal(barrier, inc=1, device_id=(u ^ bit, z), device_id_type=MESH)
    for to in others:
        pl.semaphore_signal(barrier, inc=1, device_id=to, device_id_type=MESH)
    count = len(planes) + len(others)
    if line:

        @pl.when(z > 0)
        def _():
            pl.semaphore_signal(barrier, inc=1, device_id=(u, z - 1), device_id_type=MESH)

        @pl.when(z < DEPTH - 1)
        def _():
            pl.semaphore_signal(barrier, inc=1, device_id=(u, z + 1), device_id_type=MESH)

        count = count + jnp.where((z == 0) | (z == DEPTH - 1), 1, 2)
    if maybe is not None:
        to, real = maybe

        @pl.when(real)
        def _():
            pl.semaphore_signal(barrier, inc=1, device_id=to, device_id_type=MESH)

        count = count + jnp.where(real, 1, 0)
    pl.semaphore_wait(barrier, count)


def _line_order(z):
    second = jnp.where(z == 0, 1, z - 1)
    third = jnp.where(z == 0, 2, jnp.where(z == 3, 1, z + 1))
    fourth = jnp.where(z < 2, 3, 0)
    return (z, second, third, fourth)


def _accumulate(target, source, rows):
    strip = 16

    def step(i, _):
        at = pl.ds(pl.multiple_of(i * strip, strip), strip)
        target[at, :] = target[at, :] + source[at, :]
        return 0

    lax.fori_loop(0, rows // strip, step, 0)


def _run(*parts):
    live = list(parts)
    while live:
        for part in list(live):
            try:
                next(part)
            except StopIteration:
                live.remove(part)


def _line_part(u, z, source, block, sems, share=True):
    z_send, z_recv, c_send, c_recv, own_sem = sems
    here, core = (u, z), u % 2
    own = pltpu.make_async_copy(source, block(core, z), own_sem)
    own.start()
    order = _line_order(z)

    def along(level, ref, step):
        @pl.when((z > 0) & (level >= z))
        def _():
            step(ref, 0, level, (u, z - 1))

        @pl.when((z < DEPTH - 1) & (level <= z))
        def _():
            step(ref, 1, level, (u, z + 1))

    def go(ref, way, level, to):
        _send(ref, block(core, level), z_send.at[way, level], z_recv.at[level], to)

    def gone(ref, way, level, to):
        _sent(ref, z_send.at[way, level], here)

    for i in range(4):
        level = order[i]
        ref = source if i == 0 else block(core, level)
        if i > 0:
            yield
            _expect(ref, z_recv.at[level], here)
        along(level, ref, go)
        if share:
            _send(ref, block(core, level), c_send.at[level], c_recv.at[level], (u ^ 1, z))
    yield
    if share:
        for i in range(4):
            _expect(block(1 - core, order[i]), c_recv.at[order[i]], here)
    yield
    for i in range(4):
        along(order[i], block(core, order[i]), gone)
        if share:
            _sent(block(core, order[i]), c_send.at[order[i]], here)
    own.wait()


def _plane_part(u, z, own, block, sems):
    p_send, p_recv, o_sem = sems
    here = (u, z)
    for h in range(2):
        _send(own(h), block(h, u), p_send.at[h, 0], p_recv.at[h, 0], (u ^ FIRST[h], z))
    for h in range(2):
        pltpu.make_async_copy(own(h), block(h, u), o_sem.at[h]).start()
    for h in range(2):
        yield
        _expect(block(h, u ^ FIRST[h]), p_recv.at[h, 0], here)
        to = (u ^ THEN[h], z)
        _send(own(h), block(h, u), p_send.at[h, 1], p_recv.at[h, 1], to)
        near = block(h, u ^ FIRST[h])
        _send(near, near, p_send.at[h, 2], p_recv.at[h, 2], to)
    yield
    for h in range(2):
        _expect(block(h, u ^ THEN[h]), p_recv.at[h, 1], here)
        _expect(block(h, u ^ 6), p_recv.at[h, 2], here)
    yield
    for h in range(2):
        for k in range(3):
            _sent(block(h, u), p_send.at[h, k], here)
        pltpu.make_async_copy(own(h), block(h, u), o_sem.at[h]).wait()


def _plane_share_part(u, z, block, half, sems):
    p_send, p_recv, c_send, c_recv = sems
    here = (u, z)
    halves = (pl.ds(0, half), pl.ds(half, half))

    def source(i):
        return block(u, i)

    for i in range(4):
        for h in range(2):
            at = halves[h]
            _send(source(i).at[at], block(u, i).at[at], p_send.at[i, h, 0], p_recv.at[i, h, 0], (u ^ FIRST[h], z))
        _send(source(i), block(u, i), c_send.at[i, 0], c_recv.at[i, 0], (u ^ 1, z))

    def share(i):
        for h in range(2):
            _expect(block(u ^ THEN[h], i).at[halves[h]], p_recv.at[i, h, 1], here)
            _expect(block(u ^ 6, i).at[halves[h]], p_recv.at[i, h, 2], here)
        for k, bit in enumerate((2, 4, 6)):
            ref = block(u ^ bit, i)
            _send(ref, ref, c_send.at[i, k + 1], c_recv.at[i, k + 1], (u ^ 1, z))

    for i in range(4):
        yield
        for h in range(2):
            at = halves[h]
            near = block(u ^ FIRST[h], i).at[at]
            _expect(near, p_recv.at[i, h, 0], here)
            to = (u ^ THEN[h], z)
            _send(source(i).at[at], block(u, i).at[at], p_send.at[i, h, 1], p_recv.at[i, h, 1], to)
            _send(near, near, p_send.at[i, h, 2], p_recv.at[i, h, 2], to)
        if i > 0:
            share(i - 1)
    yield
    share(3)
    yield
    for i in range(4):
        for h in range(2):
            for k in range(3):
                _sent(block(u, i).at[halves[h]], p_send.at[i, h, k], here)
        for k, bit in enumerate((0, 2, 4, 6)):
            _sent(block(u, i), c_send.at[i, k], here)
            _expect(block(u ^ 1 ^ bit, i), c_recv.at[i, k], here)


PLANE_SHARE_SEMS = [DMA((4, 2, 3)), DMA((4, 2, 3)), DMA((4, 4)), DMA((4, 4))]


def _plane_sum_part(u, z, source, work, bufs, sems, rows, then_do):
    p_buf, q_buf = bufs
    load, p_send, p_recv, q_send, q_recv = sems
    here = (u, z)
    for h in range(2):
        for j, bit in enumerate((THEN[h], 6)):
            _send(source(h, u ^ bit), p_buf.at[h, j], p_send.at[h, j], p_recv.at[h, j], (u ^ THEN[h], z))
        for j, bit in enumerate((0, FIRST[h])):
            pltpu.make_async_copy(source(h, u ^ bit), work.at[h, j], load.at[h, j]).start()
    for h in range(2):
        yield
        for j, bit in enumerate((0, FIRST[h])):
            pltpu.make_async_copy(source(h, u ^ bit), work.at[h, j], load.at[h, j]).wait()
        _expect(p_buf.at[h, 1], p_recv.at[h, 1], here)
        _accumulate(work.at[h, 1], p_buf.at[h, 1], rows)
        _send(work.at[h, 1], q_buf.at[h], q_send.at[h], q_recv.at[h], (u ^ FIRST[h], z))
        _expect(p_buf.at[h, 0], p_recv.at[h, 0], here)
        _accumulate(work.at[h, 0], p_buf.at[h, 0], rows)
    yield
    for h in range(2):
        _expect(q_buf.at[h], q_recv.at[h], here)
        _accumulate(work.at[h, 0], q_buf.at[h], rows)
    then_do()
    yield
    for h in range(2):
        for j in range(2):
            _sent(p_buf.at[h, j], p_send.at[h, j], here)
        _sent(q_buf.at[h], q_send.at[h], here)


def _line_sum_part(u, z, source, work, bufs, sems, rows, then_do):
    c_buf, z_buf = bufs
    load, c_send, c_recv, z_send, z_recv = sems
    here, core = (u, z), u % 2
    order = tuple(reversed(_line_order(z)))
    for i in range(4):
        _send(source(1 - core, order[i]), c_buf.at[i], c_send.at[i], c_recv.at[i], (u ^ 1, z))
        pltpu.make_async_copy(source(core, order[i]), work.at[i], load.at[i]).start()
    for i in range(4):
        yield
        pltpu.make_async_copy(source(core, order[i]), work.at[i], load.at[i]).wait()
        _expect(c_buf.at[i], c_recv.at[i], here)
        _accumulate(work.at[i], c_buf.at[i], rows)
        if i == 3:
            yield
        _line_end(u, z, order[i], i, work.at[i], z_buf, (z_send, z_recv), rows)
    then_do()
    yield
    for i in range(4):
        _sent(c_buf.at[i], c_send.at[i], here)
        if i < 3:
            _sent(work.at[i], z_send.at[i], here)


def _column_peers(u, z):
    return [((u ^ c, z ^ k), c, k) for c in range(2) for k in range(4) if c or k]


def _comm(kernel, outs, scratch, collective_id, specs, flops=0, moved=100_000_000, aliases={}):
    return pl.pallas_call(
        kernel,
        out_shape=outs,
        in_specs=specs[0],
        out_specs=specs[1],
        scratch_shapes=scratch,
        input_output_aliases=aliases,
        compiler_params=pltpu.CompilerParams(
            collective_id=collective_id, has_side_effects=True, vmem_limit_bytes=VMEM_BYTES
        ),
        cost_estimate=pl.CostEstimate(flops=flops, bytes_accessed=moved, transcendentals=0),
    )


LINE_SEMS = [DMA((2, 4)), DMA((4,)), DMA((4,)), DMA((4,)), DMA]
PLANE_SEMS = [DMA((2, 3)), DMA((2, 3)), DMA((2,))]
PLANE_SUM_SEMS = [DMA((2, 2)), DMA((2, 2)), DMA((2, 2)), DMA((2,)), DMA((2,))]
LINE_SUM_SEMS = [DMA((4,)), DMA((4,)), DMA((4,)), DMA((4,)), DMA((2, 4))]


def _small_part(u, z, xs, outs, sems):
    own_sem, z_send, z_recv, u_send, u_recv = sems
    here = (u, z)
    for a, (x, o) in enumerate(zip(xs, outs)):
        pltpu.make_async_copy(x, o.at[u, z], own_sem.at[a]).start()
        for k in range(1, 4):
            _send(x, o.at[u, z], z_send.at[a, k], z_recv.at[a, k], (u, z ^ k))
    yield
    for a, (x, o) in enumerate(zip(xs, outs)):
        pltpu.make_async_copy(x, o.at[u, z], own_sem.at[a]).wait()
        for k in range(1, 4):
            _expect(o.at[u, z ^ k], z_recv.at[a, k], here)
        for k in range(1, 8):
            _send(o.at[u], o.at[u], u_send.at[a, k], u_recv.at[a, k], (u ^ k, z))
    yield
    yield
    for a, (x, o) in enumerate(zip(xs, outs)):
        for k in range(1, 4):
            _sent(x, z_send.at[a, k], here)
        for k in range(1, 8):
            _sent(o.at[u], u_send.at[a, k], here)
            _expect(o.at[u ^ k], u_recv.at[a, k], here)


def _small_sems(n):
    return [DMA((n,)), DMA((n, 4)), DMA((n, 4)), DMA((n, 8)), DMA((n, 8))]


def enter(rows, weights, out_weight, smalls, collective_id):
    n = len(smalls)

    def kernel(*refs):
        x_ref, w_ref, o_ref = refs[:3]
        small_in = refs[3 : 3 + n]
        x_out, w_out, o_out = refs[3 + n : 6 + n]
        small_out = refs[6 + n : 6 + 2 * n]
        w_buf, o_buf = refs[6 + 2 * n : 8 + 2 * n]
        sems = refs[8 + 2 * n :]
        line, plane_w, plane_o, (w_own, w_send, w_recv, o_own, o_send, o_recv) = sems[:5], sems[5:8], sems[8:11], sems[11:17]
        small_sems = sems[17:]
        u, z = lax.axis_index("uly"), lax.axis_index("blk")
        here, core, chip = (u, z), u % 2, u // 2
        turned = (2 * z + core, chip)
        away = chip != z
        column = _column_peers(u, z)
        _greet(u, z, range(1, 8), others=[to for to, c, k in column if k], maybe=(turned, away))

        def weight_part():
            own = pltpu.make_async_copy(w_ref.at[core, z], w_buf.at[core, z], w_own)
            own.start()
            for i, (to, c, k) in enumerate(column):
                _send(w_ref.at[core ^ c, z ^ k], w_buf.at[core, z], w_send.at[i], w_recv.at[i], to)
            yield
            own.wait()
            for i, (to, c, k) in enumerate(column):
                _expect(w_buf.at[core ^ c, z ^ k], w_recv.at[i], here)
            yield from _plane_part(u, z, lambda h: w_buf.at[h], lambda h, v: w_out.at[v // 2, h], plane_w)
            for i, (to, c, k) in enumerate(column):
                _sent(w_ref.at[core ^ c, z ^ k], w_send.at[i], here)

        def out_part():
            @pl.when(away)
            def _():
                _send(o_ref, o_buf, o_send, o_recv, turned)

            @pl.when(jnp.logical_not(away))
            def _():
                pltpu.make_async_copy(o_ref, o_buf, o_own).start()

            yield
            yield

            @pl.when(away)
            def _():
                _expect(o_buf, o_recv, here)

            @pl.when(jnp.logical_not(away))
            def _():
                pltpu.make_async_copy(o_ref, o_buf, o_own).wait()

            half = out_weight.shape[0] // 2
            cut = [pl.ds(h * half, half) for h in range(2)]
            yield from _plane_part(u, z, lambda h: o_buf.at[cut[h]], lambda h, v: o_out.at[v // 2, cut[h]], plane_o)

            @pl.when(away)
            def _():
                _sent(o_ref, o_send, here)

        _run(
            weight_part(),
            _small_part(u, z, small_in, small_out, small_sems),
            _line_part(u, z, x_ref, lambda c, level: x_out.at[c, level], line),
            out_part(),
        )

    outs = [
        jax.ShapeDtypeStruct((2, 4) + rows.shape, rows.dtype),
        jax.ShapeDtypeStruct((4,) + weights.shape, weights.dtype),
        jax.ShapeDtypeStruct((4,) + out_weight.shape, out_weight.dtype),
    ] + [jax.ShapeDtypeStruct((8, 4) + x.shape, x.dtype) for x in smalls]
    scratch = [pltpu.VMEM(weights.shape, BF16), pltpu.VMEM(out_weight.shape, BF16)]
    scratch += LINE_SEMS + PLANE_SEMS * 2 + [DMA, DMA((7,)), DMA((7,)), DMA, DMA, DMA] + _small_sems(n)
    specs = ([IN_VMEM, IN_VMEM, ANY_SPACE] + [IN_VMEM] * n, [ANY_SPACE] * len(outs))
    return _comm(kernel, outs, scratch, collective_id, specs)(rows, weights, out_weight, *smalls)


def column_sum(x, collective_id):
    def kernel(x_ref, o_ref, buf, send, recv):
        u, z = lax.axis_index("uly"), lax.axis_index("blk")
        here = (u, z)
        column = _column_peers(u, z)
        _greet(u, z, (), others=[to for to, c, k in column])
        for i, (to, c, k) in enumerate(column):
            _send(x_ref, buf.at[i], send.at[i], recv.at[i], to)
        total = x_ref[...]
        for i in range(7):
            _expect(buf.at[i], recv.at[i], here)
            total = total + buf[i]
        o_ref[...] = total
        for i in range(7):
            _sent(x_ref, send.at[i], here)

    scratch = [pltpu.VMEM((7,) + x.shape, F32), DMA((7,)), DMA((7,))]
    out = jax.ShapeDtypeStruct(x.shape, F32)
    return _comm(kernel, out, scratch, collective_id, ([IN_VMEM], IN_VMEM))(x)


def plane_pair(first, second, rows, collective_id):
    def kernel(a_ref, b_ref, x_ref, a_out, b_out, x_out, *sems):
        u, z = lax.axis_index("uly"), lax.axis_index("blk")
        _greet(u, z, (2, 4), line=True)
        own, outs = (a_ref, b_ref), (a_out, b_out)
        _run(
            _plane_part(u, z, lambda h: own[h], lambda h, v: outs[h].at[v // 2], sems[:3]),
            _line_part(u, z, x_ref, lambda c, level: x_out.at[u * DEPTH + level], sems[3:], share=False),
        )

    outs = [jax.ShapeDtypeStruct((4,) + x.shape, x.dtype) for x in (first, second)]
    outs += [jax.ShapeDtypeStruct((32,) + rows.shape, rows.dtype)]
    specs = ([IN_VMEM] * 2 + [ANY_SPACE], [ANY_SPACE] * 3)
    return _comm(kernel, outs, PLANE_SEMS + LINE_SEMS, collective_id, specs)(first, second, rows)


def column_gather(rows, x, collective_id):
    T, D = rows.shape

    def kernel(r_ref, x_ref, r_out, x_out, *refs):
        u, z = lax.axis_index("uly"), lax.axis_index("blk")
        _greet(u, z, (1, 2, 4), line=True)
        order = _line_order(z)

        def keep(i, work):
            x_out[order[i]] = work[i, 0]

        _run(
            _line_part(u, z, r_ref, lambda c, level: r_out.at[c, level], refs[-5:]),
            _tree_sum_part(u, z, lambda who, level: x_ref.at[who * DEPTH + level], order, T, refs[:-5], keep),
        )

    outs = [jax.ShapeDtypeStruct((2, 4, T, D), BF16), jax.ShapeDtypeStruct((4, T, D), BF16)]
    specs = ([IN_VMEM, ANY_SPACE], [ANY_SPACE, IN_VMEM])
    scratch = _tree_sum_scratch(T, D) + LINE_SEMS
    return _comm(kernel, outs, scratch, collective_id, specs)(rows, x.reshape(32, T, D))


def _line_sum_scratch(T, D):
    return [pltpu.VMEM((4, T, D), BF16), pltpu.VMEM((4, T, D), BF16), pltpu.VMEM((2, 4, T, D), BF16)]


def column_scatter(x, rows, collective_id):
    T, D = x.shape[2:]

    def kernel(x_ref, g_ref, o_ref, g_out, work, c_buf, z_buf, *sems):
        u, z = lax.axis_index("uly"), lax.axis_index("blk")
        _greet(u, z, (1, 2, 4), line=True)

        def finish():
            o_ref[...] = work[3]

        _run(
            _line_sum_part(u, z, lambda c, level: x_ref.at[c, level], work, (c_buf, z_buf), sems[:5], T, finish),
            _plane_share_part(u, z, lambda who, i: g_out.at[who * DEPTH + i], T // 2, sems[5:]),
        )

    outs = [jax.ShapeDtypeStruct((T, D), BF16), jax.ShapeDtypeStruct((32, T, D), BF16)]
    scratch = _line_sum_scratch(T, D) + LINE_SUM_SEMS + PLANE_SHARE_SEMS
    specs = ([ANY_SPACE] * 2, [IN_VMEM, ANY_SPACE])
    out, gathered = _comm(kernel, outs, scratch, collective_id, specs, aliases={1: 1})(x, rows)
    return out, gathered.reshape(32 * T, D)


def _plane_sum_scratch(rows, cols):
    return [pltpu.VMEM((2, 2, rows, cols), BF16), pltpu.VMEM((2, 2, rows, cols), BF16), pltpu.VMEM((2, rows, cols), BF16)]


def key_value_sums(dk, dv, out_part, x, collective_id):
    T = x.shape[1]
    L, C = dk.shape[1:]
    R, D = out_part.shape[1:]
    half = R // 2

    def kernel(
        k_ref, v_ref, w_ref, x_ref, k_out, v_out, w_out, x_out, work, p_buf, q_buf, o_work, op_buf, oq_buf, x_work, z_buf, *sems
    ):
        u, z = lax.axis_index("uly"), lax.axis_index("blk")
        here, core, chip = (u, z), u % 2, u // 2
        turned = (2 * z + core, chip)
        away = chip != z
        _greet(u, z, (2, 4), line=True, maybe=(turned, away))
        t_send, t_recv, load, z_send, z_recv = sems[10:15]
        order = tuple(reversed(_line_order(z)))

        def finish():
            k_out[...] = work[0, 0]
            v_out[...] = work[1, 0]

        def turn():
            for h in range(2):
                rows = pl.ds(h * half, half)

                @pl.when(away)
                def _(h=h, rows=rows):
                    _send(o_work.at[h, 0], w_out.at[rows], t_send.at[h], t_recv.at[h], turned)

                @pl.when(jnp.logical_not(away))
                def _(h=h, rows=rows):
                    w_out[rows, :] = o_work[h, 0]

        def line():
            copies = [pltpu.make_async_copy(x_ref.at[order[i]], x_work.at[i], load.at[i]) for i in range(4)]
            for copy in copies:
                copy.start()
            for copy in copies:
                copy.wait()
            for i in range(4):
                _line_end(u, z, order[i], i, x_work.at[i], z_buf, (z_send, z_recv), T)
                yield
            x_out[...] = x_work[3]
            for i in range(3):
                _sent(x_work.at[i], z_send.at[i], here)

        _run(
            _plane_sum_part(
                u,
                z,
                lambda h, v: w_ref.at[v // 2, pl.ds(h * half, half)],
                o_work,
                (op_buf, oq_buf),
                sems[5:10],
                half,
                turn,
            ),
            _plane_sum_part(
                u, z, lambda h, v: (k_ref, v_ref)[h].at[v // 2], work, (p_buf, q_buf), sems[:5], L, finish
            ),
            line(),
        )

        @pl.when(away)
        def _():
            for h in range(2):
                rows = pl.ds(h * half, half)
                _expect(w_out.at[rows], t_recv.at[h], here)
                _sent(o_work.at[h, 0], t_send.at[h], here)

    outs = [jax.ShapeDtypeStruct((L, C), BF16)] * 2 + [jax.ShapeDtypeStruct((R, D), BF16), jax.ShapeDtypeStruct((T, D), BF16)]
    scratch = _plane_sum_scratch(L, C) + _plane_sum_scratch(half, D)
    scratch += [pltpu.VMEM((4, T, D), BF16), pltpu.VMEM((2, 4, T, D), BF16)] + PLANE_SUM_SEMS * 2
    scratch += [DMA((2,)), DMA((2,)), DMA((4,)), DMA((4,)), DMA((2, 4))]
    specs = ([ANY_SPACE] * 4, [IN_VMEM] * 4)
    return _comm(kernel, outs, scratch, collective_id, specs)(dk, dv, out_part, x)


def leave(x, weights, smalls, collective_id):
    n = len(smalls)
    T, D = x.shape[2:]
    rows, W = weights.shape[2:]
    R = rows // 4

    def kernel(x_ref, w_ref, *refs):
        small_in, (o_ref, w_out), small_out = refs[:n], refs[n : n + 2], refs[n + 2 : 2 * n + 2]
        work, c_buf, z_buf, w_work, wp_buf, wq_buf = refs[2 * n + 2 : 2 * n + 8]
        sems = refs[2 * n + 8 :]
        u, z = lax.axis_index("uly"), lax.axis_index("blk")
        here, core, chip = (u, z), u % 2, u // 2
        column = _column_peers(u, z)
        _greet(u, z, range(1, 8), others=[to for to, c, k in column if k])
        t_send, t_recv = sems[10:12]
        group = 2 * z + core

        def finish():
            o_ref[...] = work[3]

        def cut(c, level):
            return w_work.at[c, 0, pl.ds(pl.multiple_of(level * R, R), R)]

        def deal():
            for i, (to, c, k) in enumerate(column):
                _send(cut(core ^ c, z ^ k), w_out.at[group], t_send.at[i], t_recv.at[i], to)
            w_out[group] = cut(core, z)[...]

        _run(
            _plane_sum_part(u, z, lambda h, v: w_ref.at[v // 2, h], w_work, (wp_buf, wq_buf), sems[5:10], rows, deal),
            _line_sum_part(u, z, lambda c, level: x_ref.at[c, level], work, (c_buf, z_buf), sems[:5], T, finish),
            _small_part(u, z, small_in, small_out, sems[12:]),
        )
        for i, (to, c, k) in enumerate(column):
            _expect(w_out.at[2 * (z ^ k) + (core ^ c)], t_recv.at[i], here)
            _sent(cut(core ^ c, z ^ k), t_send.at[i], here)

    outs = [jax.ShapeDtypeStruct((T, D), BF16), jax.ShapeDtypeStruct((8, R, W), BF16)]
    outs += [jax.ShapeDtypeStruct((8, 4) + x.shape, x.dtype) for x in smalls]
    scratch = _line_sum_scratch(T, D) + _plane_sum_scratch(rows, W) + LINE_SUM_SEMS + PLANE_SUM_SEMS
    scratch += [DMA((7,)), DMA((7,))] + _small_sems(n)
    specs = ([ANY_SPACE] * 2 + [IN_VMEM] * n, [IN_VMEM] * 2 + [ANY_SPACE] * n)
    return _comm(kernel, outs, scratch, collective_id, specs)(x, weights, *smalls)


def _gather_all_kernel(x_ref, o_ref, own_sem, z_send, z_recv, p_send, p_recv, c_send, c_recv):
    u, z = lax.axis_index("uly"), lax.axis_index("blk")
    depth = DEPTH
    half = x_ref.shape[0] // 2
    halves = (pl.ds(0, half), pl.ds(half, half))
    here = (u, z)
    _greet(u, z, (1, 2, 4), line=True)
    own = pltpu.make_async_copy(x_ref, o_ref.at[u * depth + z], own_sem)
    own.start()
    order = _line_order(z)

    def block(who, level):
        return o_ref.at[who * depth + level]

    def part(who, level, h):
        return o_ref.at[who * depth + level, halves[h]]

    first, then = (2, 4), (4, 2)

    def along(level, source, step):
        @pl.when((z > 0) & (level >= z))
        def _():
            step(source, 0, level, (u, z - 1))

        @pl.when((z < depth - 1) & (level <= z))
        def _():
            step(source, 1, level, (u, z + 1))

    def go(source, way, level, to):
        _send(source, block(u, level), z_send.at[way, level], z_recv.at[level], to)

    def gone(source, way, level, to):
        _sent(source, z_send.at[way, level], here)

    def across(level, source):
        for h in range(2):
            _send(
                source.at[halves[h]], part(u, level, h), p_send.at[level, h, 0], p_recv.at[level, h, 0], (u ^ first[h], z)
            )
        _send(source, block(u, level), c_send.at[level, 0], c_recv.at[level, 0], (u ^ 1, z))

    def onward(level, source):
        for h in range(2):
            _expect(part(u ^ first[h], level, h), p_recv.at[level, h, 0], here)
            to = (u ^ then[h], z)
            _send(source.at[halves[h]], part(u, level, h), p_send.at[level, h, 1], p_recv.at[level, h, 1], to)
            _send(
                part(u ^ first[h], level, h),
                part(u ^ first[h], level, h),
                p_send.at[level, h, 2],
                p_recv.at[level, h, 2],
                to,
            )

    def share(level):
        for h in range(2):
            _expect(part(u ^ then[h], level, h), p_recv.at[level, h, 1], here)
            _expect(part(u ^ 6, level, h), p_recv.at[level, h, 2], here)
        for i, bit in enumerate((2, 4, 6)):
            _send(block(u ^ bit, level), block(u ^ bit, level), c_send.at[level, i + 1], c_recv.at[level, i + 1], (u ^ 1, z))

    sources = [x_ref] + [block(u, order[i]) for i in range(1, 4)]
    along(z, x_ref, go)
    across(z, x_ref)
    for i in range(1, 4):
        _expect(block(u, order[i]), z_recv.at[order[i]], here)
        along(order[i], sources[i], go)
        across(order[i], sources[i])
        onward(order[i - 1], sources[i - 1])
        if i >= 2:
            share(order[i - 2])
    onward(order[3], sources[3])
    share(order[2])
    share(order[3])
    for i in range(4):
        level = order[i]
        along(level, sources[i], gone)
        for h in range(2):
            for k in range(3):
                _sent(part(u, level, h), p_send.at[level, h, k], here)
        for k, bit in enumerate((0, 2, 4, 6)):
            _sent(block(u, level), c_send.at[level, k], here)
            _expect(block(u ^ 1 ^ bit, level), c_recv.at[level, k], here)
    own.wait()


def gather_all(x, collective_id):
    T, D = x.shape
    scratch = [DMA, DMA((2, 4)), DMA((4,)), DMA((4, 2, 3)), DMA((4, 2, 3)), DMA((4, 4)), DMA((4, 4))]
    out = jax.ShapeDtypeStruct((32, T, D), x.dtype)
    return _comm(_gather_all_kernel, out, scratch, collective_id, ([IN_VMEM], ANY_SPACE))(x).reshape(32 * T, D)


def _tree_sum_part(u, z, source, order, T, refs, level_done):
    work, c_buf, p_buf, q_buf, load_sem, c_send, c_recv, p_send, p_recv, q_send, q_recv = refs
    here = (u, z)
    half = T // 2
    halves = (pl.ds(0, half), pl.ds(half, half))

    def load(i, k, bit):
        return pltpu.make_async_copy(source(u ^ bit, order[i]), work.at[i, k], load_sem.at[i, k])

    for i in range(4):
        for k, bit in enumerate(CHIPS):
            _send(source(u ^ bit ^ 1, order[i]), c_buf.at[i, k], c_send.at[i, k], c_recv.at[i, k], (u ^ 1, z))
            load(i, k, bit).start()

    def add_core(i):
        for k in (3, 2, 1, 0):
            load(i, k, CHIPS[k]).wait()
            _expect(c_buf.at[i, k], c_recv.at[i, k], here)
            _accumulate(work.at[i, k], c_buf.at[i, k], T)
        for h in range(2):
            for j, bit in enumerate((THEN[h], 6)):
                k = CHIPS.index(bit)
                part = work.at[i, k, halves[h]]
                _send(part, p_buf.at[i, h, j], p_send.at[i, h, j], p_recv.at[i, h, j], (u ^ THEN[h], z))

    def add_first(i):
        for h in range(2):
            k = CHIPS.index(FIRST[h])
            _expect(p_buf.at[i, h, 1], p_recv.at[i, h, 1], here)
            _accumulate(work.at[i, k, halves[h]], p_buf.at[i, h, 1], half)
            _send(work.at[i, k, halves[h]], q_buf.at[i, h], q_send.at[i, h], q_recv.at[i, h], (u ^ FIRST[h], z))
            _expect(p_buf.at[i, h, 0], p_recv.at[i, h, 0], here)
            _accumulate(work.at[i, 0, halves[h]], p_buf.at[i, h, 0], half)

    def add_then(i):
        for h in range(2):
            _expect(q_buf.at[i, h], q_recv.at[i, h], here)
            _accumulate(work.at[i, 0, halves[h]], q_buf.at[i, h], half)
        level_done(i, work)

    for i in range(6):
        yield
        if i < 4:
            add_core(i)
        if 1 <= i < 5:
            add_first(i - 1)
        if i >= 2:
            add_then(i - 2)
    yield
    for i in range(4):
        for k in range(4):
            _sent(c_buf.at[i, k], c_send.at[i, k], here)
        for h in range(2):
            for j in range(2):
                _sent(p_buf.at[i, h, j], p_send.at[i, h, j], here)
            _sent(q_buf.at[i, h], q_send.at[i, h], here)


def _tree_sum_scratch(T, D):
    half = T // 2
    return [
        pltpu.VMEM((4, 4, T, D), BF16),
        pltpu.VMEM((4, 4, T, D), BF16),
        pltpu.VMEM((4, 2, 2, half, D), BF16),
        pltpu.VMEM((4, 2, half, D), BF16),
        DMA((4, 4)),
        DMA((4, 4)),
        DMA((4, 4)),
        DMA((4, 2, 2)),
        DMA((4, 2, 2)),
        DMA((4, 2)),
        DMA((4, 2)),
    ]


def _line_end(u, z, level, i, part, z_buf, sems, rows):
    z_send, z_recv = sems
    here = (u, z)

    @pl.when((level >= z) & (z > 0))
    def _():
        _expect(z_buf.at[0, level], z_recv.at[0, level], here)
        _accumulate(part, z_buf.at[0, level], rows)

    @pl.when((level <= z) & (z < DEPTH - 1))
    def _():
        _expect(z_buf.at[1, level], z_recv.at[1, level], here)
        _accumulate(part, z_buf.at[1, level], rows)

    if i < 3:

        @pl.when(level > z)
        def _():
            _send(part, z_buf.at[0, level], z_send.at[i], z_recv.at[0, level], (u, z + 1))

        @pl.when(level < z)
        def _():
            _send(part, z_buf.at[1, level], z_send.at[i], z_recv.at[1, level], (u, z - 1))


def scatter_all(x, collective_id):
    N, D = x.shape
    T = N // 32

    def kernel(x_ref, o_ref, z_buf, z_send, z_recv, *refs):
        u, z = lax.axis_index("uly"), lax.axis_index("blk")
        _greet(u, z, (1, 2, 4), line=True)
        order = tuple(reversed(_line_order(z)))
        work = refs[0]

        def done(i, work):
            _line_end(u, z, order[i], i, work.at[i, 0], z_buf, (z_send, z_recv), T)

        _run(_tree_sum_part(u, z, lambda who, level: x_ref.at[who * DEPTH + level], order, T, refs, done))
        o_ref[...] = work[3, 0]
        for i in range(3):
            _sent(work.at[i, 0], z_send.at[i], (u, z))

    scratch = [pltpu.VMEM((2, 4, T, D), BF16), DMA((4,)), DMA((2, 4))] + _tree_sum_scratch(T, D)
    out = jax.ShapeDtypeStruct((T, D), x.dtype)
    return _comm(kernel, out, scratch, collective_id, ([ANY_SPACE], IN_VMEM))(x.reshape(32, T, D))


class Slice:
    def __init__(self, U, Z, T, D):
        self.U, self.Z, self.T, self.D = U, Z, T, D
        self.u, self.z = lax.axis_index("uly"), lax.axis_index("blk")
        self.C = D // 8
        self.L = 8 * T
        self.group = 2 * self.z + self.u % 2
        self.first_block, self.block_step = 8 * (self.u // 2), 1

    def enter(self, rows, scaled, out_weight, pack, routes):
        R = scaled.shape[0]
        cut = scaled.reshape(R, 3, 4, 2, self.C).transpose(3, 2, 0, 1, 4).reshape(2, 4, R, 3 * self.C)
        rows, weights, outs, packs, routes = enter(rows, cut, out_weight, [pack, routes], 1)
        return (
            rows.reshape(self.L, self.D),
            weights.reshape(self.D, 3 * self.C),
            outs.reshape(self.C, self.D),
            packs.reshape(self.D, -1),
            routes,
        )

    def head_sum(self, x):
        return column_sum(x, 2)

    def head_sum_again(self, x):
        return column_sum(x, 3)

    def sequence(self, key, value, upstream):
        keys, values, self.upstream_line = plane_pair(key, value, upstream, 4)
        return keys.reshape(-1, self.C), values.reshape(-1, self.C)

    def heads_to_rows(self, x):
        return column_scatter(x.reshape(2, 4, self.T, self.D), self.upstream_line, 5)

    def rows_to_heads(self, x, out_part):
        rows, self.out_line = column_gather(x, out_part, 6)
        return rows.reshape(self.L, self.D)

    def gather(self, x):
        return gather_all(x, 7)

    def scatter_wide(self, x):
        return scatter_all(x, 8)

    def sequence_sums(self, dk, dv, out_part):
        cut = (4, self.L, self.C)
        return key_value_sums(dk.reshape(cut), dv.reshape(cut), out_part.reshape(4, -1, self.D), self.out_line, 10)

    def leave(self, first_part, weight_part, logit_grad, ffn_part, head_parts):
        T, R = self.T, self.D // 32
        thin = jnp.concatenate([ffn_part.reshape(-1, 128), head_parts.reshape(-1, 128)], axis=0)
        wide = self.D // 128
        used = thin.shape[0]
        thin = jnp.pad(thin, ((0, -used % 8), (0, 0)))
        first, weights, logit_all, thin = leave(
            first_part.reshape(2, 4, T, self.D),
            weight_part.reshape(4, 2, 4 * R, 3 * self.C),
            [logit_grad.reshape(T // 2, 2 * EXPERTS), thin],
            11,
        )
        weights = weights.reshape(8, R, 3, self.C).transpose(1, 2, 0, 3).reshape(R, 3, self.D)
        ffn = lax.dynamic_slice_in_dim(
            jnp.sum(thin[:, :, :wide], axis=(0, 1)).reshape(self.D), (self.u * 4 + self.z) * R, R, 0
        )
        mine = lax.dynamic_index_in_dim(thin.reshape(4, 2, 4, -1, 128), self.u % 2, 1, False)
        mine = lax.dynamic_index_in_dim(mine, self.u // 2, 1, False)
        heads = jnp.sum(mine[:, wide:used], axis=0).reshape(2, self.C)
        heads = lax.dynamic_slice_in_dim(heads, self.z * R, R, 1)
        return first, weights, logit_all.reshape(32 * T, EXPERTS), ffn, heads


class General:
    def __init__(self, U, Z, T, D):
        self.U, self.Z, self.T, self.D = U, Z, T, D
        self.u, self.z = lax.axis_index("uly"), lax.axis_index("blk")
        self.C = D // U
        self.L = U * T
        self.group = self.u
        self.first_block, self.block_step = self.z, Z

    def gather(self, x):
        return lax.all_gather(x, ALL, axis=0, tiled=True)

    def scatter_wide(self, x):
        return lax.psum_scatter(x, ALL, scatter_dimension=0, tiled=True)

    def enter(self, rows, scaled, out_weight, pack, routes):
        U, R = self.U, scaled.shape[0]
        swapped = lax.all_to_all(scaled.reshape(R, 3, U, self.C), "uly", split_axis=2, concat_axis=0, tiled=True)
        weights = lax.all_gather(swapped.reshape(U, R, 3 * self.C), "blk", axis=1, tiled=True)
        return (
            self.rows_all(rows),
            weights.reshape(self.D, 3 * self.C),
            lax.all_gather(out_weight, "blk", axis=0, tiled=True),
            self.gather(pack),
            self.gather(routes[None]).reshape((U, self.Z) + routes.shape),
        )

    def head_sum(self, x):
        return lax.psum(x, "uly")

    head_sum_again = head_sum

    def sequence(self, key, value, upstream):
        self.upstream = upstream
        pair = jnp.stack([key, value]).reshape(2, self.U, self.T, self.C)
        pair = lax.all_gather(pair, "blk", axis=2, tiled=False).reshape(2, -1, self.C)
        return pair[0], pair[1]

    def heads_to_rows(self, x):
        return self.rows_sum(x), self.gather(self.upstream)

    def rows_sum(self, x):
        return lax.psum_scatter(x, "uly", scatter_dimension=0, tiled=True)

    def rows_all(self, x):
        return lax.all_gather(x, "uly", axis=0, tiled=True)

    def rows_to_heads(self, x, out_part):
        self.out_sum = self.scatter_wide(out_part)
        return self.rows_all(x)

    def sequence_sums(self, dk, dv, out_part):
        pair = jnp.stack([dk, dv]).reshape(2, self.U, self.Z, self.T, self.C)
        pair = lax.psum_scatter(pair, "blk", scatter_dimension=2, tiled=True).reshape(2, self.L, self.C)
        return pair[0], pair[1], lax.psum_scatter(out_part, "blk", scatter_dimension=0, tiled=True), self.out_sum

    def leave(self, first_part, weight_part, logit_grad, ffn_part, head_parts):
        U, R = self.U, self.D // (self.U * self.Z)
        part = weight_part.reshape(U, self.Z * R, 3 * self.C)
        part = lax.psum_scatter(part, "blk", scatter_dimension=1, tiled=True)
        part = lax.all_to_all(part, "uly", split_axis=0, concat_axis=0, tiled=True)
        weights = part.reshape(U, R, 3, self.C).transpose(1, 2, 0, 3).reshape(R, 3, self.D)
        heads = lax.psum_scatter(head_parts, "blk", scatter_dimension=1, tiled=True)
        return self.rows_sum(first_part), weights, self.gather(logit_grad), self.scatter_wide(ffn_part), heads


def _row_limits(doc_ref, first, rows):
    position = first + lax.broadcasted_iota(jnp.int32, (rows, 1), 0)
    start = jnp.zeros_like(position)
    lowest = jnp.int32(0)
    for d in range(doc_ref.shape[0]):
        begin = doc_ref[d]
        start = jnp.where(begin <= position, jnp.maximum(start, begin), start)
        lowest = jnp.where(begin <= first, jnp.maximum(lowest, begin), lowest)
    return position, start, lowest


def _scores(query, key, position, start, key_first, scaling):
    raw = dot(query, key, LAST_DIM) * scaling
    key_position = key_first + lax.broadcasted_iota(jnp.int32, raw.shape, 1)
    return jnp.where((key_position <= position) & (key_position >= start), raw, NEG)


def _attend_kernel(index_ref, doc_ref, q_ref, k_ref, v_ref, o_ref, log_ref, *, chunk, scaling):
    rows = q_ref.shape[0]
    heads = q_ref.shape[1] // HEAD_DIM
    first = (pl.program_id(0) * index_ref[1] + index_ref[0]) * rows
    position, start, lowest = _row_limits(doc_ref, first, rows)

    def step(i, state):
        at = pl.multiple_of(i * chunk, chunk)
        new = []
        for h in range(heads):
            cols = pl.ds(h * HEAD_DIM, HEAD_DIM)
            top, total, out = state[h]
            scores = _scores(q_ref[:, cols], k_ref[pl.ds(at, chunk), cols], position, start, at, scaling)
            now = jnp.maximum(top, jnp.max(scores, axis=1, keepdims=True))
            weights = jnp.exp(scores - now)
            fade = jnp.exp(top - now)
            total = total * fade + jnp.sum(weights, axis=1, keepdims=True)
            out = out * fade + dot(weights.astype(BF16), v_ref[pl.ds(at, chunk), cols])
            new.append((now, total, out))
        return tuple(new)

    zero = (
        jnp.full((rows, 1), NEG, F32),
        jnp.zeros((rows, 1), F32),
        jnp.zeros((rows, HEAD_DIM), F32),
    )
    last = first + rows
    state = lax.fori_loop(lowest // chunk, (last + chunk - 1) // chunk, step, (zero,) * heads)
    for h in range(heads):
        cols = pl.ds(h * HEAD_DIM, HEAD_DIM)
        top, total, out = state[h]
        o_ref[:, cols] = out / total
        log_ref[:, cols] = jnp.broadcast_to(top + jnp.log(total), (rows, HEAD_DIM))


def _attend_back_kernel(
    index_ref, doc_ref, q_ref, g_ref, o_ref, log_ref, k_ref, v_ref, dq_ref, dk_ref, dv_ref, dk_sum, dv_sum, *, chunk, scaling
):
    rows = q_ref.shape[0]
    heads = q_ref.shape[1] // HEAD_DIM
    first = (pl.program_id(0) * index_ref[1] + index_ref[0]) * rows
    position, start, lowest = _row_limits(doc_ref, first, rows)

    @pl.when(pl.program_id(0) == 0)
    def _():
        dk_sum[...] = jnp.zeros_like(dk_sum)
        dv_sum[...] = jnp.zeros_like(dv_sum)

    deltas, logs = [], []
    for h in range(heads):
        cols = pl.ds(h * HEAD_DIM, HEAD_DIM)
        deltas.append(jnp.sum(g_ref[:, cols].astype(F32) * o_ref[:, cols], axis=1, keepdims=True))
        logs.append(log_ref[:, cols][:, :1])

    def step(i, state):
        at = pl.multiple_of(i * chunk, chunk)
        new = []
        for h in range(heads):
            cols = pl.ds(h * HEAD_DIM, HEAD_DIM)
            query, grad = q_ref[:, cols], g_ref[:, cols]
            key = k_ref[pl.ds(at, chunk), cols]
            scores = _scores(query, key, position, start, at, scaling)
            weights = jnp.exp(scores - logs[h])
            weight_grad = dot(grad, v_ref[pl.ds(at, chunk), cols], LAST_DIM)
            score_grad = (weights * (weight_grad - deltas[h])).astype(BF16)
            dv_sum[pl.ds(at, chunk), cols] += dot(weights.astype(BF16), grad, FIRST_DIM)
            dk_sum[pl.ds(at, chunk), cols] += dot(score_grad, query, FIRST_DIM)
            new.append(state[h] + dot(score_grad, key))
        return tuple(new)

    last = first + rows
    state = lax.fori_loop(
        lowest // chunk, (last + chunk - 1) // chunk, step, (jnp.zeros((rows, HEAD_DIM), F32),) * heads
    )
    for h in range(heads):
        dq_ref[:, pl.ds(h * HEAD_DIM, HEAD_DIM)] = (state[h] * scaling).astype(BF16)

    @pl.when(pl.program_id(0) == pl.num_programs(0) - 1)
    def _():
        dk_ref[...] = (dk_sum[...] * scaling).astype(BF16)
        dv_ref[...] = dv_sum[...].astype(BF16)


def _attention_specs(L, N, C, rows):
    block = pl.BlockSpec((rows, C), lambda i, *_: (i, 0))
    whole = pl.BlockSpec((N, C), lambda i, *_: (0, 0), pipeline_mode=pl.Buffered(1))
    return block, whole


def attention_forward(index, docs, query, key_all, value_all, rows, chunk):
    (L, C), N = query.shape, key_all.shape[0]
    block, whole = _attention_specs(L, N, C, rows)
    return pl.pallas_call(
        functools.partial(_attend_kernel, chunk=chunk, scaling=HEAD_DIM ** (-0.5)),
        out_shape=[jax.ShapeDtypeStruct((L, C), F32)] * 2,
        grid_spec=pltpu.PrefetchScalarGridSpec(
            num_scalar_prefetch=2, grid=(L // rows,), in_specs=[block, whole, whole], out_specs=[block, block]
        ),
        compiler_params=pltpu.CompilerParams(vmem_limit_bytes=VMEM_BYTES),
        cost_estimate=pl.CostEstimate(flops=4 * L * C * 1024, bytes_accessed=4 * N * C, transcendentals=L * 1024),
    )(index, docs, query, key_all, value_all)


def attention_backward(index, docs, query, grad, attended, logs, key_all, value_all, rows, chunk):
    (L, C), N = query.shape, key_all.shape[0]
    block, whole = _attention_specs(L, N, C, rows)
    return pl.pallas_call(
        functools.partial(_attend_back_kernel, chunk=chunk, scaling=HEAD_DIM ** (-0.5)),
        out_shape=[jax.ShapeDtypeStruct((L, C), BF16)] + [jax.ShapeDtypeStruct((N, C), BF16)] * 2,
        grid_spec=pltpu.PrefetchScalarGridSpec(
            num_scalar_prefetch=2,
            grid=(L // rows,),
            in_specs=[block, block, block, block, whole, whole],
            out_specs=[block, whole, whole],
            scratch_shapes=[pltpu.VMEM((N, C), F32)] * 2,
        ),
        compiler_params=pltpu.CompilerParams(vmem_limit_bytes=VMEM_BYTES),
        cost_estimate=pl.CostEstimate(flops=10 * L * C * 1024, bytes_accessed=8 * N * C, transcendentals=L * 1024),
    )(index, docs, query, grad, attended, logs, key_all, value_all)


def _pick_kernel(slot_ref, router_ref, x_ref, g_ref, xr_ref, gr_ref, gate_ref, *, slots, width):
    experts, group = slot_ref.shape
    logits = lax.dot_general(router_ref[...], x_ref[...], (((0,), (1,)), ((), ())), preferred_element_type=F32)
    powers = jnp.exp(logits - jnp.max(logits, axis=0, keepdims=True))
    chances = powers / jnp.sum(powers, axis=0, keepdims=True)
    row = lax.broadcasted_iota(jnp.int32, (slots, group), 0)
    picks = []
    for e in range(experts):
        hit = slot_ref[e : e + 1, :] == row
        gate = jnp.sum(jnp.where(hit, chances[e : e + 1, :], 0.0), axis=1, keepdims=True)
        gate_ref[e, 0] = jnp.broadcast_to(gate, (slots, 128))
        picks.append(jnp.where(hit, 1.0, 0.0).astype(BF16))
    pick = jnp.concatenate(picks, axis=0)
    for source, target in ((x_ref, xr_ref), (g_ref, gr_ref)):

        def step(i, _, source=source, target=target):
            cols = pl.ds(pl.multiple_of(i * width, width), width)
            rows = dot(pick, source[:, cols]).astype(BF16)
            for e in range(experts):
                target[e, 0, :, cols] = rows[e * slots : (e + 1) * slots]
            return 0

        lax.fori_loop(0, source.shape[1] // width, step, 0)


def pick_rows(slot, router, x, g, group, slots):
    EL, N = slot.shape
    D = x.shape[1]
    groups = N // group
    tokens = pl.BlockSpec((group, D), lambda i: (i, 0))
    picked = pl.BlockSpec((EL, 1, slots, D), lambda i: (0, i, 0, 0))
    rows = jax.ShapeDtypeStruct((EL, groups, slots, D), BF16)
    return pl.pallas_call(
        functools.partial(_pick_kernel, slots=slots, width=512),
        out_shape=[rows, rows, jax.ShapeDtypeStruct((EL, groups, slots, 128), F32)],
        grid=(groups,),
        in_specs=[
            pl.BlockSpec((EL, group), lambda i: (0, i)),
            pl.BlockSpec(router.shape, lambda i: (0, 0)),
            tokens,
            tokens,
        ],
        out_specs=[picked, picked, pl.BlockSpec((EL, 1, slots, 128), lambda i: (0, i, 0, 0))],
        compiler_params=pltpu.CompilerParams(vmem_limit_bytes=VMEM_BYTES),
        cost_estimate=pl.CostEstimate(
            flops=4 * EL * slots * N * D, bytes_accessed=8 * N * D, transcendentals=N * EXPERTS
        ),
    )(slot, router, x, g)


def _expert_kernel(x_ref, g_ref, gate_ref, w_ref, out_ref, entry_ref, dw_ref, gg_ref, *, width):
    x, g = x_ref[0], g_ref[0]
    gate = gate_ref[0][:, :1]
    gate_pre = dot(x, w_ref[0, 0])
    up = dot(x, w_ref[0, 1])
    back = dot(g, w_ref[0, 2])
    sig = jax.nn.sigmoid(gate_pre)
    act = gate_pre * sig
    inner = act * up
    gg_ref[0] = jnp.broadcast_to(jnp.sum(inner * back, axis=1, keepdims=True), gg_ref.shape[1:])
    inner_grad = back * gate
    gate_pre_grad = (inner_grad * up * sig * (1.0 + gate_pre * (1.0 - sig))).astype(BF16)
    up_grad = (inner_grad * act).astype(BF16)
    gated = (inner * gate).astype(BF16)
    first = pl.program_id(1) == 0

    def step(i, _):
        at = pl.ds(pl.multiple_of(i * width, width), width)
        out_ref[0, :, at] = dot(gated, w_ref[0, 2, at, :], LAST_DIM).astype(BF16)
        entry = dot(gate_pre_grad, w_ref[0, 0, at, :], LAST_DIM) + dot(up_grad, w_ref[0, 1, at, :], LAST_DIM)
        entry_ref[0, :, at] = entry.astype(BF16)
        parts = (
            dot(x_ref[0, :, at], gate_pre_grad, FIRST_DIM),
            dot(x_ref[0, :, at], up_grad, FIRST_DIM),
            dot(g_ref[0, :, at], gated, FIRST_DIM),
        )
        for k in range(3):

            @pl.when(first)
            def _(k=k):
                dw_ref[0, k, at, :] = parts[k]

            @pl.when(jnp.logical_not(first))
            def _(k=k):
                dw_ref[0, k, at, :] += parts[k]

        return 0

    lax.fori_loop(0, x_ref.shape[2] // width, step, 0)


def run_experts(x, g, gate, weights, chunk):
    EL, rows, D = x.shape
    FL = weights.shape[3]
    row_block = pl.BlockSpec((1, chunk, D), lambda e, c: (e, c, 0))
    thin = pl.BlockSpec((1, chunk, 128), lambda e, c: (e, c, 0))
    matrices = pl.BlockSpec((1, 3, D, FL), lambda e, c: (e, 0, 0, 0))
    return pl.pallas_call(
        functools.partial(_expert_kernel, width=512),
        out_shape=[
            jax.ShapeDtypeStruct(x.shape, BF16),
            jax.ShapeDtypeStruct(x.shape, BF16),
            jax.ShapeDtypeStruct(weights.shape, F32),
            jax.ShapeDtypeStruct((EL, rows, 128), F32),
        ],
        grid=(EL, rows // chunk),
        in_specs=[row_block, row_block, thin, matrices],
        out_specs=[row_block, row_block, matrices, thin],
        compiler_params=pltpu.CompilerParams(vmem_limit_bytes=VMEM_BYTES),
        cost_estimate=pl.CostEstimate(
            flops=18 * EL * rows * D * FL, bytes_accessed=8 * EL * rows * D + 18 * EL * D * FL, transcendentals=EL * rows * FL
        ),
    )(x, g, gate, weights)


def _spread_kernel(own_ref, slot_ref, gg_ref, out_ref, entry_ref, o_ref, e_ref, *, width):
    group, experts = slot_ref.shape
    slots = out_ref.shape[2]
    total = experts * slots
    D = out_ref.shape[3]
    lane = lax.broadcasted_iota(jnp.int32, (experts, total), 1)
    which = lax.broadcasted_iota(jnp.int32, (experts, total), 0)
    choose = jnp.where((lane >= which * slots) & (lane < (which + 1) * slots), 1.0, 0.0).astype(BF16)
    offset = lane[:1] - jnp.sum(jnp.where(lane >= (which + 1) * slots, slots, 0), axis=0, keepdims=True)
    mine = dot(slot_ref[...].astype(BF16), choose)
    pick = jnp.where(mine == offset.astype(F32), 1.0, 0.0).astype(BF16)
    column = lax.broadcasted_iota(jnp.int32, (slots, 128), 1)
    grads = [jnp.where(column == own_ref[0] + e, gg_ref[e, 0], 0.0).astype(BF16) for e in range(experts)]
    e_ref[:, pl.ds(D, 128)] = dot(pick, jnp.concatenate(grads, axis=0)).astype(BF16)

    def step(i, _):
        cols = pl.ds(pl.multiple_of(i * width, width), width)
        for source, target in ((out_ref, o_ref), (entry_ref, e_ref)):
            rows = jnp.concatenate([source[e, 0, :, cols] for e in range(experts)], axis=0)
            target[:, cols] = dot(pick, rows).astype(BF16)
        return 0

    lax.fori_loop(0, D // width, step, 0)


def spread_rows(own, slot, gate_grads, out_rows, entry_rows, group):
    N, EL = slot.shape
    _, groups, slots, D = out_rows.shape
    picked = pl.BlockSpec((EL, 1, slots, D), lambda i, *_: (0, i, 0, 0))
    return pl.pallas_call(
        functools.partial(_spread_kernel, width=512),
        out_shape=[jax.ShapeDtypeStruct((N, D), BF16), jax.ShapeDtypeStruct((N, D + 128), BF16)],
        grid_spec=pltpu.PrefetchScalarGridSpec(
            num_scalar_prefetch=1,
            grid=(groups,),
            in_specs=[
                pl.BlockSpec((group, EL), lambda i, *_: (i, 0)),
                pl.BlockSpec((EL, 1, slots, 128), lambda i, *_: (0, i, 0, 0)),
                picked,
                picked,
            ],
            out_specs=[
                pl.BlockSpec((group, D), lambda i, *_: (i, 0)),
                pl.BlockSpec((group, D + 128), lambda i, *_: (i, 0)),
            ],
        ),
        compiler_params=pltpu.CompilerParams(vmem_limit_bytes=VMEM_BYTES),
        cost_estimate=pl.CostEstimate(flops=4 * EL * slots * N * D, bytes_accessed=8 * N * D, transcendentals=0),
    )(own, slot, gate_grads, out_rows, entry_rows)


def body(
    hidden_in,
    out_grad,
    attn_gain,
    query_weight,
    key_weight,
    value_weight,
    out_weight,
    query_gain,
    key_gain,
    ffn_gain,
    router_weight,
    expert_weights,
    routes,
    doc_starts,
):
    U = lax.axis_size("uly")
    Z = lax.axis_size("blk")
    u = lax.axis_index("uly")
    z = lax.axis_index("blk")
    T, D = hidden_in.shape
    EL = expert_weights.shape[0]
    N = U * Z * T
    RW = query_weight.shape[0]
    move = (Slice if (U, Z, T, D) == (8, 4, 128, 2048) else General)(U, Z, T, D)
    C, L = move.C, move.L

    gain_rows = attn_gain.astype(F32)[:, None]
    own_weights = jnp.stack([query_weight, key_weight, value_weight], axis=1).astype(F32)
    scaled_rows = (own_weights * gain_rows[:, :, None]).astype(BF16)
    pack = jnp.concatenate([router_weight] + [g[:, None] for g in (ffn_gain, query_gain, key_gain)], axis=1)
    pack = jnp.pad(pack, ((0, 0), (0, 128 - pack.shape[1])))
    hidden = hidden_in.astype(F32)
    first_scale = norm_scale(hidden)
    first_rows, qkv_weight, out_rows, packed, routes_all = move.enter(
        (hidden * first_scale).astype(BF16), scaled_rows, out_weight, pack, routes.T
    )
    routes_all = routes_all.transpose(0, 1, 3, 2).reshape(N, -1)
    weight_router = packed[:, :EXPERTS]
    gain_ffn = packed[:, EXPERTS].astype(F32)
    head_gains = lax.dynamic_slice_in_dim(packed[:, EXPERTS + 1 : EXPERTS + 3], move.group * C, C, 0).astype(F32)
    gain_query, gain_key = head_gains[:, 0], head_gains[:, 1]
    qkv_pre = dot(first_rows, qkv_weight)
    query_pre, key_pre, value_pre = qkv_pre[:, :C], qkv_pre[:, C : 2 * C], qkv_pre[:, 2 * C :]
    squares = jnp.stack([jnp.sum(query_pre * query_pre, axis=1), jnp.sum(key_pre * key_pre, axis=1)])
    scales = lax.rsqrt(move.head_sum(squares.reshape(-1, 128)).reshape(2, L) / D + EPS)
    query_scale, key_scale = scales[0][:, None], scales[1][:, None]
    local = jnp.arange(L, dtype=jnp.int32)
    position = (local // T * move.block_step + move.first_block) * T + local % T
    cosine, sine = rotary_tables(position)
    cosine, sine = cosine[:, None, :], sine[:, None, :]

    def rotated(pre, scale, gain):
        split = (pre * scale * gain).reshape(L, C // HEAD_DIM, HEAD_DIM)
        return rotate_forward(split, cosine, sine).reshape(L, C).astype(BF16)

    query_rot = rotated(query_pre, query_scale, gain_query)
    key_all, value_all = move.sequence(
        rotated(key_pre, key_scale, gain_key), value_pre.astype(BF16), out_grad
    )
    index = jnp.stack([move.first_block, jnp.int32(move.block_step)]).astype(jnp.int32)
    chunk = min(512, N)
    attended, logs = attention_forward(index, doc_starts, query_rot, key_all, value_all, T, chunk)
    attended_low = attended.astype(BF16)
    mixed, upstream_all = move.heads_to_rows(dot(attended_low, out_rows).astype(BF16))
    residual = hidden + mixed.astype(F32)

    second_scale = norm_scale(residual)
    second_low = (residual * second_scale * gain_ffn).astype(BF16)
    probabilities = jax.nn.softmax(dot(second_low, weight_router), axis=-1)
    second_all = move.gather(second_low)

    group = min(512, N)
    groups = N // group
    slots = -(-(group // T * CAP) // 16) * 16
    rows = groups * slots
    own_first = u * EL
    own_experts = own_first + jnp.arange(EL, dtype=jnp.int32)
    chosen = jnp.any(routes_all[None] == own_experts[:, None, None], axis=2).reshape(EL, groups, group)
    before = jnp.arange(group)[:, None] < jnp.arange(group)[None, :]
    earlier = jnp.einsum("egs,st->egt", chosen.astype(BF16), before.astype(BF16), preferred_element_type=F32)
    slot = jnp.where(chosen, earlier.astype(jnp.int32), -1).reshape(EL, N)
    own_router = jnp.roll(weight_router, -own_first, axis=1)
    entry_in, upstream_in, gate_rows = pick_rows(slot, own_router, second_all, upstream_all, group, slots)
    out_rows_e, entry_rows, expert_grads, gate_grads = run_experts(
        entry_in.reshape(EL, rows, D),
        upstream_in.reshape(EL, rows, D),
        gate_rows.reshape(EL, rows, 128),
        expert_weights,
        min(8, groups) * slots,
    )
    split = (EL, groups, slots, D)
    out_part, entry_part = spread_rows(
        own_first.astype(jnp.int32)[None],
        slot.T,
        gate_grads.reshape(EL, groups, slots, 128),
        out_rows_e.reshape(split),
        entry_rows.reshape(split),
        group,
    )
    entry_sum = move.scatter_wide(entry_part).astype(F32)

    second_grad, prob_grad = entry_sum[:, :D], entry_sum[:, D : D + EXPERTS]
    logit_grad = (
        probabilities * (prob_grad - jnp.sum(probabilities * prob_grad, axis=1, keepdims=True))
    ).astype(BF16)
    second_grad = second_grad + dot(logit_grad, weight_router, LAST_DIM)
    upstream = out_grad.astype(F32)
    weighted = second_grad * gain_ffn
    inner_mean = jnp.mean(weighted * residual, axis=-1, keepdims=True)
    residual_grad = upstream + second_scale * weighted - residual * (second_scale**3) * inner_mean
    ffn_gain_part = jnp.sum(second_grad * residual * second_scale, axis=0)

    residual_rows = move.rows_to_heads(residual_grad.astype(BF16), out_part)
    out_weight_part = dot(attended_low, residual_rows, FIRST_DIM).astype(BF16)
    attended_grad = dot(residual_rows, out_rows, LAST_DIM).astype(BF16)
    dq, dk_part, dv_part = attention_backward(
        index, doc_starts, query_rot, attended_grad, attended, logs, key_all, value_all, T, chunk
    )
    dk, dv, out_weight_grad, out_sum = move.sequence_sums(dk_part, dv_part, out_weight_part)
    output = (residual + out_sum.astype(F32)).astype(BF16)

    def rotated_back(grad):
        return rotate_backward(grad.astype(F32).reshape(L, C // HEAD_DIM, HEAD_DIM), cosine, sine).reshape(L, C)

    query_up, key_up = rotated_back(dq), rotated_back(dk)
    inner_sums = jnp.stack(
        [jnp.sum(query_up * gain_query * query_pre, axis=1), jnp.sum(key_up * gain_key * key_pre, axis=1)]
    )
    inner_sums = move.head_sum_again(inner_sums.reshape(-1, 128)).reshape(2, L) / D

    def pre_grad(up, gain, pre, scale, mean):
        return (scale * (up * gain) - pre * (scale**3) * mean[:, None]).astype(BF16)

    pre_grads = jnp.concatenate(
        [
            pre_grad(query_up, gain_query, query_pre, query_scale, inner_sums[0]),
            pre_grad(key_up, gain_key, key_pre, key_scale, inner_sums[1]),
            dv,
        ],
        axis=1,
    )
    gain_parts = jnp.stack(
        [jnp.sum(query_up * query_pre * query_scale, axis=0), jnp.sum(key_up * key_pre * key_scale, axis=0)]
    )
    weight_part = dot(first_rows, pre_grads, FIRST_DIM).astype(BF16)
    first_part = dot(pre_grads, qkv_weight, LAST_DIM).astype(BF16)
    first_weighted, weight_sum, logit_grad_all, ffn_gain_grad, head_gain_grads = move.leave(
        first_part, weight_part, logit_grad, ffn_gain_part, gain_parts
    )
    own_columns = lax.dynamic_slice_in_dim(second_all, (u * Z + z) * RW, RW, 1)
    router_grad = dot(own_columns, logit_grad_all, FIRST_DIM)
    weight_sum = weight_sum.astype(F32)
    attn_gain_grad = jnp.sum(own_weights * weight_sum, axis=(1, 2))
    weight_grads = weight_sum * gain_rows[:, :, None]
    first_weighted = first_weighted.astype(F32)
    first_mean = jnp.mean(first_weighted * hidden, axis=-1, keepdims=True)
    hidden_grad = residual_grad + first_scale * first_weighted - hidden * (first_scale**3) * first_mean
    return (
        output,
        hidden_grad,
        attn_gain_grad,
        weight_grads[:, 0],
        weight_grads[:, 1],
        weight_grads[:, 2],
        out_weight_grad.astype(F32),
        head_gain_grads[0],
        head_gain_grads[1],
        ffn_gain_grad,
        router_grad,
        expert_grads,
    )


def solution(mesh):
    rows = P(ALL, None)
    flat = P(ALL)
    experts = P("uly", None, None, "blk")
    return jax.shard_map(
        body,
        mesh=mesh,
        in_specs=(rows, rows, flat, rows, rows, rows, rows, flat, flat, flat, rows, experts, rows, P()),
        out_specs=(rows, rows, flat, rows, rows, rows, rows, flat, flat, flat, rows, experts),
        check_vma=False,
    )
```

```python
import functools

import jax
import jax.numpy as jnp
from jax import lax
from jax.experimental import pallas as pl
from jax.experimental.pallas import tpu as pltpu
from jax.sharding import PartitionSpec as P

HEADS = 16
HEAD_DIM = 128
EXPERTS = 64
CAP = 17

EPS = 1e-05
THETA = 10000.0
NEG = -1e30
FIRST_DIM = (((0,), (0,)), ((), ()))
LAST_DIM = (((1,), (1,)), ((), ()))
ALL = ("uly", "blk")
F32 = jnp.float32
BF16 = jnp.bfloat16
VMEM_BYTES = 56 * 1024 * 1024
PICK_WIDTH = 512
SPREAD_WIDTH = 2048


def dot(a, b, dims=(((1,), (0,)), ((), ()))):
    return lax.dot_general(a, b, dims, preferred_element_type=F32)


def rotary_tables(position):
    halfway = HEAD_DIM // 2
    frequency = THETA ** (-(jnp.arange(halfway).astype(F32) * 2.0 / HEAD_DIM))
    angles = position.astype(F32)[:, None] * frequency[None, :]
    cosine = jnp.concatenate([jnp.cos(angles), jnp.cos(angles)], axis=1)
    sine = jnp.concatenate([jnp.sin(angles), jnp.sin(angles)], axis=1)
    return cosine, sine


def rotate_forward(values, cosine, sine):
    halfway = values.shape[-1] // 2
    turned = jnp.concatenate([-values[..., halfway:], values[..., :halfway]], axis=-1)
    return values * cosine + turned * sine


def rotate_backward(upstream, cosine, sine):
    halfway = upstream.shape[-1] // 2
    moved = upstream * sine
    turned = jnp.concatenate([moved[..., halfway:], -moved[..., :halfway]], axis=-1)
    return upstream * cosine + turned


def norm_scale(values):
    return lax.rsqrt(jnp.mean(values * values, axis=-1, keepdims=True) + EPS)


MESH = pl.DeviceIdType.MESH
DMA = pltpu.SemaphoreType.DMA
ANY_SPACE = pl.BlockSpec(memory_space=pl.ANY)
IN_VMEM = pl.BlockSpec(memory_space=pltpu.VMEM)
DEPTH = 4
CHIPS = (0, 2, 4, 6)
FIRST, THEN = (2, 4), (4, 2)


def _send(src, dst, send_sem, recv_sem, to):
    pltpu.make_async_remote_copy(
        src_ref=src, dst_ref=dst, send_sem=send_sem, recv_sem=recv_sem, device_id=to, device_id_type=MESH
    ).start()


def _expect(ref, sem, here):
    pltpu.make_async_remote_copy(
        src_ref=ref, dst_ref=ref, send_sem=sem, recv_sem=sem, device_id=here, device_id_type=MESH
    ).wait_recv()


def _sent(ref, sem, here):
    pltpu.make_async_remote_copy(
        src_ref=ref, dst_ref=ref, send_sem=sem, recv_sem=sem, device_id=here, device_id_type=MESH
    ).wait_send()


def _greet(u, z, planes, line=False, others=()):
    barrier = pltpu.get_barrier_semaphore()
    for bit in planes:
        pl.semaphore_signal(barrier, inc=1, device_id=(u ^ bit, z), device_id_type=MESH)
    for to in others:
        pl.semaphore_signal(barrier, inc=1, device_id=to, device_id_type=MESH)
    count = len(planes) + len(others)
    if line:

        @pl.when(z > 0)
        def _():
            pl.semaphore_signal(barrier, inc=1, device_id=(u, z - 1), device_id_type=MESH)

        @pl.when(z < DEPTH - 1)
        def _():
            pl.semaphore_signal(barrier, inc=1, device_id=(u, z + 1), device_id_type=MESH)

        count = count + jnp.where((z == 0) | (z == DEPTH - 1), 1, 2)
    pl.semaphore_wait(barrier, count)


def _line_order(z):
    second = jnp.where(z == 0, 1, z - 1)
    third = jnp.where(z == 0, 2, jnp.where(z == 3, 1, z + 1))
    fourth = jnp.where(z < 2, 3, 0)
    return (z, second, third, fourth)


def _accumulate(target, source, rows):
    strip = 16

    def step(i, _):
        at = pl.ds(pl.multiple_of(i * strip, strip), strip)
        target[at, :] = target[at, :] + source[at, :]
        return 0

    lax.fori_loop(0, rows // strip, step, 0)


def _run(*parts, order=()):
    for i in order:
        next(parts[i])
    live = list(parts)
    while live:
        for part in list(live):
            try:
                next(part)
            except StopIteration:
                live.remove(part)


def _line_part(u, z, source, block, sems, share=True):
    z_send, z_recv, c_send, c_recv, own_sem = sems
    here, core = (u, z), u % 2
    own = pltpu.make_async_copy(source, block(core, z), own_sem)
    own.start()
    order = _line_order(z)

    def along(level, ref, step):
        @pl.when((z > 0) & (level >= z))
        def _():
            step(ref, 0, level, (u, z - 1))

        @pl.when((z < DEPTH - 1) & (level <= z))
        def _():
            step(ref, 1, level, (u, z + 1))

    def go(ref, way, level, to):
        _send(ref, block(core, level), z_send.at[way, level], z_recv.at[level], to)

    def gone(ref, way, level, to):
        _sent(ref, z_send.at[way, level], here)

    for i in range(4):
        level = order[i]
        ref = source if i == 0 else block(core, level)
        if i > 0:
            yield
            _expect(ref, z_recv.at[level], here)
        along(level, ref, go)
        if share:
            _send(ref, block(core, level), c_send.at[level], c_recv.at[level], (u ^ 1, z))
    yield
    if share:
        for i in range(4):
            _expect(block(1 - core, order[i]), c_recv.at[order[i]], here)
    yield
    for i in range(4):
        along(order[i], block(core, order[i]), gone)
        if share:
            _sent(block(core, order[i]), c_send.at[order[i]], here)
    own.wait()


def _plane_part(u, z, own, block, sems):
    p_send, p_recv, o_sem = sems
    here = (u, z)
    for way, bits in enumerate((FIRST, THEN)):
        for h in range(2):
            _send(own(h), block(h, u), p_send.at[h, way], p_recv.at[h, way], (u ^ bits[h], z))
    for h in range(2):
        pltpu.make_async_copy(own(h), block(h, u), o_sem.at[h]).start()
    for h in range(2):
        yield
        _expect(block(h, u ^ FIRST[h]), p_recv.at[h, 0], here)
        near = block(h, u ^ FIRST[h])
        _send(near, near, p_send.at[h, 2], p_recv.at[h, 2], (u ^ THEN[h], z))
    yield
    for h in range(2):
        _expect(block(h, u ^ THEN[h]), p_recv.at[h, 1], here)
        _expect(block(h, u ^ 6), p_recv.at[h, 2], here)
    yield
    for h in range(2):
        for k in range(3):
            _sent(block(h, u), p_send.at[h, k], here)
        pltpu.make_async_copy(own(h), block(h, u), o_sem.at[h]).wait()


def _plane_share_part(u, z, block, half, sems):
    p_send, p_recv, c_send, c_recv = sems
    here = (u, z)
    halves = (pl.ds(0, half), pl.ds(half, half))

    def source(i):
        return block(u, i)

    for i in range(4):
        for way, bits in enumerate((FIRST, THEN)):
            for h in range(2):
                at = block(u, i).at[halves[h]]
                _send(at, at, p_send.at[i, h, way], p_recv.at[i, h, way], (u ^ bits[h], z))
        _send(source(i), block(u, i), c_send.at[i, 0], c_recv.at[i, 0], (u ^ 1, z))

    def share(i):
        for h in range(2):
            _expect(block(u ^ THEN[h], i).at[halves[h]], p_recv.at[i, h, 1], here)
            _expect(block(u ^ 6, i).at[halves[h]], p_recv.at[i, h, 2], here)
        for k, bit in enumerate((2, 4, 6)):
            ref = block(u ^ bit, i)
            _send(ref, ref, c_send.at[i, k + 1], c_recv.at[i, k + 1], (u ^ 1, z))

    for i in range(4):
        yield
        for h in range(2):
            at = halves[h]
            near = block(u ^ FIRST[h], i).at[at]
            _expect(near, p_recv.at[i, h, 0], here)
            _send(near, near, p_send.at[i, h, 2], p_recv.at[i, h, 2], (u ^ THEN[h], z))
        if i > 0:
            share(i - 1)
    yield
    share(3)
    yield
    for i in range(4):
        for h in range(2):
            for k in range(3):
                _sent(block(u, i).at[halves[h]], p_send.at[i, h, k], here)
        for k, bit in enumerate((0, 2, 4, 6)):
            _sent(block(u, i), c_send.at[i, k], here)
            _expect(block(u ^ 1 ^ bit, i), c_recv.at[i, k], here)


PLANE_SHARE_SEMS = [DMA((4, 2, 3)), DMA((4, 2, 3)), DMA((4, 4)), DMA((4, 4))]


def _plane_sum_part(u, z, source, work, bufs, sems, rows, then_do):
    p_buf, q_buf = bufs
    load, p_send, p_recv, q_send, q_recv = sems
    here = (u, z)
    for j in (1, 0):
        for h in range(2):
            bit = (THEN[h], 6)[j]
            _send(source(h, u ^ bit), p_buf.at[h, j], p_send.at[h, j], p_recv.at[h, j], (u ^ THEN[h], z))
    for h in range(2):
        for j, bit in enumerate((0, FIRST[h])):
            pltpu.make_async_copy(source(h, u ^ bit), work.at[h, j], load.at[h, j]).start()
    for h in range(2):
        yield
        for j, bit in enumerate((0, FIRST[h])):
            pltpu.make_async_copy(source(h, u ^ bit), work.at[h, j], load.at[h, j]).wait()
        _expect(p_buf.at[h, 1], p_recv.at[h, 1], here)
        _accumulate(work.at[h, 1], p_buf.at[h, 1], rows)
        _send(work.at[h, 1], q_buf.at[h], q_send.at[h], q_recv.at[h], (u ^ FIRST[h], z))
    yield
    for h in range(2):
        _expect(p_buf.at[h, 0], p_recv.at[h, 0], here)
        _accumulate(work.at[h, 0], p_buf.at[h, 0], rows)
    for h in range(2):
        _expect(q_buf.at[h], q_recv.at[h], here)
        _accumulate(work.at[h, 0], q_buf.at[h], rows)
    then_do()
    yield
    for h in range(2):
        for j in range(2):
            _sent(p_buf.at[h, j], p_send.at[h, j], here)
        _sent(q_buf.at[h], q_send.at[h], here)


def _line_sum_part(u, z, source, work, bufs, sems, rows, then_do):
    c_buf, z_buf = bufs
    load, c_send, c_recv, z_send, z_recv = sems
    here, core = (u, z), u % 2
    order = tuple(reversed(_line_order(z)))
    for i in range(4):
        _send(source(1 - core, order[i]), c_buf.at[i], c_send.at[i], c_recv.at[i], (u ^ 1, z))
        pltpu.make_async_copy(source(core, order[i]), work.at[i], load.at[i]).start()
    for i in range(4):
        yield
        pltpu.make_async_copy(source(core, order[i]), work.at[i], load.at[i]).wait()
        _expect(c_buf.at[i], c_recv.at[i], here)
        _accumulate(work.at[i], c_buf.at[i], rows)
        if i == 3:
            yield
        _line_end(u, z, order[i], i, work.at[i], z_buf, (z_send, z_recv), rows)
    then_do()
    yield
    for i in range(4):
        _sent(c_buf.at[i], c_send.at[i], here)
        if i < 3:
            _sent(work.at[i], z_send.at[i], here)


def _column_peers(u, z):
    return [((u ^ c, z ^ k), c, k) for c in range(2) for k in range(4) if c or k]


def _comm(kernel, outs, scratch, collective_id, specs, flops=0, moved=100_000_000, aliases={}):
    return pl.pallas_call(
        kernel,
        out_shape=outs,
        in_specs=specs[0],
        out_specs=specs[1],
        scratch_shapes=scratch,
        input_output_aliases=aliases,
        compiler_params=pltpu.CompilerParams(
            collective_id=collective_id, has_side_effects=True, vmem_limit_bytes=VMEM_BYTES
        ),
        cost_estimate=pl.CostEstimate(flops=flops, bytes_accessed=moved, transcendentals=0),
    )


ENTER_ORDER = (0, 2, 1, 0, 2, 1, 0, 2, 0, 2)
LEAVE_ORDER = (0, 1, 2, 1, 2, 1, 0, 0, 1, 0, 1, 1)
LINE_SEMS = [DMA((2, 4)), DMA((4,)), DMA((4,)), DMA((4,)), DMA]
PLANE_SEMS = [DMA((2, 3)), DMA((2, 3)), DMA((2,))]
PLANE_SUM_SEMS = [DMA((2, 2)), DMA((2, 2)), DMA((2, 2)), DMA((2,)), DMA((2,))]
LINE_SUM_SEMS = [DMA((4,)), DMA((4,)), DMA((4,)), DMA((4,)), DMA((2, 4))]


def _small_part(u, z, xs, outs, sems):
    own_sem, z_send, z_recv, u_send, u_recv = sems
    here = (u, z)
    for a, (x, o) in enumerate(zip(xs, outs)):
        pltpu.make_async_copy(x, o.at[u, z], own_sem.at[a]).start()
        for k in range(1, 4):
            _send(x, o.at[u, z], z_send.at[a, k], z_recv.at[a, k], (u, z ^ k))
    yield
    for a, (x, o) in enumerate(zip(xs, outs)):
        pltpu.make_async_copy(x, o.at[u, z], own_sem.at[a]).wait()
        for k in range(1, 4):
            _expect(o.at[u, z ^ k], z_recv.at[a, k], here)
        for k in range(1, 8):
            _send(o.at[u], o.at[u], u_send.at[a, k], u_recv.at[a, k], (u ^ k, z))
    yield
    yield
    for a, (x, o) in enumerate(zip(xs, outs)):
        for k in range(1, 4):
            _sent(x, z_send.at[a, k], here)
        for k in range(1, 8):
            _sent(o.at[u], u_send.at[a, k], here)
            _expect(o.at[u ^ k], u_recv.at[a, k], here)


def _small_sems(n):
    return [DMA((n,)), DMA((n, 4)), DMA((n, 4)), DMA((n, 8)), DMA((n, 8))]


def enter(rows, weights, smalls, collective_id):
    R, C = weights.shape[1], weights.shape[2] // 8
    held = (2, 4, R, 3 * C)
    n = len(smalls)

    def kernel(*refs):
        x_ref, w_ref = refs[:2]
        small_in = refs[2 : 2 + n]
        x_out, w_out = refs[2 + n : 4 + n]
        small_out = refs[4 + n : 4 + 2 * n]
        w_buf, w_send, w_recv = refs[4 + 2 * n : 7 + 2 * n]
        sems = refs[7 + 2 * n :]
        u, z = lax.axis_index("uly"), lax.axis_index("blk")
        here, core, chip = (u, z), u % 2, u // 2
        column = _column_peers(u, z)
        _greet(u, z, range(1, 8), others=[to for to, c, k in column if k])

        def weight_part():
            def cut(j, c, level):
                return w_ref.at[j, :, pl.ds(pl.multiple_of((2 * level + c) * C, C), C)]

            def slot(j, c, level):
                return w_buf.at[c, level, :, pl.ds(j * C, C)]

            for i, (to, c, k) in enumerate(column):
                for j in range(3):
                    _send(cut(j, core ^ c, z ^ k), slot(j, core, z), w_send.at[i, j], w_recv.at[i, j], to)
            for j in range(3):
                slot(j, core, z)[...] = cut(j, core, z)[...]
            yield
            for i, (to, c, k) in enumerate(column):
                for j in range(3):
                    _expect(slot(j, core ^ c, z ^ k), w_recv.at[i, j], here)
            yield from _plane_part(u, z, lambda h: w_buf.at[h], lambda h, v: w_out.at[v // 2, h], sems[:3])
            for i, (to, c, k) in enumerate(column):
                for j in range(3):
                    _sent(cut(j, core ^ c, z ^ k), w_send.at[i, j], here)

        _run(
            weight_part(),
            _small_part(u, z, small_in, small_out, sems[8:]),
            _line_part(u, z, x_ref, lambda c, level: x_out.at[c, level], sems[3:8]),
            order=ENTER_ORDER,
        )

    outs = [
        jax.ShapeDtypeStruct((2, 4) + rows.shape, rows.dtype),
        jax.ShapeDtypeStruct((4,) + held, weights.dtype),
    ] + [jax.ShapeDtypeStruct((8, 4) + x.shape, x.dtype) for x in smalls]
    scratch = [pltpu.VMEM(held, BF16), DMA((7, 3)), DMA((7, 3))] + PLANE_SEMS + LINE_SEMS + _small_sems(n)
    specs = ([IN_VMEM, IN_VMEM] + [IN_VMEM] * n, [ANY_SPACE] * len(outs))
    return _comm(kernel, outs, scratch, collective_id, specs)(rows, weights, *smalls)


def column_sum(x, collective_id):
    def kernel(x_ref, o_ref, buf, send, recv):
        u, z = lax.axis_index("uly"), lax.axis_index("blk")
        here = (u, z)
        column = _column_peers(u, z)
        _greet(u, z, (), others=[to for to, c, k in column])
        for i, (to, c, k) in enumerate(column):
            _send(x_ref, buf.at[i], send.at[i], recv.at[i], to)
        total = x_ref[...]
        for i in range(7):
            _expect(buf.at[i], recv.at[i], here)
            total = total + buf[i]
        o_ref[...] = total
        for i in range(7):
            _sent(x_ref, send.at[i], here)

    scratch = [pltpu.VMEM((7,) + x.shape, F32), DMA((7,)), DMA((7,))]
    out = jax.ShapeDtypeStruct(x.shape, F32)
    return _comm(kernel, out, scratch, collective_id, ([IN_VMEM], IN_VMEM))(x)


def plane_pair(first, second, rows, collective_id):
    def kernel(a_ref, b_ref, x_ref, a_out, b_out, x_out, *sems):
        u, z = lax.axis_index("uly"), lax.axis_index("blk")
        _greet(u, z, (2, 4), line=True)
        own, outs = (a_ref, b_ref), (a_out, b_out)
        _run(
            _plane_part(u, z, lambda h: own[h], lambda h, v: outs[h].at[v // 2], sems[:3]),
            _line_part(u, z, x_ref, lambda c, level: x_out.at[u * DEPTH + level], sems[3:], share=False),
        )

    outs = [jax.ShapeDtypeStruct((4,) + x.shape, x.dtype) for x in (first, second)]
    outs += [jax.ShapeDtypeStruct((32,) + rows.shape, rows.dtype)]
    specs = ([IN_VMEM] * 2 + [ANY_SPACE], [ANY_SPACE] * 3)
    return _comm(kernel, outs, PLANE_SEMS + LINE_SEMS, collective_id, specs)(first, second, rows)


def column_gather(rows, slot, out_rows, collective_id):
    T, D = rows.shape
    EL, _, slots, _ = out_rows.shape

    def kernel(r_ref, slot_ref, rows_ref, r_out, x_out, *refs):
        u, z = lax.axis_index("uly"), lax.axis_index("blk")
        _greet(u, z, (1, 2, 4), line=True)
        order = _line_order(z)

        def keep(i, part):
            x_out[order[i]] = part[...]

        _run(
            _line_part(u, z, r_ref, lambda c, level: r_out.at[c, level], refs[-5:]),
            _spread_part(u, z, slot_ref, rows_ref, None, order, refs[:-5], keep),
        )

    outs = [jax.ShapeDtypeStruct((2, 4, T, D), BF16), jax.ShapeDtypeStruct((4, T, D), BF16)]
    specs = ([IN_VMEM, IN_VMEM, ANY_SPACE], [ANY_SPACE, IN_VMEM])
    scratch = _spread_scratch(T, D, (EL, slots, D)) + LINE_SEMS
    return _comm(kernel, outs, scratch, collective_id, specs)(rows, slot, out_rows)


def _line_sum_scratch(T, D):
    return [pltpu.VMEM((4, T, D), BF16), pltpu.VMEM((4, T, D), BF16), pltpu.VMEM((2, 4, T, D), BF16)]


def column_scatter(x, rows, collective_id):
    T, D = x.shape[2:]

    def kernel(x_ref, g_ref, o_ref, g_out, work, c_buf, z_buf, *sems):
        u, z = lax.axis_index("uly"), lax.axis_index("blk")
        _greet(u, z, (1, 2, 4), line=True)

        def finish():
            o_ref[...] = work[3]

        _run(
            _line_sum_part(u, z, lambda c, level: x_ref.at[c, level], work, (c_buf, z_buf), sems[:5], T, finish),
            _plane_share_part(u, z, lambda who, i: g_out.at[who * DEPTH + i], T // 2, sems[5:]),
        )

    outs = [jax.ShapeDtypeStruct((T, D), BF16), jax.ShapeDtypeStruct((32, T, D), BF16)]
    scratch = _line_sum_scratch(T, D) + LINE_SUM_SEMS + PLANE_SHARE_SEMS
    specs = ([ANY_SPACE] * 2, [IN_VMEM, ANY_SPACE])
    out, gathered = _comm(kernel, outs, scratch, collective_id, specs, aliases={1: 1})(x, rows)
    return out, gathered.reshape(32 * T, D)


def _plane_sum_scratch(rows, cols):
    return [pltpu.VMEM((2, 2, rows, cols), BF16), pltpu.VMEM((2, 2, rows, cols), BF16), pltpu.VMEM((2, rows, cols), BF16)]


def key_value_sums(dk, dv, x, collective_id):
    T, D = x.shape[1:]
    L, C = dk.shape[1:]

    def kernel(k_ref, v_ref, x_ref, k_out, v_out, x_out, work, p_buf, q_buf, x_work, z_buf, *sems):
        u, z = lax.axis_index("uly"), lax.axis_index("blk")
        _greet(u, z, (2, 4), line=True)
        load, z_send, z_recv = sems[5:]
        order = tuple(reversed(_line_order(z)))

        def finish():
            k_out[...] = work[0, 0]
            v_out[...] = work[1, 0]

        def line():
            copies = [pltpu.make_async_copy(x_ref.at[order[i]], x_work.at[i], load.at[i]) for i in range(4)]
            for copy in copies:
                copy.start()
            for copy in copies:
                copy.wait()
            for i in range(4):
                _line_end(u, z, order[i], i, x_work.at[i], z_buf, (z_send, z_recv), T)
                yield
            x_out[...] = x_work[3]
            for i in range(3):
                _sent(x_work.at[i], z_send.at[i], (u, z))

        _run(
            _plane_sum_part(
                u, z, lambda h, v: (k_ref, v_ref)[h].at[v // 2], work, (p_buf, q_buf), sems[:5], L, finish
            ),
            line(),
            order=(0, 1, 0, 0),
        )

    outs = [jax.ShapeDtypeStruct((L, C), BF16)] * 2 + [jax.ShapeDtypeStruct((T, D), BF16)]
    scratch = _plane_sum_scratch(L, C) + [pltpu.VMEM((4, T, D), BF16), pltpu.VMEM((2, 4, T, D), BF16)]
    scratch += PLANE_SUM_SEMS + [DMA((4,)), DMA((4,)), DMA((2, 4))]
    specs = ([ANY_SPACE] * 3, [IN_VMEM] * 3)
    return _comm(kernel, outs, scratch, collective_id, specs)(dk, dv, x)


def leave(x, weights, smalls, collective_id):
    n = len(smalls)
    T, D = x.shape[2:]
    rows, W = weights.shape[2:]
    R, C = rows // 4, W // 3

    def kernel(x_ref, w_ref, *refs):
        small_in, (o_ref, w_out), small_out = refs[:n], refs[n : n + 2], refs[n + 2 : 2 * n + 2]
        work, c_buf, z_buf, w_work, wp_buf, wq_buf = refs[2 * n + 2 : 2 * n + 8]
        sems = refs[2 * n + 8 :]
        u, z = lax.axis_index("uly"), lax.axis_index("blk")
        here, core, chip = (u, z), u % 2, u // 2
        column = _column_peers(u, z)
        _greet(u, z, range(1, 8), others=[to for to, c, k in column if k])
        t_send, t_recv = sems[10:12]
        group = 2 * z + core

        def finish():
            o_ref[...] = work[3]

        def cut(j, c, level):
            return w_work.at[c, 0, pl.ds(pl.multiple_of(level * R, R), R), pl.ds(j * C, C)]

        def slot(j, g):
            return w_out.at[j, :, pl.ds(pl.multiple_of(g * C, C), C)]

        def deal():
            for i, (to, c, k) in enumerate(column):
                for j in range(3):
                    _send(cut(j, core ^ c, z ^ k), slot(j, group), t_send.at[i, j], t_recv.at[i, j], to)
            for j in range(3):
                slot(j, group)[...] = cut(j, core, z)[...]

        _run(
            _plane_sum_part(u, z, lambda h, v: w_ref.at[v // 2, h], w_work, (wp_buf, wq_buf), sems[5:10], rows, deal),
            _line_sum_part(u, z, lambda c, level: x_ref.at[c, level], work, (c_buf, z_buf), sems[:5], T, finish),
            _small_part(u, z, small_in, small_out, sems[12:]),
            order=LEAVE_ORDER,
        )
        for i, (to, c, k) in enumerate(column):
            for j in range(3):
                _expect(slot(j, 2 * (z ^ k) + (core ^ c)), t_recv.at[i, j], here)
                _sent(cut(j, core ^ c, z ^ k), t_send.at[i, j], here)

    outs = [jax.ShapeDtypeStruct((T, D), BF16), jax.ShapeDtypeStruct((3, R, 8 * C), BF16)]
    outs += [jax.ShapeDtypeStruct((8, 4) + x.shape, x.dtype) for x in smalls]
    scratch = _line_sum_scratch(T, D) + _plane_sum_scratch(rows, W) + LINE_SUM_SEMS + PLANE_SUM_SEMS
    scratch += [DMA((7, 3)), DMA((7, 3))] + _small_sems(n)
    specs = ([ANY_SPACE] * 2 + [IN_VMEM] * n, [IN_VMEM] * 2 + [ANY_SPACE] * n)
    return _comm(kernel, outs, scratch, collective_id, specs)(x, weights, *smalls)


class _Jobs:
    def __init__(self, load, compute):
        self.load, self.compute = load, compute
        self.queue, self.count, self.ready = [], 0, None

    def add(self, *jobs):
        self.queue += jobs

    def _next(self):
        if not self.queue:
            return None
        job = (self.count, self.queue.pop(0))
        self.count += 1
        self.load(*job, True)
        return job

    def run(self, number=1):
        for _ in range(number):
            now = self.ready or self._next()
            if now is None:
                return
            self.ready = self._next()
            self.load(*now, False)
            self.compute(*now)


def _gather_pick_kernel(
    x_ref, g_ref, slot_ref, router_ref, o_ref, xr_ref, gr_ref, gate_ref, pick, in_buf, out_buf, in_sem, out_sem, *sems, width
):
    own_sem, z_send, z_recv, p_send, p_recv, c_send, c_recv = sems
    u, z = lax.axis_index("uly"), lax.axis_index("blk")
    core = u % 2
    T, D = x_ref.shape
    experts, group = slot_ref.shape[1:]
    slots = out_buf.shape[2]
    half = T // 2
    halves = (pl.ds(0, half), pl.ds(half, half))
    here = (u, z)
    _greet(u, z, (1, 2, 4), line=True)
    own = pltpu.make_async_copy(x_ref, o_ref.at[u * DEPTH + z], own_sem)
    own.start()
    order = _line_order(z)

    def block(who, level):
        return o_ref.at[who * DEPTH + level]

    def part(who, level, h):
        return o_ref.at[who * DEPTH + level, halves[h]]

    def load(n, job, start):
        source, level, which = job[:3]
        ref = g_ref if source == "g" else o_ref
        for p in range(4):
            copy = pltpu.make_async_copy(
                ref.at[(2 * p + which) * DEPTH + level], in_buf.at[n % 2, pl.ds(p * T, T)], in_sem.at[n % 2, p]
            )
            copy.start() if start else copy.wait()

    def out_copy(n, target, at):
        return pltpu.make_async_copy(out_buf.at[n % 2], target.at[:, at], out_sem.at[n % 2])

    sent = {}

    def compute(n, job):
        source, level, which = job
        at = 2 * level + which
        rows_in, rows_out = in_buf.at[n % 2], out_buf.at[n % 2]
        row = lax.broadcasted_iota(jnp.int32, (slots, group), 0)
        if source == "g":
            picks = [jnp.where(slot_ref[at, e : e + 1, :] == row, 1.0, 0.0).astype(BF16) for e in range(experts)]
            pick[at] = jnp.concatenate(picks, axis=0)
        else:
            logits = lax.dot_general(
                router_ref[...], rows_in[...], (((0,), (1,)), ((), ())), preferred_element_type=F32
            )
            powers = jnp.exp(logits - jnp.max(logits, axis=0, keepdims=True))
            chances = powers / jnp.sum(powers, axis=0, keepdims=True)
            for e in range(experts):
                gates = jnp.where(slot_ref[at, e : e + 1, :] == row, chances[e : e + 1, :], 0.0)
                gate_ref[e, at] = jnp.broadcast_to(jnp.sum(gates, axis=1, keepdims=True), (slots, 128))
        if n >= 2:
            sent.pop(n - 2).wait()

        def step(i, _):
            cols = pl.ds(pl.multiple_of(i * width, width), width)
            rows = dot(pick[at], rows_in[:, cols]).astype(BF16)
            for e in range(experts):
                rows_out[e, :, cols] = rows[e * slots : (e + 1) * slots]
            return 0

        lax.fori_loop(0, D // width, step, 0)
        sent[n] = out_copy(n, gr_ref if source == "g" else xr_ref, at)
        sent[n].start()

    jobs = _Jobs(load, compute)
    jobs.add(*[("g", level, c) for level in range(4) for c in range(2)])

    def along(level, source, step):
        @pl.when((z > 0) & (level >= z))
        def _():
            step(source, 0, level, (u, z - 1))

        @pl.when((z < DEPTH - 1) & (level <= z))
        def _():
            step(source, 1, level, (u, z + 1))

    def go(source, way, level, to):
        _send(source, block(u, level), z_send.at[way, level], z_recv.at[level], to)

    def gone(source, way, level, to):
        _sent(source, z_send.at[way, level], here)

    sources = [x_ref] + [block(u, order[i]) for i in range(1, 4)]

    def arrive(i):
        level = order[i]
        if i:
            _expect(block(u, level), z_recv.at[level], here)
        along(level, sources[i], go)
        for way, bits in enumerate((FIRST, THEN)):
            for h in range(2):
                cut = sources[i].at[halves[h]]
                _send(cut, part(u, level, h), p_send.at[level, h, way], p_recv.at[level, h, way], (u ^ bits[h], z))
        _send(sources[i], block(u, level), c_send.at[level, 0], c_recv.at[level, 0], (u ^ 1, z))

    def onward(i):
        level = order[i]
        for h in range(2):
            near = part(u ^ FIRST[h], level, h)
            _expect(near, p_recv.at[level, h, 0], here)
            _send(near, near, p_send.at[level, h, 2], p_recv.at[level, h, 2], (u ^ THEN[h], z))

    def share(i):
        level = order[i]
        for h in range(2):
            _expect(part(u ^ THEN[h], level, h), p_recv.at[level, h, 1], here)
            _expect(part(u ^ 6, level, h), p_recv.at[level, h, 2], here)
        for k, bit in enumerate((2, 4, 6)):
            ref = block(u ^ bit, level)
            _send(ref, ref, c_send.at[level, k + 1], c_recv.at[level, k + 1], (u ^ 1, z))
        jobs.add(("x", level, core))

    def received(i):
        level = order[i]
        for k, bit in enumerate((0, 2, 4, 6)):
            _expect(block(u ^ 1 ^ bit, level), c_recv.at[level, k], here)
        jobs.add(("x", level, 1 - core))

    arrive(0)
    jobs.run(2)
    onward(0)
    jobs.run(1)
    arrive(1)
    jobs.run(2)
    own.wait()
    share(0)
    jobs.run(2)
    onward(1)
    arrive(2)
    received(0)
    jobs.run(2)
    arrive(3)
    share(1)
    received(1)
    jobs.run(1)
    onward(2)
    jobs.run(2)
    share(2)
    received(2)
    jobs.run(1)
    onward(3)
    jobs.run(2)
    share(3)
    received(3)
    jobs.run(16)
    for i in range(4):
        level = order[i]
        along(level, sources[i], gone)
        for h in range(2):
            for k in range(3):
                _sent(part(u, level, h), p_send.at[level, h, k], here)
        for k in range(4):
            _sent(block(u, level), c_send.at[level, k], here)
    for copy in sent.values():
        copy.wait()


def gather_pick(x, g_all, slot, router, slots, collective_id):
    T, D = x.shape
    groups, EL, group = slot.shape
    picked = jax.ShapeDtypeStruct((EL, groups, slots, D), BF16)
    outs = [
        jax.ShapeDtypeStruct((32, T, D), BF16),
        picked,
        picked,
        jax.ShapeDtypeStruct((EL, groups, slots, 128), F32),
    ]
    scratch = [
        pltpu.VMEM((groups, EL * slots, group), BF16),
        pltpu.VMEM((2, group, D), BF16),
        pltpu.VMEM((2, EL, slots, D), BF16),
        DMA((2, 4)),
        DMA((2,)),
        DMA,
        DMA((2, 4)),
        DMA((4,)),
        DMA((4, 2, 3)),
        DMA((4, 2, 3)),
        DMA((4, 4)),
        DMA((4, 4)),
    ]
    specs = ([IN_VMEM, ANY_SPACE, IN_VMEM, IN_VMEM], [ANY_SPACE] * 3 + [IN_VMEM])
    kernel = functools.partial(_gather_pick_kernel, width=PICK_WIDTH)
    out, xr, gr, gates = _comm(kernel, outs, scratch, collective_id, specs)(x, g_all.reshape(32, T, D), slot, router)
    return out.reshape(32 * T, D), xr, gr, gates


def _tree_sum_steps(u, z, own, bufs, sems, T):
    c_buf, p_buf, q_buf = bufs
    c_send, c_recv, p_send, p_recv, q_send, q_recv = sems
    here = (u, z)
    half = T // 2
    halves = (pl.ds(0, half), pl.ds(half, half))

    def to_sibling(i, k, ref):
        _send(ref, c_buf.at[i, k], c_send.at[i, k], c_recv.at[i, k], (u ^ 1, z))

    def add_core(i):
        for k in (3, 2, 1, 0):
            _expect(c_buf.at[i, k], c_recv.at[i, k], here)
            _accumulate(own(i, k), c_buf.at[i, k], T)
            for h in range(2):
                if k and (k == 3 or CHIPS[k] == THEN[h]):
                    j = 1 if k == 3 else 0
                    part = own(i, k).at[halves[h]]
                    _send(part, p_buf.at[i, h, j], p_send.at[i, h, j], p_recv.at[i, h, j], (u ^ THEN[h], z))

    def add_far(i):
        for h in range(2):
            part = own(i, CHIPS.index(FIRST[h])).at[halves[h]]
            _expect(p_buf.at[i, h, 1], p_recv.at[i, h, 1], here)
            _accumulate(part, p_buf.at[i, h, 1], half)
            _send(part, q_buf.at[i, h], q_send.at[i, h], q_recv.at[i, h], (u ^ FIRST[h], z))

    def add_near(i):
        for h in range(2):
            _expect(p_buf.at[i, h, 0], p_recv.at[i, h, 0], here)
            _accumulate(own(i, 0).at[halves[h]], p_buf.at[i, h, 0], half)

    def add_then(i):
        for h in range(2):
            _expect(q_buf.at[i, h], q_recv.at[i, h], here)
            _accumulate(own(i, 0).at[halves[h]], q_buf.at[i, h], half)

    def finish():
        for i in range(4):
            for k in range(4):
                _sent(c_buf.at[i, k], c_send.at[i, k], here)
            for h in range(2):
                for j in range(2):
                    _sent(p_buf.at[i, h, j], p_send.at[i, h, j], here)
                _sent(q_buf.at[i, h], q_send.at[i, h], here)

    return to_sibling, add_core, add_far, add_near, add_then, finish


def _line_end(u, z, level, i, part, z_buf, sems, rows):
    z_send, z_recv = sems
    here = (u, z)

    @pl.when((level >= z) & (z > 0))
    def _():
        _expect(z_buf.at[0, level], z_recv.at[0, level], here)
        _accumulate(part, z_buf.at[0, level], rows)

    @pl.when((level <= z) & (z < DEPTH - 1))
    def _():
        _expect(z_buf.at[1, level], z_recv.at[1, level], here)
        _accumulate(part, z_buf.at[1, level], rows)

    if i < 3:

        @pl.when(level > z)
        def _():
            _send(part, z_buf.at[0, level], z_send.at[i], z_recv.at[0, level], (u, z + 1))

        @pl.when(level < z)
        def _():
            _send(part, z_buf.at[1, level], z_send.at[i], z_recv.at[1, level], (u, z - 1))


def _spread_part(u, z, slot_ref, source, gg_ref, order, refs, level_done, later=lambda i: None):
    work, c_buf, p_buf, q_buf, side, in_buf, in_sem = refs[:7]
    core, chip = u % 2, u // 2
    other = 1 - core
    _, group, experts = slot_ref.shape
    slots, D = source.shape[2:]
    total = experts * slots
    T = group // 4

    def place(k):
        return pl.ds(pl.multiple_of((chip ^ (CHIPS[k] // 2)) * T, T), T)

    def own(i, k):
        return work.at[i, place(k)]

    to_sibling, add_core, add_far, add_near, add_then, finish = _tree_sum_steps(
        u, z, own, (c_buf, p_buf, q_buf), refs[7:], T
    )
    lane = lax.broadcasted_iota(jnp.int32, (experts, total), 1)
    which = lax.broadcasted_iota(jnp.int32, (experts, total), 0)
    choose = jnp.where((lane >= which * slots) & (lane < (which + 1) * slots), 1.0, 0.0).astype(BF16)
    offset = lane[:1] - jnp.sum(jnp.where(lane >= (which + 1) * slots, slots, 0), axis=0, keepdims=True)
    offset = offset.astype(F32)
    column = lax.broadcasted_iota(jnp.int32, (slots, 128), 1)

    def load(n, job, start):
        i, c = job
        copy = pltpu.make_async_copy(source.at[:, 2 * order[i] + c], in_buf.at[n % 2], in_sem.at[n % 2])
        copy.start() if start else copy.wait()

    def compute(n, job):
        i, c = job
        at = 2 * order[i] + c
        mine = dot(slot_ref[at].astype(BF16), choose)
        pick = jnp.where(mine == offset, 1.0, 0.0).astype(BF16)
        rows_in = in_buf.at[n % 2]
        target = work.at[i] if c is core else side.at[i]
        if gg_ref is not None:
            grads = [jnp.where(column == u * experts + e, gg_ref[e, at], 0.0).astype(BF16) for e in range(experts)]
            target[:, pl.ds(D, 128)] = dot(pick, jnp.concatenate(grads, axis=0)).astype(BF16)

        def step(j, _):
            cols = pl.ds(pl.multiple_of(j * SPREAD_WIDTH, SPREAD_WIDTH), SPREAD_WIDTH)
            rows = jnp.concatenate([rows_in[e, :, cols] for e in range(experts)], axis=0)
            target[:, cols] = dot(pick, rows).astype(BF16)
            return 0

        lax.fori_loop(0, D // SPREAD_WIDTH, step, 0)
        if c is not core:
            for k in (3, 2, 1, 0):
                to_sibling(i, k, side.at[i, place(k)])

    def end(i):
        add_then(i)
        level_done(i, own(i, 0))

    jobs = _Jobs(load, compute)
    for i in range(4):
        jobs.add((i, other), (i, core))
    jobs.run(2)
    add_core(0)
    yield
    jobs.run(2)
    add_far(0)
    add_core(1)
    yield
    add_near(0)
    jobs.run(2)
    add_far(1)
    add_core(2)
    yield
    end(0)
    later(0)
    add_near(1)
    jobs.run(2)
    add_far(2)
    add_core(3)
    yield
    end(1)
    later(1)
    add_near(2)
    add_far(3)
    yield
    end(2)
    later(2)
    add_near(3)
    yield
    end(3)
    later(3)
    yield
    finish()


def _spread_scratch(T, W, rows_shape):
    half = T // 2
    return [
        pltpu.VMEM((4, 4 * T, W), BF16),
        pltpu.VMEM((4, 4, T, W), BF16),
        pltpu.VMEM((4, 2, 2, half, W), BF16),
        pltpu.VMEM((4, 2, half, W), BF16),
        pltpu.VMEM((4, 4 * T, W), BF16),
        pltpu.VMEM((2,) + rows_shape, BF16),
        DMA((2,)),
        DMA((4, 4)),
        DMA((4, 4)),
        DMA((4, 2, 2)),
        DMA((4, 2, 2)),
        DMA((4, 2)),
        DMA((4, 2)),
    ]


def spread_scatter(slot, gate_grads, entry_rows, collective_id):
    groups, group, EL = slot.shape
    slots, D = entry_rows.shape[2:]
    T, W = group // 4, D + 128

    def kernel(slot_ref, gg_ref, entry_ref, o_ref, z_buf, z_send, z_recv, *refs):
        u, z = lax.axis_index("uly"), lax.axis_index("blk")
        order = tuple(reversed(_line_order(z)))
        parts = []

        def done(i, part):
            parts.append(part)

        def line(i):
            _line_end(u, z, order[i], i, parts[i], z_buf, (z_send, z_recv), T)

        _greet(u, z, (1, 2, 4), line=True)
        _run(_spread_part(u, z, slot_ref, entry_ref, gg_ref, order, refs, done, line))
        o_ref[...] = parts[3][...]
        for i in range(3):
            _sent(parts[i], z_send.at[i], (u, z))

    scratch = [pltpu.VMEM((2, 4, T, W), BF16), DMA((4,)), DMA((2, 4))] + _spread_scratch(T, W, (EL, slots, D))
    specs = ([IN_VMEM, IN_VMEM, ANY_SPACE], IN_VMEM)
    out = jax.ShapeDtypeStruct((T, W), BF16)
    return _comm(kernel, out, scratch, collective_id, specs)(slot, gate_grads, entry_rows)


def slots_of(chosen):
    count = chosen.shape[-1]
    before = (jnp.arange(count)[:, None] < jnp.arange(count)[None, :]).astype(BF16)
    earlier = jnp.einsum("abs,st->abt", chosen.astype(BF16), before, preferred_element_type=F32)
    return jnp.where(chosen, earlier.astype(jnp.int32), -1)


class Slice:
    def __init__(self, U, Z, T, D):
        self.U, self.Z, self.T, self.D = U, Z, T, D
        self.u, self.z = lax.axis_index("uly"), lax.axis_index("blk")
        self.C = D // 8
        self.L = 8 * T
        self.group = 2 * self.z + self.u % 2
        self.first_block, self.block_step = 8 * (self.u // 2), 1

    def enter(self, rows, scaled, out_weight, pack, routes):
        rows, weights, packs, routes = enter(rows, scaled, [pack, routes], 1)
        there = [((2 * ((z + u // 2) % 4) + u % 2), u // 2) for u in range(8) for z in range(4)]
        self.forth = [(i, 4 * u + z) for i, (u, z) in enumerate(there)]
        mine = self.permute(out_weight, self.forth)
        outs = jnp.stack([mine] + [self.permute(mine, self.across(bit)) for bit in (2, 4, 6)])
        part = jnp.arange(4, dtype=jnp.int32)
        outs = outs[(self.u // 2) ^ ((part + self.z) % 4)]
        return (
            rows.reshape(self.L, self.D),
            weights.reshape(self.D, 3 * self.C),
            outs.reshape(self.C, self.D),
            packs.reshape(self.D, -1),
            routes,
        )

    def permute(self, x, pairs):
        return lax.ppermute(x, ALL, pairs)

    def across(self, bit):
        return [(i, i ^ (4 * bit)) for i in range(32)]

    def head_sum(self, x):
        return column_sum(x, 2)

    def head_sum_again(self, x):
        return column_sum(x, 3)

    def sequence(self, key, value, upstream):
        keys, values, self.upstream_line = plane_pair(key, value, upstream, 4)
        return keys.reshape(-1, self.C), values.reshape(-1, self.C)

    def heads_to_rows(self, x):
        return column_scatter(x.reshape(2, 4, self.T, self.D), self.upstream_line, 5)

    def experts(self, second_low, upstream_all, routes, weights, router):
        EL, T, D = weights.shape[0], self.T, self.D
        slots = -(-4 * CAP // 16) * 16
        chosen = jnp.any(routes[None] == (self.u * EL + jnp.arange(EL, dtype=jnp.int32))[:, None, None, None, None], axis=3)
        chosen = chosen.reshape(EL, 4, 2, 4, T).transpose(3, 2, 0, 1, 4).reshape(8, EL, 4 * T)
        slot = slots_of(chosen)
        second_all, xr, gr, gates = gather_pick(second_low, upstream_all, slot, router, slots, 7)
        flat, cut = (EL, 8 * slots, -1), (EL, 8, slots, -1)
        out_rows, entry_rows, self.expert_grads, gate_grads = run_experts(
            xr.reshape(flat), gr.reshape(flat), gates.reshape(flat), weights, 8 * slots
        )
        self.slot, self.out_rows = slot.transpose(0, 2, 1), out_rows.reshape(cut)
        return second_all, spread_scatter(self.slot, gate_grads.reshape(cut), entry_rows.reshape(cut), 8)

    def rows_to_heads(self, x):
        rows, self.out_line = column_gather(x, self.slot, self.out_rows, 6)
        return rows.reshape(self.L, self.D), self.expert_grads

    def sequence_sums(self, dk, dv, out_part):
        cut = (4, self.L, self.C)
        dk, dv, out_sum = key_value_sums(dk.reshape(cut), dv.reshape(cut), self.out_line, 10)
        parts = out_part.reshape(4, -1, self.D)
        chip = self.u // 2

        def part(bit):
            return lax.dynamic_index_in_dim(parts, ((chip ^ (bit // 2)) - self.z) % 4, 0, False)

        total = part(0).astype(F32)
        for bit in (2, 4, 6):
            total = total + self.permute(part(bit), self.across(bit)).astype(F32)
        out_grad = self.permute(total.astype(BF16), [(b, a) for a, b in self.forth])
        return dk, dv, out_grad, out_sum

    def leave(self, first_part, weight_part, logit_grad, ffn_part, head_parts):
        T, R = self.T, self.D // 32
        thin = jnp.concatenate([ffn_part.reshape(-1, 128), head_parts.reshape(-1, 128)], axis=0)
        wide = self.D // 128
        used = thin.shape[0]
        thin = jnp.pad(thin, ((0, -used % 8), (0, 0)))
        first, weights, logit_all, thin = leave(
            first_part.reshape(2, 4, T, self.D),
            weight_part.reshape(4, 2, 4 * R, 3 * self.C),
            [logit_grad.reshape(T // 2, 2 * EXPERTS), thin],
            11,
        )
        ffn = lax.dynamic_slice_in_dim(
            jnp.sum(thin[:, :, :wide], axis=(0, 1)).reshape(self.D), (self.u * 4 + self.z) * R, R, 0
        )
        mine = lax.dynamic_index_in_dim(thin.reshape(4, 2, 4, -1, 128), self.u % 2, 1, False)
        mine = lax.dynamic_index_in_dim(mine, self.u // 2, 1, False)
        heads = jnp.sum(mine[:, wide:used], axis=0).reshape(2, self.C)
        heads = lax.dynamic_slice_in_dim(heads, self.z * R, R, 1)
        return first, weights, logit_all.reshape(32 * T, EXPERTS), ffn, heads


class General:
    def __init__(self, U, Z, T, D):
        self.U, self.Z, self.T, self.D = U, Z, T, D
        self.u, self.z = lax.axis_index("uly"), lax.axis_index("blk")
        self.C = D // U
        self.L = U * T
        self.group = self.u
        self.first_block, self.block_step = self.z, Z

    def gather(self, x):
        return lax.all_gather(x, ALL, axis=0, tiled=True)

    def scatter_wide(self, x):
        return lax.psum_scatter(x, ALL, scatter_dimension=0, tiled=True)

    def enter(self, rows, scaled, out_weight, pack, routes):
        U, R = self.U, scaled.shape[1]
        swapped = lax.all_to_all(scaled.transpose(1, 0, 2).reshape(R, 3, U, self.C), "uly", split_axis=2, concat_axis=0, tiled=True)
        weights = lax.all_gather(swapped.reshape(U, R, 3 * self.C), "blk", axis=1, tiled=True)
        return (
            self.rows_all(rows),
            weights.reshape(self.D, 3 * self.C),
            lax.all_gather(out_weight, "blk", axis=0, tiled=True),
            self.gather(pack),
            self.gather(routes[None]).reshape((U, self.Z) + routes.shape),
        )

    def head_sum(self, x):
        return lax.psum(x, "uly")

    head_sum_again = head_sum

    def sequence(self, key, value, upstream):
        self.upstream = upstream
        pair = jnp.stack([key, value]).reshape(2, self.U, self.T, self.C)
        pair = lax.all_gather(pair, "blk", axis=2, tiled=False).reshape(2, -1, self.C)
        return pair[0], pair[1]

    def heads_to_rows(self, x):
        return self.rows_sum(x), self.gather(self.upstream)

    def rows_sum(self, x):
        return lax.psum_scatter(x, "uly", scatter_dimension=0, tiled=True)

    def rows_all(self, x):
        return lax.all_gather(x, "uly", axis=0, tiled=True)

    def experts(self, second_low, upstream_all, routes, weights, router):
        EL, D = weights.shape[0], self.D
        N = upstream_all.shape[0]
        second_all = self.gather(second_low)
        group = min(512, N)
        groups = N // group
        slots = -(-(group // self.T * CAP) // 16) * 16
        rows = groups * slots
        own_first = self.u * EL
        chosen = jnp.any(routes[None] == (own_first + jnp.arange(EL, dtype=jnp.int32))[:, None, None, None, None], axis=3)
        slot = slots_of(chosen.reshape(EL, groups, group)).reshape(EL, N)
        entry_in, upstream_in, gates = pick_rows(slot, router, second_all, upstream_all, group, slots)
        flat, split = (EL, rows, -1), (EL, groups, slots, -1)
        out_rows, entry_rows, self.expert_grads, gate_grads = run_experts(
            entry_in.reshape(flat), upstream_in.reshape(flat), gates.reshape(flat), weights, min(8, groups) * slots
        )
        out_part, entry_part = spread_rows(
            own_first.astype(jnp.int32)[None],
            slot.T,
            gate_grads.reshape(split),
            out_rows.reshape(split),
            entry_rows.reshape(split),
            group,
        )
        self.out_sum = self.scatter_wide(out_part)
        return second_all, self.scatter_wide(entry_part)

    def rows_to_heads(self, x):
        return self.rows_all(x), self.expert_grads

    def sequence_sums(self, dk, dv, out_part):
        pair = jnp.stack([dk, dv]).reshape(2, self.U, self.Z, self.T, self.C)
        pair = lax.psum_scatter(pair, "blk", scatter_dimension=2, tiled=True).reshape(2, self.L, self.C)
        return pair[0], pair[1], lax.psum_scatter(out_part, "blk", scatter_dimension=0, tiled=True), self.out_sum

    def leave(self, first_part, weight_part, logit_grad, ffn_part, head_parts):
        U, R = self.U, self.D // (self.U * self.Z)
        part = weight_part.reshape(U, self.Z * R, 3 * self.C)
        part = lax.psum_scatter(part, "blk", scatter_dimension=1, tiled=True)
        part = lax.all_to_all(part, "uly", split_axis=0, concat_axis=0, tiled=True)
        weights = part.reshape(U, R, 3, self.C).transpose(2, 1, 0, 3).reshape(3, R, self.D)
        heads = lax.psum_scatter(head_parts, "blk", scatter_dimension=1, tiled=True)
        return self.rows_sum(first_part), weights, self.gather(logit_grad), self.scatter_wide(ffn_part), heads


def _row_limits(doc_ref, first, rows):
    position = first + lax.broadcasted_iota(jnp.int32, (rows, 1), 0)
    start = jnp.zeros_like(position)
    lowest = jnp.int32(0)
    for d in range(doc_ref.shape[0]):
        begin = doc_ref[d]
        start = jnp.where(begin <= position, jnp.maximum(start, begin), start)
        lowest = jnp.where(begin <= first, jnp.maximum(lowest, begin), lowest)
    return position, start, lowest


def _scores(query, key, position, start, key_first, scaling):
    raw = dot(query, key, LAST_DIM) * scaling
    key_position = key_first + lax.broadcasted_iota(jnp.int32, raw.shape, 1)
    return jnp.where((key_position <= position) & (key_position >= start), raw, NEG)


def _attend_kernel(index_ref, doc_ref, q_ref, k_ref, v_ref, o_ref, log_ref, *, chunk, scaling):
    rows = q_ref.shape[0]
    heads = q_ref.shape[1] // HEAD_DIM
    first = (pl.program_id(0) * index_ref[1] + index_ref[0]) * rows
    position, start, lowest = _row_limits(doc_ref, first, rows)

    def step(i, state):
        at = pl.multiple_of(i * chunk, chunk)
        new = []
        for h in range(heads):
            cols = pl.ds(h * HEAD_DIM, HEAD_DIM)
            top, total, out = state[h]
            scores = _scores(q_ref[:, cols], k_ref[pl.ds(at, chunk), cols], position, start, at, scaling)
            now = jnp.maximum(top, jnp.max(scores, axis=1, keepdims=True))
            weights = jnp.exp(scores - now)
            fade = jnp.exp(top - now)
            total = total * fade + jnp.sum(weights, axis=1, keepdims=True)
            out = out * fade + dot(weights.astype(BF16), v_ref[pl.ds(at, chunk), cols])
            new.append((now, total, out))
        return tuple(new)

    zero = (
        jnp.full((rows, 1), NEG, F32),
        jnp.zeros((rows, 1), F32),
        jnp.zeros((rows, HEAD_DIM), F32),
    )
    last = first + rows
    state = lax.fori_loop(lowest // chunk, (last + chunk - 1) // chunk, step, (zero,) * heads)
    for h in range(heads):
        cols = pl.ds(h * HEAD_DIM, HEAD_DIM)
        top, total, out = state[h]
        o_ref[:, cols] = out / total
        log_ref[:, cols] = jnp.broadcast_to(top + jnp.log(total), (rows, HEAD_DIM))


def _attend_back_kernel(
    index_ref, doc_ref, q_ref, g_ref, o_ref, log_ref, k_ref, v_ref, dq_ref, dk_ref, dv_ref, dk_sum, dv_sum, *, chunk, scaling
):
    rows = q_ref.shape[0]
    heads = q_ref.shape[1] // HEAD_DIM
    first = (pl.program_id(0) * index_ref[1] + index_ref[0]) * rows
    position, start, lowest = _row_limits(doc_ref, first, rows)

    @pl.when(pl.program_id(0) == 0)
    def _():
        dk_sum[...] = jnp.zeros_like(dk_sum)
        dv_sum[...] = jnp.zeros_like(dv_sum)

    deltas, logs = [], []
    for h in range(heads):
        cols = pl.ds(h * HEAD_DIM, HEAD_DIM)
        deltas.append(jnp.sum(g_ref[:, cols].astype(F32) * o_ref[:, cols], axis=1, keepdims=True))
        logs.append(log_ref[:, cols][:, :1])

    def step(i, state):
        at = pl.multiple_of(i * chunk, chunk)
        new = []
        for h in range(heads):
            cols = pl.ds(h * HEAD_DIM, HEAD_DIM)
            query, grad = q_ref[:, cols], g_ref[:, cols]
            key = k_ref[pl.ds(at, chunk), cols]
            scores = _scores(query, key, position, start, at, scaling)
            weights = jnp.exp(scores - logs[h])
            weight_grad = dot(grad, v_ref[pl.ds(at, chunk), cols], LAST_DIM)
            score_grad = (weights * (weight_grad - deltas[h])).astype(BF16)
            dv_sum[pl.ds(at, chunk), cols] += dot(weights.astype(BF16), grad, FIRST_DIM)
            dk_sum[pl.ds(at, chunk), cols] += dot(score_grad, query, FIRST_DIM)
            new.append(state[h] + dot(score_grad, key))
        return tuple(new)

    last = first + rows
    state = lax.fori_loop(
        lowest // chunk, (last + chunk - 1) // chunk, step, (jnp.zeros((rows, HEAD_DIM), F32),) * heads
    )
    for h in range(heads):
        dq_ref[:, pl.ds(h * HEAD_DIM, HEAD_DIM)] = (state[h] * scaling).astype(BF16)

    @pl.when(pl.program_id(0) == pl.num_programs(0) - 1)
    def _():
        dk_ref[...] = (dk_sum[...] * scaling).astype(BF16)
        dv_ref[...] = dv_sum[...].astype(BF16)


def _attention_specs(L, N, C, rows):
    block = pl.BlockSpec((rows, C), lambda i, *_: (i, 0))
    whole = pl.BlockSpec((N, C), lambda i, *_: (0, 0), pipeline_mode=pl.Buffered(1))
    return block, whole


def attention_forward(index, docs, query, key_all, value_all, rows, chunk):
    (L, C), N = query.shape, key_all.shape[0]
    block, whole = _attention_specs(L, N, C, rows)
    return pl.pallas_call(
        functools.partial(_attend_kernel, chunk=chunk, scaling=HEAD_DIM ** (-0.5)),
        out_shape=[jax.ShapeDtypeStruct((L, C), F32)] * 2,
        grid_spec=pltpu.PrefetchScalarGridSpec(
            num_scalar_prefetch=2, grid=(L // rows,), in_specs=[block, whole, whole], out_specs=[block, block]
        ),
        compiler_params=pltpu.CompilerParams(vmem_limit_bytes=VMEM_BYTES),
        cost_estimate=pl.CostEstimate(flops=4 * L * C * 1024, bytes_accessed=4 * N * C, transcendentals=L * 1024),
    )(index, docs, query, key_all, value_all)


def attention_backward(index, docs, query, grad, attended, logs, key_all, value_all, rows, chunk):
    (L, C), N = query.shape, key_all.shape[0]
    block, whole = _attention_specs(L, N, C, rows)
    return pl.pallas_call(
        functools.partial(_attend_back_kernel, chunk=chunk, scaling=HEAD_DIM ** (-0.5)),
        out_shape=[jax.ShapeDtypeStruct((L, C), BF16)] + [jax.ShapeDtypeStruct((N, C), BF16)] * 2,
        grid_spec=pltpu.PrefetchScalarGridSpec(
            num_scalar_prefetch=2,
            grid=(L // rows,),
            in_specs=[block, block, block, block, whole, whole],
            out_specs=[block, whole, whole],
            scratch_shapes=[pltpu.VMEM((N, C), F32)] * 2,
        ),
        compiler_params=pltpu.CompilerParams(vmem_limit_bytes=VMEM_BYTES),
        cost_estimate=pl.CostEstimate(flops=10 * L * C * 1024, bytes_accessed=8 * N * C, transcendentals=L * 1024),
    )(index, docs, query, grad, attended, logs, key_all, value_all)


def _pick_kernel(slot_ref, router_ref, x_ref, g_ref, xr_ref, gr_ref, gate_ref, *, slots, width):
    experts, group = slot_ref.shape
    logits = lax.dot_general(router_ref[...], x_ref[...], (((0,), (1,)), ((), ())), preferred_element_type=F32)
    powers = jnp.exp(logits - jnp.max(logits, axis=0, keepdims=True))
    chances = powers / jnp.sum(powers, axis=0, keepdims=True)
    row = lax.broadcasted_iota(jnp.int32, (slots, group), 0)
    picks = []
    for e in range(experts):
        hit = slot_ref[e : e + 1, :] == row
        gate = jnp.sum(jnp.where(hit, chances[e : e + 1, :], 0.0), axis=1, keepdims=True)
        gate_ref[e, 0] = jnp.broadcast_to(gate, (slots, 128))
        picks.append(jnp.where(hit, 1.0, 0.0).astype(BF16))
    pick = jnp.concatenate(picks, axis=0)
    for source, target in ((x_ref, xr_ref), (g_ref, gr_ref)):

        def step(i, _, source=source, target=target):
            cols = pl.ds(pl.multiple_of(i * width, width), width)
            rows = dot(pick, source[:, cols]).astype(BF16)
            for e in range(experts):
                target[e, 0, :, cols] = rows[e * slots : (e + 1) * slots]
            return 0

        lax.fori_loop(0, source.shape[1] // width, step, 0)


def pick_rows(slot, router, x, g, group, slots):
    EL, N = slot.shape
    D = x.shape[1]
    groups = N // group
    tokens = pl.BlockSpec((group, D), lambda i: (i, 0))
    picked = pl.BlockSpec((EL, 1, slots, D), lambda i: (0, i, 0, 0))
    rows = jax.ShapeDtypeStruct((EL, groups, slots, D), BF16)
    return pl.pallas_call(
        functools.partial(_pick_kernel, slots=slots, width=512),
        out_shape=[rows, rows, jax.ShapeDtypeStruct((EL, groups, slots, 128), F32)],
        grid=(groups,),
        in_specs=[
            pl.BlockSpec((EL, group), lambda i: (0, i)),
            pl.BlockSpec(router.shape, lambda i: (0, 0)),
            tokens,
            tokens,
        ],
        out_specs=[picked, picked, pl.BlockSpec((EL, 1, slots, 128), lambda i: (0, i, 0, 0))],
        compiler_params=pltpu.CompilerParams(vmem_limit_bytes=VMEM_BYTES),
        cost_estimate=pl.CostEstimate(
            flops=4 * EL * slots * N * D, bytes_accessed=8 * N * D, transcendentals=N * EXPERTS
        ),
    )(slot, router, x, g)


def _expert_kernel(x_ref, g_ref, gate_ref, w_ref, out_ref, entry_ref, dw_ref, gg_ref):
    x, g = x_ref[0], g_ref[0]
    gate = gate_ref[0][:, :1]
    gate_pre = dot(x, w_ref[0, 0])
    up = dot(x, w_ref[0, 1])
    back = dot(g, w_ref[0, 2])
    sig = jax.nn.sigmoid(gate_pre)
    act = gate_pre * sig
    inner = act * up
    gg_ref[0] = jnp.broadcast_to(jnp.sum(inner * back, axis=1, keepdims=True), gg_ref.shape[1:])
    inner_grad = back * gate
    gate_pre_grad = (inner_grad * up * sig * (1.0 + gate_pre * (1.0 - sig))).astype(BF16)
    up_grad = (inner_grad * act).astype(BF16)
    gated = (inner * gate).astype(BF16)
    both = jnp.concatenate([gate_pre_grad, up_grad], axis=1)
    out_ref[0] = dot(gated, w_ref[0, 2], LAST_DIM).astype(BF16)
    entry_ref[0] = dot(both, jnp.concatenate([w_ref[0, 0], w_ref[0, 1]], axis=1), LAST_DIM).astype(BF16)
    FL = w_ref.shape[3]
    pair = dot(x, both, FIRST_DIM)
    parts = (pair[:, :FL], pair[:, FL:], dot(g, gated, FIRST_DIM))
    first = pl.program_id(1) == 0
    for k in range(3):

        @pl.when(first)
        def _(k=k):
            dw_ref[0, k] = parts[k]

        @pl.when(jnp.logical_not(first))
        def _(k=k):
            dw_ref[0, k] += parts[k]


def run_experts(x, g, gate, weights, chunk):
    EL, rows, D = x.shape
    FL = weights.shape[3]
    row_block = pl.BlockSpec((1, chunk, D), lambda e, c: (e, c, 0))
    thin = pl.BlockSpec((1, chunk, 128), lambda e, c: (e, c, 0))
    matrices = pl.BlockSpec((1, 3, D, FL), lambda e, c: (e, 0, 0, 0))
    return pl.pallas_call(
        _expert_kernel,
        out_shape=[
            jax.ShapeDtypeStruct(x.shape, BF16),
            jax.ShapeDtypeStruct(x.shape, BF16),
            jax.ShapeDtypeStruct(weights.shape, F32),
            jax.ShapeDtypeStruct((EL, rows, 128), F32),
        ],
        grid=(EL, rows // chunk),
        in_specs=[row_block, row_block, thin, matrices],
        out_specs=[row_block, row_block, matrices, thin],
        compiler_params=pltpu.CompilerParams(vmem_limit_bytes=VMEM_BYTES),
        cost_estimate=pl.CostEstimate(
            flops=18 * EL * rows * D * FL, bytes_accessed=8 * EL * rows * D + 18 * EL * D * FL, transcendentals=EL * rows * FL
        ),
    )(x, g, gate, weights)


def _spread_kernel(own_ref, slot_ref, gg_ref, out_ref, entry_ref, o_ref, e_ref, *, width):
    group, experts = slot_ref.shape
    slots = out_ref.shape[2]
    total = experts * slots
    D = out_ref.shape[3]
    lane = lax.broadcasted_iota(jnp.int32, (experts, total), 1)
    which = lax.broadcasted_iota(jnp.int32, (experts, total), 0)
    choose = jnp.where((lane >= which * slots) & (lane < (which + 1) * slots), 1.0, 0.0).astype(BF16)
    offset = lane[:1] - jnp.sum(jnp.where(lane >= (which + 1) * slots, slots, 0), axis=0, keepdims=True)
    mine = dot(slot_ref[...].astype(BF16), choose)
    pick = jnp.where(mine == offset.astype(F32), 1.0, 0.0).astype(BF16)
    column = lax.broadcasted_iota(jnp.int32, (slots, 128), 1)
    grads = [jnp.where(column == own_ref[0] + e, gg_ref[e, 0], 0.0).astype(BF16) for e in range(experts)]
    e_ref[:, pl.ds(D, 128)] = dot(pick, jnp.concatenate(grads, axis=0)).astype(BF16)

    def step(i, _):
        cols = pl.ds(pl.multiple_of(i * width, width), width)
        for source, target in ((out_ref, o_ref), (entry_ref, e_ref)):
            rows = jnp.concatenate([source[e, 0, :, cols] for e in range(experts)], axis=0)
            target[:, cols] = dot(pick, rows).astype(BF16)
        return 0

    lax.fori_loop(0, D // width, step, 0)


def spread_rows(own, slot, gate_grads, out_rows, entry_rows, group):
    N, EL = slot.shape
    _, groups, slots, D = out_rows.shape
    picked = pl.BlockSpec((EL, 1, slots, D), lambda i, *_: (0, i, 0, 0))
    return pl.pallas_call(
        functools.partial(_spread_kernel, width=512),
        out_shape=[jax.ShapeDtypeStruct((N, D), BF16), jax.ShapeDtypeStruct((N, D + 128), BF16)],
        grid_spec=pltpu.PrefetchScalarGridSpec(
            num_scalar_prefetch=1,
            grid=(groups,),
            in_specs=[
                pl.BlockSpec((group, EL), lambda i, *_: (i, 0)),
                pl.BlockSpec((EL, 1, slots, 128), lambda i, *_: (0, i, 0, 0)),
                picked,
                picked,
            ],
            out_specs=[
                pl.BlockSpec((group, D), lambda i, *_: (i, 0)),
                pl.BlockSpec((group, D + 128), lambda i, *_: (i, 0)),
            ],
        ),
        compiler_params=pltpu.CompilerParams(vmem_limit_bytes=VMEM_BYTES),
        cost_estimate=pl.CostEstimate(flops=4 * EL * slots * N * D, bytes_accessed=8 * N * D, transcendentals=0),
    )(own, slot, gate_grads, out_rows, entry_rows)


def body(
    hidden_in,
    out_grad,
    attn_gain,
    query_weight,
    key_weight,
    value_weight,
    out_weight,
    query_gain,
    key_gain,
    ffn_gain,
    router_weight,
    expert_weights,
    routes,
    doc_starts,
):
    U = lax.axis_size("uly")
    Z = lax.axis_size("blk")
    u = lax.axis_index("uly")
    z = lax.axis_index("blk")
    T, D = hidden_in.shape
    EL = expert_weights.shape[0]
    N = U * Z * T
    RW = query_weight.shape[0]
    move = (Slice if (U, Z, T, D) == (8, 4, 128, 2048) else General)(U, Z, T, D)
    C, L = move.C, move.L

    gain_rows = attn_gain.astype(F32)[:, None]
    own_weights = [w.astype(F32) for w in (query_weight, key_weight, value_weight)]
    scaled_rows = jnp.stack([(w * gain_rows).astype(BF16) for w in own_weights])
    pack = jnp.concatenate([router_weight] + [g[:, None] for g in (ffn_gain, query_gain, key_gain)], axis=1)
    pack = jnp.pad(pack, ((0, 0), (0, 128 - pack.shape[1])))
    hidden = hidden_in.astype(F32)
    first_scale = norm_scale(hidden)
    first_rows, qkv_weight, out_rows, packed, routes_all = move.enter(
        (hidden * first_scale).astype(BF16), scaled_rows, out_weight, pack, routes.T
    )
    weight_router = packed[:, :EXPERTS]
    gain_ffn = packed[:, EXPERTS].astype(F32)
    head_gains = lax.dynamic_slice_in_dim(packed[:, EXPERTS + 1 : EXPERTS + 3], move.group * C, C, 0).astype(F32)
    gain_query, gain_key = head_gains[:, 0], head_gains[:, 1]
    qkv_pre = dot(first_rows, qkv_weight)
    query_pre, key_pre, value_pre = qkv_pre[:, :C], qkv_pre[:, C : 2 * C], qkv_pre[:, 2 * C :]
    squares = jnp.stack([jnp.sum(query_pre * query_pre, axis=1), jnp.sum(key_pre * key_pre, axis=1)])
    scales = lax.rsqrt(move.head_sum(squares.reshape(-1, 128)).reshape(2, L) / D + EPS)
    query_scale, key_scale = scales[0][:, None], scales[1][:, None]
    local = jnp.arange(L, dtype=jnp.int32)
    position = (local // T * move.block_step + move.first_block) * T + local % T
    cosine, sine = rotary_tables(position)
    cosine, sine = cosine[:, None, :], sine[:, None, :]

    def rotated(pre, scale, gain):
        split = (pre * scale * gain).reshape(L, C // HEAD_DIM, HEAD_DIM)
        return rotate_forward(split, cosine, sine).reshape(L, C).astype(BF16)

    query_rot = rotated(query_pre, query_scale, gain_query)
    key_all, value_all = move.sequence(
        rotated(key_pre, key_scale, gain_key), value_pre.astype(BF16), out_grad
    )
    index = jnp.stack([move.first_block, jnp.int32(move.block_step)]).astype(jnp.int32)
    chunk = min(512, N)
    attended, logs = attention_forward(index, doc_starts, query_rot, key_all, value_all, T, chunk)
    attended_low = attended.astype(BF16)
    mixed, upstream_all = move.heads_to_rows(dot(attended_low, out_rows).astype(BF16))
    residual = hidden + mixed.astype(F32)

    second_scale = norm_scale(residual)
    second_low = (residual * second_scale * gain_ffn).astype(BF16)
    probabilities = jax.nn.softmax(dot(second_low, weight_router), axis=-1)
    own_router = jnp.roll(weight_router, -u * EL, axis=1)
    second_all, entry_sum = move.experts(second_low, upstream_all, routes_all, expert_weights, own_router)
    entry_sum = entry_sum.astype(F32)

    second_grad, prob_grad = entry_sum[:, :D], entry_sum[:, D : D + EXPERTS]
    logit_grad = (
        probabilities * (prob_grad - jnp.sum(probabilities * prob_grad, axis=1, keepdims=True))
    ).astype(BF16)
    second_grad = second_grad + dot(logit_grad, weight_router, LAST_DIM)
    upstream = out_grad.astype(F32)
    weighted = second_grad * gain_ffn
    inner_mean = jnp.mean(weighted * residual, axis=-1, keepdims=True)
    residual_grad = upstream + second_scale * weighted - residual * (second_scale**3) * inner_mean
    ffn_gain_part = jnp.sum(second_grad * residual * second_scale, axis=0)

    residual_rows, expert_grads = move.rows_to_heads(residual_grad.astype(BF16))
    out_weight_part = dot(attended_low, residual_rows, FIRST_DIM).astype(BF16)
    attended_grad = dot(residual_rows, out_rows, LAST_DIM).astype(BF16)
    dq, dk_part, dv_part = attention_backward(
        index, doc_starts, query_rot, attended_grad, attended, logs, key_all, value_all, T, chunk
    )
    dk, dv, out_weight_grad, out_sum = move.sequence_sums(dk_part, dv_part, out_weight_part)
    output = (residual + out_sum.astype(F32)).astype(BF16)

    def rotated_back(grad):
        return rotate_backward(grad.astype(F32).reshape(L, C // HEAD_DIM, HEAD_DIM), cosine, sine).reshape(L, C)

    query_up, key_up = rotated_back(dq), rotated_back(dk)
    inner_sums = jnp.stack(
        [jnp.sum(query_up * gain_query * query_pre, axis=1), jnp.sum(key_up * gain_key * key_pre, axis=1)]
    )
    inner_sums = move.head_sum_again(inner_sums.reshape(-1, 128)).reshape(2, L) / D

    def pre_grad(up, gain, pre, scale, mean):
        return (scale * (up * gain) - pre * (scale**3) * mean[:, None]).astype(BF16)

    pre_grads = jnp.concatenate(
        [
            pre_grad(query_up, gain_query, query_pre, query_scale, inner_sums[0]),
            pre_grad(key_up, gain_key, key_pre, key_scale, inner_sums[1]),
            dv,
        ],
        axis=1,
    )
    gain_parts = jnp.stack(
        [jnp.sum(query_up * query_pre * query_scale, axis=0), jnp.sum(key_up * key_pre * key_scale, axis=0)]
    )
    weight_part = dot(first_rows, pre_grads, FIRST_DIM).astype(BF16)
    first_part = dot(pre_grads, qkv_weight, LAST_DIM).astype(BF16)
    first_weighted, weight_sum, logit_grad_all, ffn_gain_grad, head_gain_grads = move.leave(
        first_part, weight_part, logit_grad, ffn_gain_part, gain_parts
    )
    own_columns = lax.dynamic_slice_in_dim(second_all, (u * Z + z) * RW, RW, 1)
    router_grad = dot(own_columns, logit_grad_all, FIRST_DIM)
    weight_sum = weight_sum.astype(F32)
    attn_gain_grad = sum(jnp.sum(w * g, axis=1) for w, g in zip(own_weights, weight_sum))
    weight_grads = [g * gain_rows for g in weight_sum]
    first_weighted = first_weighted.astype(F32)
    first_mean = jnp.mean(first_weighted * hidden, axis=-1, keepdims=True)
    hidden_grad = residual_grad + first_scale * first_weighted - hidden * (first_scale**3) * first_mean
    return (
        output,
        hidden_grad,
        attn_gain_grad,
        weight_grads[0],
        weight_grads[1],
        weight_grads[2],
        out_weight_grad.astype(F32),
        head_gain_grads[0],
        head_gain_grads[1],
        ffn_gain_grad,
        router_grad,
        expert_grads,
    )


def solution(mesh):
    rows = P(ALL, None)
    flat = P(ALL)
    experts = P("uly", None, None, "blk")
    return jax.shard_map(
        body,
        mesh=mesh,
        in_specs=(rows, rows, flat, rows, rows, rows, rows, flat, flat, flat, rows, experts, rows, P()),
        out_specs=(rows, rows, flat, rows, rows, rows, rows, flat, flat, flat, rows, experts),
        check_vma=False,
    )
```

```python
import functools

import jax
import jax.numpy as jnp
from jax import lax
from jax.experimental import pallas as pl
from jax.experimental.pallas import tpu as pltpu
from jax.sharding import PartitionSpec as P

HEADS = 16
HEAD_DIM = 128
EXPERTS = 64
CAP = 17

EPS = 1e-05
THETA = 10000.0
NEG = -1e30
FIRST_DIM = (((0,), (0,)), ((), ()))
LAST_DIM = (((1,), (1,)), ((), ()))
ALL = ("uly", "blk")
F32 = jnp.float32
BF16 = jnp.bfloat16
VMEM_BYTES = 56 * 1024 * 1024
PICK_WIDTH = 512
ATTEND_CHUNK = 512
SPREAD_WIDTH = 2048


def dot(a, b, dims=(((1,), (0,)), ((), ()))):
    return lax.dot_general(a, b, dims, preferred_element_type=F32)


def rotary_tables(position):
    halfway = HEAD_DIM // 2
    frequency = THETA ** (-(jnp.arange(halfway).astype(F32) * 2.0 / HEAD_DIM))
    angles = position.astype(F32)[:, None] * frequency[None, :]
    cosine, sine = jnp.cos(angles), jnp.sin(angles)
    return jnp.concatenate([cosine, cosine], axis=1), jnp.concatenate([-sine, sine], axis=1)


def norm_scale(values):
    return lax.rsqrt(jnp.mean(values * values, axis=-1, keepdims=True) + EPS)


MESH = pl.DeviceIdType.MESH
DMA = pltpu.SemaphoreType.DMA
ANY_SPACE = pl.BlockSpec(memory_space=pl.ANY)
IN_VMEM = pl.BlockSpec(memory_space=pltpu.VMEM)
DEPTH = 4
CHIPS = (0, 2, 4, 6)
FIRST, THEN = (2, 4), (4, 2)


def _send(src, dst, send_sem, recv_sem, to):
    pltpu.make_async_remote_copy(
        src_ref=src, dst_ref=dst, send_sem=send_sem, recv_sem=recv_sem, device_id=to, device_id_type=MESH
    ).start()


def _expect(ref, sem, here):
    pltpu.make_async_remote_copy(
        src_ref=ref, dst_ref=ref, send_sem=sem, recv_sem=sem, device_id=here, device_id_type=MESH
    ).wait_recv()


def _sent(ref, sem, here):
    pltpu.make_async_remote_copy(
        src_ref=ref, dst_ref=ref, send_sem=sem, recv_sem=sem, device_id=here, device_id_type=MESH
    ).wait_send()


def _greet(u, z, planes, line=False, others=(), meanwhile=lambda: None):
    barrier = pltpu.get_barrier_semaphore()
    for bit in planes:
        pl.semaphore_signal(barrier, inc=1, device_id=(u ^ bit, z), device_id_type=MESH)
    for to in others:
        pl.semaphore_signal(barrier, inc=1, device_id=to, device_id_type=MESH)
    count = len(planes) + len(others)
    if line:

        @pl.when(z > 0)
        def _():
            pl.semaphore_signal(barrier, inc=1, device_id=(u, z - 1), device_id_type=MESH)

        @pl.when(z < DEPTH - 1)
        def _():
            pl.semaphore_signal(barrier, inc=1, device_id=(u, z + 1), device_id_type=MESH)

        count = count + jnp.where((z == 0) | (z == DEPTH - 1), 1, 2)
    meanwhile()
    pl.semaphore_wait(barrier, count)


def _line_order(z):
    second = jnp.where(z == 0, 1, z - 1)
    third = jnp.where(z == 0, 2, jnp.where(z == 3, 1, z + 1))
    fourth = jnp.where(z < 2, 3, 0)
    return (z, second, third, fourth)


def _accumulate(target, source, rows):
    strip = 16

    def step(i, _):
        at = pl.ds(pl.multiple_of(i * strip, strip), strip)
        target[at, :] = target[at, :] + source[at, :]
        return 0

    lax.fori_loop(0, rows // strip, step, 0)


def _run(*parts, order=()):
    for i in order:
        next(parts[i])
    live = list(parts)
    while live:
        for part in list(live):
            try:
                next(part)
            except StopIteration:
                live.remove(part)


def _line_part(u, z, source, block, sems, share=True):
    z_send, z_recv, c_send, c_recv, own_sem = sems
    here, core = (u, z), u % 2
    own = pltpu.make_async_copy(source, block(core, z), own_sem)
    own.start()
    order = _line_order(z)

    def along(level, ref, step):
        @pl.when((z > 0) & (level >= z))
        def _():
            step(ref, 0, level, (u, z - 1))

        @pl.when((z < DEPTH - 1) & (level <= z))
        def _():
            step(ref, 1, level, (u, z + 1))

    def go(ref, way, level, to):
        _send(ref, block(core, level), z_send.at[way, level], z_recv.at[level], to)

    def gone(ref, way, level, to):
        _sent(ref, z_send.at[way, level], here)

    for i in range(4):
        level = order[i]
        ref = source if i == 0 else block(core, level)
        if i > 0:
            yield
            _expect(ref, z_recv.at[level], here)
        along(level, ref, go)
        if share:
            _send(ref, block(core, level), c_send.at[level], c_recv.at[level], (u ^ 1, z))
    yield
    if share:
        for i in range(4):
            _expect(block(1 - core, order[i]), c_recv.at[order[i]], here)
    yield
    for i in range(4):
        along(order[i], block(core, order[i]), gone)
        if share:
            _sent(block(core, order[i]), c_send.at[order[i]], here)
    own.wait()


def _plane_part(u, z, own, block, sems):
    p_send, p_recv, o_sem = sems
    here = (u, z)
    for way, bits in enumerate((FIRST, THEN)):
        for h in range(2):
            _send(own(h), block(h, u), p_send.at[h, way], p_recv.at[h, way], (u ^ bits[h], z))
    for h in range(2):
        pltpu.make_async_copy(own(h), block(h, u), o_sem.at[h]).start()
    for h in range(2):
        yield
        _expect(block(h, u ^ FIRST[h]), p_recv.at[h, 0], here)
        near = block(h, u ^ FIRST[h])
        _send(near, near, p_send.at[h, 2], p_recv.at[h, 2], (u ^ THEN[h], z))
    yield
    for h in range(2):
        _expect(block(h, u ^ THEN[h]), p_recv.at[h, 1], here)
        _expect(block(h, u ^ 6), p_recv.at[h, 2], here)
    yield
    for h in range(2):
        for k in range(3):
            _sent(block(h, u), p_send.at[h, k], here)
        pltpu.make_async_copy(own(h), block(h, u), o_sem.at[h]).wait()


def _plane_sum_part(u, z, source, work, bufs, sems, rows, then_do):
    p_buf, q_buf = bufs
    load, p_send, p_recv, q_send, q_recv = sems
    here = (u, z)
    for j in (1, 0):
        for h in range(2):
            bit = (THEN[h], 6)[j]
            _send(source(h, u ^ bit), p_buf.at[h, j], p_send.at[h, j], p_recv.at[h, j], (u ^ THEN[h], z))
    for h in range(2):
        for j, bit in enumerate((0, FIRST[h])):
            pltpu.make_async_copy(source(h, u ^ bit), work.at[h, j], load.at[h, j]).start()
    for h in range(2):
        yield
        for j, bit in enumerate((0, FIRST[h])):
            pltpu.make_async_copy(source(h, u ^ bit), work.at[h, j], load.at[h, j]).wait()
        _expect(p_buf.at[h, 1], p_recv.at[h, 1], here)
        _accumulate(work.at[h, 1], p_buf.at[h, 1], rows)
        _send(work.at[h, 1], q_buf.at[h], q_send.at[h], q_recv.at[h], (u ^ FIRST[h], z))
    yield
    for h in range(2):
        _expect(p_buf.at[h, 0], p_recv.at[h, 0], here)
        _accumulate(work.at[h, 0], p_buf.at[h, 0], rows)
    for h in range(2):
        _expect(q_buf.at[h], q_recv.at[h], here)
        _accumulate(work.at[h, 0], q_buf.at[h], rows)
    then_do()
    yield
    for h in range(2):
        for j in range(2):
            _sent(p_buf.at[h, j], p_send.at[h, j], here)
        _sent(q_buf.at[h], q_send.at[h], here)


def _line_sum_part(u, z, source, work, bufs, sems, rows, then_do):
    c_buf, z_buf = bufs
    load, c_send, c_recv, z_send, z_recv = sems
    here, core = (u, z), u % 2
    order = tuple(reversed(_line_order(z)))
    for i in range(4):
        _send(source(1 - core, order[i]), c_buf.at[i], c_send.at[i], c_recv.at[i], (u ^ 1, z))
        pltpu.make_async_copy(source(core, order[i]), work.at[i], load.at[i]).start()
    for i in range(4):
        yield
        pltpu.make_async_copy(source(core, order[i]), work.at[i], load.at[i]).wait()
        _expect(c_buf.at[i], c_recv.at[i], here)
        _accumulate(work.at[i], c_buf.at[i], rows)
        if i == 3:
            yield
        _line_end(u, z, order[i], i, work.at[i], z_buf, (z_send, z_recv), rows)
    then_do()
    yield
    for i in range(4):
        _sent(c_buf.at[i], c_send.at[i], here)
        if i < 3:
            _sent(work.at[i], z_send.at[i], here)


def _column_peers(u, z):
    return [((u ^ c, z ^ k), c, k) for c in range(2) for k in range(4) if c or k]


def _comm(kernel, outs, scratch, collective_id, specs, flops=0, moved=100_000_000):
    return pl.pallas_call(
        kernel,
        out_shape=outs,
        in_specs=specs[0],
        out_specs=specs[1],
        scratch_shapes=scratch,
        compiler_params=pltpu.CompilerParams(
            collective_id=collective_id, has_side_effects=True, vmem_limit_bytes=VMEM_BYTES
        ),
        cost_estimate=pl.CostEstimate(flops=flops, bytes_accessed=moved, transcendentals=0),
    )


ENTER_ORDER = (0, 2, 1, 0, 2, 1, 0, 2, 0, 2)
KV_ORDER = (2, 0, 1, 0, 0, 1, 2, 1, 0, 1)
PAIR_ORDER = (2, 0, 1, 0, 0, 1, 2, 1, 0, 1)
LEAVE_ORDER = (0, 1, 2, 1, 2, 1, 0, 0, 1, 0, 1, 1)
LINE_SEMS = [DMA((2, 4)), DMA((4,)), DMA((4,)), DMA((4,)), DMA]
PLANE_SEMS = [DMA((2, 3)), DMA((2, 3)), DMA((2,))]
PLANE_SUM_SEMS = [DMA((2, 2)), DMA((2, 2)), DMA((2, 2)), DMA((2,)), DMA((2,))]
LINE_SUM_SEMS = [DMA((4,)), DMA((4,)), DMA((4,)), DMA((4,)), DMA((2, 4))]


def _small_part(u, z, xs, outs, sems):
    own_sem, z_send, z_recv, u_send, u_recv = sems
    here = (u, z)
    for a, (x, o) in enumerate(zip(xs, outs)):
        pltpu.make_async_copy(x, o.at[u, z], own_sem.at[a]).start()
        for k in range(1, 4):
            _send(x, o.at[u, z], z_send.at[a, k], z_recv.at[a, k], (u, z ^ k))
    yield
    for a, (x, o) in enumerate(zip(xs, outs)):
        pltpu.make_async_copy(x, o.at[u, z], own_sem.at[a]).wait()
        for k in range(1, 4):
            _expect(o.at[u, z ^ k], z_recv.at[a, k], here)
        for k in range(1, 8):
            _send(o.at[u], o.at[u], u_send.at[a, k], u_recv.at[a, k], (u ^ k, z))
    yield
    yield
    for a, (x, o) in enumerate(zip(xs, outs)):
        for k in range(1, 4):
            _sent(x, z_send.at[a, k], here)
        for k in range(1, 8):
            _sent(o.at[u], u_send.at[a, k], here)
            _expect(o.at[u ^ k], u_recv.at[a, k], here)


def _small_sems(n):
    return [DMA((n,)), DMA((n, 4)), DMA((n, 4)), DMA((n, 8)), DMA((n, 8))]


def _packed(router, gains):
    lane = lax.broadcasted_iota(jnp.int32, (router.shape[0], 128 - EXPERTS), 1)
    tail = jnp.zeros(lane.shape, F32)
    for j in range(1, 4):
        tail = jnp.where(lane == j - 1, gains[:, j : j + 1], tail)
    return router, tail.astype(BF16)


def enter(hidden, weights, gains, router, routes, collective_id):
    T, D = hidden.shape
    R, C = weights[0].shape[0], weights[0].shape[1] // 8
    held = (2, 4, R, 3 * C)
    strip = 16

    def kernel(h_ref, wq_ref, wk_ref, wv_ref, gain_ref, router_ref, route_ref, x_out, w_out, p_out, r_out, *refs):
        x_ref, w_ref, pack_ref, w_buf, w_send, w_recv = refs[:6]
        sems = refs[6:]
        u, z = lax.axis_index("uly"), lax.axis_index("blk")
        here, core, chip = (u, z), u % 2, u // 2
        column = _column_peers(u, z)

        def weight_part():
            def cut(j, c, level):
                return w_ref.at[j, :, pl.ds(pl.multiple_of((2 * level + c) * C, C), C)]

            def slot(j, c, level):
                return w_buf.at[c, level, :, pl.ds(j * C, C)]

            for i, (to, c, k) in enumerate(column):
                for j in range(3):
                    _send(cut(j, core ^ c, z ^ k), slot(j, core, z), w_send.at[i, j], w_recv.at[i, j], to)
            for j in range(3):
                slot(j, core, z)[...] = cut(j, core, z)[...]
            yield
            for i, (to, c, k) in enumerate(column):
                for j in range(3):
                    _expect(slot(j, core ^ c, z ^ k), w_recv.at[i, j], here)
            yield from _plane_part(u, z, lambda h: w_buf.at[h], lambda h, v: w_out.at[v // 2, h], sems[:3])
            for i, (to, c, k) in enumerate(column):
                for j in range(3):
                    _sent(cut(j, core ^ c, z ^ k), w_send.at[i, j], here)

        def prepare():
            gains = gain_ref[...].astype(F32)
            for j, ref in enumerate((wq_ref, wk_ref, wv_ref)):
                w_ref[j] = (ref[...].astype(F32) * gains[:, :1]).astype(BF16)

            def norm(i, _):
                at = pl.ds(pl.multiple_of(i * strip, strip), strip)
                value = h_ref[at, :].astype(F32)
                x_ref[at, :] = (value * norm_scale(value)).astype(BF16)
                return 0

            lax.fori_loop(0, T // strip, norm, 0)
            pack_ref[:, pl.ds(0, EXPERTS)], pack_ref[:, pl.ds(EXPERTS, 128 - EXPERTS)] = _packed(router_ref[...], gains)

        _greet(u, z, range(1, 8), others=[to for to, c, k in column if k], meanwhile=prepare)
        _run(
            weight_part(),
            _small_part(u, z, (pack_ref, route_ref), (p_out, r_out), sems[8:]),
            _line_part(u, z, x_ref, lambda c, level: x_out.at[c, level], sems[3:8]),
            order=ENTER_ORDER,
        )

    outs = [
        jax.ShapeDtypeStruct((2, 4, T, D), BF16),
        jax.ShapeDtypeStruct((4,) + held, BF16),
        jax.ShapeDtypeStruct((8, 4, R, 128), BF16),
        jax.ShapeDtypeStruct((8, 4) + routes.shape, routes.dtype),
    ]
    scratch = [pltpu.VMEM((T, D), BF16), pltpu.VMEM((3, R, D), BF16), pltpu.VMEM((R, 128), BF16)]
    scratch += [pltpu.VMEM(held, BF16), DMA((7, 3)), DMA((7, 3))] + PLANE_SEMS + LINE_SEMS + _small_sems(2)
    specs = ([IN_VMEM] * 7, [ANY_SPACE] * 4)
    return _comm(kernel, outs, scratch, collective_id, specs)(hidden, *weights, gains, router, routes)


def _column_sum_part(u, z, x_ref, total, buf, sems, then_do):
    send, recv = sems
    here = (u, z)
    column = _column_peers(u, z)
    for i, (to, c, k) in enumerate(column):
        _send(x_ref, buf.at[i], send.at[i], recv.at[i], to)
    yield
    value = x_ref[...]
    for i in range(7):
        _expect(buf.at[i], recv.at[i], here)
        value = value + buf[i]
    total[...] = value
    then_do()
    yield
    for i in range(7):
        _sent(x_ref, send.at[i], here)


def plane_pair(first, second, rows, squares, collective_id):
    R = squares.shape[0] // 2

    def kernel(a_ref, b_ref, x_ref, s_ref, a_out, b_out, x_out, s_out, k_out, buf, *sems):
        u, z = lax.axis_index("uly"), lax.axis_index("blk")
        here, chip = (u, z), u // 2
        k_send, k_recv = sems[10:]
        _greet(u, z, (2, 4, 6), others=[to for to, c, k in _column_peers(u, z)])
        own, outs = (a_ref, b_ref), (a_out, b_out)
        keys = s_out.at[pl.ds(R, R)]

        def tell():
            k_out[chip] = keys[...]
            for i, bit in enumerate((2, 4, 6)):
                _send(keys, k_out.at[chip], k_send.at[i], k_recv.at[i], (u ^ bit, z))

        _run(
            _plane_part(u, z, lambda h: own[h], lambda h, v: outs[h].at[v // 2], sems[:3]),
            _line_part(u, z, x_ref, lambda c, level: x_out.at[level], sems[3:8], share=False),
            _column_sum_part(u, z, s_ref, s_out, buf, sems[8:10], tell),
            order=PAIR_ORDER,
        )
        for i, bit in enumerate((2, 4, 6)):
            _expect(k_out.at[(u ^ bit) // 2], k_recv.at[i], here)
            _sent(keys, k_send.at[i], here)

    outs = [jax.ShapeDtypeStruct((4,) + x.shape, x.dtype) for x in (first, second)]
    outs += [jax.ShapeDtypeStruct((4,) + rows.shape, rows.dtype)]
    outs += [jax.ShapeDtypeStruct(squares.shape, F32), jax.ShapeDtypeStruct((4, R, 128), F32)]
    specs = ([IN_VMEM] * 2 + [ANY_SPACE, IN_VMEM], [ANY_SPACE] * 3 + [IN_VMEM] * 2)
    scratch = [pltpu.VMEM((7,) + squares.shape, F32)] + PLANE_SEMS + LINE_SEMS + [DMA((7,)), DMA((7,)), DMA((3,)), DMA((3,))]
    return _comm(kernel, outs, scratch, collective_id, specs)(first, second, rows, squares)


def column_gather(rows, slot, out_rows, collective_id):
    T, D = rows.shape
    EL, _, slots, _ = out_rows.shape

    def kernel(r_ref, slot_ref, rows_ref, r_out, x_out, *refs):
        u, z = lax.axis_index("uly"), lax.axis_index("blk")
        _greet(u, z, (1, 2, 4), line=True)
        order = _line_order(z)

        def keep(i, part):
            x_out[order[i]] = part[...]

        _run(
            _line_part(u, z, r_ref, lambda c, level: r_out.at[c, level], refs[-5:]),
            _spread_part(u, z, slot_ref, rows_ref, None, order, refs[:-5], keep),
        )

    outs = [jax.ShapeDtypeStruct((2, 4, T, D), BF16), jax.ShapeDtypeStruct((4, T, D), BF16)]
    specs = ([IN_VMEM, IN_VMEM, ANY_SPACE], [ANY_SPACE, IN_VMEM])
    scratch = _spread_scratch(T, D, (EL, slots, D)) + LINE_SEMS
    return _comm(kernel, outs, scratch, collective_id, specs)(rows, slot, out_rows)


def _line_sum_scratch(T, D):
    return [pltpu.VMEM((4, T, D), BF16), pltpu.VMEM((4, T, D), BF16), pltpu.VMEM((2, 4, T, D), BF16)]


def column_scatter(x, collective_id):
    T, D = x.shape[2:]

    def kernel(x_ref, o_ref, work, c_buf, z_buf, *sems):
        u, z = lax.axis_index("uly"), lax.axis_index("blk")
        _greet(u, z, (1,), line=True)

        def finish():
            o_ref[...] = work[3]

        _run(_line_sum_part(u, z, lambda c, level: x_ref.at[c, level], work, (c_buf, z_buf), sems, T, finish))

    scratch = _line_sum_scratch(T, D) + LINE_SUM_SEMS
    return _comm(kernel, jax.ShapeDtypeStruct((T, D), BF16), scratch, collective_id, ([ANY_SPACE], IN_VMEM))(x)


def _plane_sum_scratch(rows, cols):
    return [pltpu.VMEM((2, 2, rows, cols), BF16), pltpu.VMEM((2, 2, rows, cols), BF16), pltpu.VMEM((2, rows, cols), BF16)]


def key_value_sums(dk, dv, x, inner, collective_id):
    T, D = x.shape[1:]
    L, C = dk.shape[1:]
    R = inner.shape[0] // 5

    def kernel(
        k_ref, v_ref, x_ref, s_ref, k_out, v_out, x_out, s_out, work, p_buf, q_buf, x_work, z_buf, buf, total, k_buf, *sems
    ):
        u, z = lax.axis_index("uly"), lax.axis_index("blk")
        here, chip = (u, z), u // 2
        _greet(u, z, (2, 4, 6), others=[to for to, c, k in _column_peers(u, z)])
        load, z_send, z_recv, k_send, k_recv = sems[7:]
        order = tuple(reversed(_line_order(z)))

        def keys(v):
            return total.at[pl.ds(pl.multiple_of((v // 2 + 1) * R, R), R)]

        def tell():
            for i, bit in enumerate((2, 4, 6)):
                _send(keys(u ^ bit), k_buf.at[i], k_send.at[i], k_recv.at[i], (u ^ bit, z))

        def finish():
            k_out[...] = work[0, 0]
            v_out[...] = work[1, 0]

        def line():
            copies = [pltpu.make_async_copy(x_ref.at[order[i]], x_work.at[i], load.at[i]) for i in range(4)]
            for copy in copies:
                copy.start()
            for copy in copies:
                copy.wait()
            for i in range(4):
                _line_end(u, z, order[i], i, x_work.at[i], z_buf, (z_send, z_recv), T)
                yield
            x_out[...] = x_work[3]
            for i in range(3):
                _sent(x_work.at[i], z_send.at[i], (u, z))

        _run(
            _plane_sum_part(
                u, z, lambda h, v: (k_ref, v_ref)[h].at[v // 2], work, (p_buf, q_buf), sems[:5], L, finish
            ),
            line(),
            _column_sum_part(u, z, s_ref, total, buf, sems[5:7], tell),
            order=KV_ORDER,
        )
        value = keys(u)[...]
        for i, bit in enumerate((2, 4, 6)):
            _expect(k_buf.at[i], k_recv.at[i], here)
            value = value + k_buf[i]
            _sent(k_buf.at[i], k_send.at[i], here)
        s_out[pl.ds(0, R), :] = total[pl.ds(0, R), :]
        s_out[pl.ds(R, R), :] = value

    outs = [jax.ShapeDtypeStruct((L, C), BF16)] * 2 + [jax.ShapeDtypeStruct((T, D), BF16)]
    outs += [jax.ShapeDtypeStruct((2 * R, 128), F32)]
    scratch = _plane_sum_scratch(L, C) + [pltpu.VMEM((4, T, D), BF16), pltpu.VMEM((2, 4, T, D), BF16)]
    scratch += [pltpu.VMEM((7,) + inner.shape, F32), pltpu.VMEM(inner.shape, F32), pltpu.VMEM((3, R, 128), F32)]
    scratch += PLANE_SUM_SEMS + [DMA((7,)), DMA((7,)), DMA((4,)), DMA((4,)), DMA((2, 4)), DMA((3,)), DMA((3,))]
    specs = ([ANY_SPACE] * 3 + [IN_VMEM], [IN_VMEM] * 4)
    return _comm(kernel, outs, scratch, collective_id, specs)(dk, dv, x, inner)


def leave(x, weights, smalls, collective_id):
    n = len(smalls)
    T, D = x.shape[2:]
    rows, W = weights.shape[2:]
    R, C = rows // 4, W // 3

    def kernel(x_ref, w_ref, *refs):
        small_in, (o_ref, w_out), small_out = refs[:n], refs[n : n + 2], refs[n + 2 : 2 * n + 2]
        work, c_buf, z_buf, w_work, wp_buf, wq_buf = refs[2 * n + 2 : 2 * n + 8]
        sems = refs[2 * n + 8 :]
        u, z = lax.axis_index("uly"), lax.axis_index("blk")
        here, core, chip = (u, z), u % 2, u // 2
        column = _column_peers(u, z)
        _greet(u, z, range(1, 8), others=[to for to, c, k in column if k])
        t_send, t_recv = sems[10:12]
        group = 2 * z + core

        def finish():
            o_ref[...] = work[3]

        def cut(j, c, level):
            return w_work.at[c, 0, pl.ds(pl.multiple_of(level * R, R), R), pl.ds(j * C, C)]

        def slot(j, g):
            return w_out.at[j, :, pl.ds(pl.multiple_of(g * C, C), C)]

        def deal():
            for i, (to, c, k) in enumerate(column):
                for j in range(3):
                    _send(cut(j, core ^ c, z ^ k), slot(j, group), t_send.at[i, j], t_recv.at[i, j], to)
            for j in range(3):
                slot(j, group)[...] = cut(j, core, z)[...]

        _run(
            _plane_sum_part(u, z, lambda h, v: w_ref.at[v // 2, h], w_work, (wp_buf, wq_buf), sems[5:10], rows, deal),
            _line_sum_part(u, z, lambda c, level: x_ref.at[c, level], work, (c_buf, z_buf), sems[:5], T, finish),
            _small_part(u, z, small_in, small_out, sems[12:]),
            order=LEAVE_ORDER,
        )
        for i, (to, c, k) in enumerate(column):
            for j in range(3):
                _expect(slot(j, 2 * (z ^ k) + (core ^ c)), t_recv.at[i, j], here)
                _sent(cut(j, core ^ c, z ^ k), t_send.at[i, j], here)

    outs = [jax.ShapeDtypeStruct((T, D), BF16), jax.ShapeDtypeStruct((3, R, 8 * C), BF16)]
    outs += [jax.ShapeDtypeStruct((8, 4) + x.shape, x.dtype) for x in smalls]
    scratch = _line_sum_scratch(T, D) + _plane_sum_scratch(rows, W) + LINE_SUM_SEMS + PLANE_SUM_SEMS
    scratch += [DMA((7, 3)), DMA((7, 3))] + _small_sems(n)
    specs = ([ANY_SPACE] * 2 + [IN_VMEM] * n, [IN_VMEM] * 2 + [ANY_SPACE] * n)
    return _comm(kernel, outs, scratch, collective_id, specs)(x, weights, *smalls)


def _finish_kernel(
    h_ref, r_ref, rg_ref, first_ref, sum_ref, wq_ref, wk_ref, wv_ref, dw_ref, do_ref, gain_ref, out_ref, hg_ref, ag_ref, *dws
):
    out_ref[...] = (r_ref[...] + sum_ref[...].astype(F32)).astype(BF16)
    hidden, weighted = h_ref[...].astype(F32), first_ref[...].astype(F32)
    scale = norm_scale(hidden)
    mean = jnp.mean(weighted * hidden, axis=-1, keepdims=True)
    hg_ref[...] = rg_ref[...] + scale * weighted - hidden * (scale * scale * scale) * mean
    gain = gain_ref[...].astype(F32)[:, :1]
    total = jnp.zeros(dws[0].shape, F32)
    for j, ref in enumerate((wq_ref, wk_ref, wv_ref)):
        grad = dw_ref[j].astype(F32)
        total = total + grad * ref[...].astype(F32)
        dws[j][...] = grad * gain
    ag_ref[...] = jnp.sum(total, axis=1, keepdims=True)
    dws[3][...] = do_ref[...].astype(F32)


def finish(hidden, residual, residual_grad, first_weighted, out_sum, weights, weight_sum, out_weight_grad, gains):
    T, D = hidden.shape
    R = gains.shape[0]
    steps = 4 if R % 64 == 0 else 1

    def rows(count, width):
        return pl.BlockSpec((count // steps, width), lambda i: (i, 0))

    tokens, dense = rows(T, D), rows(R, D)
    return pl.pallas_call(
        _finish_kernel,
        out_shape=[
            jax.ShapeDtypeStruct((T, D), BF16),
            jax.ShapeDtypeStruct((T, D), F32),
            jax.ShapeDtypeStruct((R, 1), F32),
        ]
        + [jax.ShapeDtypeStruct((R, D), F32)] * 4,
        grid=(steps,),
        in_specs=[tokens] * 5
        + [dense] * 3
        + [pl.BlockSpec((3, R // steps, D), lambda i: (0, i, 0)), dense, rows(R, 4)],
        out_specs=[tokens, tokens, rows(R, 1)] + [dense] * 4,
        compiler_params=pltpu.CompilerParams(vmem_limit_bytes=VMEM_BYTES),
        cost_estimate=pl.CostEstimate(flops=20 * T * D, bytes_accessed=24 * T * D, transcendentals=0),
    )(hidden, residual, residual_grad, first_weighted, out_sum, *weights, weight_sum, out_weight_grad, gains)


class _Jobs:
    def __init__(self, load, compute):
        self.load, self.compute = load, compute
        self.queue, self.count, self.ready = [], 0, None

    def add(self, *jobs):
        self.queue += jobs

    def _next(self):
        if not self.queue:
            return None
        job = (self.count, self.queue.pop(0))
        self.count += 1
        self.load(*job, True)
        return job

    def run(self, number=1):
        for _ in range(number):
            now = self.ready or self._next()
            if now is None:
                return
            self.ready = self._next()
            self.load(*now, False)
            self.compute(*now)


def _gather_pick_kernel(
    x_ref, g0, g1, g2, g3, slot_ref, router_ref, o_ref, xr_ref, gr_ref, gate_ref, other_g, pick, in_buf, out_buf, in_sem, out_sem, *sems, width
):
    own_sem, z_send, z_recv, p_send, p_recv, c_send, c_recv, g_send, g_recv = sems
    own_g = (g0, g1, g2, g3)
    u, z = lax.axis_index("uly"), lax.axis_index("blk")
    core, chip = u % 2, u // 2
    other = 1 - core
    T, D = x_ref.shape
    experts, group = slot_ref.shape[1:]
    slots = out_buf.shape[2]
    half = T // 2
    halves = (pl.ds(0, half), pl.ds(half, half))
    here = (u, z)
    _greet(u, z, (1, 2, 4), line=True)
    own = pltpu.make_async_copy(x_ref, o_ref.at[u * DEPTH + z], own_sem)
    own.start()
    order = _line_order(z)

    def block(who, level):
        return o_ref.at[who * DEPTH + level]

    def part(who, level, h):
        return o_ref.at[who * DEPTH + level, halves[h]]

    def load(n, job, start):
        source, level, which = job
        steps = (0, jnp.where(which == 0, 1, 2), jnp.where(which == 0, 2, 1), 3)
        for k in range(4):
            p = chip ^ steps[k]
            if source == "x":
                ref = o_ref.at[(2 * p + which) * DEPTH + level]
            else:
                ref = (own_g[k] if which is core else other_g.at[k]).at[level]
            rows = pl.ds(pl.multiple_of(p * T, T), T)
            copy = pltpu.make_async_copy(ref, in_buf.at[n % 2, rows], in_sem.at[n % 2, k])
            copy.start() if start else copy.wait()

    def out_copy(n, target, at):
        return pltpu.make_async_copy(out_buf.at[n % 2], target.at[:, at], out_sem.at[n % 2])

    sent = {}

    def compute(n, job):
        source, level, which = job
        at = 2 * level + which
        rows_in, rows_out = in_buf.at[n % 2], out_buf.at[n % 2]
        row = lax.broadcasted_iota(jnp.int32, (slots, group), 0)
        if source == "g":
            picks = [jnp.where(slot_ref[at, e : e + 1, :] == row, 1.0, 0.0).astype(BF16) for e in range(experts)]
            pick[at] = jnp.concatenate(picks, axis=0)
        else:
            logits = dot(rows_in[...], router_ref[...])
            powers = jnp.exp(logits - jnp.max(logits, axis=1, keepdims=True))
            chances = powers / jnp.sum(powers, axis=1, keepdims=True)
            high = chances.astype(BF16)
            low = (chances - high.astype(F32)).astype(BF16)
            gates = dot(pick[at], jnp.concatenate([high, low], axis=1))
            lane = lax.broadcasted_iota(jnp.int32, (slots, 2 * EXPERTS), 1)
            for e in range(experts):
                part = gates[e * slots : (e + 1) * slots]
                part = jnp.where((lane == e) | (lane == EXPERTS + e), part, 0.0)
                gate_ref[e, at] = jnp.broadcast_to(jnp.sum(part, axis=1, keepdims=True), (slots, 128))
        if n >= 2:
            sent.pop(n - 2).wait()

        def step(i, _):
            cols = pl.ds(pl.multiple_of(i * width, width), width)
            rows = dot(pick[at], rows_in[:, cols]).astype(BF16)
            for e in range(experts):
                rows_out[e, :, cols] = rows[e * slots : (e + 1) * slots]
            return 0

        lax.fori_loop(0, D // width, step, 0)
        sent[n] = out_copy(n, gr_ref if source == "g" else xr_ref, at)
        sent[n].start()

    jobs = _Jobs(load, compute)
    jobs.add(*[("g", level, core) for level in range(4)])

    def along(level, source, step):
        @pl.when((z > 0) & (level >= z))
        def _():
            step(source, 0, level, (u, z - 1))

        @pl.when((z < DEPTH - 1) & (level <= z))
        def _():
            step(source, 1, level, (u, z + 1))

    def go(source, way, level, to):
        _send(source, block(u, level), z_send.at[way, level], z_recv.at[level], to)

    def gone(source, way, level, to):
        _sent(source, z_send.at[way, level], here)

    sources = [x_ref] + [block(u, order[i]) for i in range(1, 4)]

    def arrive(i):
        level = order[i]
        if i:
            _expect(block(u, level), z_recv.at[level], here)
        along(level, sources[i], go)
        for way, bits in enumerate((FIRST, THEN)):
            for h in range(2):
                cut = sources[i].at[halves[h]]
                _send(cut, part(u, level, h), p_send.at[level, h, way], p_recv.at[level, h, way], (u ^ bits[h], z))
        _send(sources[i], block(u, level), c_send.at[level, 0], c_recv.at[level, 0], (u ^ 1, z))

    def onward(i):
        level = order[i]
        for h in range(2):
            near = part(u ^ FIRST[h], level, h)
            _expect(near, p_recv.at[level, h, 0], here)
            _send(near, near, p_send.at[level, h, 2], p_recv.at[level, h, 2], (u ^ THEN[h], z))

    def share(i):
        level = order[i]
        for h in range(2):
            _expect(part(u ^ THEN[h], level, h), p_recv.at[level, h, 1], here)
            _expect(part(u ^ 6, level, h), p_recv.at[level, h, 2], here)
        for k, bit in enumerate((2, 4, 6)):
            ref = block(u ^ bit, level)
            _send(ref, ref, c_send.at[level, k + 1], c_recv.at[level, k + 1], (u ^ 1, z))
        jobs.add(("x", level, core))

    def received(i):
        level = order[i]
        for k, bit in enumerate((0, 2, 4, 6)):
            _expect(block(u ^ 1 ^ bit, level), c_recv.at[level, k], here)
        jobs.add(("x", level, other))

    arrive(0)
    for k in range(4):
        _send(own_g[k], other_g.at[k], g_send.at[k], g_recv.at[k], (u ^ 1, z))
    jobs.run(2)
    onward(0)
    jobs.run(1)
    arrive(1)
    for k in range(4):
        _expect(other_g.at[k], g_recv.at[k], here)
    jobs.add(*[("g", level, other) for level in range(4)])
    jobs.run(2)
    own.wait()
    share(0)
    jobs.run(2)
    onward(1)
    arrive(2)
    received(0)
    jobs.run(2)
    arrive(3)
    share(1)
    received(1)
    jobs.run(1)
    onward(2)
    jobs.run(2)
    share(2)
    received(2)
    jobs.run(1)
    onward(3)
    jobs.run(2)
    share(3)
    received(3)
    jobs.run(16)
    for i in range(4):
        level = order[i]
        along(level, sources[i], gone)
        for h in range(2):
            for k in range(3):
                _sent(part(u, level, h), p_send.at[level, h, k], here)
        for k in range(4):
            _sent(block(u, level), c_send.at[level, k], here)
    for k in range(4):
        _sent(other_g.at[k], g_send.at[k], here)
    for copy in sent.values():
        copy.wait()


def gather_pick(x, g, slot, router, slots, collective_id):
    T, D = x.shape
    groups, EL, group = slot.shape
    picked = jax.ShapeDtypeStruct((EL, groups, slots, D), BF16)
    outs = [
        jax.ShapeDtypeStruct((32, T, D), BF16),
        picked,
        picked,
        jax.ShapeDtypeStruct((EL, groups, slots, 128), F32),
        jax.ShapeDtypeStruct((4, 4, T, D), BF16),
    ]
    scratch = [
        pltpu.VMEM((groups, EL * slots, group), BF16),
        pltpu.VMEM((2, group, D), BF16),
        pltpu.VMEM((2, EL, slots, D), BF16),
        DMA((2, 4)),
        DMA((2,)),
        DMA,
        DMA((2, 4)),
        DMA((4,)),
        DMA((4, 2, 3)),
        DMA((4, 2, 3)),
        DMA((4, 4)),
        DMA((4, 4)),
        DMA((4,)),
        DMA((4,)),
    ]
    specs = ([IN_VMEM] + [ANY_SPACE] * 4 + [IN_VMEM] * 2, [ANY_SPACE] * 3 + [IN_VMEM, ANY_SPACE])
    kernel = functools.partial(_gather_pick_kernel, width=PICK_WIDTH)
    out, xr, gr, gates, _ = _comm(kernel, outs, scratch, collective_id, specs)(x, *g, slot, router)
    return out.reshape(32 * T, D), xr, gr, gates


def _tree_sum_steps(u, z, own, bufs, sems, T):
    c_buf, p_buf, q_buf = bufs
    c_send, c_recv, p_send, p_recv, q_send, q_recv = sems
    here = (u, z)
    half = T // 2
    halves = (pl.ds(0, half), pl.ds(half, half))

    def to_sibling(i, k, ref):
        _send(ref, c_buf.at[i, k], c_send.at[i, k], c_recv.at[i, k], (u ^ 1, z))

    def add_core(i):
        for k in (3, 2, 1, 0):
            _expect(c_buf.at[i, k], c_recv.at[i, k], here)
            _accumulate(own(i, k), c_buf.at[i, k], T)
            for h in range(2):
                if k and (k == 3 or CHIPS[k] == THEN[h]):
                    j = 1 if k == 3 else 0
                    part = own(i, k).at[halves[h]]
                    _send(part, p_buf.at[i, h, j], p_send.at[i, h, j], p_recv.at[i, h, j], (u ^ THEN[h], z))

    def add_far(i):
        for h in range(2):
            part = own(i, CHIPS.index(FIRST[h])).at[halves[h]]
            _expect(p_buf.at[i, h, 1], p_recv.at[i, h, 1], here)
            _accumulate(part, p_buf.at[i, h, 1], half)
            _send(part, q_buf.at[i, h], q_send.at[i, h], q_recv.at[i, h], (u ^ FIRST[h], z))

    def add_near(i):
        for h in range(2):
            _expect(p_buf.at[i, h, 0], p_recv.at[i, h, 0], here)
            _accumulate(own(i, 0).at[halves[h]], p_buf.at[i, h, 0], half)

    def add_then(i):
        for h in range(2):
            _expect(q_buf.at[i, h], q_recv.at[i, h], here)
            _accumulate(own(i, 0).at[halves[h]], q_buf.at[i, h], half)

    def finish():
        for i in range(4):
            for k in range(4):
                _sent(c_buf.at[i, k], c_send.at[i, k], here)
            for h in range(2):
                for j in range(2):
                    _sent(p_buf.at[i, h, j], p_send.at[i, h, j], here)
                _sent(q_buf.at[i, h], q_send.at[i, h], here)

    return to_sibling, add_core, add_far, add_near, add_then, finish


def _line_end(u, z, level, i, part, z_buf, sems, rows):
    z_send, z_recv = sems
    here = (u, z)

    @pl.when((level >= z) & (z > 0))
    def _():
        _expect(z_buf.at[0, level], z_recv.at[0, level], here)
        _accumulate(part, z_buf.at[0, level], rows)

    @pl.when((level <= z) & (z < DEPTH - 1))
    def _():
        _expect(z_buf.at[1, level], z_recv.at[1, level], here)
        _accumulate(part, z_buf.at[1, level], rows)

    if i < 3:

        @pl.when(level > z)
        def _():
            _send(part, z_buf.at[0, level], z_send.at[i], z_recv.at[0, level], (u, z + 1))

        @pl.when(level < z)
        def _():
            _send(part, z_buf.at[1, level], z_send.at[i], z_recv.at[1, level], (u, z - 1))


def _spread_part(u, z, slot_ref, source, gg_ref, order, refs, level_done, later=lambda i: None):
    work, c_buf, p_buf, q_buf, side, in_buf, in_sem = refs[:7]
    core, chip = u % 2, u // 2
    other = 1 - core
    _, group, experts = slot_ref.shape
    slots, D = source.shape[2:]
    total = experts * slots
    T = group // 4

    def place(k):
        return pl.ds(pl.multiple_of((chip ^ (CHIPS[k] // 2)) * T, T), T)

    def own(i, k):
        return work.at[i, place(k)]

    to_sibling, add_core, add_far, add_near, add_then, finish = _tree_sum_steps(
        u, z, own, (c_buf, p_buf, q_buf), refs[7:], T
    )
    lane = lax.broadcasted_iota(jnp.int32, (experts, total), 1)
    which = lax.broadcasted_iota(jnp.int32, (experts, total), 0)
    choose = jnp.where((lane >= which * slots) & (lane < (which + 1) * slots), 1.0, 0.0).astype(BF16)
    offset = lane[:1] - jnp.sum(jnp.where(lane >= (which + 1) * slots, slots, 0), axis=0, keepdims=True)
    offset = offset.astype(F32)
    column = lax.broadcasted_iota(jnp.int32, (slots, 128), 1)

    def load(n, job, start):
        i, c = job
        copy = pltpu.make_async_copy(source.at[:, 2 * order[i] + c], in_buf.at[n % 2], in_sem.at[n % 2])
        copy.start() if start else copy.wait()

    def compute(n, job):
        i, c = job
        at = 2 * order[i] + c
        mine = dot(slot_ref[at].astype(BF16), choose)
        pick = jnp.where(mine == offset, 1.0, 0.0).astype(BF16)
        rows_in = in_buf.at[n % 2]
        target = work.at[i] if c is core else side.at[i]
        if gg_ref is not None:
            grads = [jnp.where(column == u * experts + e, gg_ref[e, at], 0.0).astype(BF16) for e in range(experts)]
            target[:, pl.ds(D, 128)] = dot(pick, jnp.concatenate(grads, axis=0)).astype(BF16)

        def step(j, _):
            cols = pl.ds(pl.multiple_of(j * SPREAD_WIDTH, SPREAD_WIDTH), SPREAD_WIDTH)
            rows = jnp.concatenate([rows_in[e, :, cols] for e in range(experts)], axis=0)
            target[:, cols] = dot(pick, rows).astype(BF16)
            return 0

        lax.fori_loop(0, D // SPREAD_WIDTH, step, 0)
        if c is not core:
            for k in (3, 2, 1, 0):
                to_sibling(i, k, side.at[i, place(k)])

    def end(i):
        add_then(i)
        level_done(i, own(i, 0))

    jobs = _Jobs(load, compute)
    for i in range(4):
        jobs.add((i, other), (i, core))
    jobs.run(2)
    add_core(0)
    yield
    jobs.run(2)
    add_far(0)
    add_core(1)
    yield
    add_near(0)
    jobs.run(2)
    add_far(1)
    add_core(2)
    yield
    end(0)
    later(0)
    add_near(1)
    jobs.run(2)
    add_far(2)
    add_core(3)
    yield
    end(1)
    later(1)
    add_near(2)
    add_far(3)
    yield
    end(2)
    later(2)
    add_near(3)
    yield
    end(3)
    later(3)
    yield
    finish()


def _spread_scratch(T, W, rows_shape):
    half = T // 2
    return [
        pltpu.VMEM((4, 4 * T, W), BF16),
        pltpu.VMEM((4, 4, T, W), BF16),
        pltpu.VMEM((4, 2, 2, half, W), BF16),
        pltpu.VMEM((4, 2, half, W), BF16),
        pltpu.VMEM((4, 4 * T, W), BF16),
        pltpu.VMEM((2,) + rows_shape, BF16),
        DMA((2,)),
        DMA((4, 4)),
        DMA((4, 4)),
        DMA((4, 2, 2)),
        DMA((4, 2, 2)),
        DMA((4, 2)),
        DMA((4, 2)),
    ]


def spread_scatter(slot, gate_grads, entry_rows, collective_id):
    groups, group, EL = slot.shape
    slots, D = entry_rows.shape[2:]
    T, W = group // 4, D + 128

    def kernel(slot_ref, gg_ref, entry_ref, o_ref, z_buf, z_send, z_recv, *refs):
        u, z = lax.axis_index("uly"), lax.axis_index("blk")
        order = tuple(reversed(_line_order(z)))
        parts = []

        def done(i, part):
            parts.append(part)

        def line(i):
            _line_end(u, z, order[i], i, parts[i], z_buf, (z_send, z_recv), T)

        _greet(u, z, (1, 2, 4), line=True)
        _run(_spread_part(u, z, slot_ref, entry_ref, gg_ref, order, refs, done, line))
        o_ref[...] = parts[3][...]
        for i in range(3):
            _sent(parts[i], z_send.at[i], (u, z))

    scratch = [pltpu.VMEM((2, 4, T, W), BF16), DMA((4,)), DMA((2, 4))] + _spread_scratch(T, W, (EL, slots, D))
    specs = ([IN_VMEM, IN_VMEM, ANY_SPACE], IN_VMEM)
    out = jax.ShapeDtypeStruct((T, W), BF16)
    return _comm(kernel, out, scratch, collective_id, specs)(slot, gate_grads, entry_rows)


def slots_of(chosen):
    count = chosen.shape[-1]
    before = (jnp.arange(count)[:, None] < jnp.arange(count)[None, :]).astype(BF16)
    earlier = jnp.einsum("abs,st->abt", chosen.astype(BF16), before, preferred_element_type=F32)
    return jnp.where(chosen, earlier.astype(jnp.int32), -1)


class Slice:
    def __init__(self, U, Z, T, D):
        self.U, self.Z, self.T, self.D = U, Z, T, D
        self.u, self.z = lax.axis_index("uly"), lax.axis_index("blk")
        self.C = D // 8
        self.L = 8 * T
        self.group = 2 * self.z + self.u % 2
        self.first_block, self.block_step = 8 * (self.u // 2), 1

    def enter(self, hidden, weights, gains, out_weight, router, routes):
        rows, weights, packs, routes = enter(hidden, weights, gains, router, routes, 1)
        there = [((2 * ((z + u // 2) % 4) + u % 2), u // 2) for u in range(8) for z in range(4)]
        self.forth = [(i, 4 * u + z) for i, (u, z) in enumerate(there)]
        rows, mine = lax.optimization_barrier((rows, self.permute(out_weight, self.forth)))
        self.out_parts = [mine] + [self.permute(mine, self.across(bit)) for bit in (2, 4, 6)]
        self.parts = [((self.u // 2) ^ k) - self.z + 4 for k in range(4)]
        self.parts = [p % 4 for p in self.parts]
        return (
            rows.reshape(self.L, self.D),
            weights.reshape(self.D, 3 * self.C),
            packs.reshape(self.D, -1),
            routes,
        )

    def permute(self, x, pairs):
        return lax.ppermute(x, ALL, pairs)

    def across(self, bit):
        return [(i, i ^ (4 * bit)) for i in range(32)]

    def sequence(self, key, value, squares, upstream):
        keys, values, own, stats, k_stat = plane_pair(key, value, upstream, squares.reshape(-1, 128), 4)
        own, *self.out_parts = lax.optimization_barrier((own, *self.out_parts))
        first = [(i, i ^ (8 if i // 4 % 2 == 0 else 16)) for i in range(32)]
        self.then = [(i, i ^ (16 if i // 4 % 2 == 0 else 8)) for i in range(32)]
        self.upstream = (own, self.permute(own, first))
        return keys.reshape(-1, self.C), values.reshape(-1, self.C), stats.reshape(2, -1, 128), k_stat.reshape(-1, 128)

    def heads_to_rows(self, x):
        x, own, near = lax.optimization_barrier((x, *self.upstream))
        self.upstream = (own, near, self.permute(own, self.then), self.permute(near, self.then))
        return column_scatter(x.reshape(2, 4, self.T, self.D), 5)

    def experts(self, second_low, routes, weights, router):
        EL, T, D = weights.shape[0], self.T, self.D
        slots = -(-4 * CAP // 16) * 16
        chosen = jnp.any(routes[None] == (self.u * EL + jnp.arange(EL, dtype=jnp.int32))[:, None, None, None, None], axis=3)
        chosen = chosen.reshape(EL, 4, 2, 4, T).transpose(3, 2, 0, 1, 4).reshape(8, EL, 4 * T)
        slot = slots_of(chosen)
        second_all, xr, gr, gates = gather_pick(second_low, self.upstream, slot, router, slots, 7)
        flat, cut = (EL, 8 * slots, -1), (EL, 8, slots, -1)
        out_rows, entry_rows, self.expert_grads, gate_grads = run_experts(
            xr.reshape(flat), gr.reshape(flat), gates.reshape(flat), weights, 8 * slots
        )
        self.slot, self.out_rows = slot.transpose(0, 2, 1), out_rows.reshape(cut)
        return second_all, spread_scatter(self.slot, gate_grads.reshape(cut), entry_rows.reshape(cut), 8)

    def rows_to_heads(self, x):
        rows, self.out_line = column_gather(x, self.slot, self.out_rows, 6)
        return rows.reshape(self.L, self.D), self.expert_grads

    def sequence_sums(self, dk, dv, out_part, q_inner, k_inner):
        cut = (4, self.L, self.C)
        inner = jnp.concatenate([q_inner, k_inner.reshape(-1, 128)], axis=0)
        dk, dv, out_sum, inner = key_value_sums(dk.reshape(cut), dv.reshape(cut), self.out_line, inner, 10)
        parts = out_part.reshape(4, -1, self.D)
        mine, *others = [lax.dynamic_index_in_dim(parts, p, 0, False) for p in self.parts]
        dk, *others = lax.optimization_barrier((dk, *others))
        self.out_terms = [mine] + [self.permute(x, self.across(bit)) for x, bit in zip(others, (2, 4, 6))]
        return dk, dv, out_sum, inner.reshape(2, -1, 128)

    def leave(self, first_part, weight_part, logit_grad, ffn_part, head_parts):
        T, R = self.T, self.D // 32
        first_part, *terms = lax.optimization_barrier((first_part, *self.out_terms))
        out_grad = sum(x.astype(F32) for x in terms).astype(BF16)
        out_grad = self.permute(out_grad, [(b, a) for a, b in self.forth])
        thin = jnp.concatenate([ffn_part.reshape(-1, 128), head_parts.reshape(-1, 128)], axis=0)
        wide = self.D // 128
        used = thin.shape[0]
        thin = jnp.pad(thin, ((0, -used % 8), (0, 0)))
        first, weights, logit_all, thin = leave(
            first_part.reshape(2, 4, T, self.D),
            weight_part.reshape(4, 2, 4 * R, 3 * self.C),
            [logit_grad.reshape(T // 2, 2 * EXPERTS), thin],
            11,
        )
        ffn = lax.dynamic_slice_in_dim(
            jnp.sum(thin[:, :, :wide], axis=(0, 1)).reshape(self.D), (self.u * 4 + self.z) * R, R, 0
        )
        mine = lax.dynamic_index_in_dim(thin.reshape(4, 2, 4, -1, 128), self.u % 2, 1, False)
        mine = lax.dynamic_index_in_dim(mine, self.u // 2, 1, False)
        heads = jnp.sum(mine[:, wide:used], axis=0).reshape(2, self.C)
        heads = lax.dynamic_slice_in_dim(heads, self.z * R, R, 1)
        return first, weights, out_grad, logit_all.reshape(32 * T, EXPERTS), ffn, heads


class General:
    def __init__(self, U, Z, T, D):
        self.U, self.Z, self.T, self.D = U, Z, T, D
        self.u, self.z = lax.axis_index("uly"), lax.axis_index("blk")
        self.C = D // U
        self.L = U * T
        self.group = self.u
        self.parts = range(4)
        self.first_block, self.block_step = self.z, Z

    def gather(self, x):
        return lax.all_gather(x, ALL, axis=0, tiled=True)

    def scatter_wide(self, x):
        return lax.psum_scatter(x, ALL, scatter_dimension=0, tiled=True)

    def enter(self, hidden, weights, gains, out_weight, router, routes):
        U, R = self.U, router.shape[0]
        gains, hidden = gains.astype(F32), hidden.astype(F32)
        scaled = jnp.stack([(w.astype(F32) * gains[:, :1]).astype(BF16) for w in weights])
        pack = jnp.concatenate(_packed(router, gains), axis=1)
        rows = (hidden * norm_scale(hidden)).astype(BF16)
        self.out_parts = jnp.split(lax.all_gather(out_weight, "blk", axis=0, tiled=True), 4)
        swapped = lax.all_to_all(scaled.transpose(1, 0, 2).reshape(R, 3, U, self.C), "uly", split_axis=2, concat_axis=0, tiled=True)
        weights = lax.all_gather(swapped.reshape(U, R, 3 * self.C), "blk", axis=1, tiled=True)
        return (
            self.rows_all(rows),
            weights.reshape(self.D, 3 * self.C),
            self.gather(pack),
            self.gather(routes[None]).reshape((U, self.Z) + routes.shape),
        )

    def sequence(self, key, value, squares, upstream):
        self.upstream = upstream
        pair = jnp.stack([key, value]).reshape(2, self.U, self.T, self.C)
        pair = lax.all_gather(pair, "blk", axis=2, tiled=False).reshape(2, -1, self.C)
        stats = lax.psum(squares, "uly")
        k_stat = lax.all_gather(stats[1].reshape(self.U, -1, 128), "blk", axis=1, tiled=False).reshape(-1, 128)
        return pair[0], pair[1], stats, k_stat

    def heads_to_rows(self, x):
        return self.rows_sum(x)

    def rows_sum(self, x):
        return lax.psum_scatter(x, "uly", scatter_dimension=0, tiled=True)

    def rows_all(self, x):
        return lax.all_gather(x, "uly", axis=0, tiled=True)

    def experts(self, second_low, routes, weights, router):
        EL, D = weights.shape[0], self.D
        second_all, upstream_all = self.gather(second_low), self.gather(self.upstream)
        N = upstream_all.shape[0]
        group = min(512, N)
        groups = N // group
        slots = -(-(group // self.T * CAP) // 16) * 16
        rows = groups * slots
        own_first = self.u * EL
        chosen = jnp.any(routes[None] == (own_first + jnp.arange(EL, dtype=jnp.int32))[:, None, None, None, None], axis=3)
        slot = slots_of(chosen.reshape(EL, groups, group)).reshape(EL, N)
        entry_in, upstream_in, gates = pick_rows(slot, router, second_all, upstream_all, group, slots)
        flat, split = (EL, rows, -1), (EL, groups, slots, -1)
        out_rows, entry_rows, self.expert_grads, gate_grads = run_experts(
            entry_in.reshape(flat), upstream_in.reshape(flat), gates.reshape(flat), weights, min(8, groups) * slots
        )
        out_part, entry_part = spread_rows(
            own_first.astype(jnp.int32)[None],
            slot.T,
            gate_grads.reshape(split),
            out_rows.reshape(split),
            entry_rows.reshape(split),
            group,
        )
        self.out_sum = self.scatter_wide(out_part)
        return second_all, self.scatter_wide(entry_part)

    def rows_to_heads(self, x):
        return self.rows_all(x), self.expert_grads

    def sequence_sums(self, dk, dv, out_part, q_inner, k_inner):
        pair = jnp.stack([dk, dv]).reshape(2, self.U, self.Z, self.T, self.C)
        pair = lax.psum_scatter(pair, "blk", scatter_dimension=2, tiled=True).reshape(2, self.L, self.C)
        k_inner = lax.psum_scatter(
            k_inner.reshape(self.U, self.Z, -1, 128), "blk", scatter_dimension=1, tiled=True
        ).reshape(-1, 128)
        inner = lax.psum(jnp.stack([q_inner, k_inner]), "uly")
        self.out_grad = lax.psum_scatter(out_part, "blk", scatter_dimension=0, tiled=True)
        return pair[0], pair[1], self.out_sum, inner

    def leave(self, first_part, weight_part, logit_grad, ffn_part, head_parts):
        U, R = self.U, self.D // (self.U * self.Z)
        part = weight_part.reshape(U, self.Z * R, 3 * self.C)
        part = lax.psum_scatter(part, "blk", scatter_dimension=1, tiled=True)
        part = lax.all_to_all(part, "uly", split_axis=0, concat_axis=0, tiled=True)
        weights = part.reshape(U, R, 3, self.C).transpose(2, 1, 0, 3).reshape(3, R, self.D)
        heads = lax.psum_scatter(head_parts, "blk", scatter_dimension=1, tiled=True)
        first = self.rows_sum(first_part)
        return first, weights, self.out_grad, self.gather(logit_grad), self.scatter_wide(ffn_part), heads


def _row_limits(doc_ref, first, rows):
    position = first + lax.broadcasted_iota(jnp.int32, (rows, 1), 0)
    start = jnp.zeros_like(position)
    lowest = jnp.int32(0)
    for d in range(doc_ref.shape[0]):
        begin = doc_ref[d]
        start = jnp.where(begin <= position, jnp.maximum(start, begin), start)
        lowest = jnp.where(begin <= first, jnp.maximum(lowest, begin), lowest)
    return position, start, lowest


def _norm_row(squares, width):
    return lax.rsqrt(squares * (1.0 / width) + EPS)


def _as_column(row):
    return jnp.broadcast_to(row, (128, 128)).T


def _row_sums(values):
    ones = jnp.ones((8, values.shape[1]), F32)
    return lax.dot_general(ones, values, LAST_DIM, precision=lax.Precision.HIGHEST, preferred_element_type=F32)[:1]


def _key_scales(stat_ref, at, chunk, width):
    rows = stat_ref[pl.ds(pl.multiple_of(at // 128, chunk // 128), chunk // 128), :]
    return _norm_row(jnp.concatenate([rows[r : r + 1] for r in range(chunk // 128)], axis=1), width)


def _scores(query, key, factor, position, start, key_first):
    raw = dot(query, key, LAST_DIM) * factor
    key_position = key_first + lax.broadcasted_iota(jnp.int32, raw.shape, 1)
    return jnp.where((key_position <= position) & (key_position >= start), raw, NEG)


def _scaled_query(q_ref, stat_ref, width):
    heads = q_ref.shape[1] // HEAD_DIM
    scale = _as_column(_norm_row(stat_ref[pl.ds(pl.program_id(0), 1), :], width))
    cols = [pl.ds(h * HEAD_DIM, HEAD_DIM) for h in range(heads)]
    return [(q_ref[:, at].astype(F32) * scale).astype(BF16) for at in cols], cols


def _lay_parts(index_ref, parts, whole):
    @pl.when(pl.program_id(0) == 0)
    def _():
        for i, part in enumerate(parts):
            height = part.shape[0]
            whole[pl.ds(pl.multiple_of(index_ref[2 + i] * height, height), height), :] = part[...]


def _attend_kernel(
    index_ref, doc_ref, q_stat, k_stat, q_ref, k_ref, v_ref, w0, w1, w2, w3, o_ref, log_ref, mix_ref, whole, *, chunk, scaling, width
):
    rows = q_ref.shape[0]
    _lay_parts(index_ref, (w0, w1, w2, w3), whole)
    heads = q_ref.shape[1] // HEAD_DIM
    first = (pl.program_id(0) * index_ref[1] + index_ref[0]) * rows
    position, start, lowest = _row_limits(doc_ref, first, rows)
    queries, cols = _scaled_query(q_ref, q_stat, width)

    def step(i, state):
        at = pl.multiple_of(i * chunk, chunk)
        factor = _key_scales(k_stat, at, chunk, width) * scaling
        new = []
        for h in range(heads):
            top, total, out = state[h]
            scores = _scores(queries[h], k_ref[pl.ds(at, chunk), cols[h]], factor, position, start, at)
            now = jnp.maximum(top, jnp.max(scores, axis=1, keepdims=True))
            weights = jnp.exp(scores - now)
            fade = jnp.exp(top - now)
            total = total * fade + jnp.sum(weights, axis=1, keepdims=True)
            out = out * fade + dot(weights.astype(BF16), v_ref[pl.ds(at, chunk), cols[h]])
            new.append((now, total, out))
        return tuple(new)

    zero = (
        jnp.full((rows, 1), NEG, F32),
        jnp.zeros((rows, 1), F32),
        jnp.zeros((rows, HEAD_DIM), F32),
    )
    last = first + rows
    state = lax.fori_loop(lowest // chunk, (last + chunk - 1) // chunk, step, (zero,) * heads)
    for h in range(heads):
        top, total, out = state[h]
        o_ref[:, cols[h]] = out / total
        log_ref[:, cols[h]] = jnp.broadcast_to(top + jnp.log(total), (rows, HEAD_DIM))
    mix_ref[...] = dot(o_ref[...].astype(BF16), whole[...]).astype(BF16)


def _attend_back_kernel(
    index_ref,
    doc_ref,
    q_stat,
    k_stat,
    q_ref,
    r_ref,
    o_ref,
    log_ref,
    k_ref,
    v_ref,
    w0,
    w1,
    w2,
    w3,
    dq_ref,
    dk_ref,
    dv_ref,
    dw_ref,
    mq_ref,
    mk_ref,
    dk_sum,
    dv_sum,
    dw_sum,
    whole,
    *,
    chunk,
    scaling,
    width,
):
    rows = q_ref.shape[0]
    _lay_parts(index_ref, (w0, w1, w2, w3), whole)
    heads = q_ref.shape[1] // HEAD_DIM
    first = (pl.program_id(0) * index_ref[1] + index_ref[0]) * rows
    position, start, lowest = _row_limits(doc_ref, first, rows)
    queries, cols = _scaled_query(q_ref, q_stat, width)

    @pl.when(pl.program_id(0) == 0)
    def _():
        dk_sum[...] = jnp.zeros_like(dk_sum)
        dv_sum[...] = jnp.zeros_like(dv_sum)
        dw_sum[...] = jnp.zeros_like(dw_sum)
        mk_ref[...] = jnp.zeros_like(mk_ref)

    upstream = r_ref[...]
    dw_sum[...] += dot(o_ref[...].astype(BF16), upstream, FIRST_DIM)
    all_grads = dot(upstream, whole[...], LAST_DIM).astype(BF16)
    grads = [all_grads[:, h * HEAD_DIM : (h + 1) * HEAD_DIM] for h in range(heads)]
    deltas = [jnp.sum(grads[h].astype(F32) * o_ref[:, cols[h]], axis=1, keepdims=True) for h in range(heads)]
    logs = [log_ref[:, at][:, :1] for at in cols]

    def step(i, state):
        at = pl.multiple_of(i * chunk, chunk)
        scale = _key_scales(k_stat, at, chunk, width)
        new = []
        key_inner = jnp.zeros((1, chunk), F32)
        query_inner = state[-1]
        for h in range(heads):
            grad = grads[h]
            key = k_ref[pl.ds(at, chunk), cols[h]]
            scores = _scores(queries[h], key, scale * scaling, position, start, at)
            weights = jnp.exp(scores - logs[h])
            weight_grad = dot(grad, v_ref[pl.ds(at, chunk), cols[h]], LAST_DIM)
            score_grad = weights * (weight_grad - deltas[h])
            inner = score_grad * scores
            key_inner = key_inner + jnp.sum(inner, axis=0, keepdims=True)
            query_inner = query_inner + jnp.sum(inner, axis=1, keepdims=True)
            dv_sum[pl.ds(at, chunk), cols[h]] += dot(weights.astype(BF16), grad, FIRST_DIM)
            dk_sum[pl.ds(at, chunk), cols[h]] += dot(score_grad.astype(BF16), queries[h], FIRST_DIM)
            new.append(state[h] + dot((score_grad * scale).astype(BF16), key))
        mk_ref[pl.ds(i, 1), :] += key_inner
        return tuple(new) + (query_inner,)

    last = first + rows
    zeros = (jnp.zeros((rows, HEAD_DIM), F32),) * heads + (jnp.zeros((rows, 1), F32),)
    state = lax.fori_loop(lowest // chunk, (last + chunk - 1) // chunk, step, zeros)
    for h in range(heads):
        dq_ref[:, cols[h]] = (state[h] * scaling).astype(BF16)
    mq_ref[pl.ds(pl.program_id(0), 1), :] = jnp.broadcast_to(state[-1], (rows, 128)).T[:1]

    @pl.when(pl.program_id(0) == pl.num_programs(0) - 1)
    def _():
        dk_ref[...] = (dk_sum[...] * scaling).astype(BF16)
        dv_ref[...] = dv_sum[...].astype(BF16)
        dw_ref[...] = dw_sum[...].astype(BF16)


def _resident(*shape):
    return pl.BlockSpec(shape, lambda i, *_: (0,) * len(shape), pipeline_mode=pl.Buffered(1))


def attention_forward(index, docs, q_stat, k_stat, query, key_all, value_all, out_parts, rows, chunk):
    (L, C), N = query.shape, key_all.shape[0]
    D = out_parts[0].shape[1]
    block = pl.BlockSpec((rows, C), lambda i, *_: (i, 0))
    stats = [_resident(*q_stat.shape), _resident(*k_stat.shape)]
    return pl.pallas_call(
        functools.partial(_attend_kernel, chunk=chunk, scaling=HEAD_DIM ** (-0.5), width=HEADS * HEAD_DIM),
        out_shape=[jax.ShapeDtypeStruct((L, C), F32)] * 2 + [jax.ShapeDtypeStruct((L, D), BF16)],
        grid_spec=pltpu.PrefetchScalarGridSpec(
            num_scalar_prefetch=2,
            grid=(L // rows,),
            in_specs=stats + [block, _resident(N, C), _resident(N, C)] + [_resident(C // 4, D)] * 4,
            out_specs=[block, block, pl.BlockSpec((rows, D), lambda i, *_: (i, 0))],
            scratch_shapes=[pltpu.VMEM((C, D), BF16)],
        ),
        compiler_params=pltpu.CompilerParams(vmem_limit_bytes=VMEM_BYTES),
        cost_estimate=pl.CostEstimate(flops=4 * L * C * 1024, bytes_accessed=4 * N * C, transcendentals=L * 1024),
    )(index, docs, q_stat, k_stat, query, key_all, value_all, *out_parts)


def attention_backward(
    index, docs, q_stat, k_stat, query, residual_grad, attended, logs, key_all, value_all, out_parts, rows, chunk
):
    (L, C), N = query.shape, key_all.shape[0]
    D = residual_grad.shape[1]
    block = pl.BlockSpec((rows, C), lambda i, *_: (i, 0))
    whole = _resident(N, C)
    stats = [_resident(*q_stat.shape), _resident(*k_stat.shape)]
    return pl.pallas_call(
        functools.partial(_attend_back_kernel, chunk=chunk, scaling=HEAD_DIM ** (-0.5), width=HEADS * HEAD_DIM),
        out_shape=[jax.ShapeDtypeStruct((L, C), BF16)]
        + [jax.ShapeDtypeStruct((N, C), BF16)] * 2
        + [jax.ShapeDtypeStruct((C, D), BF16)]
        + [jax.ShapeDtypeStruct(q_stat.shape, F32), jax.ShapeDtypeStruct((N // chunk, chunk), F32)],
        grid_spec=pltpu.PrefetchScalarGridSpec(
            num_scalar_prefetch=2,
            grid=(L // rows,),
            in_specs=stats
            + [block, pl.BlockSpec((rows, D), lambda i, *_: (i, 0)), block, block, whole, whole]
            + [_resident(C // 4, D)] * 4,
            out_specs=[block, whole, whole, _resident(C, D), stats[0], _resident(N // chunk, chunk)],
            scratch_shapes=[pltpu.VMEM((N, C), F32)] * 2 + [pltpu.VMEM((C, D), F32), pltpu.VMEM((C, D), BF16)],
        ),
        compiler_params=pltpu.CompilerParams(vmem_limit_bytes=VMEM_BYTES),
        cost_estimate=pl.CostEstimate(flops=10 * L * C * 1024, bytes_accessed=8 * N * C, transcendentals=L * 1024),
    )(index, docs, q_stat, k_stat, query, residual_grad, attended, logs, key_all, value_all, *out_parts)


def _project_kernel(x_ref, w_ref, gain_ref, cos_ref, sin_ref, pre_ref, q_ref, k_ref, v_ref, stat_ref):
    rows = x_ref.shape[0]
    C = q_ref.shape[1]
    pre = dot(x_ref[...], w_ref[...])
    pre_ref[...] = pre[:, : 2 * C]
    v_ref[...] = pre[:, 2 * C :].astype(BF16)
    cosine, sine = cos_ref[...], sin_ref[...]
    for j, out in enumerate((q_ref, k_ref)):
        part = pre[:, j * C : (j + 1) * C]
        sums = _row_sums(part * part)
        for r in range(rows // 128):
            stat_ref[j, pl.ds(pl.program_id(0) * (rows // 128) + r, 1), :] = sums[:, r * 128 : (r + 1) * 128]
        scaled = part * gain_ref[j : j + 1, :]
        for h in range(C // HEAD_DIM):
            one = scaled[:, h * HEAD_DIM : (h + 1) * HEAD_DIM]
            turned = pltpu.roll(one, HEAD_DIM // 2, 1)
            out[:, pl.ds(h * HEAD_DIM, HEAD_DIM)] = (one * cosine + turned * sine).astype(BF16)


def project(x, weights, gains, cosine, sine):
    L, D = x.shape
    C = weights.shape[1] // 3
    rows = 256

    def block(width):
        return pl.BlockSpec((rows, width), lambda i: (i, 0))

    return pl.pallas_call(
        _project_kernel,
        out_shape=[jax.ShapeDtypeStruct((L, 2 * C), F32)]
        + [jax.ShapeDtypeStruct((L, C), BF16)] * 3
        + [jax.ShapeDtypeStruct((2, L // 128, 128), F32)],
        grid=(L // rows,),
        in_specs=[block(D), _resident(D, 3 * C), _resident(8, C), block(HEAD_DIM), block(HEAD_DIM)],
        out_specs=[block(2 * C), block(C), block(C), block(C), _resident(2, L // 128, 128)],
        compiler_params=pltpu.CompilerParams(vmem_limit_bytes=VMEM_BYTES),
        cost_estimate=pl.CostEstimate(flops=6 * L * D * C, bytes_accessed=2 * L * D + 6 * D * C, transcendentals=0),
    )(x, weights, gains, cosine, sine)


def _project_back_kernel(
    dq_ref, dk_ref, dv_ref, pre_ref, stat_ref, inner_ref, gain_ref, cos_ref, sin_ref, x_ref, w_ref, dw_ref, first_ref, dg_ref, total, *, width
):
    rows, C = dq_ref.shape
    cosine, sine = cos_ref[...], sin_ref[...]
    start = pl.program_id(0) == 0

    @pl.when(start)
    def _():
        dg_ref[...] = jnp.zeros_like(dg_ref)

    grads = []
    for j, ref in enumerate((dq_ref, dk_ref)):
        scales, means = [], []
        for r in range(rows // 128):
            at = pl.ds(pl.program_id(0) * (rows // 128) + r, 1)
            scale = _norm_row(stat_ref[j, at, :], width)
            scales.append(_as_column(scale))
            means.append(_as_column(inner_ref[j, at, :] * scale * scale * (1.0 / width)))
        scale, mean = jnp.concatenate(scales, axis=0), jnp.concatenate(means, axis=0)
        for h in range(C // HEAD_DIM):
            at = pl.ds(h * HEAD_DIM, HEAD_DIM)
            up = ref[:, at].astype(F32)
            up = up * cosine + pltpu.roll(up * sine, HEAD_DIM // 2, 1)
            pre = pre_ref[:, pl.ds(j * C + h * HEAD_DIM, HEAD_DIM)]
            grads.append((scale * up * gain_ref[j : j + 1, at] - pre * mean).astype(BF16))
            dg_ref[j : j + 1, at] += jnp.sum(up * pre * scale, axis=0, keepdims=True)
    grads.append(dv_ref[...])
    both = jnp.concatenate(grads, axis=1)
    first_ref[...] = dot(both, w_ref[...], LAST_DIM).astype(BF16)
    part = dot(x_ref[...], both, FIRST_DIM)

    @pl.when(start)
    def _():
        total[...] = part

    @pl.when(jnp.logical_not(start))
    def _():
        total[...] += part

    @pl.when(pl.program_id(0) == pl.num_programs(0) - 1)
    def _():
        dw_ref[...] = total[...].astype(BF16)


def project_back(dq, dk, dv, pre, stats, inner, gains, cosine, sine, x, weights):
    L, D = x.shape
    C = weights.shape[1] // 3
    rows = min(512, L)

    def block(width):
        return pl.BlockSpec((rows, width), lambda i: (i, 0))

    return pl.pallas_call(
        functools.partial(_project_back_kernel, width=D),
        out_shape=[
            jax.ShapeDtypeStruct((D, 3 * C), BF16),
            jax.ShapeDtypeStruct((L, D), BF16),
            jax.ShapeDtypeStruct((8, C), F32),
        ],
        grid=(L // rows,),
        in_specs=[block(C)] * 3
        + [block(2 * C), _resident(*stats.shape), _resident(*inner.shape), _resident(8, C)]
        + [block(HEAD_DIM), block(HEAD_DIM), block(D), _resident(D, 3 * C)],
        out_specs=[_resident(D, 3 * C), block(D), _resident(8, C)],
        scratch_shapes=[pltpu.VMEM((D, 3 * C), F32)],
        compiler_params=pltpu.CompilerParams(vmem_limit_bytes=VMEM_BYTES),
        cost_estimate=pl.CostEstimate(flops=12 * L * D * C, bytes_accessed=4 * L * D + 12 * D * C, transcendentals=0),
    )(dq, dk, dv, pre, stats, inner, gains, cosine, sine, x, weights)


def _pick_kernel(slot_ref, router_ref, x_ref, g_ref, xr_ref, gr_ref, gate_ref, *, slots, width):
    experts, group = slot_ref.shape
    logits = lax.dot_general(router_ref[...], x_ref[...], (((0,), (1,)), ((), ())), preferred_element_type=F32)
    powers = jnp.exp(logits - jnp.max(logits, axis=0, keepdims=True))
    chances = powers / jnp.sum(powers, axis=0, keepdims=True)
    row = lax.broadcasted_iota(jnp.int32, (slots, group), 0)
    picks = []
    for e in range(experts):
        hit = slot_ref[e : e + 1, :] == row
        gate = jnp.sum(jnp.where(hit, chances[e : e + 1, :], 0.0), axis=1, keepdims=True)
        gate_ref[e, 0] = jnp.broadcast_to(gate, (slots, 128))
        picks.append(jnp.where(hit, 1.0, 0.0).astype(BF16))
    pick = jnp.concatenate(picks, axis=0)
    for source, target in ((x_ref, xr_ref), (g_ref, gr_ref)):

        def step(i, _, source=source, target=target):
            cols = pl.ds(pl.multiple_of(i * width, width), width)
            rows = dot(pick, source[:, cols]).astype(BF16)
            for e in range(experts):
                target[e, 0, :, cols] = rows[e * slots : (e + 1) * slots]
            return 0

        lax.fori_loop(0, source.shape[1] // width, step, 0)


def pick_rows(slot, router, x, g, group, slots):
    EL, N = slot.shape
    D = x.shape[1]
    groups = N // group
    tokens = pl.BlockSpec((group, D), lambda i: (i, 0))
    picked = pl.BlockSpec((EL, 1, slots, D), lambda i: (0, i, 0, 0))
    rows = jax.ShapeDtypeStruct((EL, groups, slots, D), BF16)
    return pl.pallas_call(
        functools.partial(_pick_kernel, slots=slots, width=512),
        out_shape=[rows, rows, jax.ShapeDtypeStruct((EL, groups, slots, 128), F32)],
        grid=(groups,),
        in_specs=[
            pl.BlockSpec((EL, group), lambda i: (0, i)),
            pl.BlockSpec(router.shape, lambda i: (0, 0)),
            tokens,
            tokens,
        ],
        out_specs=[picked, picked, pl.BlockSpec((EL, 1, slots, 128), lambda i: (0, i, 0, 0))],
        compiler_params=pltpu.CompilerParams(vmem_limit_bytes=VMEM_BYTES),
        cost_estimate=pl.CostEstimate(
            flops=4 * EL * slots * N * D, bytes_accessed=8 * N * D, transcendentals=N * EXPERTS
        ),
    )(slot, router, x, g)


def _expert_kernel(x_ref, g_ref, gate_ref, w_ref, out_ref, entry_ref, dw_ref, gg_ref):
    x, g = x_ref[0], g_ref[0]
    gate = gate_ref[0][:, :1]
    gate_pre = dot(x, w_ref[0, 0])
    up = dot(x, w_ref[0, 1])
    back = dot(g, w_ref[0, 2])
    sig = jax.nn.sigmoid(gate_pre)
    act = gate_pre * sig
    inner = act * up
    gg_ref[0] = jnp.broadcast_to(jnp.sum(inner * back, axis=1, keepdims=True), gg_ref.shape[1:])
    inner_grad = back * gate
    gate_pre_grad = (inner_grad * up * sig * (1.0 + gate_pre * (1.0 - sig))).astype(BF16)
    up_grad = (inner_grad * act).astype(BF16)
    gated = (inner * gate).astype(BF16)
    both = jnp.concatenate([gate_pre_grad, up_grad], axis=1)
    out_ref[0] = dot(gated, w_ref[0, 2], LAST_DIM).astype(BF16)
    entry_ref[0] = dot(both, jnp.concatenate([w_ref[0, 0], w_ref[0, 1]], axis=1), LAST_DIM).astype(BF16)
    FL = w_ref.shape[3]
    pair = dot(x, both, FIRST_DIM)
    parts = (pair[:, :FL], pair[:, FL:], dot(g, gated, FIRST_DIM))
    first = pl.program_id(1) == 0
    for k in range(3):

        @pl.when(first)
        def _(k=k):
            dw_ref[0, k] = parts[k]

        @pl.when(jnp.logical_not(first))
        def _(k=k):
            dw_ref[0, k] += parts[k]


def run_experts(x, g, gate, weights, chunk):
    EL, rows, D = x.shape
    FL = weights.shape[3]
    row_block = pl.BlockSpec((1, chunk, D), lambda e, c: (e, c, 0))
    thin = pl.BlockSpec((1, chunk, 128), lambda e, c: (e, c, 0))
    matrices = pl.BlockSpec((1, 3, D, FL), lambda e, c: (e, 0, 0, 0))
    return pl.pallas_call(
        _expert_kernel,
        out_shape=[
            jax.ShapeDtypeStruct(x.shape, BF16),
            jax.ShapeDtypeStruct(x.shape, BF16),
            jax.ShapeDtypeStruct(weights.shape, F32),
            jax.ShapeDtypeStruct((EL, rows, 128), F32),
        ],
        grid=(EL, rows // chunk),
        in_specs=[row_block, row_block, thin, matrices],
        out_specs=[row_block, row_block, matrices, thin],
        compiler_params=pltpu.CompilerParams(vmem_limit_bytes=VMEM_BYTES),
        cost_estimate=pl.CostEstimate(
            flops=18 * EL * rows * D * FL, bytes_accessed=8 * EL * rows * D + 18 * EL * D * FL, transcendentals=EL * rows * FL
        ),
    )(x, g, gate, weights)


def _spread_kernel(own_ref, slot_ref, gg_ref, out_ref, entry_ref, o_ref, e_ref, *, width):
    group, experts = slot_ref.shape
    slots = out_ref.shape[2]
    total = experts * slots
    D = out_ref.shape[3]
    lane = lax.broadcasted_iota(jnp.int32, (experts, total), 1)
    which = lax.broadcasted_iota(jnp.int32, (experts, total), 0)
    choose = jnp.where((lane >= which * slots) & (lane < (which + 1) * slots), 1.0, 0.0).astype(BF16)
    offset = lane[:1] - jnp.sum(jnp.where(lane >= (which + 1) * slots, slots, 0), axis=0, keepdims=True)
    mine = dot(slot_ref[...].astype(BF16), choose)
    pick = jnp.where(mine == offset.astype(F32), 1.0, 0.0).astype(BF16)
    column = lax.broadcasted_iota(jnp.int32, (slots, 128), 1)
    grads = [jnp.where(column == own_ref[0] + e, gg_ref[e, 0], 0.0).astype(BF16) for e in range(experts)]
    e_ref[:, pl.ds(D, 128)] = dot(pick, jnp.concatenate(grads, axis=0)).astype(BF16)

    def step(i, _):
        cols = pl.ds(pl.multiple_of(i * width, width), width)
        for source, target in ((out_ref, o_ref), (entry_ref, e_ref)):
            rows = jnp.concatenate([source[e, 0, :, cols] for e in range(experts)], axis=0)
            target[:, cols] = dot(pick, rows).astype(BF16)
        return 0

    lax.fori_loop(0, D // width, step, 0)


def spread_rows(own, slot, gate_grads, out_rows, entry_rows, group):
    N, EL = slot.shape
    _, groups, slots, D = out_rows.shape
    picked = pl.BlockSpec((EL, 1, slots, D), lambda i, *_: (0, i, 0, 0))
    return pl.pallas_call(
        functools.partial(_spread_kernel, width=512),
        out_shape=[jax.ShapeDtypeStruct((N, D), BF16), jax.ShapeDtypeStruct((N, D + 128), BF16)],
        grid_spec=pltpu.PrefetchScalarGridSpec(
            num_scalar_prefetch=1,
            grid=(groups,),
            in_specs=[
                pl.BlockSpec((group, EL), lambda i, *_: (i, 0)),
                pl.BlockSpec((EL, 1, slots, 128), lambda i, *_: (0, i, 0, 0)),
                picked,
                picked,
            ],
            out_specs=[
                pl.BlockSpec((group, D), lambda i, *_: (i, 0)),
                pl.BlockSpec((group, D + 128), lambda i, *_: (i, 0)),
            ],
        ),
        compiler_params=pltpu.CompilerParams(vmem_limit_bytes=VMEM_BYTES),
        cost_estimate=pl.CostEstimate(flops=4 * EL * slots * N * D, bytes_accessed=8 * N * D, transcendentals=0),
    )(own, slot, gate_grads, out_rows, entry_rows)


def body(
    hidden_in,
    out_grad,
    attn_gain,
    query_weight,
    key_weight,
    value_weight,
    out_weight,
    query_gain,
    key_gain,
    ffn_gain,
    router_weight,
    expert_weights,
    routes,
    doc_starts,
):
    U = lax.axis_size("uly")
    Z = lax.axis_size("blk")
    u = lax.axis_index("uly")
    z = lax.axis_index("blk")
    T, D = hidden_in.shape
    EL = expert_weights.shape[0]
    N = U * Z * T
    RW = query_weight.shape[0]
    move = (Slice if (U, Z, T, D) == (8, 4, 128, 2048) else General)(U, Z, T, D)
    C, L = move.C, move.L

    own_weights = (query_weight, key_weight, value_weight)
    gains = jnp.stack([attn_gain, ffn_gain, query_gain, key_gain], axis=1)
    first_rows, qkv_weight, packed, routes_all = move.enter(
        hidden_in, own_weights, gains, out_weight, router_weight, routes.T
    )
    hidden = hidden_in.astype(F32)
    weight_router = packed[:, :EXPERTS]
    gain_ffn = packed[:, EXPERTS].astype(F32)
    head_gains = lax.dynamic_slice_in_dim(packed[:, EXPERTS + 1 : EXPERTS + 3], move.group * C, C, 0).astype(F32)
    head_gains = jnp.pad(head_gains.T, ((0, 6), (0, 0)))
    local = jnp.arange(L, dtype=jnp.int32)
    cosine, sine = rotary_tables((local // T * move.block_step + move.first_block) * T + local % T)
    pre, query_rot, key_rot, value, squares = project(first_rows, qkv_weight, head_gains, cosine, sine)
    key_all, value_all, stats, k_stat = move.sequence(key_rot, value, squares, out_grad)
    index = jnp.stack([jnp.int32(i) for i in (move.first_block, move.block_step, *move.parts)])
    chunk = min(ATTEND_CHUNK, N)
    attended, logs, mixed = attention_forward(
        index, doc_starts, stats[0], k_stat, query_rot, key_all, value_all, move.out_parts, T, chunk
    )
    residual = hidden + move.heads_to_rows(mixed).astype(F32)

    second_scale = norm_scale(residual)
    second_low = (residual * second_scale * gain_ffn).astype(BF16)
    probabilities = jax.nn.softmax(dot(second_low, weight_router), axis=-1)
    own_router = jnp.roll(weight_router, -u * EL, axis=1)
    second_all, entry_sum = move.experts(second_low, routes_all, expert_weights, own_router)
    entry_sum = entry_sum.astype(F32)

    second_grad, prob_grad = entry_sum[:, :D], entry_sum[:, D : D + EXPERTS]
    logit_grad = (
        probabilities * (prob_grad - jnp.sum(probabilities * prob_grad, axis=1, keepdims=True))
    ).astype(BF16)
    second_grad = second_grad + dot(logit_grad, weight_router, LAST_DIM)
    upstream = out_grad.astype(F32)
    weighted = second_grad * gain_ffn
    inner_mean = jnp.mean(weighted * residual, axis=-1, keepdims=True)
    residual_grad = upstream + second_scale * weighted - residual * (second_scale**3) * inner_mean
    ffn_gain_part = jnp.sum(second_grad * residual * second_scale, axis=0)

    residual_rows, expert_grads = move.rows_to_heads(residual_grad.astype(BF16))
    dq, dk_part, dv_part, out_weight_part, q_inner, k_inner = attention_backward(
        index,
        doc_starts,
        stats[0],
        k_stat,
        query_rot,
        residual_rows,
        attended,
        logs,
        key_all,
        value_all,
        move.out_parts,
        T,
        chunk,
    )
    dk, dv, out_sum, inner = move.sequence_sums(dk_part, dv_part, out_weight_part, q_inner, k_inner)
    weight_part, first_part, gain_parts = project_back(
        dq, dk, dv, pre, stats, inner, head_gains, cosine, sine, first_rows, qkv_weight
    )
    gain_parts = gain_parts[:2]
    first_weighted, weight_sum, out_weight_grad, logit_grad_all, ffn_gain_grad, head_gain_grads = move.leave(
        first_part, weight_part, logit_grad, ffn_gain_part, gain_parts
    )
    own_columns = lax.dynamic_slice_in_dim(second_all, (u * Z + z) * RW, RW, 1)
    router_grad = dot(own_columns, logit_grad_all, FIRST_DIM)
    output, hidden_grad, attn_gain_grad, *weight_grads = finish(
        hidden_in, residual, residual_grad, first_weighted, out_sum, own_weights, weight_sum, out_weight_grad, gains
    )
    return (
        output,
        hidden_grad,
        attn_gain_grad[:, 0],
        weight_grads[0],
        weight_grads[1],
        weight_grads[2],
        weight_grads[3],
        head_gain_grads[0],
        head_gain_grads[1],
        ffn_gain_grad,
        router_grad,
        expert_grads,
    )


def solution(mesh):
    rows = P(ALL, None)
    flat = P(ALL)
    experts = P("uly", None, None, "blk")
    return jax.shard_map(
        body,
        mesh=mesh,
        in_specs=(rows, rows, flat, rows, rows, rows, rows, flat, flat, flat, rows, experts, rows, P()),
        out_specs=(rows, rows, flat, rows, rows, rows, rows, flat, flat, flat, rows, experts),
        check_vma=False,
    )
```

```python
import functools

import jax
import jax.numpy as jnp
from jax import lax
from jax.experimental import pallas as pl
from jax.experimental.pallas import tpu as pltpu
from jax.sharding import PartitionSpec as P

HEADS = 16
HEAD_DIM = 128
EXPERTS = 64
CAP = 17

EPS = 1e-05
THETA = 10000.0
NEG = -1e30
FIRST_DIM = (((0,), (0,)), ((), ()))
LAST_DIM = (((1,), (1,)), ((), ()))
ALL = ("uly", "blk")
F32 = jnp.float32
BF16 = jnp.bfloat16
VMEM_BYTES = 56 * 1024 * 1024
PICK_WIDTH = 512
ATTEND_CHUNK = 512
ATTEND_ROWS = 512
BACK_ROWS = 1024
SPREAD_WIDTH = 2048


def dot(a, b, dims=(((1,), (0,)), ((), ()))):
    return lax.dot_general(a, b, dims, preferred_element_type=F32)


def rotary_tables(position):
    halfway = HEAD_DIM // 2
    frequency = THETA ** (-(jnp.arange(halfway).astype(F32) * 2.0 / HEAD_DIM))
    angles = position.astype(F32)[:, None] * frequency[None, :]
    cosine, sine = jnp.cos(angles), jnp.sin(angles)
    return jnp.concatenate([cosine, cosine], axis=1), jnp.concatenate([-sine, sine], axis=1)


def norm_scale(values):
    return lax.rsqrt(jnp.mean(values * values, axis=-1, keepdims=True) + EPS)


MESH = pl.DeviceIdType.MESH
DMA = pltpu.SemaphoreType.DMA
ANY_SPACE = pl.BlockSpec(memory_space=pl.ANY)
IN_VMEM = pl.BlockSpec(memory_space=pltpu.VMEM)
DEPTH = 4
CHIPS = (0, 2, 4, 6)
FIRST, THEN = (2, 4), (4, 2)


def _send(src, dst, send_sem, recv_sem, to):
    pltpu.make_async_remote_copy(
        src_ref=src, dst_ref=dst, send_sem=send_sem, recv_sem=recv_sem, device_id=to, device_id_type=MESH
    ).start()


def _expect(ref, sem, here):
    pltpu.make_async_remote_copy(
        src_ref=ref, dst_ref=ref, send_sem=sem, recv_sem=sem, device_id=here, device_id_type=MESH
    ).wait_recv()


def _sent(ref, sem, here):
    pltpu.make_async_remote_copy(
        src_ref=ref, dst_ref=ref, send_sem=sem, recv_sem=sem, device_id=here, device_id_type=MESH
    ).wait_send()


def _greet(u, z, planes, line=False, others=(), meanwhile=lambda: None):
    barrier = pltpu.get_barrier_semaphore()
    for bit in planes:
        pl.semaphore_signal(barrier, inc=1, device_id=(u ^ bit, z), device_id_type=MESH)
    for to in others:
        pl.semaphore_signal(barrier, inc=1, device_id=to, device_id_type=MESH)
    count = len(planes) + len(others)
    if line:

        @pl.when(z > 0)
        def _():
            pl.semaphore_signal(barrier, inc=1, device_id=(u, z - 1), device_id_type=MESH)

        @pl.when(z < DEPTH - 1)
        def _():
            pl.semaphore_signal(barrier, inc=1, device_id=(u, z + 1), device_id_type=MESH)

        count = count + jnp.where((z == 0) | (z == DEPTH - 1), 1, 2)
    meanwhile()
    pl.semaphore_wait(barrier, count)


def _line_order(z):
    second = jnp.where(z == 0, 1, z - 1)
    third = jnp.where(z == 0, 2, jnp.where(z == 3, 1, z + 1))
    fourth = jnp.where(z < 2, 3, 0)
    return (z, second, third, fourth)


def _accumulate(target, source, rows):
    strip = 16

    def step(i, _):
        at = pl.ds(pl.multiple_of(i * strip, strip), strip)
        target[at, :] = target[at, :] + source[at, :]
        return 0

    lax.fori_loop(0, rows // strip, step, 0)


def _run(*parts, order=()):
    for i in order:
        next(parts[i])
    live = list(parts)
    while live:
        for part in list(live):
            try:
                next(part)
            except StopIteration:
                live.remove(part)


def _line_part(u, z, source, block, sems, share=True):
    z_send, z_recv, c_send, c_recv, own_sem = sems
    here, core = (u, z), u % 2
    own = pltpu.make_async_copy(source, block(core, z), own_sem)
    own.start()
    order = _line_order(z)

    def along(level, ref, step):
        @pl.when((z > 0) & (level >= z))
        def _():
            step(ref, 0, level, (u, z - 1))

        @pl.when((z < DEPTH - 1) & (level <= z))
        def _():
            step(ref, 1, level, (u, z + 1))

    def go(ref, way, level, to):
        _send(ref, block(core, level), z_send.at[way, level], z_recv.at[level], to)

    def gone(ref, way, level, to):
        _sent(ref, z_send.at[way, level], here)

    for i in range(4):
        level = order[i]
        ref = source if i == 0 else block(core, level)
        if i > 0:
            yield
            _expect(ref, z_recv.at[level], here)
        along(level, ref, go)
        if share:
            _send(ref, block(core, level), c_send.at[level], c_recv.at[level], (u ^ 1, z))
    yield
    if share:
        for i in range(4):
            _expect(block(1 - core, order[i]), c_recv.at[order[i]], here)
    yield
    for i in range(4):
        along(order[i], block(core, order[i]), gone)
        if share:
            _sent(block(core, order[i]), c_send.at[order[i]], here)
    own.wait()


def _plane_part(u, z, own, block, sems):
    p_send, p_recv, o_sem = sems
    here = (u, z)
    for way, bits in enumerate((FIRST, THEN)):
        for h in range(2):
            _send(own(h), block(h, u), p_send.at[h, way], p_recv.at[h, way], (u ^ bits[h], z))
    for h in range(2):
        pltpu.make_async_copy(own(h), block(h, u), o_sem.at[h]).start()
    for h in range(2):
        yield
        _expect(block(h, u ^ FIRST[h]), p_recv.at[h, 0], here)
        near = block(h, u ^ FIRST[h])
        _send(near, near, p_send.at[h, 2], p_recv.at[h, 2], (u ^ THEN[h], z))
    yield
    for h in range(2):
        _expect(block(h, u ^ THEN[h]), p_recv.at[h, 1], here)
        _expect(block(h, u ^ 6), p_recv.at[h, 2], here)
    yield
    for h in range(2):
        for k in range(3):
            _sent(block(h, u), p_send.at[h, k], here)
        pltpu.make_async_copy(own(h), block(h, u), o_sem.at[h]).wait()


def _plane_sum_part(u, z, source, work, bufs, sems, rows, then_do):
    p_buf, q_buf = bufs
    load, p_send, p_recv, q_send, q_recv = sems
    here = (u, z)
    for j in (1, 0):
        for h in range(2):
            bit = (THEN[h], 6)[j]
            _send(source(h, u ^ bit), p_buf.at[h, j], p_send.at[h, j], p_recv.at[h, j], (u ^ THEN[h], z))
    for h in range(2):
        for j, bit in enumerate((0, FIRST[h])):
            pltpu.make_async_copy(source(h, u ^ bit), work.at[h, j], load.at[h, j]).start()
    for h in range(2):
        yield
        for j, bit in enumerate((0, FIRST[h])):
            pltpu.make_async_copy(source(h, u ^ bit), work.at[h, j], load.at[h, j]).wait()
        _expect(p_buf.at[h, 1], p_recv.at[h, 1], here)
        _accumulate(work.at[h, 1], p_buf.at[h, 1], rows)
        _send(work.at[h, 1], q_buf.at[h], q_send.at[h], q_recv.at[h], (u ^ FIRST[h], z))
    yield
    for h in range(2):
        _expect(p_buf.at[h, 0], p_recv.at[h, 0], here)
        _accumulate(work.at[h, 0], p_buf.at[h, 0], rows)
    for h in range(2):
        _expect(q_buf.at[h], q_recv.at[h], here)
        _accumulate(work.at[h, 0], q_buf.at[h], rows)
    then_do()
    yield
    for h in range(2):
        for j in range(2):
            _sent(p_buf.at[h, j], p_send.at[h, j], here)
        _sent(q_buf.at[h], q_send.at[h], here)


def _line_sum_part(u, z, source, work, bufs, sems, rows, then_do):
    c_buf, z_buf = bufs
    load, c_send, c_recv, z_send, z_recv = sems
    here, core = (u, z), u % 2
    order = tuple(reversed(_line_order(z)))
    for i in range(4):
        _send(source(1 - core, order[i]), c_buf.at[i], c_send.at[i], c_recv.at[i], (u ^ 1, z))
        pltpu.make_async_copy(source(core, order[i]), work.at[i], load.at[i]).start()
    for i in range(4):
        yield
        pltpu.make_async_copy(source(core, order[i]), work.at[i], load.at[i]).wait()
        _expect(c_buf.at[i], c_recv.at[i], here)
        _accumulate(work.at[i], c_buf.at[i], rows)
        if i == 3:
            yield
        _line_end(u, z, order[i], i, work.at[i], z_buf, (z_send, z_recv), rows)
    then_do()
    yield
    for i in range(4):
        _sent(c_buf.at[i], c_send.at[i], here)
        if i < 3:
            _sent(work.at[i], z_send.at[i], here)


def _column_peers(u, z):
    return [((u ^ c, z ^ k), c, k) for c in range(2) for k in range(4) if c or k]


def _comm(kernel, outs, scratch, collective_id, specs, flops=0, moved=100_000_000):
    return pl.pallas_call(
        kernel,
        out_shape=outs,
        in_specs=specs[0],
        out_specs=specs[1],
        scratch_shapes=scratch,
        compiler_params=pltpu.CompilerParams(
            collective_id=collective_id, has_side_effects=True, vmem_limit_bytes=VMEM_BYTES
        ),
        cost_estimate=pl.CostEstimate(flops=flops, bytes_accessed=moved, transcendentals=0),
    )


ENTER_ORDER = (0, 2, 1, 0, 2, 1, 0, 2, 0, 2)
KV_ORDER = (2, 0, 1, 0, 0, 1, 2, 1, 0, 1)
PAIR_ORDER = (1, 0, 2, 1, 0, 0, 1, 2, 1, 0)
LEAVE_ORDER = (0, 1, 2, 1, 2, 1, 0, 0, 1, 0, 1, 1)
LINE_SEMS = [DMA((2, 4)), DMA((4,)), DMA((4,)), DMA((4,)), DMA]
PLANE_SEMS = [DMA((2, 3)), DMA((2, 3)), DMA((2,))]
PLANE_SUM_SEMS = [DMA((2, 2)), DMA((2, 2)), DMA((2, 2)), DMA((2,)), DMA((2,))]
LINE_SUM_SEMS = [DMA((4,)), DMA((4,)), DMA((4,)), DMA((4,)), DMA((2, 4))]


def _small_part(u, z, xs, outs, sems):
    own_sem, z_send, z_recv, u_send, u_recv = sems
    here = (u, z)
    for a, (x, o) in enumerate(zip(xs, outs)):
        pltpu.make_async_copy(x, o.at[u, z], own_sem.at[a]).start()
        for k in range(1, 4):
            _send(x, o.at[u, z], z_send.at[a, k], z_recv.at[a, k], (u, z ^ k))
    yield
    for a, (x, o) in enumerate(zip(xs, outs)):
        pltpu.make_async_copy(x, o.at[u, z], own_sem.at[a]).wait()
        for k in range(1, 4):
            _expect(o.at[u, z ^ k], z_recv.at[a, k], here)
        for k in range(1, 8):
            _send(o.at[u], o.at[u], u_send.at[a, k], u_recv.at[a, k], (u ^ k, z))
    yield
    yield
    for a, (x, o) in enumerate(zip(xs, outs)):
        for k in range(1, 4):
            _sent(x, z_send.at[a, k], here)
        for k in range(1, 8):
            _sent(o.at[u], u_send.at[a, k], here)
            _expect(o.at[u ^ k], u_recv.at[a, k], here)


def _small_sems(n):
    return [DMA((n,)), DMA((n, 4)), DMA((n, 4)), DMA((n, 8)), DMA((n, 8))]


def _packed(router, gains):
    lane = lax.broadcasted_iota(jnp.int32, (router.shape[0], 128 - EXPERTS), 1)
    tail = jnp.zeros(lane.shape, F32)
    for j in range(1, 4):
        tail = jnp.where(lane == j - 1, gains[:, j : j + 1], tail)
    return router, tail.astype(BF16)


def enter(hidden, weights, gains, router, routes, collective_id):
    T, D = hidden.shape
    R, C = weights[0].shape[0], weights[0].shape[1] // 8
    held = (2, 4, R, 3 * C)
    strip = 16

    def kernel(h_ref, wq_ref, wk_ref, wv_ref, gain_ref, router_ref, route_ref, x_out, w_out, p_out, r_out, *refs):
        x_ref, w_ref, pack_ref, w_buf, w_send, w_recv = refs[:6]
        sems = refs[6:]
        u, z = lax.axis_index("uly"), lax.axis_index("blk")
        here, core, chip = (u, z), u % 2, u // 2
        column = _column_peers(u, z)

        def weight_part():
            def cut(j, c, level):
                return w_ref.at[j, :, pl.ds(pl.multiple_of((2 * level + c) * C, C), C)]

            def slot(j, c, level):
                return w_buf.at[c, level, :, pl.ds(j * C, C)]

            for i, (to, c, k) in enumerate(column):
                for j in range(3):
                    _send(cut(j, core ^ c, z ^ k), slot(j, core, z), w_send.at[i, j], w_recv.at[i, j], to)
            for j in range(3):
                slot(j, core, z)[...] = cut(j, core, z)[...]
            yield
            for i, (to, c, k) in enumerate(column):
                for j in range(3):
                    _expect(slot(j, core ^ c, z ^ k), w_recv.at[i, j], here)
            yield from _plane_part(u, z, lambda h: w_buf.at[h], lambda h, v: w_out.at[v // 2, h], sems[:3])
            for i, (to, c, k) in enumerate(column):
                for j in range(3):
                    _sent(cut(j, core ^ c, z ^ k), w_send.at[i, j], here)

        def prepare():
            gains = gain_ref[...].astype(F32)
            for j, ref in enumerate((wq_ref, wk_ref, wv_ref)):
                w_ref[j] = (ref[...].astype(F32) * gains[:, :1]).astype(BF16)

            def norm(i, _):
                at = pl.ds(pl.multiple_of(i * strip, strip), strip)
                value = h_ref[at, :].astype(F32)
                x_ref[at, :] = (value * norm_scale(value)).astype(BF16)
                return 0

            lax.fori_loop(0, T // strip, norm, 0)
            pack_ref[:, pl.ds(0, EXPERTS)], pack_ref[:, pl.ds(EXPERTS, 128 - EXPERTS)] = _packed(router_ref[...], gains)

        _greet(u, z, range(1, 8), others=[to for to, c, k in column if k], meanwhile=prepare)
        _run(
            weight_part(),
            _small_part(u, z, (pack_ref, route_ref), (p_out, r_out), sems[8:]),
            _line_part(u, z, x_ref, lambda c, level: x_out.at[c, level], sems[3:8]),
            order=ENTER_ORDER,
        )

    outs = [
        jax.ShapeDtypeStruct((2, 4, T, D), BF16),
        jax.ShapeDtypeStruct((4,) + held, BF16),
        jax.ShapeDtypeStruct((8, 4, R, 128), BF16),
        jax.ShapeDtypeStruct((8, 4) + routes.shape, routes.dtype),
    ]
    scratch = [pltpu.VMEM((T, D), BF16), pltpu.VMEM((3, R, D), BF16), pltpu.VMEM((R, 128), BF16)]
    scratch += [pltpu.VMEM(held, BF16), DMA((7, 3)), DMA((7, 3))] + PLANE_SEMS + LINE_SEMS + _small_sems(2)
    specs = ([IN_VMEM] * 7, [ANY_SPACE] * 4)
    return _comm(kernel, outs, scratch, collective_id, specs)(hidden, *weights, gains, router, routes)


def _column_sum_part(u, z, x_ref, total, buf, sems, then_do):
    send, recv = sems
    here = (u, z)
    column = _column_peers(u, z)
    for i, (to, c, k) in enumerate(column):
        _send(x_ref, buf.at[i], send.at[i], recv.at[i], to)
    yield
    value = x_ref[...]
    for i in range(7):
        _expect(buf.at[i], recv.at[i], here)
        value = value + buf[i]
    total[...] = value
    then_do()
    yield
    for i in range(7):
        _sent(x_ref, send.at[i], here)


def plane_pair(first, second, rows, squares, collective_id):
    R = squares.shape[0] // 2

    def kernel(a_ref, b_ref, x_ref, s_ref, a_out, b_out, x_out, s_out, k_out, buf, *sems):
        u, z = lax.axis_index("uly"), lax.axis_index("blk")
        here, chip = (u, z), u // 2
        k_send, k_recv = sems[10:]
        _greet(u, z, (2, 4, 6), others=[to for to, c, k in _column_peers(u, z)])
        own, outs = (a_ref, b_ref), (a_out, b_out)
        keys = s_out.at[pl.ds(R, R)]

        def tell():
            k_out[chip] = keys[...]
            for i, bit in enumerate((2, 4, 6)):
                _send(keys, k_out.at[chip], k_send.at[i], k_recv.at[i], (u ^ bit, z))

        _run(
            _plane_part(u, z, lambda h: own[h], lambda h, v: outs[h].at[v // 2], sems[:3]),
            _line_part(u, z, x_ref, lambda c, level: x_out.at[level], sems[3:8], share=False),
            _column_sum_part(u, z, s_ref, s_out, buf, sems[8:10], tell),
            order=PAIR_ORDER,
        )
        for i, bit in enumerate((2, 4, 6)):
            _expect(k_out.at[(u ^ bit) // 2], k_recv.at[i], here)
            _sent(keys, k_send.at[i], here)

    outs = [jax.ShapeDtypeStruct((4,) + x.shape, x.dtype) for x in (first, second)]
    outs += [jax.ShapeDtypeStruct((4,) + rows.shape, rows.dtype)]
    outs += [jax.ShapeDtypeStruct(squares.shape, F32), jax.ShapeDtypeStruct((4, R, 128), F32)]
    specs = ([IN_VMEM] * 2 + [ANY_SPACE, IN_VMEM], [ANY_SPACE] * 3 + [IN_VMEM] * 2)
    scratch = [pltpu.VMEM((7,) + squares.shape, F32)] + PLANE_SEMS + LINE_SEMS + [DMA((7,)), DMA((7,)), DMA((3,)), DMA((3,))]
    return _comm(kernel, outs, scratch, collective_id, specs)(first, second, rows, squares)


def column_gather(rows, slot, out_rows, collective_id):
    T, D = rows.shape
    EL, _, slots, _ = out_rows.shape

    def kernel(r_ref, slot_ref, rows_ref, r_out, x_out, *refs):
        u, z = lax.axis_index("uly"), lax.axis_index("blk")
        _greet(u, z, (1, 2, 4), line=True)
        order = _line_order(z)

        def keep(i, part):
            x_out[order[i]] = part[...]

        _run(
            _line_part(u, z, r_ref, lambda c, level: r_out.at[c, level], refs[-5:]),
            _spread_part(u, z, slot_ref, rows_ref, None, order, refs[:-5], keep),
        )

    outs = [jax.ShapeDtypeStruct((2, 4, T, D), BF16), jax.ShapeDtypeStruct((4, T, D), BF16)]
    specs = ([IN_VMEM, IN_VMEM, ANY_SPACE], [ANY_SPACE, IN_VMEM])
    scratch = _spread_scratch(T, D, (EL, slots, D)) + LINE_SEMS
    return _comm(kernel, outs, scratch, collective_id, specs)(rows, slot, out_rows)


def _line_sum_scratch(T, D):
    return [pltpu.VMEM((4, T, D), BF16), pltpu.VMEM((4, T, D), BF16), pltpu.VMEM((2, 4, T, D), BF16)]


def column_scatter(x, collective_id):
    T, D = x.shape[2:]

    def kernel(x_ref, o_ref, work, c_buf, z_buf, *sems):
        u, z = lax.axis_index("uly"), lax.axis_index("blk")
        _greet(u, z, (1,), line=True)

        def finish():
            o_ref[...] = work[3]

        _run(_line_sum_part(u, z, lambda c, level: x_ref.at[c, level], work, (c_buf, z_buf), sems, T, finish))

    scratch = _line_sum_scratch(T, D) + LINE_SUM_SEMS
    return _comm(kernel, jax.ShapeDtypeStruct((T, D), BF16), scratch, collective_id, ([ANY_SPACE], IN_VMEM))(x)


def _plane_sum_scratch(rows, cols):
    return [pltpu.VMEM((2, 2, rows, cols), BF16), pltpu.VMEM((2, 2, rows, cols), BF16), pltpu.VMEM((2, rows, cols), BF16)]


def key_value_sums(dk, dv, x, inner, collective_id):
    T, D = x.shape[1:]
    L, C = dk.shape[1:]
    R = inner.shape[0] // 5

    def kernel(
        k_ref, v_ref, x_ref, s_ref, k_out, v_out, x_out, s_out, work, p_buf, q_buf, x_work, z_buf, buf, total, k_buf, *sems
    ):
        u, z = lax.axis_index("uly"), lax.axis_index("blk")
        here, chip = (u, z), u // 2
        _greet(u, z, (2, 4, 6), others=[to for to, c, k in _column_peers(u, z)])
        load, z_send, z_recv, k_send, k_recv = sems[7:]
        order = tuple(reversed(_line_order(z)))

        def keys(v):
            return total.at[pl.ds(pl.multiple_of((v // 2 + 1) * R, R), R)]

        def tell():
            for i, bit in enumerate((2, 4, 6)):
                _send(keys(u ^ bit), k_buf.at[i], k_send.at[i], k_recv.at[i], (u ^ bit, z))

        def finish():
            k_out[...] = work[0, 0]
            v_out[...] = work[1, 0]

        def line():
            copies = [pltpu.make_async_copy(x_ref.at[order[i]], x_work.at[i], load.at[i]) for i in range(4)]
            for copy in copies:
                copy.start()
            for copy in copies:
                copy.wait()
            for i in range(4):
                _line_end(u, z, order[i], i, x_work.at[i], z_buf, (z_send, z_recv), T)
                yield
            x_out[...] = x_work[3]
            for i in range(3):
                _sent(x_work.at[i], z_send.at[i], (u, z))

        _run(
            _plane_sum_part(
                u, z, lambda h, v: (k_ref, v_ref)[h].at[v // 2], work, (p_buf, q_buf), sems[:5], L, finish
            ),
            line(),
            _column_sum_part(u, z, s_ref, total, buf, sems[5:7], tell),
            order=KV_ORDER,
        )
        value = keys(u)[...]
        for i, bit in enumerate((2, 4, 6)):
            _expect(k_buf.at[i], k_recv.at[i], here)
            value = value + k_buf[i]
            _sent(k_buf.at[i], k_send.at[i], here)
        s_out[pl.ds(0, R), :] = total[pl.ds(0, R), :]
        s_out[pl.ds(R, R), :] = value

    outs = [jax.ShapeDtypeStruct((L, C), BF16)] * 2 + [jax.ShapeDtypeStruct((T, D), BF16)]
    outs += [jax.ShapeDtypeStruct((2 * R, 128), F32)]
    scratch = _plane_sum_scratch(L, C) + [pltpu.VMEM((4, T, D), BF16), pltpu.VMEM((2, 4, T, D), BF16)]
    scratch += [pltpu.VMEM((7,) + inner.shape, F32), pltpu.VMEM(inner.shape, F32), pltpu.VMEM((3, R, 128), F32)]
    scratch += PLANE_SUM_SEMS + [DMA((7,)), DMA((7,)), DMA((4,)), DMA((4,)), DMA((2, 4)), DMA((3,)), DMA((3,))]
    specs = ([ANY_SPACE] * 3 + [IN_VMEM], [IN_VMEM] * 4)
    return _comm(kernel, outs, scratch, collective_id, specs)(dk, dv, x, inner)


def leave(x, weights, smalls, collective_id):
    n = len(smalls)
    T, D = x.shape[2:]
    rows, W = weights.shape[2:]
    R, C = rows // 4, W // 3

    def kernel(x_ref, w_ref, *refs):
        small_in, (o_ref, w_out), small_out = refs[:n], refs[n : n + 2], refs[n + 2 : 2 * n + 2]
        work, c_buf, z_buf, w_work, wp_buf, wq_buf = refs[2 * n + 2 : 2 * n + 8]
        sems = refs[2 * n + 8 :]
        u, z = lax.axis_index("uly"), lax.axis_index("blk")
        here, core, chip = (u, z), u % 2, u // 2
        column = _column_peers(u, z)
        _greet(u, z, range(1, 8), others=[to for to, c, k in column if k])
        t_send, t_recv = sems[10:12]
        group = 2 * z + core

        def finish():
            o_ref[...] = work[3]

        def cut(j, c, level):
            return w_work.at[c, 0, pl.ds(pl.multiple_of(level * R, R), R), pl.ds(j * C, C)]

        def slot(j, g):
            return w_out.at[j, :, pl.ds(pl.multiple_of(g * C, C), C)]

        def deal():
            for i, (to, c, k) in enumerate(column):
                for j in range(3):
                    _send(cut(j, core ^ c, z ^ k), slot(j, group), t_send.at[i, j], t_recv.at[i, j], to)
            for j in range(3):
                slot(j, group)[...] = cut(j, core, z)[...]

        _run(
            _plane_sum_part(u, z, lambda h, v: w_ref.at[v // 2, h], w_work, (wp_buf, wq_buf), sems[5:10], rows, deal),
            _line_sum_part(u, z, lambda c, level: x_ref.at[c, level], work, (c_buf, z_buf), sems[:5], T, finish),
            _small_part(u, z, small_in, small_out, sems[12:]),
            order=LEAVE_ORDER,
        )
        for i, (to, c, k) in enumerate(column):
            for j in range(3):
                _expect(slot(j, 2 * (z ^ k) + (core ^ c)), t_recv.at[i, j], here)
                _sent(cut(j, core ^ c, z ^ k), t_send.at[i, j], here)

    outs = [jax.ShapeDtypeStruct((T, D), BF16), jax.ShapeDtypeStruct((3, R, 8 * C), BF16)]
    outs += [jax.ShapeDtypeStruct((8, 4) + x.shape, x.dtype) for x in smalls]
    scratch = _line_sum_scratch(T, D) + _plane_sum_scratch(rows, W) + LINE_SUM_SEMS + PLANE_SUM_SEMS
    scratch += [DMA((7, 3)), DMA((7, 3))] + _small_sems(n)
    specs = ([ANY_SPACE] * 2 + [IN_VMEM] * n, [IN_VMEM] * 2 + [ANY_SPACE] * n)
    return _comm(kernel, outs, scratch, collective_id, specs)(x, weights, *smalls)


def _finish_kernel(
    h_ref, r_ref, rg_ref, first_ref, sum_ref, wq_ref, wk_ref, wv_ref, dw_ref, do_ref, gain_ref, out_ref, hg_ref, ag_ref, *dws
):
    out_ref[...] = (r_ref[...] + sum_ref[...].astype(F32)).astype(BF16)
    hidden, weighted = h_ref[...].astype(F32), first_ref[...].astype(F32)
    scale = norm_scale(hidden)
    mean = jnp.mean(weighted * hidden, axis=-1, keepdims=True)
    hg_ref[...] = rg_ref[...] + scale * weighted - hidden * (scale * scale * scale) * mean
    gain = gain_ref[...].astype(F32)[:, :1]
    total = jnp.zeros(dws[0].shape, F32)
    for j, ref in enumerate((wq_ref, wk_ref, wv_ref)):
        grad = dw_ref[j].astype(F32)
        total = total + grad * ref[...].astype(F32)
        dws[j][...] = grad * gain
    ag_ref[...] = jnp.sum(total, axis=1, keepdims=True)
    dws[3][...] = do_ref[...].astype(F32)


def finish(hidden, residual, residual_grad, first_weighted, out_sum, weights, weight_sum, out_weight_grad, gains):
    T, D = hidden.shape
    R = gains.shape[0]
    steps = 4 if R % 64 == 0 else 1

    def rows(count, width):
        return pl.BlockSpec((count // steps, width), lambda i: (i, 0))

    tokens, dense = rows(T, D), rows(R, D)
    return pl.pallas_call(
        _finish_kernel,
        out_shape=[
            jax.ShapeDtypeStruct((T, D), BF16),
            jax.ShapeDtypeStruct((T, D), F32),
            jax.ShapeDtypeStruct((R, 1), F32),
        ]
        + [jax.ShapeDtypeStruct((R, D), F32)] * 4,
        grid=(steps,),
        in_specs=[tokens] * 5
        + [dense] * 3
        + [pl.BlockSpec((3, R // steps, D), lambda i: (0, i, 0)), dense, rows(R, 4)],
        out_specs=[tokens, tokens, rows(R, 1)] + [dense] * 4,
        compiler_params=pltpu.CompilerParams(vmem_limit_bytes=VMEM_BYTES),
        cost_estimate=pl.CostEstimate(flops=20 * T * D, bytes_accessed=24 * T * D, transcendentals=0),
    )(hidden, residual, residual_grad, first_weighted, out_sum, *weights, weight_sum, out_weight_grad, gains)


class _Jobs:
    def __init__(self, load, compute):
        self.load, self.compute = load, compute
        self.queue, self.count, self.ready = [], 0, None

    def add(self, *jobs):
        self.queue += jobs

    def _next(self):
        if not self.queue:
            return None
        job = (self.count, self.queue.pop(0))
        self.count += 1
        self.load(*job, True)
        return job

    def run(self, number=1):
        for _ in range(number):
            now = self.ready or self._next()
            if now is None:
                return
            self.ready = self._next()
            self.load(*now, False)
            self.compute(*now)


def _gather_pick_kernel(
    x_ref, g0, g1, g2, g3, slot_ref, router_ref, o_ref, xr_ref, gr_ref, gate_ref, other_g, pick, in_buf, out_buf, in_sem, out_sem, *sems, width
):
    own_sem, z_send, z_recv, p_send, p_recv, c_send, c_recv, g_send, g_recv = sems
    own_g = (g0, g1, g2, g3)
    u, z = lax.axis_index("uly"), lax.axis_index("blk")
    core, chip = u % 2, u // 2
    other = 1 - core
    T, D = x_ref.shape
    experts, group = slot_ref.shape[1:]
    slots = out_buf.shape[2]
    half = T // 2
    halves = (pl.ds(0, half), pl.ds(half, half))
    here = (u, z)
    _greet(u, z, (1, 2, 4), line=True)
    own = pltpu.make_async_copy(x_ref, o_ref.at[u * DEPTH + z], own_sem)
    own.start()
    order = _line_order(z)

    def block(who, level):
        return o_ref.at[who * DEPTH + level]

    def part(who, level, h):
        return o_ref.at[who * DEPTH + level, halves[h]]

    def load(n, job, start):
        source, level, which = job
        steps = (0, jnp.where(which == 0, 1, 2), jnp.where(which == 0, 2, 1), 3)
        for k in range(4):
            p = chip ^ steps[k]
            if source == "x":
                ref = o_ref.at[(2 * p + which) * DEPTH + level]
            else:
                ref = (own_g[k] if which is core else other_g.at[k]).at[level]
            rows = pl.ds(pl.multiple_of(p * T, T), T)
            copy = pltpu.make_async_copy(ref, in_buf.at[n % 2, rows], in_sem.at[n % 2, k])
            copy.start() if start else copy.wait()

    def out_copy(n, target, at):
        return pltpu.make_async_copy(out_buf.at[n % 2], target.at[:, at], out_sem.at[n % 2])

    sent = {}

    def compute(n, job):
        source, level, which = job
        at = 2 * level + which
        rows_in, rows_out = in_buf.at[n % 2], out_buf.at[n % 2]
        row = lax.broadcasted_iota(jnp.int32, (slots, group), 0)
        if source == "g":
            picks = [jnp.where(slot_ref[at, e : e + 1, :] == row, 1.0, 0.0).astype(BF16) for e in range(experts)]
            pick[at] = jnp.concatenate(picks, axis=0)
        else:
            logits = dot(rows_in[...], router_ref[...])
            powers = jnp.exp(logits - jnp.max(logits, axis=1, keepdims=True))
            chances = powers / jnp.sum(powers, axis=1, keepdims=True)
            high = chances.astype(BF16)
            low = (chances - high.astype(F32)).astype(BF16)
            gates = dot(pick[at], jnp.concatenate([high, low], axis=1))
            lane = lax.broadcasted_iota(jnp.int32, (slots, 2 * EXPERTS), 1)
            for e in range(experts):
                part = gates[e * slots : (e + 1) * slots]
                part = jnp.where((lane == e) | (lane == EXPERTS + e), part, 0.0)
                gate_ref[e, at] = jnp.broadcast_to(jnp.sum(part, axis=1, keepdims=True), (slots, 128))
        if n >= 2:
            sent.pop(n - 2).wait()

        def step(i, _):
            cols = pl.ds(pl.multiple_of(i * width, width), width)
            rows = dot(pick[at], rows_in[:, cols]).astype(BF16)
            for e in range(experts):
                rows_out[e, :, cols] = rows[e * slots : (e + 1) * slots]
            return 0

        lax.fori_loop(0, D // width, step, 0)
        sent[n] = out_copy(n, gr_ref if source == "g" else xr_ref, at)
        sent[n].start()

    jobs = _Jobs(load, compute)
    jobs.add(*[("g", level, core) for level in range(4)])

    def along(level, source, step):
        @pl.when((z > 0) & (level >= z))
        def _():
            step(source, 0, level, (u, z - 1))

        @pl.when((z < DEPTH - 1) & (level <= z))
        def _():
            step(source, 1, level, (u, z + 1))

    def go(source, way, level, to):
        _send(source, block(u, level), z_send.at[way, level], z_recv.at[level], to)

    def gone(source, way, level, to):
        _sent(source, z_send.at[way, level], here)

    sources = [x_ref] + [block(u, order[i]) for i in range(1, 4)]

    def arrive(i):
        level = order[i]
        if i:
            _expect(block(u, level), z_recv.at[level], here)
        along(level, sources[i], go)
        for way, bits in enumerate((FIRST, THEN)):
            for h in range(2):
                cut = sources[i].at[halves[h]]
                _send(cut, part(u, level, h), p_send.at[level, h, way], p_recv.at[level, h, way], (u ^ bits[h], z))
        _send(sources[i], block(u, level), c_send.at[level, 0], c_recv.at[level, 0], (u ^ 1, z))

    def onward(i):
        level = order[i]
        for h in range(2):
            near = part(u ^ FIRST[h], level, h)
            _expect(near, p_recv.at[level, h, 0], here)
            _send(near, near, p_send.at[level, h, 2], p_recv.at[level, h, 2], (u ^ THEN[h], z))

    def share(i):
        level = order[i]
        for h in range(2):
            _expect(part(u ^ THEN[h], level, h), p_recv.at[level, h, 1], here)
            _expect(part(u ^ 6, level, h), p_recv.at[level, h, 2], here)
        for k, bit in enumerate((2, 4, 6)):
            ref = block(u ^ bit, level)
            _send(ref, ref, c_send.at[level, k + 1], c_recv.at[level, k + 1], (u ^ 1, z))
        jobs.add(("x", level, core))

    def received(i):
        level = order[i]
        for k, bit in enumerate((0, 2, 4, 6)):
            _expect(block(u ^ 1 ^ bit, level), c_recv.at[level, k], here)
        jobs.add(("x", level, other))

    arrive(0)
    for k in range(4):
        _send(own_g[k], other_g.at[k], g_send.at[k], g_recv.at[k], (u ^ 1, z))
    jobs.run(2)
    onward(0)
    jobs.run(1)
    arrive(1)
    for k in range(4):
        _expect(other_g.at[k], g_recv.at[k], here)
    jobs.add(*[("g", level, other) for level in range(4)])
    jobs.run(2)
    own.wait()
    share(0)
    jobs.run(2)
    onward(1)
    arrive(2)
    received(0)
    jobs.run(2)
    arrive(3)
    share(1)
    received(1)
    jobs.run(1)
    onward(2)
    jobs.run(2)
    share(2)
    received(2)
    jobs.run(1)
    onward(3)
    jobs.run(2)
    share(3)
    received(3)
    jobs.run(16)
    for i in range(4):
        level = order[i]
        along(level, sources[i], gone)
        for h in range(2):
            for k in range(3):
                _sent(part(u, level, h), p_send.at[level, h, k], here)
        for k in range(4):
            _sent(block(u, level), c_send.at[level, k], here)
    for k in range(4):
        _sent(other_g.at[k], g_send.at[k], here)
    for copy in sent.values():
        copy.wait()


def gather_pick(x, g, slot, router, slots, collective_id):
    T, D = x.shape
    groups, EL, group = slot.shape
    picked = jax.ShapeDtypeStruct((EL, groups, slots, D), BF16)
    outs = [
        jax.ShapeDtypeStruct((32, T, D), BF16),
        picked,
        picked,
        jax.ShapeDtypeStruct((EL, groups, slots, 128), F32),
        jax.ShapeDtypeStruct((4, 4, T, D), BF16),
    ]
    scratch = [
        pltpu.VMEM((groups, EL * slots, group), BF16),
        pltpu.VMEM((2, group, D), BF16),
        pltpu.VMEM((2, EL, slots, D), BF16),
        DMA((2, 4)),
        DMA((2,)),
        DMA,
        DMA((2, 4)),
        DMA((4,)),
        DMA((4, 2, 3)),
        DMA((4, 2, 3)),
        DMA((4, 4)),
        DMA((4, 4)),
        DMA((4,)),
        DMA((4,)),
    ]
    specs = ([IN_VMEM] + [ANY_SPACE] * 4 + [IN_VMEM] * 2, [ANY_SPACE] * 3 + [IN_VMEM, ANY_SPACE])
    kernel = functools.partial(_gather_pick_kernel, width=PICK_WIDTH)
    out, xr, gr, gates, _ = _comm(kernel, outs, scratch, collective_id, specs)(x, *g, slot, router)
    return out.reshape(32 * T, D), xr, gr, gates


def _tree_sum_steps(u, z, own, bufs, sems, T):
    c_buf, p_buf, q_buf = bufs
    c_send, c_recv, p_send, p_recv, q_send, q_recv = sems
    here = (u, z)
    half = T // 2
    halves = (pl.ds(0, half), pl.ds(half, half))

    def to_sibling(i, k, ref):
        _send(ref, c_buf.at[i, k], c_send.at[i, k], c_recv.at[i, k], (u ^ 1, z))

    def add_core(i):
        for k in (3, 2, 1, 0):
            _expect(c_buf.at[i, k], c_recv.at[i, k], here)
            _accumulate(own(i, k), c_buf.at[i, k], T)
            for h in range(2):
                if k and (k == 3 or CHIPS[k] == THEN[h]):
                    j = 1 if k == 3 else 0
                    part = own(i, k).at[halves[h]]
                    _send(part, p_buf.at[i, h, j], p_send.at[i, h, j], p_recv.at[i, h, j], (u ^ THEN[h], z))

    def add_far(i):
        for h in range(2):
            part = own(i, CHIPS.index(FIRST[h])).at[halves[h]]
            _expect(p_buf.at[i, h, 1], p_recv.at[i, h, 1], here)
            _accumulate(part, p_buf.at[i, h, 1], half)
            _send(part, q_buf.at[i, h], q_send.at[i, h], q_recv.at[i, h], (u ^ FIRST[h], z))

    def add_near(i):
        for h in range(2):
            _expect(p_buf.at[i, h, 0], p_recv.at[i, h, 0], here)
            _accumulate(own(i, 0).at[halves[h]], p_buf.at[i, h, 0], half)

    def add_then(i):
        for h in range(2):
            _expect(q_buf.at[i, h], q_recv.at[i, h], here)
            _accumulate(own(i, 0).at[halves[h]], q_buf.at[i, h], half)

    def finish():
        for i in range(4):
            for k in range(4):
                _sent(c_buf.at[i, k], c_send.at[i, k], here)
            for h in range(2):
                for j in range(2):
                    _sent(p_buf.at[i, h, j], p_send.at[i, h, j], here)
                _sent(q_buf.at[i, h], q_send.at[i, h], here)

    return to_sibling, add_core, add_far, add_near, add_then, finish


def _line_end(u, z, level, i, part, z_buf, sems, rows):
    z_send, z_recv = sems
    here = (u, z)

    @pl.when((level >= z) & (z > 0))
    def _():
        _expect(z_buf.at[0, level], z_recv.at[0, level], here)
        _accumulate(part, z_buf.at[0, level], rows)

    @pl.when((level <= z) & (z < DEPTH - 1))
    def _():
        _expect(z_buf.at[1, level], z_recv.at[1, level], here)
        _accumulate(part, z_buf.at[1, level], rows)

    if i < 3:

        @pl.when(level > z)
        def _():
            _send(part, z_buf.at[0, level], z_send.at[i], z_recv.at[0, level], (u, z + 1))

        @pl.when(level < z)
        def _():
            _send(part, z_buf.at[1, level], z_send.at[i], z_recv.at[1, level], (u, z - 1))


def _spread_part(u, z, slot_ref, source, gg_ref, order, refs, level_done, later=lambda i: None):
    work, c_buf, p_buf, q_buf, side, in_buf, in_sem = refs[:7]
    core, chip = u % 2, u // 2
    other = 1 - core
    _, group, experts = slot_ref.shape
    slots, D = source.shape[2:]
    total = experts * slots
    T = group // 4

    def place(k):
        return pl.ds(pl.multiple_of((chip ^ (CHIPS[k] // 2)) * T, T), T)

    def own(i, k):
        return work.at[i, place(k)]

    to_sibling, add_core, add_far, add_near, add_then, finish = _tree_sum_steps(
        u, z, own, (c_buf, p_buf, q_buf), refs[7:], T
    )
    lane = lax.broadcasted_iota(jnp.int32, (experts, total), 1)
    which = lax.broadcasted_iota(jnp.int32, (experts, total), 0)
    choose = jnp.where((lane >= which * slots) & (lane < (which + 1) * slots), 1.0, 0.0).astype(BF16)
    offset = lane[:1] - jnp.sum(jnp.where(lane >= (which + 1) * slots, slots, 0), axis=0, keepdims=True)
    offset = offset.astype(F32)
    column = lax.broadcasted_iota(jnp.int32, (slots, 128), 1)

    def load(n, job, start):
        i, c = job
        copy = pltpu.make_async_copy(source.at[:, 2 * order[i] + c], in_buf.at[n % 2], in_sem.at[n % 2])
        copy.start() if start else copy.wait()

    def compute(n, job):
        i, c = job
        at = 2 * order[i] + c
        mine = dot(slot_ref[at].astype(BF16), choose)
        pick = jnp.where(mine == offset, 1.0, 0.0).astype(BF16)
        rows_in = in_buf.at[n % 2]
        target = work.at[i] if c is core else side.at[i]
        if gg_ref is not None:
            grads = [jnp.where(column == u * experts + e, gg_ref[e, at], 0.0).astype(BF16) for e in range(experts)]
            target[:, pl.ds(D, 128)] = dot(pick, jnp.concatenate(grads, axis=0)).astype(BF16)

        def step(j, _):
            cols = pl.ds(pl.multiple_of(j * SPREAD_WIDTH, SPREAD_WIDTH), SPREAD_WIDTH)
            rows = jnp.concatenate([rows_in[e, :, cols] for e in range(experts)], axis=0)
            target[:, cols] = dot(pick, rows).astype(BF16)
            return 0

        lax.fori_loop(0, D // SPREAD_WIDTH, step, 0)
        if c is not core:
            for k in (3, 2, 1, 0):
                to_sibling(i, k, side.at[i, place(k)])

    def end(i):
        add_then(i)
        level_done(i, own(i, 0))

    jobs = _Jobs(load, compute)
    for i in range(4):
        jobs.add((i, other), (i, core))
    jobs.run(2)
    add_core(0)
    yield
    jobs.run(2)
    add_far(0)
    add_core(1)
    yield
    add_near(0)
    jobs.run(2)
    add_far(1)
    add_core(2)
    yield
    end(0)
    later(0)
    add_near(1)
    jobs.run(2)
    add_far(2)
    add_core(3)
    yield
    end(1)
    later(1)
    add_near(2)
    add_far(3)
    yield
    end(2)
    later(2)
    add_near(3)
    yield
    end(3)
    later(3)
    yield
    finish()


def _spread_scratch(T, W, rows_shape):
    half = T // 2
    return [
        pltpu.VMEM((4, 4 * T, W), BF16),
        pltpu.VMEM((4, 4, T, W), BF16),
        pltpu.VMEM((4, 2, 2, half, W), BF16),
        pltpu.VMEM((4, 2, half, W), BF16),
        pltpu.VMEM((4, 4 * T, W), BF16),
        pltpu.VMEM((2,) + rows_shape, BF16),
        DMA((2,)),
        DMA((4, 4)),
        DMA((4, 4)),
        DMA((4, 2, 2)),
        DMA((4, 2, 2)),
        DMA((4, 2)),
        DMA((4, 2)),
    ]


def spread_scatter(slot, gate_grads, entry_rows, collective_id):
    groups, group, EL = slot.shape
    slots, D = entry_rows.shape[2:]
    T, W = group // 4, D + 128

    def kernel(slot_ref, gg_ref, entry_ref, o_ref, z_buf, z_send, z_recv, *refs):
        u, z = lax.axis_index("uly"), lax.axis_index("blk")
        order = tuple(reversed(_line_order(z)))
        parts = []

        def done(i, part):
            parts.append(part)

        def line(i):
            _line_end(u, z, order[i], i, parts[i], z_buf, (z_send, z_recv), T)

        _greet(u, z, (1, 2, 4), line=True)
        _run(_spread_part(u, z, slot_ref, entry_ref, gg_ref, order, refs, done, line))
        o_ref[...] = parts[3][...]
        for i in range(3):
            _sent(parts[i], z_send.at[i], (u, z))

    scratch = [pltpu.VMEM((2, 4, T, W), BF16), DMA((4,)), DMA((2, 4))] + _spread_scratch(T, W, (EL, slots, D))
    specs = ([IN_VMEM, IN_VMEM, ANY_SPACE], IN_VMEM)
    out = jax.ShapeDtypeStruct((T, W), BF16)
    return _comm(kernel, out, scratch, collective_id, specs)(slot, gate_grads, entry_rows)


def slots_of(chosen):
    count = chosen.shape[-1]
    before = (jnp.arange(count)[:, None] < jnp.arange(count)[None, :]).astype(BF16)
    earlier = jnp.einsum("abs,st->abt", chosen.astype(BF16), before, preferred_element_type=F32)
    return jnp.where(chosen, earlier.astype(jnp.int32), -1)


class Slice:
    def __init__(self, U, Z, T, D):
        self.U, self.Z, self.T, self.D = U, Z, T, D
        self.u, self.z = lax.axis_index("uly"), lax.axis_index("blk")
        self.C = D // 8
        self.L = 8 * T
        self.group = 2 * self.z + self.u % 2
        self.first_block, self.block_step = 8 * (self.u // 2), 1
        self.rows = ATTEND_ROWS

    def enter(self, hidden, weights, gains, out_weight, router, routes):
        rows, weights, packs, routes = enter(hidden, weights, gains, router, routes, 1)
        there = [((2 * ((z + u // 2) % 4) + u % 2), u // 2) for u in range(8) for z in range(4)]
        self.forth = [(i, 4 * u + z) for i, (u, z) in enumerate(there)]
        rows, mine = lax.optimization_barrier((rows, self.permute(out_weight, self.forth)))
        self.out_parts = [mine] + [self.permute(mine, self.across(bit)) for bit in (2, 4, 6)]
        self.parts = [((self.u // 2) ^ k) - self.z + 4 for k in range(4)]
        self.parts = [p % 4 for p in self.parts]
        return (
            rows.reshape(self.L, self.D),
            weights.reshape(self.D, 3 * self.C),
            packs.reshape(self.D, -1),
            routes,
        )

    def permute(self, x, pairs):
        return lax.ppermute(x, ALL, pairs)

    def across(self, bit):
        return [(i, i ^ (4 * bit)) for i in range(32)]

    def sequence(self, key, value, squares, upstream):
        keys, values, own, stats, k_stat = plane_pair(key, value, upstream, squares.reshape(-1, 128), 4)
        own, *self.out_parts = lax.optimization_barrier((own, *self.out_parts))
        first = [(i, i ^ (8 if i // 4 % 2 == 0 else 16)) for i in range(32)]
        self.then = [(i, i ^ (16 if i // 4 % 2 == 0 else 8)) for i in range(32)]
        self.upstream = (own, self.permute(own, first))
        return keys.reshape(-1, self.C), values.reshape(-1, self.C), stats.reshape(2, -1, 128), k_stat.reshape(-1, 128)

    def heads_to_rows(self, x):
        x, own, near = lax.optimization_barrier((x, *self.upstream))
        self.upstream = (own, near, self.permute(own, self.then), self.permute(near, self.then))
        return column_scatter(x.reshape(2, 4, self.T, self.D), 5)

    def experts(self, second_low, routes, weights, router):
        EL, T, D = weights.shape[0], self.T, self.D
        slots = -(-4 * CAP // 16) * 16
        chosen = jnp.any(routes[None] == (self.u * EL + jnp.arange(EL, dtype=jnp.int32))[:, None, None, None, None], axis=3)
        chosen = chosen.reshape(EL, 4, 2, 4, T).transpose(3, 2, 0, 1, 4).reshape(8, EL, 4 * T)
        slot = slots_of(chosen)
        second_all, xr, gr, gates = gather_pick(second_low, self.upstream, slot, router, slots, 7)
        flat, cut = (EL, 8 * slots, -1), (EL, 8, slots, -1)
        out_rows, entry_rows, self.expert_grads, gate_grads = run_experts(
            xr.reshape(flat), gr.reshape(flat), gates.reshape(flat), weights, 8 * slots
        )
        self.slot, self.out_rows = slot.transpose(0, 2, 1), out_rows.reshape(cut)
        return second_all, spread_scatter(self.slot, gate_grads.reshape(cut), entry_rows.reshape(cut), 8)

    def rows_to_heads(self, x):
        rows, self.out_line = column_gather(x, self.slot, self.out_rows, 6)
        return rows.reshape(self.L, self.D), self.expert_grads

    def sequence_sums(self, dk, dv, out_part, q_inner, k_inner):
        cut = (4, self.L, self.C)
        inner = jnp.concatenate([q_inner, k_inner.reshape(-1, 128)], axis=0)
        dk, dv, out_sum, inner = key_value_sums(dk.reshape(cut), dv.reshape(cut), self.out_line, inner, 10)
        parts = out_part.reshape(4, -1, self.D)
        mine, *others = [lax.dynamic_index_in_dim(parts, p, 0, False) for p in self.parts]
        dk, *others = lax.optimization_barrier((dk, *others))
        self.out_terms = [mine] + [self.permute(x, self.across(bit)) for x, bit in zip(others, (2, 4, 6))]
        return dk, dv, out_sum, inner.reshape(2, -1, 128)

    def leave(self, first_part, weight_part, logit_grad, ffn_part, head_parts):
        T, R = self.T, self.D // 32
        first_part, *terms = lax.optimization_barrier((first_part, *self.out_terms))
        out_grad = sum(x.astype(F32) for x in terms).astype(BF16)
        out_grad = self.permute(out_grad, [(b, a) for a, b in self.forth])
        thin = jnp.concatenate([ffn_part.reshape(-1, 128), head_parts.reshape(-1, 128)], axis=0)
        wide = self.D // 128
        used = thin.shape[0]
        thin = jnp.pad(thin, ((0, -used % 8), (0, 0)))
        first, weights, logit_all, thin = leave(
            first_part.reshape(2, 4, T, self.D),
            weight_part.reshape(4, 2, 4 * R, 3 * self.C),
            [logit_grad.reshape(T // 2, 2 * EXPERTS), thin],
            11,
        )
        ffn = lax.dynamic_slice_in_dim(
            jnp.sum(thin[:, :, :wide], axis=(0, 1)).reshape(self.D), (self.u * 4 + self.z) * R, R, 0
        )
        mine = lax.dynamic_index_in_dim(thin.reshape(4, 2, 4, -1, 128), self.u % 2, 1, False)
        mine = lax.dynamic_index_in_dim(mine, self.u // 2, 1, False)
        heads = jnp.sum(mine[:, wide:used], axis=0).reshape(2, self.C)
        heads = lax.dynamic_slice_in_dim(heads, self.z * R, R, 1)
        return first, weights, out_grad, logit_all.reshape(32 * T, EXPERTS), ffn, heads


class General:
    def __init__(self, U, Z, T, D):
        self.U, self.Z, self.T, self.D = U, Z, T, D
        self.u, self.z = lax.axis_index("uly"), lax.axis_index("blk")
        self.C = D // U
        self.L = U * T
        self.group = self.u
        self.parts = range(4)
        self.first_block, self.block_step = self.z, Z
        self.rows = T

    def gather(self, x):
        return lax.all_gather(x, ALL, axis=0, tiled=True)

    def scatter_wide(self, x):
        return lax.psum_scatter(x, ALL, scatter_dimension=0, tiled=True)

    def enter(self, hidden, weights, gains, out_weight, router, routes):
        U, R = self.U, router.shape[0]
        gains, hidden = gains.astype(F32), hidden.astype(F32)
        scaled = jnp.stack([(w.astype(F32) * gains[:, :1]).astype(BF16) for w in weights])
        pack = jnp.concatenate(_packed(router, gains), axis=1)
        rows = (hidden * norm_scale(hidden)).astype(BF16)
        self.out_parts = jnp.split(lax.all_gather(out_weight, "blk", axis=0, tiled=True), 4)
        swapped = lax.all_to_all(scaled.transpose(1, 0, 2).reshape(R, 3, U, self.C), "uly", split_axis=2, concat_axis=0, tiled=True)
        weights = lax.all_gather(swapped.reshape(U, R, 3 * self.C), "blk", axis=1, tiled=True)
        return (
            self.rows_all(rows),
            weights.reshape(self.D, 3 * self.C),
            self.gather(pack),
            self.gather(routes[None]).reshape((U, self.Z) + routes.shape),
        )

    def sequence(self, key, value, squares, upstream):
        self.upstream = upstream
        pair = jnp.stack([key, value]).reshape(2, self.U, self.T, self.C)
        pair = lax.all_gather(pair, "blk", axis=2, tiled=False).reshape(2, -1, self.C)
        stats = lax.psum(squares, "uly")
        k_stat = lax.all_gather(stats[1].reshape(self.U, -1, 128), "blk", axis=1, tiled=False).reshape(-1, 128)
        return pair[0], pair[1], stats, k_stat

    def heads_to_rows(self, x):
        return self.rows_sum(x)

    def rows_sum(self, x):
        return lax.psum_scatter(x, "uly", scatter_dimension=0, tiled=True)

    def rows_all(self, x):
        return lax.all_gather(x, "uly", axis=0, tiled=True)

    def experts(self, second_low, routes, weights, router):
        EL, D = weights.shape[0], self.D
        second_all, upstream_all = self.gather(second_low), self.gather(self.upstream)
        N = upstream_all.shape[0]
        group = min(512, N)
        groups = N // group
        slots = -(-(group // self.T * CAP) // 16) * 16
        rows = groups * slots
        own_first = self.u * EL
        chosen = jnp.any(routes[None] == (own_first + jnp.arange(EL, dtype=jnp.int32))[:, None, None, None, None], axis=3)
        slot = slots_of(chosen.reshape(EL, groups, group)).reshape(EL, N)
        entry_in, upstream_in, gates = pick_rows(slot, router, second_all, upstream_all, group, slots)
        flat, split = (EL, rows, -1), (EL, groups, slots, -1)
        out_rows, entry_rows, self.expert_grads, gate_grads = run_experts(
            entry_in.reshape(flat), upstream_in.reshape(flat), gates.reshape(flat), weights, min(8, groups) * slots
        )
        out_part, entry_part = spread_rows(
            own_first.astype(jnp.int32)[None],
            slot.T,
            gate_grads.reshape(split),
            out_rows.reshape(split),
            entry_rows.reshape(split),
            group,
        )
        self.out_sum = self.scatter_wide(out_part)
        return second_all, self.scatter_wide(entry_part)

    def rows_to_heads(self, x):
        return self.rows_all(x), self.expert_grads

    def sequence_sums(self, dk, dv, out_part, q_inner, k_inner):
        pair = jnp.stack([dk, dv]).reshape(2, self.U, self.Z, self.T, self.C)
        pair = lax.psum_scatter(pair, "blk", scatter_dimension=2, tiled=True).reshape(2, self.L, self.C)
        k_inner = lax.psum_scatter(
            k_inner.reshape(self.U, self.Z, -1, 128), "blk", scatter_dimension=1, tiled=True
        ).reshape(-1, 128)
        inner = lax.psum(jnp.stack([q_inner, k_inner]), "uly")
        self.out_grad = lax.psum_scatter(out_part, "blk", scatter_dimension=0, tiled=True)
        return pair[0], pair[1], self.out_sum, inner

    def leave(self, first_part, weight_part, logit_grad, ffn_part, head_parts):
        U, R = self.U, self.D // (self.U * self.Z)
        part = weight_part.reshape(U, self.Z * R, 3 * self.C)
        part = lax.psum_scatter(part, "blk", scatter_dimension=1, tiled=True)
        part = lax.all_to_all(part, "uly", split_axis=0, concat_axis=0, tiled=True)
        weights = part.reshape(U, R, 3, self.C).transpose(2, 1, 0, 3).reshape(3, R, self.D)
        heads = lax.psum_scatter(head_parts, "blk", scatter_dimension=1, tiled=True)
        first = self.rows_sum(first_part)
        return first, weights, self.out_grad, self.gather(logit_grad), self.scatter_wide(ffn_part), heads


def _row_limits(doc_ref, first, rows):
    position = first + lax.broadcasted_iota(jnp.int32, (rows, 1), 0)
    start = jnp.zeros_like(position)
    lowest = jnp.int32(0)
    for d in range(doc_ref.shape[0]):
        begin = doc_ref[d]
        start = jnp.where(begin <= position, jnp.maximum(start, begin), start)
        lowest = jnp.where(begin <= first, jnp.maximum(lowest, begin), lowest)
    return position, start, lowest


def _norm_row(squares, width):
    return lax.rsqrt(squares * (1.0 / width) + EPS)


def _as_column(row):
    return jnp.broadcast_to(row, (128, 128)).T


def _row_sums(values):
    ones = jnp.ones((8, values.shape[1]), F32)
    return lax.dot_general(ones, values, LAST_DIM, precision=lax.Precision.HIGHEST, preferred_element_type=F32)[:1]


def _key_scales(stat_ref, at, chunk, width):
    rows = stat_ref[pl.ds(pl.multiple_of(at // 128, chunk // 128), chunk // 128), :]
    return _norm_row(jnp.concatenate([rows[r : r + 1] for r in range(chunk // 128)], axis=1), width)


def _scores(query, key, factor, position, start, key_first):
    raw = dot(query, key, LAST_DIM) * factor
    key_position = key_first + lax.broadcasted_iota(jnp.int32, raw.shape, 1)
    return jnp.where((key_position <= position) & (key_position >= start), raw, NEG)


def _scaled_query(q_ref, stat_ref, width):
    heads, units = q_ref.shape[1] // HEAD_DIM, q_ref.shape[0] // 128
    scale = jnp.concatenate(
        [_as_column(_norm_row(stat_ref[pl.ds(pl.program_id(0) * units + r, 1), :], width)) for r in range(units)], axis=0
    )
    cols = [pl.ds(h * HEAD_DIM, HEAD_DIM) for h in range(heads)]
    return [(q_ref[:, at].astype(F32) * scale).astype(BF16) for at in cols], cols


def _lay_parts(index_ref, parts, whole):
    @pl.when(pl.program_id(0) == 0)
    def _():
        for i, part in enumerate(parts):
            height = part.shape[0]
            whole[pl.ds(pl.multiple_of(index_ref[2 + i] * height, height), height), :] = part[...]


def _attend_kernel(
    index_ref, doc_ref, q_stat, k_stat, q_ref, k_ref, v_ref, w0, w1, w2, w3, o_ref, log_ref, mix_ref, whole, *, chunk, scaling, width
):
    rows = q_ref.shape[0]
    _lay_parts(index_ref, (w0, w1, w2, w3), whole)
    heads = q_ref.shape[1] // HEAD_DIM
    first = (pl.program_id(0) * index_ref[1] + index_ref[0]) * rows
    position, start, lowest = _row_limits(doc_ref, first, rows)
    queries, cols = _scaled_query(q_ref, q_stat, width)

    def step(i, state):
        at = pl.multiple_of(i * chunk, chunk)
        factor = _key_scales(k_stat, at, chunk, width) * scaling
        new = []
        for h in range(heads):
            top, total, out = state[h]
            scores = _scores(queries[h], k_ref[pl.ds(at, chunk), cols[h]], factor, position, start, at)
            now = jnp.maximum(top, jnp.max(scores, axis=1, keepdims=True))
            weights = jnp.exp(scores - now)
            fade = jnp.exp(top - now)
            total = total * fade + jnp.sum(weights, axis=1, keepdims=True)
            out = out * fade + dot(weights.astype(BF16), v_ref[pl.ds(at, chunk), cols[h]])
            new.append((now, total, out))
        return tuple(new)

    zero = (
        jnp.full((rows, 1), NEG, F32),
        jnp.zeros((rows, 1), F32),
        jnp.zeros((rows, HEAD_DIM), F32),
    )
    last = first + rows
    state = lax.fori_loop(lowest // chunk, (last + chunk - 1) // chunk, step, (zero,) * heads)
    for h in range(heads):
        top, total, out = state[h]
        o_ref[:, cols[h]] = out / total
        log_ref[:, cols[h]] = jnp.broadcast_to(top + jnp.log(total), (rows, HEAD_DIM))
    mix_ref[...] = dot(o_ref[...].astype(BF16), whole[...]).astype(BF16)


def _attend_back_kernel(
    index_ref,
    doc_ref,
    q_stat,
    k_stat,
    q_ref,
    r_ref,
    o_ref,
    log_ref,
    k_ref,
    v_ref,
    w0,
    w1,
    w2,
    w3,
    dq_ref,
    dk_ref,
    dv_ref,
    dw_ref,
    mq_ref,
    mk_ref,
    dk_sum,
    dv_sum,
    dw_sum,
    whole,
    *,
    chunk,
    scaling,
    width,
):
    rows = q_ref.shape[0]
    _lay_parts(index_ref, (w0, w1, w2, w3), whole)
    heads = q_ref.shape[1] // HEAD_DIM
    first = (pl.program_id(0) * index_ref[1] + index_ref[0]) * rows
    position, start, lowest = _row_limits(doc_ref, first, rows)
    queries, cols = _scaled_query(q_ref, q_stat, width)

    @pl.when(pl.program_id(0) == 0)
    def _():
        dk_sum[...] = jnp.zeros_like(dk_sum)
        dv_sum[...] = jnp.zeros_like(dv_sum)
        dw_sum[...] = jnp.zeros_like(dw_sum)
        mk_ref[...] = jnp.zeros_like(mk_ref)

    upstream = r_ref[...]
    dw_sum[...] += dot(o_ref[...].astype(BF16), upstream, FIRST_DIM)
    all_grads = dot(upstream, whole[...], LAST_DIM).astype(BF16)
    grads = [all_grads[:, h * HEAD_DIM : (h + 1) * HEAD_DIM] for h in range(heads)]
    deltas = [jnp.sum(grads[h].astype(F32) * o_ref[:, cols[h]], axis=1, keepdims=True) for h in range(heads)]
    logs = [log_ref[:, at][:, :1] for at in cols]

    def step(i, state):
        at = pl.multiple_of(i * chunk, chunk)
        scale = _key_scales(k_stat, at, chunk, width)
        new = []
        key_inner = jnp.zeros((1, chunk), F32)
        query_inner = state[-1]
        for h in range(heads):
            grad = grads[h]
            key = k_ref[pl.ds(at, chunk), cols[h]]
            scores = _scores(queries[h], key, scale * scaling, position, start, at)
            weights = jnp.exp(scores - logs[h])
            weight_grad = dot(grad, v_ref[pl.ds(at, chunk), cols[h]], LAST_DIM)
            score_grad = weights * (weight_grad - deltas[h])
            inner = score_grad * scores
            key_inner = key_inner + jnp.sum(inner, axis=0, keepdims=True)
            query_inner = query_inner + jnp.sum(inner, axis=1, keepdims=True)
            dv_sum[pl.ds(at, chunk), cols[h]] += dot(weights.astype(BF16), grad, FIRST_DIM)
            dk_sum[pl.ds(at, chunk), cols[h]] += dot(score_grad.astype(BF16), queries[h], FIRST_DIM)
            new.append(state[h] + dot((score_grad * scale).astype(BF16), key))
        mk_ref[pl.ds(i, 1), :] += key_inner
        return tuple(new) + (query_inner,)

    last = first + rows
    zeros = (jnp.zeros((rows, HEAD_DIM), F32),) * heads + (jnp.zeros((rows, 1), F32),)
    state = lax.fori_loop(lowest // chunk, (last + chunk - 1) // chunk, step, zeros)
    for h in range(heads):
        dq_ref[:, cols[h]] = (state[h] * scaling).astype(BF16)
    for r in range(rows // 128):
        inner = jnp.broadcast_to(state[-1][r * 128 : (r + 1) * 128], (128, 128)).T[:1]
        mq_ref[pl.ds(pl.program_id(0) * (rows // 128) + r, 1), :] = inner

    @pl.when(pl.program_id(0) == pl.num_programs(0) - 1)
    def _():
        dk_ref[...] = (dk_sum[...] * scaling).astype(BF16)
        dv_ref[...] = dv_sum[...].astype(BF16)
        dw_ref[...] = dw_sum[...].astype(BF16)


def _resident(*shape):
    return pl.BlockSpec(shape, lambda i, *_: (0,) * len(shape), pipeline_mode=pl.Buffered(1))


def attention_forward(index, docs, q_stat, k_stat, query, key_all, value_all, out_parts, rows, chunk):
    (L, C), N = query.shape, key_all.shape[0]
    D = out_parts[0].shape[1]
    block = pl.BlockSpec((rows, C), lambda i, *_: (i, 0))
    stats = [_resident(*q_stat.shape), _resident(*k_stat.shape)]
    return pl.pallas_call(
        functools.partial(_attend_kernel, chunk=chunk, scaling=HEAD_DIM ** (-0.5), width=HEADS * HEAD_DIM),
        out_shape=[jax.ShapeDtypeStruct((L, C), F32)] * 2 + [jax.ShapeDtypeStruct((L, D), BF16)],
        grid_spec=pltpu.PrefetchScalarGridSpec(
            num_scalar_prefetch=2,
            grid=(L // rows,),
            in_specs=stats + [block, _resident(N, C), _resident(N, C)] + [_resident(C // 4, D)] * 4,
            out_specs=[block, block, pl.BlockSpec((rows, D), lambda i, *_: (i, 0))],
            scratch_shapes=[pltpu.VMEM((C, D), BF16)],
        ),
        compiler_params=pltpu.CompilerParams(vmem_limit_bytes=VMEM_BYTES),
        cost_estimate=pl.CostEstimate(flops=4 * L * C * 1024, bytes_accessed=4 * N * C, transcendentals=L * 1024),
    )(index, docs, q_stat, k_stat, query, key_all, value_all, *out_parts)


def attention_backward(
    index, docs, q_stat, k_stat, query, residual_grad, attended, logs, key_all, value_all, out_parts, rows, chunk
):
    (L, C), N = query.shape, key_all.shape[0]
    D = residual_grad.shape[1]
    block = pl.BlockSpec((rows, C), lambda i, *_: (i, 0))
    whole = _resident(N, C)
    stats = [_resident(*q_stat.shape), _resident(*k_stat.shape)]
    return pl.pallas_call(
        functools.partial(_attend_back_kernel, chunk=chunk, scaling=HEAD_DIM ** (-0.5), width=HEADS * HEAD_DIM),
        out_shape=[jax.ShapeDtypeStruct((L, C), BF16)]
        + [jax.ShapeDtypeStruct((N, C), BF16)] * 2
        + [jax.ShapeDtypeStruct((C, D), BF16)]
        + [jax.ShapeDtypeStruct(q_stat.shape, F32), jax.ShapeDtypeStruct((N // chunk, chunk), F32)],
        grid_spec=pltpu.PrefetchScalarGridSpec(
            num_scalar_prefetch=2,
            grid=(L // rows,),
            in_specs=stats
            + [block, pl.BlockSpec((rows, D), lambda i, *_: (i, 0)), block, block, whole, whole]
            + [_resident(C // 4, D)] * 4,
            out_specs=[block, whole, whole, _resident(C, D), stats[0], _resident(N // chunk, chunk)],
            scratch_shapes=[pltpu.VMEM((N, C), F32)] * 2 + [pltpu.VMEM((C, D), F32), pltpu.VMEM((C, D), BF16)],
        ),
        compiler_params=pltpu.CompilerParams(vmem_limit_bytes=VMEM_BYTES),
        cost_estimate=pl.CostEstimate(flops=10 * L * C * 1024, bytes_accessed=8 * N * C, transcendentals=L * 1024),
    )(index, docs, q_stat, k_stat, query, residual_grad, attended, logs, key_all, value_all, *out_parts)


def _project_kernel(x_ref, w_ref, gain_ref, cos_ref, sin_ref, pre_ref, q_ref, k_ref, v_ref, stat_ref):
    rows = x_ref.shape[0]
    C = q_ref.shape[1]
    pre = dot(x_ref[...], w_ref[...])
    pre_ref[...] = pre[:, : 2 * C]
    v_ref[...] = pre[:, 2 * C :].astype(BF16)
    cosine, sine = cos_ref[...], sin_ref[...]
    for j, out in enumerate((q_ref, k_ref)):
        part = pre[:, j * C : (j + 1) * C]
        sums = _row_sums(part * part)
        for r in range(rows // 128):
            stat_ref[j, pl.ds(pl.program_id(0) * (rows // 128) + r, 1), :] = sums[:, r * 128 : (r + 1) * 128]
        scaled = part * gain_ref[j : j + 1, :]
        for h in range(C // HEAD_DIM):
            one = scaled[:, h * HEAD_DIM : (h + 1) * HEAD_DIM]
            turned = pltpu.roll(one, HEAD_DIM // 2, 1)
            out[:, pl.ds(h * HEAD_DIM, HEAD_DIM)] = (one * cosine + turned * sine).astype(BF16)


def project(x, weights, gains, cosine, sine):
    L, D = x.shape
    C = weights.shape[1] // 3
    rows = 256

    def block(width):
        return pl.BlockSpec((rows, width), lambda i: (i, 0))

    return pl.pallas_call(
        _project_kernel,
        out_shape=[jax.ShapeDtypeStruct((L, 2 * C), F32)]
        + [jax.ShapeDtypeStruct((L, C), BF16)] * 3
        + [jax.ShapeDtypeStruct((2, L // 128, 128), F32)],
        grid=(L // rows,),
        in_specs=[block(D), _resident(D, 3 * C), _resident(8, C), block(HEAD_DIM), block(HEAD_DIM)],
        out_specs=[block(2 * C), block(C), block(C), block(C), _resident(2, L // 128, 128)],
        compiler_params=pltpu.CompilerParams(vmem_limit_bytes=VMEM_BYTES),
        cost_estimate=pl.CostEstimate(flops=6 * L * D * C, bytes_accessed=2 * L * D + 6 * D * C, transcendentals=0),
    )(x, weights, gains, cosine, sine)


def _project_back_kernel(
    dq_ref, dk_ref, dv_ref, pre_ref, stat_ref, inner_ref, gain_ref, cos_ref, sin_ref, x_ref, w_ref, dw_ref, first_ref, dg_ref, total, *, width
):
    rows, C = dq_ref.shape
    cosine, sine = cos_ref[...], sin_ref[...]
    start = pl.program_id(0) == 0

    @pl.when(start)
    def _():
        dg_ref[...] = jnp.zeros_like(dg_ref)

    grads = []
    for j, ref in enumerate((dq_ref, dk_ref)):
        scales, means = [], []
        for r in range(rows // 128):
            at = pl.ds(pl.program_id(0) * (rows // 128) + r, 1)
            scale = _norm_row(stat_ref[j, at, :], width)
            scales.append(_as_column(scale))
            means.append(_as_column(inner_ref[j, at, :] * scale * scale * (1.0 / width)))
        scale, mean = jnp.concatenate(scales, axis=0), jnp.concatenate(means, axis=0)
        for h in range(C // HEAD_DIM):
            at = pl.ds(h * HEAD_DIM, HEAD_DIM)
            up = ref[:, at].astype(F32)
            up = up * cosine + pltpu.roll(up * sine, HEAD_DIM // 2, 1)
            pre = pre_ref[:, pl.ds(j * C + h * HEAD_DIM, HEAD_DIM)]
            grads.append((scale * up * gain_ref[j : j + 1, at] - pre * mean).astype(BF16))
            dg_ref[j : j + 1, at] += jnp.sum(up * pre * scale, axis=0, keepdims=True)
    grads.append(dv_ref[...])
    both = jnp.concatenate(grads, axis=1)
    first_ref[...] = dot(both, w_ref[...], LAST_DIM).astype(BF16)
    part = dot(x_ref[...], both, FIRST_DIM)

    @pl.when(start)
    def _():
        total[...] = part

    @pl.when(jnp.logical_not(start))
    def _():
        total[...] += part

    @pl.when(pl.program_id(0) == pl.num_programs(0) - 1)
    def _():
        dw_ref[...] = total[...].astype(BF16)


def project_back(dq, dk, dv, pre, stats, inner, gains, cosine, sine, x, weights):
    L, D = x.shape
    C = weights.shape[1] // 3
    rows = min(BACK_ROWS, L)

    def block(width):
        return pl.BlockSpec((rows, width), lambda i: (i, 0))

    return pl.pallas_call(
        functools.partial(_project_back_kernel, width=D),
        out_shape=[
            jax.ShapeDtypeStruct((D, 3 * C), BF16),
            jax.ShapeDtypeStruct((L, D), BF16),
            jax.ShapeDtypeStruct((8, C), F32),
        ],
        grid=(L // rows,),
        in_specs=[block(C)] * 3
        + [block(2 * C), _resident(*stats.shape), _resident(*inner.shape), _resident(8, C)]
        + [block(HEAD_DIM), block(HEAD_DIM), block(D), _resident(D, 3 * C)],
        out_specs=[_resident(D, 3 * C), block(D), _resident(8, C)],
        scratch_shapes=[pltpu.VMEM((D, 3 * C), F32)],
        compiler_params=pltpu.CompilerParams(vmem_limit_bytes=VMEM_BYTES),
        cost_estimate=pl.CostEstimate(flops=12 * L * D * C, bytes_accessed=4 * L * D + 12 * D * C, transcendentals=0),
    )(dq, dk, dv, pre, stats, inner, gains, cosine, sine, x, weights)


def _pick_kernel(slot_ref, router_ref, x_ref, g_ref, xr_ref, gr_ref, gate_ref, *, slots, width):
    experts, group = slot_ref.shape
    logits = lax.dot_general(router_ref[...], x_ref[...], (((0,), (1,)), ((), ())), preferred_element_type=F32)
    powers = jnp.exp(logits - jnp.max(logits, axis=0, keepdims=True))
    chances = powers / jnp.sum(powers, axis=0, keepdims=True)
    row = lax.broadcasted_iota(jnp.int32, (slots, group), 0)
    picks = []
    for e in range(experts):
        hit = slot_ref[e : e + 1, :] == row
        gate = jnp.sum(jnp.where(hit, chances[e : e + 1, :], 0.0), axis=1, keepdims=True)
        gate_ref[e, 0] = jnp.broadcast_to(gate, (slots, 128))
        picks.append(jnp.where(hit, 1.0, 0.0).astype(BF16))
    pick = jnp.concatenate(picks, axis=0)
    for source, target in ((x_ref, xr_ref), (g_ref, gr_ref)):

        def step(i, _, source=source, target=target):
            cols = pl.ds(pl.multiple_of(i * width, width), width)
            rows = dot(pick, source[:, cols]).astype(BF16)
            for e in range(experts):
                target[e, 0, :, cols] = rows[e * slots : (e + 1) * slots]
            return 0

        lax.fori_loop(0, source.shape[1] // width, step, 0)


def pick_rows(slot, router, x, g, group, slots):
    EL, N = slot.shape
    D = x.shape[1]
    groups = N // group
    tokens = pl.BlockSpec((group, D), lambda i: (i, 0))
    picked = pl.BlockSpec((EL, 1, slots, D), lambda i: (0, i, 0, 0))
    rows = jax.ShapeDtypeStruct((EL, groups, slots, D), BF16)
    return pl.pallas_call(
        functools.partial(_pick_kernel, slots=slots, width=512),
        out_shape=[rows, rows, jax.ShapeDtypeStruct((EL, groups, slots, 128), F32)],
        grid=(groups,),
        in_specs=[
            pl.BlockSpec((EL, group), lambda i: (0, i)),
            pl.BlockSpec(router.shape, lambda i: (0, 0)),
            tokens,
            tokens,
        ],
        out_specs=[picked, picked, pl.BlockSpec((EL, 1, slots, 128), lambda i: (0, i, 0, 0))],
        compiler_params=pltpu.CompilerParams(vmem_limit_bytes=VMEM_BYTES),
        cost_estimate=pl.CostEstimate(
            flops=4 * EL * slots * N * D, bytes_accessed=8 * N * D, transcendentals=N * EXPERTS
        ),
    )(slot, router, x, g)


def _expert_kernel(x_ref, g_ref, gate_ref, w_ref, out_ref, entry_ref, dw_ref, gg_ref):
    x, g = x_ref[0], g_ref[0]
    gate = gate_ref[0][:, :1]
    gate_pre = dot(x, w_ref[0, 0])
    up = dot(x, w_ref[0, 1])
    back = dot(g, w_ref[0, 2])
    sig = jax.nn.sigmoid(gate_pre)
    act = gate_pre * sig
    inner = act * up
    gg_ref[0] = jnp.broadcast_to(jnp.sum(inner * back, axis=1, keepdims=True), gg_ref.shape[1:])
    inner_grad = back * gate
    gate_pre_grad = (inner_grad * up * sig * (1.0 + gate_pre * (1.0 - sig))).astype(BF16)
    up_grad = (inner_grad * act).astype(BF16)
    gated = (inner * gate).astype(BF16)
    both = jnp.concatenate([gate_pre_grad, up_grad], axis=1)
    out_ref[0] = dot(gated, w_ref[0, 2], LAST_DIM).astype(BF16)
    entry_ref[0] = dot(both, jnp.concatenate([w_ref[0, 0], w_ref[0, 1]], axis=1), LAST_DIM).astype(BF16)
    FL = w_ref.shape[3]
    pair = dot(x, both, FIRST_DIM)
    parts = (pair[:, :FL], pair[:, FL:], dot(g, gated, FIRST_DIM))
    first = pl.program_id(1) == 0
    for k in range(3):

        @pl.when(first)
        def _(k=k):
            dw_ref[0, k] = parts[k]

        @pl.when(jnp.logical_not(first))
        def _(k=k):
            dw_ref[0, k] += parts[k]


def run_experts(x, g, gate, weights, chunk):
    EL, rows, D = x.shape
    FL = weights.shape[3]
    row_block = pl.BlockSpec((1, chunk, D), lambda e, c: (e, c, 0))
    thin = pl.BlockSpec((1, chunk, 128), lambda e, c: (e, c, 0))
    matrices = pl.BlockSpec((1, 3, D, FL), lambda e, c: (e, 0, 0, 0))
    return pl.pallas_call(
        _expert_kernel,
        out_shape=[
            jax.ShapeDtypeStruct(x.shape, BF16),
            jax.ShapeDtypeStruct(x.shape, BF16),
            jax.ShapeDtypeStruct(weights.shape, F32),
            jax.ShapeDtypeStruct((EL, rows, 128), F32),
        ],
        grid=(EL, rows // chunk),
        in_specs=[row_block, row_block, thin, matrices],
        out_specs=[row_block, row_block, matrices, thin],
        compiler_params=pltpu.CompilerParams(vmem_limit_bytes=VMEM_BYTES),
        cost_estimate=pl.CostEstimate(
            flops=18 * EL * rows * D * FL, bytes_accessed=8 * EL * rows * D + 18 * EL * D * FL, transcendentals=EL * rows * FL
        ),
    )(x, g, gate, weights)


def _spread_kernel(own_ref, slot_ref, gg_ref, out_ref, entry_ref, o_ref, e_ref, *, width):
    group, experts = slot_ref.shape
    slots = out_ref.shape[2]
    total = experts * slots
    D = out_ref.shape[3]
    lane = lax.broadcasted_iota(jnp.int32, (experts, total), 1)
    which = lax.broadcasted_iota(jnp.int32, (experts, total), 0)
    choose = jnp.where((lane >= which * slots) & (lane < (which + 1) * slots), 1.0, 0.0).astype(BF16)
    offset = lane[:1] - jnp.sum(jnp.where(lane >= (which + 1) * slots, slots, 0), axis=0, keepdims=True)
    mine = dot(slot_ref[...].astype(BF16), choose)
    pick = jnp.where(mine == offset.astype(F32), 1.0, 0.0).astype(BF16)
    column = lax.broadcasted_iota(jnp.int32, (slots, 128), 1)
    grads = [jnp.where(column == own_ref[0] + e, gg_ref[e, 0], 0.0).astype(BF16) for e in range(experts)]
    e_ref[:, pl.ds(D, 128)] = dot(pick, jnp.concatenate(grads, axis=0)).astype(BF16)

    def step(i, _):
        cols = pl.ds(pl.multiple_of(i * width, width), width)
        for source, target in ((out_ref, o_ref), (entry_ref, e_ref)):
            rows = jnp.concatenate([source[e, 0, :, cols] for e in range(experts)], axis=0)
            target[:, cols] = dot(pick, rows).astype(BF16)
        return 0

    lax.fori_loop(0, D // width, step, 0)


def spread_rows(own, slot, gate_grads, out_rows, entry_rows, group):
    N, EL = slot.shape
    _, groups, slots, D = out_rows.shape
    picked = pl.BlockSpec((EL, 1, slots, D), lambda i, *_: (0, i, 0, 0))
    return pl.pallas_call(
        functools.partial(_spread_kernel, width=512),
        out_shape=[jax.ShapeDtypeStruct((N, D), BF16), jax.ShapeDtypeStruct((N, D + 128), BF16)],
        grid_spec=pltpu.PrefetchScalarGridSpec(
            num_scalar_prefetch=1,
            grid=(groups,),
            in_specs=[
                pl.BlockSpec((group, EL), lambda i, *_: (i, 0)),
                pl.BlockSpec((EL, 1, slots, 128), lambda i, *_: (0, i, 0, 0)),
                picked,
                picked,
            ],
            out_specs=[
                pl.BlockSpec((group, D), lambda i, *_: (i, 0)),
                pl.BlockSpec((group, D + 128), lambda i, *_: (i, 0)),
            ],
        ),
        compiler_params=pltpu.CompilerParams(vmem_limit_bytes=VMEM_BYTES),
        cost_estimate=pl.CostEstimate(flops=4 * EL * slots * N * D, bytes_accessed=8 * N * D, transcendentals=0),
    )(own, slot, gate_grads, out_rows, entry_rows)


def body(
    hidden_in,
    out_grad,
    attn_gain,
    query_weight,
    key_weight,
    value_weight,
    out_weight,
    query_gain,
    key_gain,
    ffn_gain,
    router_weight,
    expert_weights,
    routes,
    doc_starts,
):
    U = lax.axis_size("uly")
    Z = lax.axis_size("blk")
    u = lax.axis_index("uly")
    z = lax.axis_index("blk")
    T, D = hidden_in.shape
    EL = expert_weights.shape[0]
    N = U * Z * T
    RW = query_weight.shape[0]
    move = (Slice if (U, Z, T, D) == (8, 4, 128, 2048) else General)(U, Z, T, D)
    C, L = move.C, move.L

    own_weights = (query_weight, key_weight, value_weight)
    gains = jnp.stack([attn_gain, ffn_gain, query_gain, key_gain], axis=1)
    first_rows, qkv_weight, packed, routes_all = move.enter(
        hidden_in, own_weights, gains, out_weight, router_weight, routes.T
    )
    hidden = hidden_in.astype(F32)
    weight_router = packed[:, :EXPERTS]
    gain_ffn = packed[:, EXPERTS].astype(F32)
    head_gains = lax.dynamic_slice_in_dim(packed[:, EXPERTS + 1 : EXPERTS + 3], move.group * C, C, 0).astype(F32)
    head_gains = jnp.pad(head_gains.T, ((0, 6), (0, 0)))
    local = jnp.arange(L, dtype=jnp.int32)
    cosine, sine = rotary_tables((local // T * move.block_step + move.first_block) * T + local % T)
    pre, query_rot, key_rot, value, squares = project(first_rows, qkv_weight, head_gains, cosine, sine)
    key_all, value_all, stats, k_stat = move.sequence(key_rot, value, squares, out_grad)
    index = jnp.stack([jnp.int32(i) for i in (move.first_block * T // move.rows, move.block_step, *move.parts)])
    chunk = min(ATTEND_CHUNK, N)
    attended, logs, mixed = attention_forward(
        index, doc_starts, stats[0], k_stat, query_rot, key_all, value_all, move.out_parts, move.rows, chunk
    )
    residual = hidden + move.heads_to_rows(mixed).astype(F32)

    second_scale = norm_scale(residual)
    second_low = (residual * second_scale * gain_ffn).astype(BF16)
    probabilities = jax.nn.softmax(dot(second_low, weight_router), axis=-1)
    own_router = jnp.roll(weight_router, -u * EL, axis=1)
    second_all, entry_sum = move.experts(second_low, routes_all, expert_weights, own_router)
    entry_sum = entry_sum.astype(F32)

    second_grad, prob_grad = entry_sum[:, :D], entry_sum[:, D : D + EXPERTS]
    logit_grad = (
        probabilities * (prob_grad - jnp.sum(probabilities * prob_grad, axis=1, keepdims=True))
    ).astype(BF16)
    second_grad = second_grad + dot(logit_grad, weight_router, LAST_DIM)
    upstream = out_grad.astype(F32)
    weighted = second_grad * gain_ffn
    inner_mean = jnp.mean(weighted * residual, axis=-1, keepdims=True)
    residual_grad = upstream + second_scale * weighted - residual * (second_scale**3) * inner_mean
    ffn_gain_part = jnp.sum(second_grad * residual * second_scale, axis=0)

    residual_rows, expert_grads = move.rows_to_heads(residual_grad.astype(BF16))
    dq, dk_part, dv_part, out_weight_part, q_inner, k_inner = attention_backward(
        index,
        doc_starts,
        stats[0],
        k_stat,
        query_rot,
        residual_rows,
        attended,
        logs,
        key_all,
        value_all,
        move.out_parts,
        move.rows,
        chunk,
    )
    dk, dv, out_sum, inner = move.sequence_sums(dk_part, dv_part, out_weight_part, q_inner, k_inner)
    weight_part, first_part, gain_parts = project_back(
        dq, dk, dv, pre, stats, inner, head_gains, cosine, sine, first_rows, qkv_weight
    )
    gain_parts = gain_parts[:2]
    first_weighted, weight_sum, out_weight_grad, logit_grad_all, ffn_gain_grad, head_gain_grads = move.leave(
        first_part, weight_part, logit_grad, ffn_gain_part, gain_parts
    )
    own_columns = lax.dynamic_slice_in_dim(second_all, (u * Z + z) * RW, RW, 1)
    router_grad = dot(own_columns, logit_grad_all, FIRST_DIM)
    output, hidden_grad, attn_gain_grad, *weight_grads = finish(
        hidden_in, residual, residual_grad, first_weighted, out_sum, own_weights, weight_sum, out_weight_grad, gains
    )
    return (
        output,
        hidden_grad,
        attn_gain_grad[:, 0],
        weight_grads[0],
        weight_grads[1],
        weight_grads[2],
        weight_grads[3],
        head_gain_grads[0],
        head_gain_grads[1],
        ffn_gain_grad,
        router_grad,
        expert_grads,
    )


def solution(mesh):
    rows = P(ALL, None)
    flat = P(ALL)
    experts = P("uly", None, None, "blk")
    return jax.shard_map(
        body,
        mesh=mesh,
        in_specs=(rows, rows, flat, rows, rows, rows, rows, flat, flat, flat, rows, experts, rows, P()),
        out_specs=(rows, rows, flat, rows, rows, rows, rows, flat, flat, flat, rows, experts),
        check_vma=False,
    )
```

```python
import functools

import jax
import jax.numpy as jnp
from jax import lax
from jax.experimental import pallas as pl
from jax.experimental.pallas import tpu as pltpu
from jax.sharding import PartitionSpec as P

HEADS = 16
HEAD_DIM = 128
EXPERTS = 64
CAP = 17

EPS = 1e-05
THETA = 10000.0
NEG = -1e30
FIRST_DIM = (((0,), (0,)), ((), ()))
LAST_DIM = (((1,), (1,)), ((), ()))
ALL = ("uly", "blk")
F32 = jnp.float32
BF16 = jnp.bfloat16
VMEM_BYTES = 56 * 1024 * 1024
PICK_WIDTH = 512
ATTEND_CHUNK = 512
ATTEND_ROWS = 512
BACK_ROWS = 1024
PROJECT_ROWS = 256
SPREAD_WIDTH = 2048


def dot(a, b, dims=(((1,), (0,)), ((), ()))):
    return lax.dot_general(a, b, dims, preferred_element_type=F32)


def rotary_tables(position):
    halfway = HEAD_DIM // 2
    frequency = THETA ** (-(jnp.arange(halfway).astype(F32) * 2.0 / HEAD_DIM))
    angles = position.astype(F32)[:, None] * frequency[None, :]
    cosine, sine = jnp.cos(angles), jnp.sin(angles)
    return jnp.concatenate([cosine, cosine], axis=1), jnp.concatenate([-sine, sine], axis=1)


def norm_scale(values):
    return lax.rsqrt(jnp.mean(values * values, axis=-1, keepdims=True) + EPS)


MESH = pl.DeviceIdType.MESH
DMA = pltpu.SemaphoreType.DMA
ANY_SPACE = pl.BlockSpec(memory_space=pl.ANY)
IN_VMEM = pl.BlockSpec(memory_space=pltpu.VMEM)
DEPTH = 4
CHIPS = (0, 2, 4, 6)
FIRST, THEN = (2, 4), (4, 2)


def _send(src, dst, send_sem, recv_sem, to):
    pltpu.make_async_remote_copy(
        src_ref=src, dst_ref=dst, send_sem=send_sem, recv_sem=recv_sem, device_id=to, device_id_type=MESH
    ).start()


def _expect(ref, sem, here):
    pltpu.make_async_remote_copy(
        src_ref=ref, dst_ref=ref, send_sem=sem, recv_sem=sem, device_id=here, device_id_type=MESH
    ).wait_recv()


def _sent(ref, sem, here):
    pltpu.make_async_remote_copy(
        src_ref=ref, dst_ref=ref, send_sem=sem, recv_sem=sem, device_id=here, device_id_type=MESH
    ).wait_send()


def _greet(u, z, planes, line=False, others=(), meanwhile=lambda: None):
    barrier = pltpu.get_barrier_semaphore()
    for bit in planes:
        pl.semaphore_signal(barrier, inc=1, device_id=(u ^ bit, z), device_id_type=MESH)
    for to in others:
        pl.semaphore_signal(barrier, inc=1, device_id=to, device_id_type=MESH)
    count = len(planes) + len(others)
    if line:

        @pl.when(z > 0)
        def _():
            pl.semaphore_signal(barrier, inc=1, device_id=(u, z - 1), device_id_type=MESH)

        @pl.when(z < DEPTH - 1)
        def _():
            pl.semaphore_signal(barrier, inc=1, device_id=(u, z + 1), device_id_type=MESH)

        count = count + jnp.where((z == 0) | (z == DEPTH - 1), 1, 2)
    meanwhile()
    pl.semaphore_wait(barrier, count)


def _line_order(z):
    second = jnp.where(z == 0, 1, z - 1)
    third = jnp.where(z == 0, 2, jnp.where(z == 3, 1, z + 1))
    fourth = jnp.where(z < 2, 3, 0)
    return (z, second, third, fourth)


def _accumulate(target, source, rows):
    strip = 16

    def step(i, _):
        at = pl.ds(pl.multiple_of(i * strip, strip), strip)
        target[at, :] = target[at, :] + source[at, :]
        return 0

    lax.fori_loop(0, rows // strip, step, 0)


def _run(*parts, order=()):
    for i in order:
        next(parts[i])
    live = list(parts)
    while live:
        for part in list(live):
            try:
                next(part)
            except StopIteration:
                live.remove(part)


def _line_part(u, z, source, block, sems, share=True, place=None):
    z_send, z_recv, c_send, c_recv, own_sem = sems
    here, core = (u, z), u % 2
    if place is None:
        own = pltpu.make_async_copy(source, block(core, z), own_sem)
        own.start()
    else:
        def block(_, level):
            return place(level, z)

    order = _line_order(z)

    def along(level, ref, step):
        @pl.when((z > 0) & (level >= z))
        def _():
            step(ref, 0, level, (u, z - 1))

        @pl.when((z < DEPTH - 1) & (level <= z))
        def _():
            step(ref, 1, level, (u, z + 1))

    def go(ref, way, level, to):
        there = block(core, level) if place is None else place(level, to[1])
        _send(ref, there, z_send.at[way, level], z_recv.at[level], to)

    def gone(ref, way, level, to):
        _sent(ref, z_send.at[way, level], here)

    for i in range(4):
        level = order[i]
        ref = source if i == 0 else block(core, level)
        if i > 0:
            yield
            _expect(ref, z_recv.at[level], here)
        along(level, ref, go)
        if share:
            _send(ref, block(core, level), c_send.at[level], c_recv.at[level], (u ^ 1, z))
    yield
    if share:
        for i in range(4):
            _expect(block(1 - core, order[i]), c_recv.at[order[i]], here)
    yield
    for i in range(4):
        along(order[i], source, gone)
        if share:
            _sent(source, c_send.at[order[i]], here)
    if place is None:
        own.wait()


def _plane_part(u, z, own, block, sems):
    p_send, p_recv, o_sem = sems
    here = (u, z)
    for way, bits in enumerate((FIRST, THEN)):
        for h in range(2):
            _send(own(h), block(h, u), p_send.at[h, way], p_recv.at[h, way], (u ^ bits[h], z))
    for h in range(2):
        pltpu.make_async_copy(own(h), block(h, u), o_sem.at[h]).start()
    for h in range(2):
        yield
        _expect(block(h, u ^ FIRST[h]), p_recv.at[h, 0], here)
        near = block(h, u ^ FIRST[h])
        _send(near, near, p_send.at[h, 2], p_recv.at[h, 2], (u ^ THEN[h], z))
    yield
    for h in range(2):
        _expect(block(h, u ^ THEN[h]), p_recv.at[h, 1], here)
        _expect(block(h, u ^ 6), p_recv.at[h, 2], here)
    yield
    for h in range(2):
        for k in range(3):
            _sent(block(h, u), p_send.at[h, k], here)
        pltpu.make_async_copy(own(h), block(h, u), o_sem.at[h]).wait()


def _plane_sum_part(u, z, source, work, bufs, sems, rows, then_do):
    p_buf, q_buf = bufs
    load, p_send, p_recv, q_send, q_recv = sems
    here = (u, z)
    for j in (1, 0):
        for h in range(2):
            bit = (THEN[h], 6)[j]
            _send(source(h, u ^ bit), p_buf.at[h, j], p_send.at[h, j], p_recv.at[h, j], (u ^ THEN[h], z))
    for h in range(2):
        for j, bit in enumerate((0, FIRST[h])):
            pltpu.make_async_copy(source(h, u ^ bit), work.at[h, j], load.at[h, j]).start()
    for h in range(2):
        yield
        for j, bit in enumerate((0, FIRST[h])):
            pltpu.make_async_copy(source(h, u ^ bit), work.at[h, j], load.at[h, j]).wait()
        _expect(p_buf.at[h, 1], p_recv.at[h, 1], here)
        _accumulate(work.at[h, 1], p_buf.at[h, 1], rows)
        _send(work.at[h, 1], q_buf.at[h], q_send.at[h], q_recv.at[h], (u ^ FIRST[h], z))
    yield
    for h in range(2):
        _expect(p_buf.at[h, 0], p_recv.at[h, 0], here)
        _accumulate(work.at[h, 0], p_buf.at[h, 0], rows)
    for h in range(2):
        _expect(q_buf.at[h], q_recv.at[h], here)
        _accumulate(work.at[h, 0], q_buf.at[h], rows)
    then_do()
    yield
    for h in range(2):
        for j in range(2):
            _sent(p_buf.at[h, j], p_send.at[h, j], here)
        _sent(q_buf.at[h], q_send.at[h], here)


def _line_sum_part(u, z, source, work, bufs, sems, rows, then_do):
    c_buf, z_buf = bufs
    load, c_send, c_recv, z_send, z_recv = sems
    here, core = (u, z), u % 2
    order = tuple(reversed(_line_order(z)))
    for i in range(4):
        _send(source(1 - core, order[i]), c_buf.at[i], c_send.at[i], c_recv.at[i], (u ^ 1, z))
        pltpu.make_async_copy(source(core, order[i]), work.at[i], load.at[i]).start()
    for i in range(4):
        yield
        pltpu.make_async_copy(source(core, order[i]), work.at[i], load.at[i]).wait()
        _expect(c_buf.at[i], c_recv.at[i], here)
        _accumulate(work.at[i], c_buf.at[i], rows)
        if i == 3:
            yield
        _line_end(u, z, order[i], i, work.at[i], z_buf, (z_send, z_recv), rows)
    then_do()
    yield
    for i in range(4):
        _sent(c_buf.at[i], c_send.at[i], here)
        if i < 3:
            _sent(work.at[i], z_send.at[i], here)


def _column_peers(u, z):
    return [((u ^ c, z ^ k), c, k) for c in range(2) for k in range(4) if c or k]


def _comm(kernel, outs, scratch, collective_id, specs, flops=0, moved=100_000_000):
    return pl.pallas_call(
        kernel,
        out_shape=outs,
        in_specs=specs[0],
        out_specs=specs[1],
        scratch_shapes=scratch,
        compiler_params=pltpu.CompilerParams(
            collective_id=collective_id, has_side_effects=True, vmem_limit_bytes=VMEM_BYTES
        ),
        cost_estimate=pl.CostEstimate(flops=flops, bytes_accessed=moved, transcendentals=0),
    )


ENTER_ORDER = (0, 2, 3, 1, 3, 3, 0, 2, 1, 0, 2, 0, 2)
KV_ORDER = (2, 0, 1, 0, 0, 1, 2, 1, 0, 1)
PAIR_ORDER = (1, 0, 2, 1, 0, 0, 1, 2, 1, 0)
LEAVE_ORDER = (0, 1, 2, 1, 2, 1, 0, 0, 1, 0, 1, 1)
LINE_SEMS = [DMA((2, 4)), DMA((4,)), DMA((4,)), DMA((4,)), DMA]
PLANE_SEMS = [DMA((2, 3)), DMA((2, 3)), DMA((2,))]
PLANE_SUM_SEMS = [DMA((2, 2)), DMA((2, 2)), DMA((2, 2)), DMA((2,)), DMA((2,))]
LINE_SUM_SEMS = [DMA((4,)), DMA((4,)), DMA((4,)), DMA((4,)), DMA((2, 4))]


def _small_part(u, z, xs, outs, sems):
    own_sem, z_send, z_recv, u_send, u_recv = sems
    here = (u, z)
    for a, (x, o) in enumerate(zip(xs, outs)):
        pltpu.make_async_copy(x, o.at[u, z], own_sem.at[a]).start()
        for k in range(1, 4):
            _send(x, o.at[u, z], z_send.at[a, k], z_recv.at[a, k], (u, z ^ k))
    yield
    for a, (x, o) in enumerate(zip(xs, outs)):
        pltpu.make_async_copy(x, o.at[u, z], own_sem.at[a]).wait()
        for k in range(1, 4):
            _expect(o.at[u, z ^ k], z_recv.at[a, k], here)
        for k in range(1, 8):
            _send(o.at[u], o.at[u], u_send.at[a, k], u_recv.at[a, k], (u ^ k, z))
    yield
    yield
    for a, (x, o) in enumerate(zip(xs, outs)):
        for k in range(1, 4):
            _sent(x, z_send.at[a, k], here)
        for k in range(1, 8):
            _sent(o.at[u], u_send.at[a, k], here)
            _expect(o.at[u ^ k], u_recv.at[a, k], here)


def _small_sems(n):
    return [DMA((n,)), DMA((n, 4)), DMA((n, 4)), DMA((n, 8)), DMA((n, 8))]


def _packed(router, gains):
    lane = lax.broadcasted_iota(jnp.int32, (router.shape[0], 128 - EXPERTS), 1)
    tail = jnp.zeros(lane.shape, F32)
    for j in range(1, 4):
        tail = jnp.where(lane == j - 1, gains[:, j : j + 1], tail)
    return router, tail.astype(BF16)


def enter(hidden, weights, gains, router, routes, out_grad, collective_id):
    T, D = hidden.shape
    R, C = weights[0].shape[0], weights[0].shape[1] // 8
    held = (2, 4, R, 3 * C)
    strip = 16

    def kernel(h_ref, wq_ref, wk_ref, wv_ref, gain_ref, router_ref, route_ref, g_ref, x_out, w_out, p_out, r_out, g_out, *refs):
        x_ref, w_ref, pack_ref, w_buf, w_send, w_recv = refs[:6]
        half = [pl.ds(h * (T // 2), T // 2) for h in range(2)]
        sems = refs[6:]
        u, z = lax.axis_index("uly"), lax.axis_index("blk")
        here, core, chip = (u, z), u % 2, u // 2
        column = _column_peers(u, z)

        def weight_part():
            def cut(j, c, level):
                return w_ref.at[j, :, pl.ds(pl.multiple_of((2 * level + c) * C, C), C)]

            def slot(j, c, level):
                return w_buf.at[c, level, :, pl.ds(j * C, C)]

            for i, (to, c, k) in enumerate(column):
                for j in range(3):
                    _send(cut(j, core ^ c, z ^ k), slot(j, core, z), w_send.at[i, j], w_recv.at[i, j], to)
            for j in range(3):
                slot(j, core, z)[...] = cut(j, core, z)[...]
            yield
            for i, (to, c, k) in enumerate(column):
                for j in range(3):
                    _expect(slot(j, core ^ c, z ^ k), w_recv.at[i, j], here)
            yield from _plane_part(u, z, lambda h: w_buf.at[h], lambda h, v: w_out.at[v // 2, h], sems[:3])
            for i, (to, c, k) in enumerate(column):
                for j in range(3):
                    _sent(cut(j, core ^ c, z ^ k), w_send.at[i, j], here)

        def prepare():
            gains = gain_ref[...].astype(F32)
            for j, ref in enumerate((wq_ref, wk_ref, wv_ref)):
                w_ref[j] = (ref[...].astype(F32) * gains[:, :1]).astype(BF16)

            def norm(i, _):
                at = pl.ds(pl.multiple_of(i * strip, strip), strip)
                value = h_ref[at, :].astype(F32)
                x_ref[at, :] = (value * norm_scale(value)).astype(BF16)
                return 0

            lax.fori_loop(0, T // strip, norm, 0)
            pack_ref[:, pl.ds(0, EXPERTS)], pack_ref[:, pl.ds(EXPERTS, 128 - EXPERTS)] = _packed(router_ref[...], gains)

        _greet(u, z, range(1, 8), others=[to for to, c, k in column if k], meanwhile=prepare)
        _run(
            weight_part(),
            _small_part(u, z, (pack_ref, route_ref), (p_out, r_out), sems[11:]),
            _line_part(u, z, x_ref, lambda c, level: x_out.at[c, level], sems[3:8]),
            _plane_part(u, z, lambda h: g_ref.at[half[h]], lambda h, v: g_out.at[v // 2, half[h]], sems[8:11]),
            order=ENTER_ORDER,
        )

    outs = [
        jax.ShapeDtypeStruct((2, 4, T, D), BF16),
        jax.ShapeDtypeStruct((4,) + held, BF16),
        jax.ShapeDtypeStruct((8, 4, R, 128), BF16),
        jax.ShapeDtypeStruct((8, 4) + routes.shape, routes.dtype),
        jax.ShapeDtypeStruct((4, T, D), BF16),
    ]
    scratch = [pltpu.VMEM((T, D), BF16), pltpu.VMEM((3, R, D), BF16), pltpu.VMEM((R, 128), BF16)]
    scratch += [pltpu.VMEM(held, BF16), DMA((7, 3)), DMA((7, 3))] + PLANE_SEMS + LINE_SEMS + PLANE_SEMS + _small_sems(2)
    specs = ([IN_VMEM] * 7 + [ANY_SPACE], [ANY_SPACE] * 5)
    return _comm(kernel, outs, scratch, collective_id, specs)(hidden, *weights, gains, router, routes, out_grad)


def _column_sum_part(u, z, x_ref, total, buf, sems, then_do):
    send, recv = sems
    here = (u, z)
    column = _column_peers(u, z)
    for i, (to, c, k) in enumerate(column):
        _send(x_ref, buf.at[i], send.at[i], recv.at[i], to)
    yield
    value = x_ref[...]
    for i in range(7):
        _expect(buf.at[i], recv.at[i], here)
        value = value + buf[i]
    total[...] = value
    then_do()
    yield
    for i in range(7):
        _sent(x_ref, send.at[i], here)


def plane_pair(first, second, rows, squares, collective_id):
    R = squares.shape[0] // 2

    def kernel(a_ref, b_ref, x_ref, s_ref, a_out, b_out, x_out, s_out, k_out, buf, *sems):
        u, z = lax.axis_index("uly"), lax.axis_index("blk")
        here, chip = (u, z), u // 2
        k_send, k_recv = sems[10:]
        _greet(u, z, (2, 4, 6), others=[to for to, c, k in _column_peers(u, z)])
        own, outs = (a_ref, b_ref), (a_out, b_out)
        keys = s_out.at[pl.ds(R, R)]

        def tell():
            k_out[chip] = keys[...]
            for i, bit in enumerate((2, 4, 6)):
                _send(keys, k_out.at[chip], k_send.at[i], k_recv.at[i], (u ^ bit, z))

        _run(
            _plane_part(u, z, lambda h: own[h], lambda h, v: outs[h].at[v // 2], sems[:3]),
            _line_part(
                u, z, x_ref, None, sems[3:8], share=False, place=lambda level, at: x_out.at[(level - at + 3) % 4]
            ),
            _column_sum_part(u, z, s_ref, s_out, buf, sems[8:10], tell),
            order=PAIR_ORDER,
        )
        for i, bit in enumerate((2, 4, 6)):
            _expect(k_out.at[(u ^ bit) // 2], k_recv.at[i], here)
            _sent(keys, k_send.at[i], here)

    outs = [jax.ShapeDtypeStruct((4,) + x.shape, x.dtype) for x in (first, second)]
    outs += [jax.ShapeDtypeStruct((3,) + rows.shape, rows.dtype)]
    outs += [jax.ShapeDtypeStruct(squares.shape, F32), jax.ShapeDtypeStruct((4, R, 128), F32)]
    specs = ([IN_VMEM] * 2 + [ANY_SPACE, IN_VMEM], [ANY_SPACE] * 3 + [IN_VMEM] * 2)
    scratch = [pltpu.VMEM((7,) + squares.shape, F32)] + PLANE_SEMS + LINE_SEMS + [DMA((7,)), DMA((7,)), DMA((3,)), DMA((3,))]
    return _comm(kernel, outs, scratch, collective_id, specs)(first, second, rows, squares)


def column_gather(rows, slot, out_rows, collective_id):
    T, D = rows.shape
    EL, _, slots, _ = out_rows.shape

    def kernel(r_ref, slot_ref, rows_ref, r_out, x_out, *refs):
        u, z = lax.axis_index("uly"), lax.axis_index("blk")
        _greet(u, z, (1, 2, 4), line=True)
        order = _line_order(z)

        def keep(i, part):
            x_out[order[i]] = part[...]

        _run(
            _line_part(u, z, r_ref, lambda c, level: r_out.at[c, level], refs[-5:]),
            _spread_part(u, z, slot_ref, rows_ref, None, order, refs[:-5], keep),
        )

    outs = [jax.ShapeDtypeStruct((2, 4, T, D), BF16), jax.ShapeDtypeStruct((4, T, D), BF16)]
    specs = ([IN_VMEM, IN_VMEM, ANY_SPACE], [ANY_SPACE, IN_VMEM])
    scratch = _spread_scratch(T, D, (EL, slots, D)) + LINE_SEMS
    return _comm(kernel, outs, scratch, collective_id, specs)(rows, slot, out_rows)


def _line_sum_scratch(T, D):
    return [pltpu.VMEM((4, T, D), BF16), pltpu.VMEM((4, T, D), BF16), pltpu.VMEM((2, 4, T, D), BF16)]


def column_scatter(x, collective_id):
    T, D = x.shape[2:]

    def kernel(x_ref, o_ref, work, c_buf, z_buf, *sems):
        u, z = lax.axis_index("uly"), lax.axis_index("blk")
        _greet(u, z, (1,), line=True)

        def finish():
            o_ref[...] = work[3]

        _run(_line_sum_part(u, z, lambda c, level: x_ref.at[c, level], work, (c_buf, z_buf), sems, T, finish))

    scratch = _line_sum_scratch(T, D) + LINE_SUM_SEMS
    return _comm(kernel, jax.ShapeDtypeStruct((T, D), BF16), scratch, collective_id, ([ANY_SPACE], IN_VMEM))(x)


def _plane_sum_scratch(rows, cols):
    return [pltpu.VMEM((2, 2, rows, cols), BF16), pltpu.VMEM((2, 2, rows, cols), BF16), pltpu.VMEM((2, rows, cols), BF16)]


def key_value_sums(dk, dv, x, inner, collective_id):
    T, D = x.shape[1:]
    L, C = dk.shape[1:]
    R = inner.shape[0] // 5

    def kernel(
        k_ref, v_ref, x_ref, s_ref, k_out, v_out, x_out, s_out, work, p_buf, q_buf, x_work, z_buf, buf, total, k_buf, *sems
    ):
        u, z = lax.axis_index("uly"), lax.axis_index("blk")
        here, chip = (u, z), u // 2
        _greet(u, z, (2, 4, 6), others=[to for to, c, k in _column_peers(u, z)])
        load, z_send, z_recv, k_send, k_recv = sems[7:]
        order = tuple(reversed(_line_order(z)))

        def keys(v):
            return total.at[pl.ds(pl.multiple_of((v // 2 + 1) * R, R), R)]

        def tell():
            for i, bit in enumerate((2, 4, 6)):
                _send(keys(u ^ bit), k_buf.at[i], k_send.at[i], k_recv.at[i], (u ^ bit, z))

        def finish():
            k_out[...] = work[0, 0]
            v_out[...] = work[1, 0]

        def line():
            copies = [pltpu.make_async_copy(x_ref.at[order[i]], x_work.at[i], load.at[i]) for i in range(4)]
            for copy in copies:
                copy.start()
            for copy in copies:
                copy.wait()
            for i in range(4):
                _line_end(u, z, order[i], i, x_work.at[i], z_buf, (z_send, z_recv), T)
                yield
            x_out[...] = x_work[3]
            for i in range(3):
                _sent(x_work.at[i], z_send.at[i], (u, z))

        _run(
            _plane_sum_part(
                u, z, lambda h, v: (k_ref, v_ref)[h].at[v // 2], work, (p_buf, q_buf), sems[:5], L, finish
            ),
            line(),
            _column_sum_part(u, z, s_ref, total, buf, sems[5:7], tell),
            order=KV_ORDER,
        )
        value = keys(u)[...]
        for i, bit in enumerate((2, 4, 6)):
            _expect(k_buf.at[i], k_recv.at[i], here)
            value = value + k_buf[i]
            _sent(k_buf.at[i], k_send.at[i], here)
        s_out[pl.ds(0, R), :] = total[pl.ds(0, R), :]
        s_out[pl.ds(R, R), :] = value

    outs = [jax.ShapeDtypeStruct((L, C), BF16)] * 2 + [jax.ShapeDtypeStruct((T, D), BF16)]
    outs += [jax.ShapeDtypeStruct((2 * R, 128), F32)]
    scratch = _plane_sum_scratch(L, C) + [pltpu.VMEM((4, T, D), BF16), pltpu.VMEM((2, 4, T, D), BF16)]
    scratch += [pltpu.VMEM((7,) + inner.shape, F32), pltpu.VMEM(inner.shape, F32), pltpu.VMEM((3, R, 128), F32)]
    scratch += PLANE_SUM_SEMS + [DMA((7,)), DMA((7,)), DMA((4,)), DMA((4,)), DMA((2, 4)), DMA((3,)), DMA((3,))]
    specs = ([ANY_SPACE] * 3 + [IN_VMEM], [IN_VMEM] * 4)
    return _comm(kernel, outs, scratch, collective_id, specs)(dk, dv, x, inner)


def leave(x, weights, smalls, collective_id):
    n = len(smalls)
    T, D = x.shape[2:]
    rows, W = weights.shape[2:]
    R, C = rows // 4, W // 3

    def kernel(x_ref, w_ref, *refs):
        small_in, (o_ref, w_out), small_out = refs[:n], refs[n : n + 2], refs[n + 2 : 2 * n + 2]
        work, c_buf, z_buf, w_work, wp_buf, wq_buf = refs[2 * n + 2 : 2 * n + 8]
        sems = refs[2 * n + 8 :]
        u, z = lax.axis_index("uly"), lax.axis_index("blk")
        here, core, chip = (u, z), u % 2, u // 2
        column = _column_peers(u, z)
        _greet(u, z, range(1, 8), others=[to for to, c, k in column if k])
        t_send, t_recv = sems[10:12]
        group = 2 * z + core

        def finish():
            o_ref[...] = work[3]

        def cut(j, c, level):
            return w_work.at[c, 0, pl.ds(pl.multiple_of(level * R, R), R), pl.ds(j * C, C)]

        def slot(j, g):
            return w_out.at[j, :, pl.ds(pl.multiple_of(g * C, C), C)]

        def deal():
            for i, (to, c, k) in enumerate(column):
                for j in range(3):
                    _send(cut(j, core ^ c, z ^ k), slot(j, group), t_send.at[i, j], t_recv.at[i, j], to)
            for j in range(3):
                slot(j, group)[...] = cut(j, core, z)[...]

        _run(
            _plane_sum_part(u, z, lambda h, v: w_ref.at[v // 2, h], w_work, (wp_buf, wq_buf), sems[5:10], rows, deal),
            _line_sum_part(u, z, lambda c, level: x_ref.at[c, level], work, (c_buf, z_buf), sems[:5], T, finish),
            _small_part(u, z, small_in, small_out, sems[12:]),
            order=LEAVE_ORDER,
        )
        for i, (to, c, k) in enumerate(column):
            for j in range(3):
                _expect(slot(j, 2 * (z ^ k) + (core ^ c)), t_recv.at[i, j], here)
                _sent(cut(j, core ^ c, z ^ k), t_send.at[i, j], here)

    outs = [jax.ShapeDtypeStruct((T, D), BF16), jax.ShapeDtypeStruct((3, R, 8 * C), BF16)]
    outs += [jax.ShapeDtypeStruct((8, 4) + x.shape, x.dtype) for x in smalls]
    scratch = _line_sum_scratch(T, D) + _plane_sum_scratch(rows, W) + LINE_SUM_SEMS + PLANE_SUM_SEMS
    scratch += [DMA((7, 3)), DMA((7, 3))] + _small_sems(n)
    specs = ([ANY_SPACE] * 2 + [IN_VMEM] * n, [IN_VMEM] * 2 + [ANY_SPACE] * n)
    return _comm(kernel, outs, scratch, collective_id, specs)(x, weights, *smalls)


def _finish_kernel(
    h_ref, r_ref, rg_ref, first_ref, sum_ref, wq_ref, wk_ref, wv_ref, dw_ref, do_ref, gain_ref, out_ref, hg_ref, ag_ref, *dws
):
    out_ref[...] = (r_ref[...] + sum_ref[...].astype(F32)).astype(BF16)
    hidden, weighted = h_ref[...].astype(F32), first_ref[...].astype(F32)
    scale = norm_scale(hidden)
    mean = jnp.mean(weighted * hidden, axis=-1, keepdims=True)
    hg_ref[...] = rg_ref[...] + scale * weighted - hidden * (scale * scale * scale) * mean
    gain = gain_ref[...].astype(F32)[:, :1]
    total = jnp.zeros(dws[0].shape, F32)
    for j, ref in enumerate((wq_ref, wk_ref, wv_ref)):
        grad = dw_ref[j].astype(F32)
        total = total + grad * ref[...].astype(F32)
        dws[j][...] = grad * gain
    ag_ref[...] = jnp.sum(total, axis=1, keepdims=True)
    dws[3][...] = do_ref[...].astype(F32)


def finish(hidden, residual, residual_grad, first_weighted, out_sum, weights, weight_sum, out_weight_grad, gains):
    T, D = hidden.shape
    R = gains.shape[0]
    steps = 4 if R % 64 == 0 else 1

    def rows(count, width):
        return pl.BlockSpec((count // steps, width), lambda i: (i, 0))

    tokens, dense = rows(T, D), rows(R, D)
    return pl.pallas_call(
        _finish_kernel,
        out_shape=[
            jax.ShapeDtypeStruct((T, D), BF16),
            jax.ShapeDtypeStruct((T, D), F32),
            jax.ShapeDtypeStruct((R, 1), F32),
        ]
        + [jax.ShapeDtypeStruct((R, D), F32)] * 4,
        grid=(steps,),
        in_specs=[tokens] * 5
        + [dense] * 3
        + [pl.BlockSpec((3, R // steps, D), lambda i: (0, i, 0)), dense, rows(R, 4)],
        out_specs=[tokens, tokens, rows(R, 1)] + [dense] * 4,
        compiler_params=pltpu.CompilerParams(vmem_limit_bytes=VMEM_BYTES),
        cost_estimate=pl.CostEstimate(flops=20 * T * D, bytes_accessed=24 * T * D, transcendentals=0),
    )(hidden, residual, residual_grad, first_weighted, out_sum, *weights, weight_sum, out_weight_grad, gains)


class _Jobs:
    def __init__(self, load, compute):
        self.load, self.compute = load, compute
        self.queue, self.count, self.ready = [], 0, None

    def add(self, *jobs):
        self.queue += jobs

    def _next(self):
        if not self.queue:
            return None
        job = (self.count, self.queue.pop(0))
        self.count += 1
        self.load(*job, True)
        return job

    def run(self, number=1):
        for _ in range(number):
            now = self.ready or self._next()
            if now is None:
                return
            self.ready = self._next()
            self.load(*now, False)
            self.compute(*now)


def _gather_pick_kernel(
    x_ref, here_g, g0, g1, g2, g3, slot_ref, router_ref, o_ref, xr_ref, gr_ref, gate_ref, other_here, other_g, pick, in_buf, out_buf, in_sem, out_sem, *sems, width
):
    own_sem, z_send, z_recv, p_send, p_recv, c_send, c_recv, g_send, g_recv, h_send, h_recv = sems
    own_g = (g0, g1, g2, g3)
    u, z = lax.axis_index("uly"), lax.axis_index("blk")
    core, chip = u % 2, u // 2
    other = 1 - core
    T, D = x_ref.shape
    experts, group = slot_ref.shape[1:]
    slots = out_buf.shape[2]
    half = T // 2
    halves = (pl.ds(0, half), pl.ds(half, half))
    here = (u, z)
    _greet(u, z, (1, 2, 4), line=True)
    own = pltpu.make_async_copy(x_ref, o_ref.at[u * DEPTH + z], own_sem)
    own.start()
    order = _line_order(z)

    def block(who, level):
        return o_ref.at[who * DEPTH + level]

    def part(who, level, h):
        return o_ref.at[who * DEPTH + level, halves[h]]

    def load(n, job, start):
        source, level, which = job
        steps = (0, jnp.where(which == 0, 1, 2), jnp.where(which == 0, 2, 1), 3)
        for k in range(4):
            p = chip ^ steps[k]
            if source == "x":
                ref = o_ref.at[(2 * p + which) * DEPTH + level]
            elif source == 0:
                ref = (here_g if which is core else other_here).at[p]
            else:
                ref = (own_g[k] if which is core else other_g.at[k]).at[source - 1]
            rows = pl.ds(pl.multiple_of(p * T, T), T)
            copy = pltpu.make_async_copy(ref, in_buf.at[n % 2, rows], in_sem.at[n % 2, k])
            copy.start() if start else copy.wait()

    def out_copy(n, target, at):
        return pltpu.make_async_copy(out_buf.at[n % 2], target.at[:, at], out_sem.at[n % 2])

    sent = {}

    def compute(n, job):
        source, level, which = job
        at = 2 * level + which
        rows_in, rows_out = in_buf.at[n % 2], out_buf.at[n % 2]
        row = lax.broadcasted_iota(jnp.int32, (slots, group), 0)
        if source != "x":
            picks = [jnp.where(slot_ref[at, e : e + 1, :] == row, 1.0, 0.0).astype(BF16) for e in range(experts)]
            pick[at] = jnp.concatenate(picks, axis=0)
        else:
            logits = dot(rows_in[...], router_ref[...])
            powers = jnp.exp(logits - jnp.max(logits, axis=1, keepdims=True))
            chances = powers / jnp.sum(powers, axis=1, keepdims=True)
            high = chances.astype(BF16)
            low = (chances - high.astype(F32)).astype(BF16)
            gates = dot(pick[at], jnp.concatenate([high, low], axis=1))
            for e in range(experts):
                gate_ref[e, at] = gates[e * slots : (e + 1) * slots]
        if n >= 2:
            sent.pop(n - 2).wait()

        def step(i, _):
            cols = pl.ds(pl.multiple_of(i * width, width), width)
            rows = dot(pick[at], rows_in[:, cols]).astype(BF16)
            for e in range(experts):
                rows_out[e, :, cols] = rows[e * slots : (e + 1) * slots]
            return 0

        lax.fori_loop(0, D // width, step, 0)
        sent[n] = out_copy(n, xr_ref if source == "x" else gr_ref, at)
        sent[n].start()

    jobs = _Jobs(load, compute)
    jobs.add(*[(j, (z + j) % 4, core) for j in range(4)])

    def along(level, source, step):
        @pl.when((z > 0) & (level >= z))
        def _():
            step(source, 0, level, (u, z - 1))

        @pl.when((z < DEPTH - 1) & (level <= z))
        def _():
            step(source, 1, level, (u, z + 1))

    def go(source, way, level, to):
        _send(source, block(u, level), z_send.at[way, level], z_recv.at[level], to)

    def gone(source, way, level, to):
        _sent(source, z_send.at[way, level], here)

    sources = [x_ref] + [block(u, order[i]) for i in range(1, 4)]

    def arrive(i):
        level = order[i]
        if i:
            _expect(block(u, level), z_recv.at[level], here)
        along(level, sources[i], go)
        for way, bits in enumerate((FIRST, THEN)):
            for h in range(2):
                cut = sources[i].at[halves[h]]
                _send(cut, part(u, level, h), p_send.at[level, h, way], p_recv.at[level, h, way], (u ^ bits[h], z))
        _send(sources[i], block(u, level), c_send.at[level, 0], c_recv.at[level, 0], (u ^ 1, z))

    def onward(i):
        level = order[i]
        for h in range(2):
            near = part(u ^ FIRST[h], level, h)
            _expect(near, p_recv.at[level, h, 0], here)
            _send(near, near, p_send.at[level, h, 2], p_recv.at[level, h, 2], (u ^ THEN[h], z))

    def share(i):
        level = order[i]
        for h in range(2):
            _expect(part(u ^ THEN[h], level, h), p_recv.at[level, h, 1], here)
            _expect(part(u ^ 6, level, h), p_recv.at[level, h, 2], here)
        for k, bit in enumerate((2, 4, 6)):
            ref = block(u ^ bit, level)
            _send(ref, ref, c_send.at[level, k + 1], c_recv.at[level, k + 1], (u ^ 1, z))
        jobs.add(("x", level, core))

    def received(i):
        level = order[i]
        for k, bit in enumerate((0, 2, 4, 6)):
            _expect(block(u ^ 1 ^ bit, level), c_recv.at[level, k], here)
        jobs.add(("x", level, other))

    arrive(0)
    _send(here_g, other_here, h_send, h_recv, (u ^ 1, z))
    for k in range(4):
        _send(own_g[k], other_g.at[k], g_send.at[k], g_recv.at[k], (u ^ 1, z))
    jobs.run(2)
    onward(0)
    jobs.run(1)
    arrive(1)
    _expect(other_here, h_recv, here)
    for k in range(4):
        _expect(other_g.at[k], g_recv.at[k], here)
    jobs.add(*[(j, (z + j) % 4, other) for j in range(4)])
    jobs.run(2)
    own.wait()
    share(0)
    jobs.run(2)
    onward(1)
    arrive(2)
    received(0)
    jobs.run(2)
    arrive(3)
    share(1)
    received(1)
    jobs.run(1)
    onward(2)
    jobs.run(2)
    share(2)
    received(2)
    jobs.run(1)
    onward(3)
    jobs.run(2)
    share(3)
    received(3)
    jobs.run(16)
    for i in range(4):
        level = order[i]
        along(level, sources[i], gone)
        for h in range(2):
            for k in range(3):
                _sent(part(u, level, h), p_send.at[level, h, k], here)
        for k in range(4):
            _sent(block(u, level), c_send.at[level, k], here)
    _sent(other_here, h_send, here)
    for k in range(4):
        _sent(other_g.at[k], g_send.at[k], here)
    for copy in sent.values():
        copy.wait()


def gather_pick(x, here_g, g, slot, router, slots, collective_id):
    T, D = x.shape
    groups, EL, group = slot.shape
    picked = jax.ShapeDtypeStruct((EL, groups, slots, D), BF16)
    outs = [
        jax.ShapeDtypeStruct((32, T, D), BF16),
        picked,
        picked,
        jax.ShapeDtypeStruct((EL, groups, slots, 128), F32),
        jax.ShapeDtypeStruct((4, T, D), BF16),
        jax.ShapeDtypeStruct((4, 3, T, D), BF16),
    ]
    scratch = [
        pltpu.VMEM((groups, EL * slots, group), BF16),
        pltpu.VMEM((2, group, D), BF16),
        pltpu.VMEM((2, EL, slots, D), BF16),
        DMA((2, 4)),
        DMA((2,)),
        DMA,
        DMA((2, 4)),
        DMA((4,)),
        DMA((4, 2, 3)),
        DMA((4, 2, 3)),
        DMA((4, 4)),
        DMA((4, 4)),
        DMA((4,)),
        DMA((4,)),
        DMA,
        DMA,
    ]
    specs = ([IN_VMEM] + [ANY_SPACE] * 5 + [IN_VMEM] * 2, [ANY_SPACE] * 3 + [IN_VMEM] + [ANY_SPACE] * 2)
    kernel = functools.partial(_gather_pick_kernel, width=PICK_WIDTH)
    out, xr, gr, gates, *_ = _comm(kernel, outs, scratch, collective_id, specs)(x, here_g, *g, slot, router)
    return out.reshape(32 * T, D), xr, gr, gates


def _tree_sum_steps(u, z, own, bufs, sems, T):
    c_buf, p_buf, q_buf = bufs
    c_send, c_recv, p_send, p_recv, q_send, q_recv = sems
    here = (u, z)
    half = T // 2
    halves = (pl.ds(0, half), pl.ds(half, half))

    def to_sibling(i, k, ref):
        _send(ref, c_buf.at[i, k], c_send.at[i, k], c_recv.at[i, k], (u ^ 1, z))

    def add_core(i):
        for k in (3, 2, 1, 0):
            _expect(c_buf.at[i, k], c_recv.at[i, k], here)
            _accumulate(own(i, k), c_buf.at[i, k], T)
            for h in range(2):
                if k and (k == 3 or CHIPS[k] == THEN[h]):
                    j = 1 if k == 3 else 0
                    part = own(i, k).at[halves[h]]
                    _send(part, p_buf.at[i, h, j], p_send.at[i, h, j], p_recv.at[i, h, j], (u ^ THEN[h], z))

    def add_far(i):
        for h in range(2):
            part = own(i, CHIPS.index(FIRST[h])).at[halves[h]]
            _expect(p_buf.at[i, h, 1], p_recv.at[i, h, 1], here)
            _accumulate(part, p_buf.at[i, h, 1], half)
            _send(part, q_buf.at[i, h], q_send.at[i, h], q_recv.at[i, h], (u ^ FIRST[h], z))

    def add_near(i):
        for h in range(2):
            _expect(p_buf.at[i, h, 0], p_recv.at[i, h, 0], here)
            _accumulate(own(i, 0).at[halves[h]], p_buf.at[i, h, 0], half)

    def add_then(i):
        for h in range(2):
            _expect(q_buf.at[i, h], q_recv.at[i, h], here)
            _accumulate(own(i, 0).at[halves[h]], q_buf.at[i, h], half)

    def finish():
        for i in range(4):
            for k in range(4):
                _sent(c_buf.at[i, k], c_send.at[i, k], here)
            for h in range(2):
                for j in range(2):
                    _sent(p_buf.at[i, h, j], p_send.at[i, h, j], here)
                _sent(q_buf.at[i, h], q_send.at[i, h], here)

    return to_sibling, add_core, add_far, add_near, add_then, finish


def _line_end(u, z, level, i, part, z_buf, sems, rows):
    z_send, z_recv = sems
    here = (u, z)

    @pl.when((level >= z) & (z > 0))
    def _():
        _expect(z_buf.at[0, level], z_recv.at[0, level], here)
        _accumulate(part, z_buf.at[0, level], rows)

    @pl.when((level <= z) & (z < DEPTH - 1))
    def _():
        _expect(z_buf.at[1, level], z_recv.at[1, level], here)
        _accumulate(part, z_buf.at[1, level], rows)

    if i < 3:

        @pl.when(level > z)
        def _():
            _send(part, z_buf.at[0, level], z_send.at[i], z_recv.at[0, level], (u, z + 1))

        @pl.when(level < z)
        def _():
            _send(part, z_buf.at[1, level], z_send.at[i], z_recv.at[1, level], (u, z - 1))


def _spread_part(u, z, slot_ref, source, gg_ref, order, refs, level_done, later=lambda i: None):
    work, c_buf, p_buf, q_buf, side, in_buf, in_sem = refs[:7]
    core, chip = u % 2, u // 2
    other = 1 - core
    _, group, experts = slot_ref.shape
    slots, D = source.shape[2:]
    total = experts * slots
    T = group // 4

    def place(k):
        return pl.ds(pl.multiple_of((chip ^ (CHIPS[k] // 2)) * T, T), T)

    def own(i, k):
        return work.at[i, place(k)]

    to_sibling, add_core, add_far, add_near, add_then, finish = _tree_sum_steps(
        u, z, own, (c_buf, p_buf, q_buf), refs[7:], T
    )
    lane = lax.broadcasted_iota(jnp.int32, (experts, total), 1)
    which = lax.broadcasted_iota(jnp.int32, (experts, total), 0)
    choose = jnp.where((lane >= which * slots) & (lane < (which + 1) * slots), 1.0, 0.0).astype(BF16)
    offset = lane[:1] - jnp.sum(jnp.where(lane >= (which + 1) * slots, slots, 0), axis=0, keepdims=True)
    offset = offset.astype(F32)
    column = lax.broadcasted_iota(jnp.int32, (slots, 128), 1)

    def load(n, job, start):
        i, c = job
        copy = pltpu.make_async_copy(source.at[:, 2 * order[i] + c], in_buf.at[n % 2], in_sem.at[n % 2])
        copy.start() if start else copy.wait()

    def compute(n, job):
        i, c = job
        at = 2 * order[i] + c
        mine = dot(slot_ref[at].astype(BF16), choose)
        pick = jnp.where(mine == offset, 1.0, 0.0).astype(BF16)
        rows_in = in_buf.at[n % 2]
        target = work.at[i] if c is core else side.at[i]
        if gg_ref is not None:
            grads = [jnp.where(column == u * experts + e, gg_ref[e, at], 0.0).astype(BF16) for e in range(experts)]
            target[:, pl.ds(D, 128)] = dot(pick, jnp.concatenate(grads, axis=0)).astype(BF16)

        def step(j, _):
            cols = pl.ds(pl.multiple_of(j * SPREAD_WIDTH, SPREAD_WIDTH), SPREAD_WIDTH)
            rows = jnp.concatenate([rows_in[e, :, cols] for e in range(experts)], axis=0)
            target[:, cols] = dot(pick, rows).astype(BF16)
            return 0

        lax.fori_loop(0, D // SPREAD_WIDTH, step, 0)
        if c is not core:
            for k in (3, 2, 1, 0):
                to_sibling(i, k, side.at[i, place(k)])

    def end(i):
        add_then(i)
        level_done(i, own(i, 0))

    jobs = _Jobs(load, compute)
    for i in range(4):
        jobs.add((i, other), (i, core))
    jobs.run(2)
    add_core(0)
    yield
    jobs.run(2)
    add_far(0)
    add_core(1)
    yield
    add_near(0)
    jobs.run(2)
    add_far(1)
    add_core(2)
    yield
    end(0)
    later(0)
    add_near(1)
    jobs.run(2)
    add_far(2)
    add_core(3)
    yield
    end(1)
    later(1)
    add_near(2)
    add_far(3)
    yield
    end(2)
    later(2)
    add_near(3)
    yield
    end(3)
    later(3)
    yield
    finish()


def _spread_scratch(T, W, rows_shape):
    half = T // 2
    return [
        pltpu.VMEM((4, 4 * T, W), BF16),
        pltpu.VMEM((4, 4, T, W), BF16),
        pltpu.VMEM((4, 2, 2, half, W), BF16),
        pltpu.VMEM((4, 2, half, W), BF16),
        pltpu.VMEM((4, 4 * T, W), BF16),
        pltpu.VMEM((2,) + rows_shape, BF16),
        DMA((2,)),
        DMA((4, 4)),
        DMA((4, 4)),
        DMA((4, 2, 2)),
        DMA((4, 2, 2)),
        DMA((4, 2)),
        DMA((4, 2)),
    ]


def spread_scatter(slot, gate_grads, entry_rows, collective_id):
    groups, group, EL = slot.shape
    slots, D = entry_rows.shape[2:]
    T, W = group // 4, D + 128

    def kernel(slot_ref, gg_ref, entry_ref, o_ref, z_buf, z_send, z_recv, *refs):
        u, z = lax.axis_index("uly"), lax.axis_index("blk")
        order = tuple(reversed(_line_order(z)))
        parts = []

        def done(i, part):
            parts.append(part)

        def line(i):
            _line_end(u, z, order[i], i, parts[i], z_buf, (z_send, z_recv), T)

        _greet(u, z, (1, 2, 4), line=True)
        _run(_spread_part(u, z, slot_ref, entry_ref, gg_ref, order, refs, done, line))
        o_ref[...] = parts[3][...]
        for i in range(3):
            _sent(parts[i], z_send.at[i], (u, z))

    scratch = [pltpu.VMEM((2, 4, T, W), BF16), DMA((4,)), DMA((2, 4))] + _spread_scratch(T, W, (EL, slots, D))
    specs = ([IN_VMEM, IN_VMEM, ANY_SPACE], IN_VMEM)
    out = jax.ShapeDtypeStruct((T, W), BF16)
    return _comm(kernel, out, scratch, collective_id, specs)(slot, gate_grads, entry_rows)


def slots_of(chosen):
    count = chosen.shape[-1]
    before = (jnp.arange(count)[:, None] < jnp.arange(count)[None, :]).astype(BF16)
    earlier = jnp.einsum("abs,st->abt", chosen.astype(BF16), before, preferred_element_type=F32)
    return jnp.where(chosen, earlier.astype(jnp.int32), -1)


class Slice:
    def __init__(self, U, Z, T, D):
        self.U, self.Z, self.T, self.D = U, Z, T, D
        self.u, self.z = lax.axis_index("uly"), lax.axis_index("blk")
        self.C = D // 8
        self.L = 8 * T
        self.group = 2 * self.z + self.u % 2
        self.first_block, self.block_step = 8 * (self.u // 2), 1
        self.rows = ATTEND_ROWS

    def enter(self, hidden, weights, gains, out_weight, router, routes, out_grad):
        rows, weights, packs, routes, self.here = enter(hidden, weights, gains, router, routes, out_grad, 1)
        there = [((2 * ((z + u // 2) % 4) + u % 2), u // 2) for u in range(8) for z in range(4)]
        self.forth = [(i, 4 * u + z) for i, (u, z) in enumerate(there)]
        rows, mine = lax.optimization_barrier((rows, self.permute(out_weight, self.forth)))
        self.out_parts = [mine] + [self.permute(mine, self.across(bit)) for bit in (2, 4, 6)]
        self.parts = [((self.u // 2) ^ k) - self.z + 4 for k in range(4)]
        self.parts = [p % 4 for p in self.parts]
        return (
            rows.reshape(self.L, self.D),
            weights.reshape(self.D, 3 * self.C),
            packs.reshape(self.D, -1),
            routes,
        )

    def permute(self, x, pairs):
        return lax.ppermute(x, ALL, pairs)

    def across(self, bit):
        return [(i, i ^ (4 * bit)) for i in range(32)]

    def sequence(self, key, value, squares, upstream):
        keys, values, own, stats, k_stat = plane_pair(key, value, upstream, squares.reshape(-1, 128), 4)
        own, *self.out_parts = lax.optimization_barrier((own, *self.out_parts))
        first = [(i, i ^ (8 if i // 4 % 2 == 0 else 16)) for i in range(32)]
        self.then = [(i, i ^ (16 if i // 4 % 2 == 0 else 8)) for i in range(32)]
        self.upstream = (own, self.permute(own, first))
        return keys.reshape(-1, self.C), values.reshape(-1, self.C), stats.reshape(2, -1, 128), k_stat.reshape(-1, 128)

    def heads_to_rows(self, x):
        x, own, near, *self.prepared = lax.optimization_barrier((x, *self.upstream, *self.prepared))
        self.upstream = (own, near, self.permute(own, self.then), self.permute(near, self.then))
        return column_scatter(x.reshape(2, 4, self.T, self.D), 5)

    def prepare(self, routes, EL, router):
        T = self.T
        chosen = jnp.any(routes[None] == (self.u * EL + jnp.arange(EL, dtype=jnp.int32))[:, None, None, None, None], axis=3)
        chosen = chosen.reshape(EL, 4, 2, 4, T).transpose(3, 2, 0, 1, 4).reshape(8, EL, 4 * T)
        slot = slots_of(chosen)
        self.prepared = (slot, slot.transpose(0, 2, 1), router)

    def experts(self, second_low, weights):
        EL, D = weights.shape[0], self.D
        slots = -(-4 * CAP // 16) * 16
        slot, self.slot, router = self.prepared
        second_all, xr, gr, gates = gather_pick(second_low, self.here, self.upstream, slot, router, slots, 7)
        flat, cut = (EL, 8 * slots, -1), (EL, 8, slots, -1)
        out_rows, entry_rows, self.expert_grads, gate_grads = run_experts(
            xr.reshape(flat), gr.reshape(flat), gates.reshape(flat), weights, 8 * slots
        )
        self.out_rows = out_rows.reshape(cut)
        return second_all, spread_scatter(self.slot, gate_grads.reshape(cut), entry_rows.reshape(cut), 8)

    def rows_to_heads(self, x):
        rows, self.out_line = column_gather(x, self.slot, self.out_rows, 6)
        return rows.reshape(self.L, self.D), self.expert_grads

    def sequence_sums(self, dk, dv, out_part, q_inner, k_inner):
        cut = (4, self.L, self.C)
        inner = jnp.concatenate([q_inner, k_inner.reshape(-1, 128)], axis=0)
        dk, dv, out_sum, inner = key_value_sums(dk.reshape(cut), dv.reshape(cut), self.out_line, inner, 10)
        parts = out_part.reshape(4, -1, self.D)
        mine, *others = [lax.dynamic_index_in_dim(parts, p, 0, False) for p in self.parts]
        dk, *others = lax.optimization_barrier((dk, *others))
        self.out_terms = [mine] + [self.permute(x, self.across(bit)) for x, bit in zip(others, (2, 4, 6))]
        return dk, dv, out_sum, inner.reshape(2, -1, 128)

    def leave(self, first_part, weight_part, logit_grad, ffn_part, head_parts):
        T, R = self.T, self.D // 32
        first_part, *terms = lax.optimization_barrier((first_part, *self.out_terms))
        out_grad = sum(x.astype(F32) for x in terms).astype(BF16)
        out_grad = self.permute(out_grad, [(b, a) for a, b in self.forth])
        thin = jnp.concatenate([ffn_part.reshape(-1, 128), head_parts.reshape(-1, 128)], axis=0)
        wide = self.D // 128
        used = thin.shape[0]
        thin = jnp.pad(thin, ((0, -used % 8), (0, 0)))
        first, weights, logit_all, thin = leave(
            first_part.reshape(2, 4, T, self.D),
            weight_part.reshape(4, 2, 4 * R, 3 * self.C),
            [logit_grad.reshape(T // 2, 2 * EXPERTS), thin],
            11,
        )
        ffn = lax.dynamic_slice_in_dim(
            jnp.sum(thin[:, :, :wide], axis=(0, 1)).reshape(self.D), (self.u * 4 + self.z) * R, R, 0
        )
        mine = lax.dynamic_index_in_dim(thin.reshape(4, 2, 4, -1, 128), self.u % 2, 1, False)
        mine = lax.dynamic_index_in_dim(mine, self.u // 2, 1, False)
        heads = jnp.sum(mine[:, wide:used], axis=0).reshape(2, self.C)
        heads = lax.dynamic_slice_in_dim(heads, self.z * R, R, 1)
        return first, weights, out_grad, logit_all.reshape(32 * T, EXPERTS), ffn, heads


class General:
    def __init__(self, U, Z, T, D):
        self.U, self.Z, self.T, self.D = U, Z, T, D
        self.u, self.z = lax.axis_index("uly"), lax.axis_index("blk")
        self.C = D // U
        self.L = U * T
        self.group = self.u
        self.parts = range(4)
        self.first_block, self.block_step = self.z, Z
        self.rows = T

    def gather(self, x):
        return lax.all_gather(x, ALL, axis=0, tiled=True)

    def scatter_wide(self, x):
        return lax.psum_scatter(x, ALL, scatter_dimension=0, tiled=True)

    def enter(self, hidden, weights, gains, out_weight, router, routes, out_grad):
        U, R = self.U, router.shape[0]
        gains, hidden = gains.astype(F32), hidden.astype(F32)
        scaled = jnp.stack([(w.astype(F32) * gains[:, :1]).astype(BF16) for w in weights])
        pack = jnp.concatenate(_packed(router, gains), axis=1)
        rows = (hidden * norm_scale(hidden)).astype(BF16)
        self.out_parts = jnp.split(lax.all_gather(out_weight, "blk", axis=0, tiled=True), 4)
        swapped = lax.all_to_all(scaled.transpose(1, 0, 2).reshape(R, 3, U, self.C), "uly", split_axis=2, concat_axis=0, tiled=True)
        weights = lax.all_gather(swapped.reshape(U, R, 3 * self.C), "blk", axis=1, tiled=True)
        return (
            self.rows_all(rows),
            weights.reshape(self.D, 3 * self.C),
            self.gather(pack),
            self.gather(routes[None]).reshape((U, self.Z) + routes.shape),
        )

    def sequence(self, key, value, squares, upstream):
        self.upstream = upstream
        pair = jnp.stack([key, value]).reshape(2, self.U, self.T, self.C)
        pair = lax.all_gather(pair, "blk", axis=2, tiled=False).reshape(2, -1, self.C)
        stats = lax.psum(squares, "uly")
        k_stat = lax.all_gather(stats[1].reshape(self.U, -1, 128), "blk", axis=1, tiled=False).reshape(-1, 128)
        return pair[0], pair[1], stats, k_stat

    def heads_to_rows(self, x):
        return self.rows_sum(x)

    def rows_sum(self, x):
        return lax.psum_scatter(x, "uly", scatter_dimension=0, tiled=True)

    def rows_all(self, x):
        return lax.all_gather(x, "uly", axis=0, tiled=True)

    def prepare(self, routes, EL, router):
        self.prepared = (routes, router)

    def experts(self, second_low, weights):
        EL, D = weights.shape[0], self.D
        routes, router = self.prepared
        second_all, upstream_all = self.gather(second_low), self.gather(self.upstream)
        N = upstream_all.shape[0]
        group = min(512, N)
        groups = N // group
        slots = -(-(group // self.T * CAP) // 16) * 16
        rows = groups * slots
        own_first = self.u * EL
        chosen = jnp.any(routes[None] == (own_first + jnp.arange(EL, dtype=jnp.int32))[:, None, None, None, None], axis=3)
        slot = slots_of(chosen.reshape(EL, groups, group)).reshape(EL, N)
        entry_in, upstream_in, gates = pick_rows(slot, router, second_all, upstream_all, group, slots)
        flat, split = (EL, rows, -1), (EL, groups, slots, -1)
        out_rows, entry_rows, self.expert_grads, gate_grads = run_experts(
            entry_in.reshape(flat), upstream_in.reshape(flat), gates.reshape(flat), weights, min(8, groups) * slots
        )
        out_part, entry_part = spread_rows(
            own_first.astype(jnp.int32)[None],
            slot.T,
            gate_grads.reshape(split),
            out_rows.reshape(split),
            entry_rows.reshape(split),
            group,
        )
        self.out_sum = self.scatter_wide(out_part)
        return second_all, self.scatter_wide(entry_part)

    def rows_to_heads(self, x):
        return self.rows_all(x), self.expert_grads

    def sequence_sums(self, dk, dv, out_part, q_inner, k_inner):
        pair = jnp.stack([dk, dv]).reshape(2, self.U, self.Z, self.T, self.C)
        pair = lax.psum_scatter(pair, "blk", scatter_dimension=2, tiled=True).reshape(2, self.L, self.C)
        k_inner = lax.psum_scatter(
            k_inner.reshape(self.U, self.Z, -1, 128), "blk", scatter_dimension=1, tiled=True
        ).reshape(-1, 128)
        inner = lax.psum(jnp.stack([q_inner, k_inner]), "uly")
        self.out_grad = lax.psum_scatter(out_part, "blk", scatter_dimension=0, tiled=True)
        return pair[0], pair[1], self.out_sum, inner

    def leave(self, first_part, weight_part, logit_grad, ffn_part, head_parts):
        U, R = self.U, self.D // (self.U * self.Z)
        part = weight_part.reshape(U, self.Z * R, 3 * self.C)
        part = lax.psum_scatter(part, "blk", scatter_dimension=1, tiled=True)
        part = lax.all_to_all(part, "uly", split_axis=0, concat_axis=0, tiled=True)
        weights = part.reshape(U, R, 3, self.C).transpose(2, 1, 0, 3).reshape(3, R, self.D)
        heads = lax.psum_scatter(head_parts, "blk", scatter_dimension=1, tiled=True)
        first = self.rows_sum(first_part)
        return first, weights, self.out_grad, self.gather(logit_grad), self.scatter_wide(ffn_part), heads


def _row_limits(doc_ref, first, rows):
    position = first + lax.broadcasted_iota(jnp.int32, (rows, 1), 0)
    start = jnp.zeros_like(position)
    lowest = jnp.int32(0)
    for d in range(doc_ref.shape[0]):
        begin = doc_ref[d]
        start = jnp.where(begin <= position, jnp.maximum(start, begin), start)
        lowest = jnp.where(begin <= first, jnp.maximum(lowest, begin), lowest)
    return position, start, lowest


def _norm_row(squares, width):
    return lax.rsqrt(squares * (1.0 / width) + EPS)


def _as_column(row):
    return jnp.broadcast_to(row, (128, 128)).T


def _row_sums(values):
    ones = jnp.ones((8, values.shape[1]), F32)
    return lax.dot_general(ones, values, LAST_DIM, precision=lax.Precision.HIGHEST, preferred_element_type=F32)[:1]


def _key_scales(stat_ref, at, chunk, width):
    rows = stat_ref[pl.ds(pl.multiple_of(at // 128, chunk // 128), chunk // 128), :]
    return _norm_row(jnp.concatenate([rows[r : r + 1] for r in range(chunk // 128)], axis=1), width)


def _scores(query, key, factor, position, start, key_first):
    raw = dot(query, key, LAST_DIM) * factor
    key_position = key_first + lax.broadcasted_iota(jnp.int32, raw.shape, 1)
    return jnp.where((key_position <= position) & (key_position >= start), raw, NEG)


def _scaled_query(q_ref, stat_ref, width):
    heads, units = q_ref.shape[1] // HEAD_DIM, q_ref.shape[0] // 128
    scale = jnp.concatenate(
        [_as_column(_norm_row(stat_ref[pl.ds(pl.program_id(0) * units + r, 1), :], width)) for r in range(units)], axis=0
    )
    cols = [pl.ds(h * HEAD_DIM, HEAD_DIM) for h in range(heads)]
    return [(q_ref[:, at].astype(F32) * scale).astype(BF16) for at in cols], cols


def _lay_parts(index_ref, parts, whole):
    @pl.when(pl.program_id(0) == 0)
    def _():
        for i, part in enumerate(parts):
            height = part.shape[0]
            whole[pl.ds(pl.multiple_of(index_ref[2 + i] * height, height), height), :] = part[...]


def _attend_kernel(
    index_ref, doc_ref, q_stat, k_stat, q_ref, k_ref, v_ref, w0, w1, w2, w3, o_ref, log_ref, mix_ref, whole, *, chunk, scaling, width
):
    rows = q_ref.shape[0]
    _lay_parts(index_ref, (w0, w1, w2, w3), whole)
    heads = q_ref.shape[1] // HEAD_DIM
    first = (pl.program_id(0) * index_ref[1] + index_ref[0]) * rows
    position, start, lowest = _row_limits(doc_ref, first, rows)
    queries, cols = _scaled_query(q_ref, q_stat, width)

    def step(i, state):
        at = pl.multiple_of(i * chunk, chunk)
        factor = _key_scales(k_stat, at, chunk, width) * scaling
        new = []
        for h in range(heads):
            top, total, out = state[h]
            scores = _scores(queries[h], k_ref[pl.ds(at, chunk), cols[h]], factor, position, start, at)
            now = jnp.maximum(top, jnp.max(scores, axis=1, keepdims=True))
            weights = jnp.exp(scores - now)
            fade = jnp.exp(top - now)
            total = total * fade + jnp.sum(weights, axis=1, keepdims=True)
            out = out * fade + dot(weights.astype(BF16), v_ref[pl.ds(at, chunk), cols[h]])
            new.append((now, total, out))
        return tuple(new)

    zero = (
        jnp.full((rows, 1), NEG, F32),
        jnp.zeros((rows, 1), F32),
        jnp.zeros((rows, HEAD_DIM), F32),
    )
    last = first + rows
    state = lax.fori_loop(lowest // chunk, (last + chunk - 1) // chunk, step, (zero,) * heads)
    for h in range(heads):
        top, total, out = state[h]
        o_ref[:, cols[h]] = out / total
        log_ref[:, cols[h]] = jnp.broadcast_to(top + jnp.log(total), (rows, HEAD_DIM))
    mix_ref[...] = dot(o_ref[...].astype(BF16), whole[...]).astype(BF16)


def _attend_back_kernel(
    index_ref,
    doc_ref,
    q_stat,
    k_stat,
    q_ref,
    r_ref,
    o_ref,
    log_ref,
    k_ref,
    v_ref,
    w0,
    w1,
    w2,
    w3,
    dq_ref,
    dk_ref,
    dv_ref,
    dw_ref,
    mq_ref,
    mk_ref,
    dk_sum,
    dv_sum,
    dw_sum,
    whole,
    *,
    chunk,
    scaling,
    width,
):
    rows = q_ref.shape[0]
    _lay_parts(index_ref, (w0, w1, w2, w3), whole)
    heads = q_ref.shape[1] // HEAD_DIM
    first = (pl.program_id(0) * index_ref[1] + index_ref[0]) * rows
    position, start, lowest = _row_limits(doc_ref, first, rows)
    queries, cols = _scaled_query(q_ref, q_stat, width)

    @pl.when(pl.program_id(0) == 0)
    def _():
        dk_sum[...] = jnp.zeros_like(dk_sum)
        dv_sum[...] = jnp.zeros_like(dv_sum)
        dw_sum[...] = jnp.zeros_like(dw_sum)
        mk_ref[...] = jnp.zeros_like(mk_ref)

    upstream = r_ref[...]
    dw_sum[...] += dot(o_ref[...].astype(BF16), upstream, FIRST_DIM)
    all_grads = dot(upstream, whole[...], LAST_DIM).astype(BF16)
    grads = [all_grads[:, h * HEAD_DIM : (h + 1) * HEAD_DIM] for h in range(heads)]
    deltas = [jnp.sum(grads[h].astype(F32) * o_ref[:, cols[h]], axis=1, keepdims=True) for h in range(heads)]
    logs = [log_ref[:, at][:, :1] for at in cols]

    def step(i, state):
        at = pl.multiple_of(i * chunk, chunk)
        scale = _key_scales(k_stat, at, chunk, width)
        new = []
        key_inner = jnp.zeros((1, chunk), F32)
        query_inner = state[-1]
        for h in range(heads):
            grad = grads[h]
            key = k_ref[pl.ds(at, chunk), cols[h]]
            scores = _scores(queries[h], key, scale * scaling, position, start, at)
            weights = jnp.exp(scores - logs[h])
            weight_grad = dot(grad, v_ref[pl.ds(at, chunk), cols[h]], LAST_DIM)
            score_grad = weights * (weight_grad - deltas[h])
            inner = score_grad * scores
            key_inner = key_inner + jnp.sum(inner, axis=0, keepdims=True)
            query_inner = query_inner + jnp.sum(inner, axis=1, keepdims=True)
            dv_sum[pl.ds(at, chunk), cols[h]] += dot(weights.astype(BF16), grad, FIRST_DIM)
            dk_sum[pl.ds(at, chunk), cols[h]] += dot(score_grad.astype(BF16), queries[h], FIRST_DIM)
            new.append(state[h] + dot((score_grad * scale).astype(BF16), key))
        mk_ref[pl.ds(i, 1), :] += key_inner
        return tuple(new) + (query_inner,)

    last = first + rows
    zeros = (jnp.zeros((rows, HEAD_DIM), F32),) * heads + (jnp.zeros((rows, 1), F32),)
    state = lax.fori_loop(lowest // chunk, (last + chunk - 1) // chunk, step, zeros)
    for h in range(heads):
        dq_ref[:, cols[h]] = (state[h] * scaling).astype(BF16)
    for r in range(rows // 128):
        inner = jnp.broadcast_to(state[-1][r * 128 : (r + 1) * 128], (128, 128)).T[:1]
        mq_ref[pl.ds(pl.program_id(0) * (rows // 128) + r, 1), :] = inner

    @pl.when(pl.program_id(0) == pl.num_programs(0) - 1)
    def _():
        dk_ref[...] = (dk_sum[...] * scaling).astype(BF16)
        dv_ref[...] = dv_sum[...].astype(BF16)
        dw_ref[...] = dw_sum[...].astype(BF16)


def _resident(*shape):
    return pl.BlockSpec(shape, lambda i, *_: (0,) * len(shape), pipeline_mode=pl.Buffered(1))


def attention_forward(index, docs, q_stat, k_stat, query, key_all, value_all, out_parts, rows, chunk):
    (L, C), N = query.shape, key_all.shape[0]
    D = out_parts[0].shape[1]
    block = pl.BlockSpec((rows, C), lambda i, *_: (i, 0))
    stats = [_resident(*q_stat.shape), _resident(*k_stat.shape)]
    return pl.pallas_call(
        functools.partial(_attend_kernel, chunk=chunk, scaling=HEAD_DIM ** (-0.5), width=HEADS * HEAD_DIM),
        out_shape=[jax.ShapeDtypeStruct((L, C), F32)] * 2 + [jax.ShapeDtypeStruct((L, D), BF16)],
        grid_spec=pltpu.PrefetchScalarGridSpec(
            num_scalar_prefetch=2,
            grid=(L // rows,),
            in_specs=stats + [block, _resident(N, C), _resident(N, C)] + [_resident(C // 4, D)] * 4,
            out_specs=[block, block, pl.BlockSpec((rows, D), lambda i, *_: (i, 0))],
            scratch_shapes=[pltpu.VMEM((C, D), BF16)],
        ),
        compiler_params=pltpu.CompilerParams(vmem_limit_bytes=VMEM_BYTES),
        cost_estimate=pl.CostEstimate(flops=4 * L * C * 1024, bytes_accessed=4 * N * C, transcendentals=L * 1024),
    )(index, docs, q_stat, k_stat, query, key_all, value_all, *out_parts)


def attention_backward(
    index, docs, q_stat, k_stat, query, residual_grad, attended, logs, key_all, value_all, out_parts, rows, chunk
):
    (L, C), N = query.shape, key_all.shape[0]
    D = residual_grad.shape[1]
    block = pl.BlockSpec((rows, C), lambda i, *_: (i, 0))
    whole = _resident(N, C)
    stats = [_resident(*q_stat.shape), _resident(*k_stat.shape)]
    return pl.pallas_call(
        functools.partial(_attend_back_kernel, chunk=chunk, scaling=HEAD_DIM ** (-0.5), width=HEADS * HEAD_DIM),
        out_shape=[jax.ShapeDtypeStruct((L, C), BF16)]
        + [jax.ShapeDtypeStruct((N, C), BF16)] * 2
        + [jax.ShapeDtypeStruct((C, D), BF16)]
        + [jax.ShapeDtypeStruct(q_stat.shape, F32), jax.ShapeDtypeStruct((N // chunk, chunk), F32)],
        grid_spec=pltpu.PrefetchScalarGridSpec(
            num_scalar_prefetch=2,
            grid=(L // rows,),
            in_specs=stats
            + [block, pl.BlockSpec((rows, D), lambda i, *_: (i, 0)), block, block, whole, whole]
            + [_resident(C // 4, D)] * 4,
            out_specs=[block, whole, whole, _resident(C, D), stats[0], _resident(N // chunk, chunk)],
            scratch_shapes=[pltpu.VMEM((N, C), F32)] * 2 + [pltpu.VMEM((C, D), F32), pltpu.VMEM((C, D), BF16)],
        ),
        compiler_params=pltpu.CompilerParams(vmem_limit_bytes=VMEM_BYTES),
        cost_estimate=pl.CostEstimate(flops=10 * L * C * 1024, bytes_accessed=8 * N * C, transcendentals=L * 1024),
    )(index, docs, q_stat, k_stat, query, residual_grad, attended, logs, key_all, value_all, *out_parts)


def _project_kernel(x_ref, w_ref, gain_ref, cos_ref, sin_ref, pre_ref, q_ref, k_ref, v_ref, stat_ref):
    rows = x_ref.shape[0]
    C = q_ref.shape[1]
    pre = dot(x_ref[...], w_ref[...])
    pre_ref[...] = pre[:, : 2 * C]
    v_ref[...] = pre[:, 2 * C :].astype(BF16)
    cosine, sine = cos_ref[...], sin_ref[...]
    for j, out in enumerate((q_ref, k_ref)):
        part = pre[:, j * C : (j + 1) * C]
        sums = _row_sums(part * part)
        for r in range(rows // 128):
            stat_ref[j, pl.ds(pl.program_id(0) * (rows // 128) + r, 1), :] = sums[:, r * 128 : (r + 1) * 128]
        scaled = part * gain_ref[j : j + 1, :]
        for h in range(C // HEAD_DIM):
            one = scaled[:, h * HEAD_DIM : (h + 1) * HEAD_DIM]
            turned = pltpu.roll(one, HEAD_DIM // 2, 1)
            out[:, pl.ds(h * HEAD_DIM, HEAD_DIM)] = (one * cosine + turned * sine).astype(BF16)


def project(x, weights, gains, cosine, sine):
    L, D = x.shape
    C = weights.shape[1] // 3
    rows = min(PROJECT_ROWS, L)

    def block(width):
        return pl.BlockSpec((rows, width), lambda i: (i, 0))

    return pl.pallas_call(
        _project_kernel,
        out_shape=[jax.ShapeDtypeStruct((L, 2 * C), F32)]
        + [jax.ShapeDtypeStruct((L, C), BF16)] * 3
        + [jax.ShapeDtypeStruct((2, L // 128, 128), F32)],
        grid=(L // rows,),
        in_specs=[block(D), _resident(D, 3 * C), _resident(8, C), block(HEAD_DIM), block(HEAD_DIM)],
        out_specs=[block(2 * C), block(C), block(C), block(C), _resident(2, L // 128, 128)],
        compiler_params=pltpu.CompilerParams(vmem_limit_bytes=VMEM_BYTES),
        cost_estimate=pl.CostEstimate(flops=6 * L * D * C, bytes_accessed=2 * L * D + 6 * D * C, transcendentals=0),
    )(x, weights, gains, cosine, sine)


def _project_back_kernel(
    dq_ref, dk_ref, dv_ref, pre_ref, stat_ref, inner_ref, gain_ref, cos_ref, sin_ref, x_ref, w_ref, dw_ref, first_ref, dg_ref, total, *, width
):
    rows, C = dq_ref.shape
    cosine, sine = cos_ref[...], sin_ref[...]
    start = pl.program_id(0) == 0

    @pl.when(start)
    def _():
        dg_ref[...] = jnp.zeros_like(dg_ref)

    grads = []
    for j, ref in enumerate((dq_ref, dk_ref)):
        scales, means = [], []
        for r in range(rows // 128):
            at = pl.ds(pl.program_id(0) * (rows // 128) + r, 1)
            scale = _norm_row(stat_ref[j, at, :], width)
            scales.append(_as_column(scale))
            means.append(_as_column(inner_ref[j, at, :] * scale * scale * (1.0 / width)))
        scale, mean = jnp.concatenate(scales, axis=0), jnp.concatenate(means, axis=0)
        for h in range(C // HEAD_DIM):
            at = pl.ds(h * HEAD_DIM, HEAD_DIM)
            up = ref[:, at].astype(F32)
            up = up * cosine + pltpu.roll(up * sine, HEAD_DIM // 2, 1)
            pre = pre_ref[:, pl.ds(j * C + h * HEAD_DIM, HEAD_DIM)]
            grads.append((scale * up * gain_ref[j : j + 1, at] - pre * mean).astype(BF16))
            dg_ref[j : j + 1, at] += jnp.sum(up * pre * scale, axis=0, keepdims=True)
    grads.append(dv_ref[...])
    both = jnp.concatenate(grads, axis=1)
    first_ref[...] = dot(both, w_ref[...], LAST_DIM).astype(BF16)
    part = dot(x_ref[...], both, FIRST_DIM)

    @pl.when(start)
    def _():
        total[...] = part

    @pl.when(jnp.logical_not(start))
    def _():
        total[...] += part

    @pl.when(pl.program_id(0) == pl.num_programs(0) - 1)
    def _():
        dw_ref[...] = total[...].astype(BF16)


def project_back(dq, dk, dv, pre, stats, inner, gains, cosine, sine, x, weights):
    L, D = x.shape
    C = weights.shape[1] // 3
    rows = min(BACK_ROWS, L)

    def block(width):
        return pl.BlockSpec((rows, width), lambda i: (i, 0))

    return pl.pallas_call(
        functools.partial(_project_back_kernel, width=D),
        out_shape=[
            jax.ShapeDtypeStruct((D, 3 * C), BF16),
            jax.ShapeDtypeStruct((L, D), BF16),
            jax.ShapeDtypeStruct((8, C), F32),
        ],
        grid=(L // rows,),
        in_specs=[block(C)] * 3
        + [block(2 * C), _resident(*stats.shape), _resident(*inner.shape), _resident(8, C)]
        + [block(HEAD_DIM), block(HEAD_DIM), block(D), _resident(D, 3 * C)],
        out_specs=[_resident(D, 3 * C), block(D), _resident(8, C)],
        scratch_shapes=[pltpu.VMEM((D, 3 * C), F32)],
        compiler_params=pltpu.CompilerParams(vmem_limit_bytes=VMEM_BYTES),
        cost_estimate=pl.CostEstimate(flops=12 * L * D * C, bytes_accessed=4 * L * D + 12 * D * C, transcendentals=0),
    )(dq, dk, dv, pre, stats, inner, gains, cosine, sine, x, weights)


def _pick_kernel(slot_ref, router_ref, x_ref, g_ref, xr_ref, gr_ref, gate_ref, *, slots, width):
    experts, group = slot_ref.shape
    logits = lax.dot_general(router_ref[...], x_ref[...], (((0,), (1,)), ((), ())), preferred_element_type=F32)
    powers = jnp.exp(logits - jnp.max(logits, axis=0, keepdims=True))
    chances = powers / jnp.sum(powers, axis=0, keepdims=True)
    row = lax.broadcasted_iota(jnp.int32, (slots, group), 0)
    picks = []
    for e in range(experts):
        hit = slot_ref[e : e + 1, :] == row
        gate = jnp.sum(jnp.where(hit, chances[e : e + 1, :], 0.0), axis=1, keepdims=True)
        lane = lax.broadcasted_iota(jnp.int32, (slots, 128), 1)
        gate_ref[e, 0] = jnp.where(lane == e, gate, 0.0)
        picks.append(jnp.where(hit, 1.0, 0.0).astype(BF16))
    pick = jnp.concatenate(picks, axis=0)
    for source, target in ((x_ref, xr_ref), (g_ref, gr_ref)):

        def step(i, _, source=source, target=target):
            cols = pl.ds(pl.multiple_of(i * width, width), width)
            rows = dot(pick, source[:, cols]).astype(BF16)
            for e in range(experts):
                target[e, 0, :, cols] = rows[e * slots : (e + 1) * slots]
            return 0

        lax.fori_loop(0, source.shape[1] // width, step, 0)


def pick_rows(slot, router, x, g, group, slots):
    EL, N = slot.shape
    D = x.shape[1]
    groups = N // group
    tokens = pl.BlockSpec((group, D), lambda i: (i, 0))
    picked = pl.BlockSpec((EL, 1, slots, D), lambda i: (0, i, 0, 0))
    rows = jax.ShapeDtypeStruct((EL, groups, slots, D), BF16)
    return pl.pallas_call(
        functools.partial(_pick_kernel, slots=slots, width=512),
        out_shape=[rows, rows, jax.ShapeDtypeStruct((EL, groups, slots, 128), F32)],
        grid=(groups,),
        in_specs=[
            pl.BlockSpec((EL, group), lambda i: (0, i)),
            pl.BlockSpec(router.shape, lambda i: (0, 0)),
            tokens,
            tokens,
        ],
        out_specs=[picked, picked, pl.BlockSpec((EL, 1, slots, 128), lambda i: (0, i, 0, 0))],
        compiler_params=pltpu.CompilerParams(vmem_limit_bytes=VMEM_BYTES),
        cost_estimate=pl.CostEstimate(
            flops=4 * EL * slots * N * D, bytes_accessed=8 * N * D, transcendentals=N * EXPERTS
        ),
    )(slot, router, x, g)


def _expert_kernel(x_ref, g_ref, gate_ref, w_ref, out_ref, entry_ref, dw_ref, gg_ref):
    x, g = x_ref[0], g_ref[0]
    lane = lax.broadcasted_iota(jnp.int32, gate_ref.shape[1:], 1)
    gate = jnp.where(lane % EXPERTS == pl.program_id(0), gate_ref[0], 0.0)
    gate = jnp.sum(gate, axis=1, keepdims=True)
    gate_pre = dot(x, w_ref[0, 0])
    up = dot(x, w_ref[0, 1])
    back = dot(g, w_ref[0, 2])
    sig = jax.nn.sigmoid(gate_pre)
    act = gate_pre * sig
    inner = act * up
    gg_ref[0] = jnp.broadcast_to(jnp.sum(inner * back, axis=1, keepdims=True), gg_ref.shape[1:])
    inner_grad = back * gate
    gate_pre_grad = (inner_grad * up * sig * (1.0 + gate_pre * (1.0 - sig))).astype(BF16)
    up_grad = (inner_grad * act).astype(BF16)
    gated = (inner * gate).astype(BF16)
    both = jnp.concatenate([gate_pre_grad, up_grad], axis=1)
    out_ref[0] = dot(gated, w_ref[0, 2], LAST_DIM).astype(BF16)
    entry_ref[0] = dot(both, jnp.concatenate([w_ref[0, 0], w_ref[0, 1]], axis=1), LAST_DIM).astype(BF16)
    FL = w_ref.shape[3]
    pair = dot(x, both, FIRST_DIM)
    parts = (pair[:, :FL], pair[:, FL:], dot(g, gated, FIRST_DIM))
    first = pl.program_id(1) == 0
    for k in range(3):

        @pl.when(first)
        def _(k=k):
            dw_ref[0, k] = parts[k]

        @pl.when(jnp.logical_not(first))
        def _(k=k):
            dw_ref[0, k] += parts[k]


def run_experts(x, g, gate, weights, chunk):
    EL, rows, D = x.shape
    FL = weights.shape[3]
    row_block = pl.BlockSpec((1, chunk, D), lambda e, c: (e, c, 0))
    thin = pl.BlockSpec((1, chunk, 128), lambda e, c: (e, c, 0))
    matrices = pl.BlockSpec((1, 3, D, FL), lambda e, c: (e, 0, 0, 0))
    return pl.pallas_call(
        _expert_kernel,
        out_shape=[
            jax.ShapeDtypeStruct(x.shape, BF16),
            jax.ShapeDtypeStruct(x.shape, BF16),
            jax.ShapeDtypeStruct(weights.shape, F32),
            jax.ShapeDtypeStruct((EL, rows, 128), F32),
        ],
        grid=(EL, rows // chunk),
        in_specs=[row_block, row_block, thin, matrices],
        out_specs=[row_block, row_block, matrices, thin],
        compiler_params=pltpu.CompilerParams(vmem_limit_bytes=VMEM_BYTES),
        cost_estimate=pl.CostEstimate(
            flops=18 * EL * rows * D * FL, bytes_accessed=8 * EL * rows * D + 18 * EL * D * FL, transcendentals=EL * rows * FL
        ),
    )(x, g, gate, weights)


def _spread_kernel(own_ref, slot_ref, gg_ref, out_ref, entry_ref, o_ref, e_ref, *, width):
    group, experts = slot_ref.shape
    slots = out_ref.shape[2]
    total = experts * slots
    D = out_ref.shape[3]
    lane = lax.broadcasted_iota(jnp.int32, (experts, total), 1)
    which = lax.broadcasted_iota(jnp.int32, (experts, total), 0)
    choose = jnp.where((lane >= which * slots) & (lane < (which + 1) * slots), 1.0, 0.0).astype(BF16)
    offset = lane[:1] - jnp.sum(jnp.where(lane >= (which + 1) * slots, slots, 0), axis=0, keepdims=True)
    mine = dot(slot_ref[...].astype(BF16), choose)
    pick = jnp.where(mine == offset.astype(F32), 1.0, 0.0).astype(BF16)
    column = lax.broadcasted_iota(jnp.int32, (slots, 128), 1)
    grads = [jnp.where(column == own_ref[0] + e, gg_ref[e, 0], 0.0).astype(BF16) for e in range(experts)]
    e_ref[:, pl.ds(D, 128)] = dot(pick, jnp.concatenate(grads, axis=0)).astype(BF16)

    def step(i, _):
        cols = pl.ds(pl.multiple_of(i * width, width), width)
        for source, target in ((out_ref, o_ref), (entry_ref, e_ref)):
            rows = jnp.concatenate([source[e, 0, :, cols] for e in range(experts)], axis=0)
            target[:, cols] = dot(pick, rows).astype(BF16)
        return 0

    lax.fori_loop(0, D // width, step, 0)


def spread_rows(own, slot, gate_grads, out_rows, entry_rows, group):
    N, EL = slot.shape
    _, groups, slots, D = out_rows.shape
    picked = pl.BlockSpec((EL, 1, slots, D), lambda i, *_: (0, i, 0, 0))
    return pl.pallas_call(
        functools.partial(_spread_kernel, width=512),
        out_shape=[jax.ShapeDtypeStruct((N, D), BF16), jax.ShapeDtypeStruct((N, D + 128), BF16)],
        grid_spec=pltpu.PrefetchScalarGridSpec(
            num_scalar_prefetch=1,
            grid=(groups,),
            in_specs=[
                pl.BlockSpec((group, EL), lambda i, *_: (i, 0)),
                pl.BlockSpec((EL, 1, slots, 128), lambda i, *_: (0, i, 0, 0)),
                picked,
                picked,
            ],
            out_specs=[
                pl.BlockSpec((group, D), lambda i, *_: (i, 0)),
                pl.BlockSpec((group, D + 128), lambda i, *_: (i, 0)),
            ],
        ),
        compiler_params=pltpu.CompilerParams(vmem_limit_bytes=VMEM_BYTES),
        cost_estimate=pl.CostEstimate(flops=4 * EL * slots * N * D, bytes_accessed=8 * N * D, transcendentals=0),
    )(own, slot, gate_grads, out_rows, entry_rows)


def body(
    hidden_in,
    out_grad,
    attn_gain,
    query_weight,
    key_weight,
    value_weight,
    out_weight,
    query_gain,
    key_gain,
    ffn_gain,
    router_weight,
    expert_weights,
    routes,
    doc_starts,
):
    U = lax.axis_size("uly")
    Z = lax.axis_size("blk")
    u = lax.axis_index("uly")
    z = lax.axis_index("blk")
    T, D = hidden_in.shape
    EL = expert_weights.shape[0]
    N = U * Z * T
    RW = query_weight.shape[0]
    move = (Slice if (U, Z, T, D) == (8, 4, 128, 2048) else General)(U, Z, T, D)
    C, L = move.C, move.L

    own_weights = (query_weight, key_weight, value_weight)
    gains = jnp.stack([attn_gain, ffn_gain, query_gain, key_gain], axis=1)
    first_rows, qkv_weight, packed, routes_all = move.enter(
        hidden_in, own_weights, gains, out_weight, router_weight, routes.T, out_grad
    )
    hidden = hidden_in.astype(F32)
    weight_router = packed[:, :EXPERTS]
    gain_ffn = packed[:, EXPERTS].astype(F32)
    head_gains = lax.dynamic_slice_in_dim(packed[:, EXPERTS + 1 : EXPERTS + 3], move.group * C, C, 0).astype(F32)
    head_gains = jnp.pad(head_gains.T, ((0, 6), (0, 0)))
    local = jnp.arange(L, dtype=jnp.int32)
    cosine, sine = rotary_tables((local // T * move.block_step + move.first_block) * T + local % T)
    pre, query_rot, key_rot, value, squares = project(first_rows, qkv_weight, head_gains, cosine, sine)
    key_all, value_all, stats, k_stat = move.sequence(key_rot, value, squares, out_grad)
    index = jnp.stack([jnp.int32(i) for i in (move.first_block * T // move.rows, move.block_step, *move.parts)])
    chunk = min(ATTEND_CHUNK, N)
    attended, logs, mixed = attention_forward(
        index, doc_starts, stats[0], k_stat, query_rot, key_all, value_all, move.out_parts, move.rows, chunk
    )
    move.prepare(routes_all, EL, jnp.roll(weight_router, -u * EL, axis=1))
    residual = hidden + move.heads_to_rows(mixed).astype(F32)

    second_scale = norm_scale(residual)
    second_low = (residual * second_scale * gain_ffn).astype(BF16)
    probabilities = jax.nn.softmax(dot(second_low, weight_router), axis=-1)
    second_all, entry_sum = move.experts(second_low, expert_weights)
    entry_sum = entry_sum.astype(F32)

    second_grad, prob_grad = entry_sum[:, :D], entry_sum[:, D : D + EXPERTS]
    logit_grad = (
        probabilities * (prob_grad - jnp.sum(probabilities * prob_grad, axis=1, keepdims=True))
    ).astype(BF16)
    second_grad = second_grad + dot(logit_grad, weight_router, LAST_DIM)
    upstream = out_grad.astype(F32)
    weighted = second_grad * gain_ffn
    inner_mean = jnp.mean(weighted * residual, axis=-1, keepdims=True)
    residual_grad = upstream + second_scale * weighted - residual * (second_scale**3) * inner_mean
    ffn_gain_part = jnp.sum(second_grad * residual * second_scale, axis=0)

    residual_rows, expert_grads = move.rows_to_heads(residual_grad.astype(BF16))
    dq, dk_part, dv_part, out_weight_part, q_inner, k_inner = attention_backward(
        index,
        doc_starts,
        stats[0],
        k_stat,
        query_rot,
        residual_rows,
        attended,
        logs,
        key_all,
        value_all,
        move.out_parts,
        move.rows,
        chunk,
    )
    dk, dv, out_sum, inner = move.sequence_sums(dk_part, dv_part, out_weight_part, q_inner, k_inner)
    weight_part, first_part, gain_parts = project_back(
        dq, dk, dv, pre, stats, inner, head_gains, cosine, sine, first_rows, qkv_weight
    )
    gain_parts = gain_parts[:2]
    first_weighted, weight_sum, out_weight_grad, logit_grad_all, ffn_gain_grad, head_gain_grads = move.leave(
        first_part, weight_part, logit_grad, ffn_gain_part, gain_parts
    )
    own_columns = lax.dynamic_slice_in_dim(second_all, (u * Z + z) * RW, RW, 1)
    router_grad = dot(own_columns, logit_grad_all, FIRST_DIM)
    output, hidden_grad, attn_gain_grad, *weight_grads = finish(
        hidden_in, residual, residual_grad, first_weighted, out_sum, own_weights, weight_sum, out_weight_grad, gains
    )
    return (
        output,
        hidden_grad,
        attn_gain_grad[:, 0],
        weight_grads[0],
        weight_grads[1],
        weight_grads[2],
        weight_grads[3],
        head_gain_grads[0],
        head_gain_grads[1],
        ffn_gain_grad,
        router_grad,
        expert_grads,
    )


def solution(mesh):
    rows = P(ALL, None)
    flat = P(ALL)
    experts = P("uly", None, None, "blk")
    return jax.shard_map(
        body,
        mesh=mesh,
        in_specs=(rows, rows, flat, rows, rows, rows, rows, flat, flat, flat, rows, experts, rows, P()),
        out_specs=(rows, rows, flat, rows, rows, rows, rows, flat, flat, flat, rows, experts),
        check_vma=False,
    )
```

```python
import functools

import jax
import jax.numpy as jnp
from jax import lax
from jax.experimental import pallas as pl
from jax.experimental.pallas import tpu as pltpu
from jax.sharding import PartitionSpec as P

HEADS = 16
HEAD_DIM = 128
EXPERTS = 64
CAP = 17

EPS = 1e-05
THETA = 10000.0
NEG = -1e30
FIRST_DIM = (((0,), (0,)), ((), ()))
LAST_DIM = (((1,), (1,)), ((), ()))
ALL = ("uly", "blk")
F32 = jnp.float32
BF16 = jnp.bfloat16
VMEM_BYTES = 56 * 1024 * 1024
PICK_WIDTH = 512
ATTEND_CHUNK = 512
ATTEND_ROWS = 512
BACK_ROWS = 1024
PROJECT_ROWS = 256
SPREAD_WIDTH = 2048


def dot(a, b, dims=(((1,), (0,)), ((), ()))):
    return lax.dot_general(a, b, dims, preferred_element_type=F32)


def rotary_tables(position):
    halfway = HEAD_DIM // 2
    frequency = THETA ** (-(jnp.arange(halfway).astype(F32) * 2.0 / HEAD_DIM))
    angles = position.astype(F32)[:, None] * frequency[None, :]
    cosine, sine = jnp.cos(angles), jnp.sin(angles)
    return jnp.concatenate([cosine, cosine], axis=1), jnp.concatenate([-sine, sine], axis=1)


def norm_scale(values):
    return lax.rsqrt(jnp.mean(values * values, axis=-1, keepdims=True) + EPS)


MESH = pl.DeviceIdType.MESH
DMA = pltpu.SemaphoreType.DMA
ANY_SPACE = pl.BlockSpec(memory_space=pl.ANY)
IN_VMEM = pl.BlockSpec(memory_space=pltpu.VMEM)
DEPTH = 4
CHIPS = (0, 2, 4, 6)
FIRST, THEN = (2, 4), (4, 2)


def _send(src, dst, send_sem, recv_sem, to):
    pltpu.make_async_remote_copy(
        src_ref=src, dst_ref=dst, send_sem=send_sem, recv_sem=recv_sem, device_id=to, device_id_type=MESH
    ).start()


def _expect(ref, sem, here):
    pltpu.make_async_remote_copy(
        src_ref=ref, dst_ref=ref, send_sem=sem, recv_sem=sem, device_id=here, device_id_type=MESH
    ).wait_recv()


def _sent(ref, sem, here):
    pltpu.make_async_remote_copy(
        src_ref=ref, dst_ref=ref, send_sem=sem, recv_sem=sem, device_id=here, device_id_type=MESH
    ).wait_send()


def _greet(u, z, planes, line=False, others=(), meanwhile=lambda: None):
    barrier = pltpu.get_barrier_semaphore()
    for bit in planes:
        pl.semaphore_signal(barrier, inc=1, device_id=(u ^ bit, z), device_id_type=MESH)
    for to in others:
        pl.semaphore_signal(barrier, inc=1, device_id=to, device_id_type=MESH)
    count = len(planes) + len(others)
    if line:

        @pl.when(z > 0)
        def _():
            pl.semaphore_signal(barrier, inc=1, device_id=(u, z - 1), device_id_type=MESH)

        @pl.when(z < DEPTH - 1)
        def _():
            pl.semaphore_signal(barrier, inc=1, device_id=(u, z + 1), device_id_type=MESH)

        count = count + jnp.where((z == 0) | (z == DEPTH - 1), 1, 2)
    meanwhile()
    pl.semaphore_wait(barrier, count)


def _line_order(z):
    second = jnp.where(z == 0, 1, z - 1)
    third = jnp.where(z == 0, 2, jnp.where(z == 3, 1, z + 1))
    fourth = jnp.where(z < 2, 3, 0)
    return (z, second, third, fourth)


def _accumulate(target, source, rows):
    strip = 16

    def step(i, _):
        at = pl.ds(pl.multiple_of(i * strip, strip), strip)
        target[at, :] = target[at, :] + source[at, :]
        return 0

    lax.fori_loop(0, rows // strip, step, 0)


def _run(*parts, order=()):
    for i in order:
        next(parts[i])
    live = list(parts)
    while live:
        for part in list(live):
            try:
                next(part)
            except StopIteration:
                live.remove(part)


def _line_part(u, z, source, block, sems, share=True, place=None):
    z_send, z_recv, c_send, c_recv, own_sem = sems
    here, core = (u, z), u % 2
    if place is None:
        own = pltpu.make_async_copy(source, block(core, z), own_sem)
        own.start()
    else:
        def block(_, level):
            return place(level, z)

    order = _line_order(z)

    def along(level, ref, step):
        @pl.when((z > 0) & (level >= z))
        def _():
            step(ref, 0, level, (u, z - 1))

        @pl.when((z < DEPTH - 1) & (level <= z))
        def _():
            step(ref, 1, level, (u, z + 1))

    def go(ref, way, level, to):
        there = block(core, level) if place is None else place(level, to[1])
        _send(ref, there, z_send.at[way, level], z_recv.at[level], to)

    def gone(ref, way, level, to):
        _sent(ref, z_send.at[way, level], here)

    for i in range(4):
        level = order[i]
        ref = source if i == 0 else block(core, level)
        if i > 0:
            yield
            _expect(ref, z_recv.at[level], here)
        along(level, ref, go)
        if share:
            _send(ref, block(core, level), c_send.at[level], c_recv.at[level], (u ^ 1, z))
    yield
    if share:
        for i in range(4):
            _expect(block(1 - core, order[i]), c_recv.at[order[i]], here)
    yield
    for i in range(4):
        along(order[i], source, gone)
        if share:
            _sent(source, c_send.at[order[i]], here)
    if place is None:
        own.wait()


def _plane_part(u, z, own, block, sems):
    p_send, p_recv, o_sem = sems
    here = (u, z)
    for way, bits in enumerate((FIRST, THEN)):
        for h in range(2):
            _send(own(h), block(h, u), p_send.at[h, way], p_recv.at[h, way], (u ^ bits[h], z))
    for h in range(2):
        pltpu.make_async_copy(own(h), block(h, u), o_sem.at[h]).start()
    for h in range(2):
        yield
        _expect(block(h, u ^ FIRST[h]), p_recv.at[h, 0], here)
        near = block(h, u ^ FIRST[h])
        _send(near, near, p_send.at[h, 2], p_recv.at[h, 2], (u ^ THEN[h], z))
    yield
    for h in range(2):
        _expect(block(h, u ^ THEN[h]), p_recv.at[h, 1], here)
        _expect(block(h, u ^ 6), p_recv.at[h, 2], here)
    yield
    for h in range(2):
        for k in range(3):
            _sent(block(h, u), p_send.at[h, k], here)
        pltpu.make_async_copy(own(h), block(h, u), o_sem.at[h]).wait()


def _plane_sum_part(u, z, source, work, bufs, sems, rows, then_do):
    p_buf, q_buf = bufs
    load, p_send, p_recv, q_send, q_recv = sems
    here = (u, z)
    for j in (1, 0):
        for h in range(2):
            bit = (THEN[h], 6)[j]
            _send(source(h, u ^ bit), p_buf.at[h, j], p_send.at[h, j], p_recv.at[h, j], (u ^ THEN[h], z))
    for h in range(2):
        for j, bit in enumerate((0, FIRST[h])):
            pltpu.make_async_copy(source(h, u ^ bit), work.at[h, j], load.at[h, j]).start()
    for h in range(2):
        yield
        for j, bit in enumerate((0, FIRST[h])):
            pltpu.make_async_copy(source(h, u ^ bit), work.at[h, j], load.at[h, j]).wait()
        _expect(p_buf.at[h, 1], p_recv.at[h, 1], here)
        _accumulate(work.at[h, 1], p_buf.at[h, 1], rows)
        _send(work.at[h, 1], q_buf.at[h], q_send.at[h], q_recv.at[h], (u ^ FIRST[h], z))
    yield
    for h in range(2):
        _expect(p_buf.at[h, 0], p_recv.at[h, 0], here)
        _accumulate(work.at[h, 0], p_buf.at[h, 0], rows)
    for h in range(2):
        _expect(q_buf.at[h], q_recv.at[h], here)
        _accumulate(work.at[h, 0], q_buf.at[h], rows)
    then_do()
    yield
    for h in range(2):
        for j in range(2):
            _sent(p_buf.at[h, j], p_send.at[h, j], here)
        _sent(q_buf.at[h], q_send.at[h], here)


def _line_sum_part(u, z, source, work, bufs, sems, rows, then_do):
    c_buf, z_buf = bufs
    load, c_send, c_recv, z_send, z_recv = sems
    here, core = (u, z), u % 2
    order = tuple(reversed(_line_order(z)))
    for i in range(4):
        _send(source(1 - core, order[i]), c_buf.at[i], c_send.at[i], c_recv.at[i], (u ^ 1, z))
        pltpu.make_async_copy(source(core, order[i]), work.at[i], load.at[i]).start()
    for i in range(4):
        yield
        pltpu.make_async_copy(source(core, order[i]), work.at[i], load.at[i]).wait()
        _expect(c_buf.at[i], c_recv.at[i], here)
        _accumulate(work.at[i], c_buf.at[i], rows)
        if i == 3:
            yield
        _line_end(u, z, order[i], i, work.at[i], z_buf, (z_send, z_recv), rows)
    then_do()
    yield
    for i in range(4):
        _sent(c_buf.at[i], c_send.at[i], here)
        if i < 3:
            _sent(work.at[i], z_send.at[i], here)


def _column_peers(u, z):
    return [((u ^ c, z ^ k), c, k) for c in range(2) for k in range(4) if c or k]


def _comm(kernel, outs, scratch, collective_id, specs, flops=0, moved=100_000_000):
    return pl.pallas_call(
        kernel,
        out_shape=outs,
        in_specs=specs[0],
        out_specs=specs[1],
        scratch_shapes=scratch,
        compiler_params=pltpu.CompilerParams(
            collective_id=collective_id, has_side_effects=True, vmem_limit_bytes=VMEM_BYTES
        ),
        cost_estimate=pl.CostEstimate(flops=flops, bytes_accessed=moved, transcendentals=0),
    )


ENTER_ORDER = (0, 2, 3, 1, 3, 3, 0, 2, 1, 0, 2, 0, 2)
KV_ORDER = (2, 0, 1, 0, 0, 1, 2, 1, 0, 1)
PAIR_ORDER = (1, 0, 2, 1, 0, 0, 1, 2, 1, 0)
LEAVE_ORDER = (0, 1, 2, 1, 2, 1, 0, 0, 1, 3, 3, 0, 1, 3, 3, 1)
LINE_SEMS = [DMA((2, 4)), DMA((4,)), DMA((4,)), DMA((4,)), DMA]
PLANE_SEMS = [DMA((2, 3)), DMA((2, 3)), DMA((2,))]
PLANE_SUM_SEMS = [DMA((2, 2)), DMA((2, 2)), DMA((2, 2)), DMA((2,)), DMA((2,))]
LINE_SUM_SEMS = [DMA((4,)), DMA((4,)), DMA((4,)), DMA((4,)), DMA((2, 4))]


def _small_part(u, z, xs, outs, sems):
    own_sem, z_send, z_recv, u_send, u_recv = sems
    here = (u, z)
    for a, (x, o) in enumerate(zip(xs, outs)):
        pltpu.make_async_copy(x, o.at[u, z], own_sem.at[a]).start()
        for k in range(1, 4):
            _send(x, o.at[u, z], z_send.at[a, k], z_recv.at[a, k], (u, z ^ k))
    yield
    for a, (x, o) in enumerate(zip(xs, outs)):
        pltpu.make_async_copy(x, o.at[u, z], own_sem.at[a]).wait()
        for k in range(1, 4):
            _expect(o.at[u, z ^ k], z_recv.at[a, k], here)
        for k in range(1, 8):
            _send(o.at[u], o.at[u], u_send.at[a, k], u_recv.at[a, k], (u ^ k, z))
    yield
    yield
    for a, (x, o) in enumerate(zip(xs, outs)):
        for k in range(1, 4):
            _sent(x, z_send.at[a, k], here)
        for k in range(1, 8):
            _sent(o.at[u], u_send.at[a, k], here)
            _expect(o.at[u ^ k], u_recv.at[a, k], here)


def _small_sems(n):
    return [DMA((n,)), DMA((n, 4)), DMA((n, 4)), DMA((n, 8)), DMA((n, 8))]


def _packed(router, gains):
    lane = lax.broadcasted_iota(jnp.int32, (router.shape[0], 128 - EXPERTS), 1)
    tail = jnp.zeros(lane.shape, F32)
    for j in range(1, 4):
        tail = jnp.where(lane == j - 1, gains[:, j : j + 1], tail)
    return router, tail.astype(BF16)


def enter(hidden, weights, gains, router, routes, out_grad, collective_id):
    T, D = hidden.shape
    R, C = weights[0].shape[0], weights[0].shape[1] // 8
    held = (2, 4, R, 3 * C)
    strip = 16

    def kernel(h_ref, wq_ref, wk_ref, wv_ref, gain_ref, router_ref, route_ref, g_ref, x_out, w_out, p_out, r_out, g_out, *refs):
        x_ref, w_ref, pack_ref, w_buf, w_send, w_recv = refs[:6]
        half = [pl.ds(h * (T // 2), T // 2) for h in range(2)]
        sems = refs[6:]
        u, z = lax.axis_index("uly"), lax.axis_index("blk")
        here, core, chip = (u, z), u % 2, u // 2
        column = _column_peers(u, z)

        def weight_part():
            def cut(j, c, level):
                return w_ref.at[j, :, pl.ds(pl.multiple_of((2 * level + c) * C, C), C)]

            def slot(j, c, level):
                return w_buf.at[c, level, :, pl.ds(j * C, C)]

            for i, (to, c, k) in enumerate(column):
                for j in range(3):
                    _send(cut(j, core ^ c, z ^ k), slot(j, core, z), w_send.at[i, j], w_recv.at[i, j], to)
            for j in range(3):
                slot(j, core, z)[...] = cut(j, core, z)[...]
            yield
            for i, (to, c, k) in enumerate(column):
                for j in range(3):
                    _expect(slot(j, core ^ c, z ^ k), w_recv.at[i, j], here)
            yield from _plane_part(u, z, lambda h: w_buf.at[h], lambda h, v: w_out.at[v // 2, h], sems[:3])
            for i, (to, c, k) in enumerate(column):
                for j in range(3):
                    _sent(cut(j, core ^ c, z ^ k), w_send.at[i, j], here)

        def prepare():
            gains = gain_ref[...].astype(F32)
            for j, ref in enumerate((wq_ref, wk_ref, wv_ref)):
                w_ref[j] = (ref[...].astype(F32) * gains[:, :1]).astype(BF16)

            def norm(i, _):
                at = pl.ds(pl.multiple_of(i * strip, strip), strip)
                value = h_ref[at, :].astype(F32)
                x_ref[at, :] = (value * norm_scale(value)).astype(BF16)
                return 0

            lax.fori_loop(0, T // strip, norm, 0)
            pack_ref[:, pl.ds(0, EXPERTS)], pack_ref[:, pl.ds(EXPERTS, 128 - EXPERTS)] = _packed(router_ref[...], gains)

        _greet(u, z, range(1, 8), others=[to for to, c, k in column if k], meanwhile=prepare)
        _run(
            weight_part(),
            _small_part(u, z, (pack_ref, route_ref), (p_out, r_out), sems[11:]),
            _line_part(u, z, x_ref, lambda c, level: x_out.at[c, level], sems[3:8]),
            _plane_part(u, z, lambda h: g_ref.at[half[h]], lambda h, v: g_out.at[v // 2, half[h]], sems[8:11]),
            order=ENTER_ORDER,
        )

    outs = [
        jax.ShapeDtypeStruct((2, 4, T, D), BF16),
        jax.ShapeDtypeStruct((4,) + held, BF16),
        jax.ShapeDtypeStruct((8, 4, R, 128), BF16),
        jax.ShapeDtypeStruct((8, 4) + routes.shape, routes.dtype),
        jax.ShapeDtypeStruct((4, T, D), BF16),
    ]
    scratch = [pltpu.VMEM((T, D), BF16), pltpu.VMEM((3, R, D), BF16), pltpu.VMEM((R, 128), BF16)]
    scratch += [pltpu.VMEM(held, BF16), DMA((7, 3)), DMA((7, 3))] + PLANE_SEMS + LINE_SEMS + PLANE_SEMS + _small_sems(2)
    specs = ([IN_VMEM] * 7 + [ANY_SPACE], [ANY_SPACE] * 5)
    return _comm(kernel, outs, scratch, collective_id, specs)(hidden, *weights, gains, router, routes, out_grad)


def _column_sum_part(u, z, x_ref, total, buf, sems, then_do):
    send, recv = sems
    here = (u, z)
    column = _column_peers(u, z)
    for i, (to, c, k) in enumerate(column):
        _send(x_ref, buf.at[i], send.at[i], recv.at[i], to)
    yield
    value = x_ref[...]
    for i in range(7):
        _expect(buf.at[i], recv.at[i], here)
        value = value + buf[i]
    total[...] = value
    then_do()
    yield
    for i in range(7):
        _sent(x_ref, send.at[i], here)


def plane_pair(first, second, rows, squares, collective_id):
    R = squares.shape[0] // 2

    def kernel(a_ref, b_ref, x_ref, s_ref, a_out, b_out, x_out, s_out, k_out, buf, *sems):
        u, z = lax.axis_index("uly"), lax.axis_index("blk")
        here, chip = (u, z), u // 2
        k_send, k_recv = sems[10:]
        _greet(u, z, (2, 4, 6), others=[to for to, c, k in _column_peers(u, z)])
        own, outs = (a_ref, b_ref), (a_out, b_out)
        keys = s_out.at[pl.ds(R, R)]

        def tell():
            k_out[chip] = keys[...]
            for i, bit in enumerate((2, 4, 6)):
                _send(keys, k_out.at[chip], k_send.at[i], k_recv.at[i], (u ^ bit, z))

        _run(
            _plane_part(u, z, lambda h: own[h], lambda h, v: outs[h].at[v // 2], sems[:3]),
            _line_part(
                u, z, x_ref, None, sems[3:8], share=False, place=lambda level, at: x_out.at[(level - at + 3) % 4]
            ),
            _column_sum_part(u, z, s_ref, s_out, buf, sems[8:10], tell),
            order=PAIR_ORDER,
        )
        for i, bit in enumerate((2, 4, 6)):
            _expect(k_out.at[(u ^ bit) // 2], k_recv.at[i], here)
            _sent(keys, k_send.at[i], here)

    outs = [jax.ShapeDtypeStruct((4,) + x.shape, x.dtype) for x in (first, second)]
    outs += [jax.ShapeDtypeStruct((3,) + rows.shape, rows.dtype)]
    outs += [jax.ShapeDtypeStruct(squares.shape, F32), jax.ShapeDtypeStruct((4, R, 128), F32)]
    specs = ([IN_VMEM] * 2 + [ANY_SPACE, IN_VMEM], [ANY_SPACE] * 3 + [IN_VMEM] * 2)
    scratch = [pltpu.VMEM((7,) + squares.shape, F32)] + PLANE_SEMS + LINE_SEMS + [DMA((7,)), DMA((7,)), DMA((3,)), DMA((3,))]
    return _comm(kernel, outs, scratch, collective_id, specs)(first, second, rows, squares)


def column_gather(rows, slot, out_rows, collective_id):
    T, D = rows.shape
    EL, _, slots, _ = out_rows.shape

    def kernel(r_ref, slot_ref, rows_ref, r_out, x_out, part_out, stage, stage_sem, *refs):
        u, z = lax.axis_index("uly"), lax.axis_index("blk")
        _greet(u, z, (1, 2, 4), line=True)
        order = _line_order(z)[1:]

        def keep(i, part):
            x_out[(order[i] - z + 3) % 4] = part[...]

        extra = (stage, part_out, stage_sem)
        _run(
            _line_part(u, z, r_ref, lambda c, level: r_out.at[c, level], refs[-5:]),
            _spread_part(u, z, slot_ref, rows_ref, None, order, refs[:-5], keep, extra=extra),
        )

    outs = [
        jax.ShapeDtypeStruct((2, 4, T, D), BF16),
        jax.ShapeDtypeStruct((3, T, D), BF16),
        jax.ShapeDtypeStruct((2, 4 * T, D), BF16),
    ]
    specs = ([IN_VMEM, IN_VMEM, ANY_SPACE], [ANY_SPACE, IN_VMEM, ANY_SPACE])
    scratch = [pltpu.VMEM((2, 4 * T, D), BF16), DMA((2,))] + _spread_scratch(T, D, (EL, slots, D), 3) + LINE_SEMS
    return _comm(kernel, outs, scratch, collective_id, specs)(rows, slot, out_rows)


def _line_sum_scratch(T, D):
    return [pltpu.VMEM((4, T, D), BF16), pltpu.VMEM((4, T, D), BF16), pltpu.VMEM((2, 4, T, D), BF16)]


def column_scatter(x, collective_id):
    T, D = x.shape[2:]

    def kernel(x_ref, o_ref, work, c_buf, z_buf, *sems):
        u, z = lax.axis_index("uly"), lax.axis_index("blk")
        _greet(u, z, (1,), line=True)

        def finish():
            o_ref[...] = work[3]

        _run(_line_sum_part(u, z, lambda c, level: x_ref.at[c, level], work, (c_buf, z_buf), sems, T, finish))

    scratch = _line_sum_scratch(T, D) + LINE_SUM_SEMS
    return _comm(kernel, jax.ShapeDtypeStruct((T, D), BF16), scratch, collective_id, ([ANY_SPACE], IN_VMEM))(x)


def _plane_sum_scratch(rows, cols):
    return [pltpu.VMEM((2, 2, rows, cols), BF16), pltpu.VMEM((2, 2, rows, cols), BF16), pltpu.VMEM((2, rows, cols), BF16)]


def key_value_sums(dk, dv, x, inner, collective_id):
    T, D = x.shape[1:]
    L, C = dk.shape[1:]
    R = inner.shape[0] // 5

    def kernel(
        k_ref, v_ref, x_ref, s_ref, k_out, v_out, x_out, s_out, work, p_buf, q_buf, x_work, z_buf, buf, total, k_buf, *sems
    ):
        u, z = lax.axis_index("uly"), lax.axis_index("blk")
        here, chip = (u, z), u // 2
        _greet(u, z, (2, 4, 6), others=[to for to, c, k in _column_peers(u, z)])
        load, z_send, z_recv, k_send, k_recv = sems[7:]
        order = tuple(reversed(_line_order(z)))

        def keys(v):
            return total.at[pl.ds(pl.multiple_of((v // 2 + 1) * R, R), R)]

        def tell():
            for i, bit in enumerate((2, 4, 6)):
                _send(keys(u ^ bit), k_buf.at[i], k_send.at[i], k_recv.at[i], (u ^ bit, z))

        def finish():
            k_out[...] = work[0, 0]
            v_out[...] = work[1, 0]

        def line():
            copies = [
                pltpu.make_async_copy(x_ref.at[(order[i] - z + 3) % 4], x_work.at[i], load.at[i]) for i in range(3)
            ]
            for copy in copies:
                copy.start()
            x_work[3] = jnp.zeros((T, D), BF16)
            for copy in copies:
                copy.wait()
            for i in range(4):
                _line_end(u, z, order[i], i, x_work.at[i], z_buf, (z_send, z_recv), T)
                yield
            x_out[...] = x_work[3]
            for i in range(3):
                _sent(x_work.at[i], z_send.at[i], (u, z))

        _run(
            _plane_sum_part(
                u, z, lambda h, v: (k_ref, v_ref)[h].at[v // 2], work, (p_buf, q_buf), sems[:5], L, finish
            ),
            line(),
            _column_sum_part(u, z, s_ref, total, buf, sems[5:7], tell),
            order=KV_ORDER,
        )
        value = keys(u)[...]
        for i, bit in enumerate((2, 4, 6)):
            _expect(k_buf.at[i], k_recv.at[i], here)
            value = value + k_buf[i]
            _sent(k_buf.at[i], k_send.at[i], here)
        s_out[pl.ds(0, R), :] = total[pl.ds(0, R), :]
        s_out[pl.ds(R, R), :] = value

    outs = [jax.ShapeDtypeStruct((L, C), BF16)] * 2 + [jax.ShapeDtypeStruct((T, D), BF16)]
    outs += [jax.ShapeDtypeStruct((2 * R, 128), F32)]
    scratch = _plane_sum_scratch(L, C) + [pltpu.VMEM((4, T, D), BF16), pltpu.VMEM((2, 4, T, D), BF16)]
    scratch += [pltpu.VMEM((7,) + inner.shape, F32), pltpu.VMEM(inner.shape, F32), pltpu.VMEM((3, R, 128), F32)]
    scratch += PLANE_SUM_SEMS + [DMA((7,)), DMA((7,)), DMA((4,)), DMA((4,)), DMA((2, 4)), DMA((3,)), DMA((3,))]
    specs = ([ANY_SPACE] * 3 + [IN_VMEM], [IN_VMEM] * 4)
    return _comm(kernel, outs, scratch, collective_id, specs)(dk, dv, x, inner)


def leave(x, weights, smalls, ready, collective_id):
    n = len(smalls)
    T, D = x.shape[2:]
    rows, W = weights.shape[2:]
    R, C = rows // 4, W // 3

    def kernel(x_ref, w_ref, ready_ref, *refs):
        small_in, (o_ref, w_out, own_ref), small_out = refs[:n], refs[n : n + 3], refs[n + 3 : 2 * n + 3]
        work, c_buf, z_buf, w_work, wp_buf, wq_buf = refs[2 * n + 3 : 2 * n + 9]
        tree = refs[2 * n + 9 : 2 * n + 20]
        sems = refs[2 * n + 20 :]

        def keep(part):
            own_ref[...] = part[...]

        u, z = lax.axis_index("uly"), lax.axis_index("blk")
        here, core, chip = (u, z), u % 2, u // 2
        column = _column_peers(u, z)
        _greet(u, z, range(1, 8), others=[to for to, c, k in column if k])
        t_send, t_recv = sems[10:12]
        group = 2 * z + core

        def finish():
            o_ref[...] = work[3]

        def cut(j, c, level):
            return w_work.at[c, 0, pl.ds(pl.multiple_of(level * R, R), R), pl.ds(j * C, C)]

        def slot(j, g):
            return w_out.at[j, :, pl.ds(pl.multiple_of(g * C, C), C)]

        def deal():
            for i, (to, c, k) in enumerate(column):
                for j in range(3):
                    _send(cut(j, core ^ c, z ^ k), slot(j, group), t_send.at[i, j], t_recv.at[i, j], to)
            for j in range(3):
                slot(j, group)[...] = cut(j, core, z)[...]

        _run(
            _plane_sum_part(u, z, lambda h, v: w_ref.at[v // 2, h], w_work, (wp_buf, wq_buf), sems[5:10], rows, deal),
            _line_sum_part(u, z, lambda c, level: x_ref.at[c, level], work, (c_buf, z_buf), sems[:5], T, finish),
            _small_part(u, z, small_in, small_out, sems[12:]),
            _tree_part(u, z, ready_ref, tree, T, keep),
            order=LEAVE_ORDER,
        )
        for i, (to, c, k) in enumerate(column):
            for j in range(3):
                _expect(slot(j, 2 * (z ^ k) + (core ^ c)), t_recv.at[i, j], here)
                _sent(cut(j, core ^ c, z ^ k), t_send.at[i, j], here)

    outs = [jax.ShapeDtypeStruct((T, D), BF16), jax.ShapeDtypeStruct((3, R, 8 * C), BF16), jax.ShapeDtypeStruct((T, D), BF16)]
    outs += [jax.ShapeDtypeStruct((8, 4) + x.shape, x.dtype) for x in smalls]
    scratch = _line_sum_scratch(T, D) + _plane_sum_scratch(rows, W) + _tree_scratch(T, D) + LINE_SUM_SEMS + PLANE_SUM_SEMS
    scratch += [DMA((7, 3)), DMA((7, 3))] + _small_sems(n)
    specs = ([ANY_SPACE] * 3 + [IN_VMEM] * n, [IN_VMEM] * 3 + [ANY_SPACE] * n)
    return _comm(kernel, outs, scratch, collective_id, specs)(x, weights, ready, *smalls)


def _finish_kernel(
    h_ref, r_ref, rg_ref, first_ref, sum_ref, own_ref, wq_ref, wk_ref, wv_ref, dw_ref, do_ref, gain_ref, out_ref, hg_ref, ag_ref, *dws
):
    out_ref[...] = (r_ref[...] + (sum_ref[...].astype(F32) + own_ref[...].astype(F32))).astype(BF16)
    hidden, weighted = h_ref[...].astype(F32), first_ref[...].astype(F32)
    scale = norm_scale(hidden)
    mean = jnp.mean(weighted * hidden, axis=-1, keepdims=True)
    hg_ref[...] = rg_ref[...] + scale * weighted - hidden * (scale * scale * scale) * mean
    gain = gain_ref[...].astype(F32)[:, :1]
    total = jnp.zeros(dws[0].shape, F32)
    for j, ref in enumerate((wq_ref, wk_ref, wv_ref)):
        grad = dw_ref[j].astype(F32)
        total = total + grad * ref[...].astype(F32)
        dws[j][...] = grad * gain
    ag_ref[...] = jnp.sum(total, axis=1, keepdims=True)
    dws[3][...] = do_ref[...].astype(F32)


def finish(hidden, residual, residual_grad, first_weighted, out_sum, out_own, weights, weight_sum, out_weight_grad, gains):
    T, D = hidden.shape
    R = gains.shape[0]
    steps = 4 if R % 64 == 0 else 1

    def rows(count, width):
        return pl.BlockSpec((count // steps, width), lambda i: (i, 0))

    tokens, dense = rows(T, D), rows(R, D)
    return pl.pallas_call(
        _finish_kernel,
        out_shape=[
            jax.ShapeDtypeStruct((T, D), BF16),
            jax.ShapeDtypeStruct((T, D), F32),
            jax.ShapeDtypeStruct((R, 1), F32),
        ]
        + [jax.ShapeDtypeStruct((R, D), F32)] * 4,
        grid=(steps,),
        in_specs=[tokens] * 6
        + [dense] * 3
        + [pl.BlockSpec((3, R // steps, D), lambda i: (0, i, 0)), dense, rows(R, 4)],
        out_specs=[tokens, tokens, rows(R, 1)] + [dense] * 4,
        compiler_params=pltpu.CompilerParams(vmem_limit_bytes=VMEM_BYTES),
        cost_estimate=pl.CostEstimate(flops=20 * T * D, bytes_accessed=24 * T * D, transcendentals=0),
    )(hidden, residual, residual_grad, first_weighted, out_sum, out_own, *weights, weight_sum, out_weight_grad, gains)


class _Jobs:
    def __init__(self, load, compute):
        self.load, self.compute = load, compute
        self.queue, self.count, self.ready = [], 0, None

    def add(self, *jobs):
        self.queue += jobs

    def _next(self):
        if not self.queue:
            return None
        job = (self.count, self.queue.pop(0))
        self.count += 1
        self.load(*job, True)
        return job

    def run(self, number=1):
        for _ in range(number):
            now = self.ready or self._next()
            if now is None:
                return
            self.ready = self._next()
            self.load(*now, False)
            self.compute(*now)


def _gather_pick_kernel(
    x_ref, here_g, g0, g1, g2, g3, slot_ref, router_ref, o_ref, xr_ref, gr_ref, gate_ref, other_here, other_g, pick, in_buf, out_buf, in_sem, out_sem, *sems, width
):
    own_sem, z_send, z_recv, p_send, p_recv, c_send, c_recv, g_send, g_recv, h_send, h_recv = sems
    own_g = (g0, g1, g2, g3)
    u, z = lax.axis_index("uly"), lax.axis_index("blk")
    core, chip = u % 2, u // 2
    other = 1 - core
    T, D = x_ref.shape
    experts, group = slot_ref.shape[1:]
    slots = out_buf.shape[2]
    half = T // 2
    halves = (pl.ds(0, half), pl.ds(half, half))
    here = (u, z)
    _greet(u, z, (1, 2, 4), line=True)
    own = pltpu.make_async_copy(x_ref, o_ref.at[u * DEPTH + z], own_sem)
    own.start()
    order = _line_order(z)

    def block(who, level):
        return o_ref.at[who * DEPTH + level]

    def part(who, level, h):
        return o_ref.at[who * DEPTH + level, halves[h]]

    def load(n, job, start):
        source, level, which = job
        steps = (0, jnp.where(which == 0, 1, 2), jnp.where(which == 0, 2, 1), 3)
        for k in range(4):
            p = chip ^ steps[k]
            if source == "x":
                ref = o_ref.at[(2 * p + which) * DEPTH + level]
            elif source == 0:
                ref = (here_g if which is core else other_here).at[p]
            else:
                ref = (own_g[k] if which is core else other_g.at[k]).at[source - 1]
            rows = pl.ds(pl.multiple_of(p * T, T), T)
            copy = pltpu.make_async_copy(ref, in_buf.at[n % 2, rows], in_sem.at[n % 2, k])
            copy.start() if start else copy.wait()

    def out_copy(n, target, at):
        return pltpu.make_async_copy(out_buf.at[n % 2], target.at[:, at], out_sem.at[n % 2])

    sent = {}

    def compute(n, job):
        source, level, which = job
        at = 2 * level + which
        rows_in, rows_out = in_buf.at[n % 2], out_buf.at[n % 2]
        row = lax.broadcasted_iota(jnp.int32, (slots, group), 0)
        if source != "x":
            picks = [jnp.where(slot_ref[at, e : e + 1, :] == row, 1.0, 0.0).astype(BF16) for e in range(experts)]
            pick[at] = jnp.concatenate(picks, axis=0)
        else:
            logits = dot(rows_in[...], router_ref[...])
            powers = jnp.exp(logits - jnp.max(logits, axis=1, keepdims=True))
            chances = powers / jnp.sum(powers, axis=1, keepdims=True)
            high = chances.astype(BF16)
            low = (chances - high.astype(F32)).astype(BF16)
            gates = dot(pick[at], jnp.concatenate([high, low], axis=1))
            for e in range(experts):
                gate_ref[e, at] = gates[e * slots : (e + 1) * slots]
        if n >= 2:
            sent.pop(n - 2).wait()

        def step(i, _):
            cols = pl.ds(pl.multiple_of(i * width, width), width)
            rows = dot(pick[at], rows_in[:, cols]).astype(BF16)
            for e in range(experts):
                rows_out[e, :, cols] = rows[e * slots : (e + 1) * slots]
            return 0

        lax.fori_loop(0, D // width, step, 0)
        sent[n] = out_copy(n, xr_ref if source == "x" else gr_ref, at)
        sent[n].start()

    jobs = _Jobs(load, compute)
    jobs.add(*[(j, (z + j) % 4, core) for j in range(4)])

    def along(level, source, step):
        @pl.when((z > 0) & (level >= z))
        def _():
            step(source, 0, level, (u, z - 1))

        @pl.when((z < DEPTH - 1) & (level <= z))
        def _():
            step(source, 1, level, (u, z + 1))

    def go(source, way, level, to):
        _send(source, block(u, level), z_send.at[way, level], z_recv.at[level], to)

    def gone(source, way, level, to):
        _sent(source, z_send.at[way, level], here)

    sources = [x_ref] + [block(u, order[i]) for i in range(1, 4)]

    def arrive(i):
        level = order[i]
        if i:
            _expect(block(u, level), z_recv.at[level], here)
        along(level, sources[i], go)
        for way, bits in enumerate((FIRST, THEN)):
            for h in range(2):
                cut = sources[i].at[halves[h]]
                _send(cut, part(u, level, h), p_send.at[level, h, way], p_recv.at[level, h, way], (u ^ bits[h], z))
        _send(sources[i], block(u, level), c_send.at[level, 0], c_recv.at[level, 0], (u ^ 1, z))

    def onward(i):
        level = order[i]
        for h in range(2):
            near = part(u ^ FIRST[h], level, h)
            _expect(near, p_recv.at[level, h, 0], here)
            _send(near, near, p_send.at[level, h, 2], p_recv.at[level, h, 2], (u ^ THEN[h], z))

    def share(i):
        level = order[i]
        for h in range(2):
            _expect(part(u ^ THEN[h], level, h), p_recv.at[level, h, 1], here)
            _expect(part(u ^ 6, level, h), p_recv.at[level, h, 2], here)
        for k, bit in enumerate((2, 4, 6)):
            ref = block(u ^ bit, level)
            _send(ref, ref, c_send.at[level, k + 1], c_recv.at[level, k + 1], (u ^ 1, z))
        jobs.add(("x", level, core))

    def received(i):
        level = order[i]
        for k, bit in enumerate((0, 2, 4, 6)):
            _expect(block(u ^ 1 ^ bit, level), c_recv.at[level, k], here)
        jobs.add(("x", level, other))

    arrive(0)
    _send(here_g, other_here, h_send, h_recv, (u ^ 1, z))
    for k in range(4):
        _send(own_g[k], other_g.at[k], g_send.at[k], g_recv.at[k], (u ^ 1, z))
    jobs.run(2)
    onward(0)
    jobs.run(1)
    arrive(1)
    _expect(other_here, h_recv, here)
    for k in range(4):
        _expect(other_g.at[k], g_recv.at[k], here)
    jobs.add(*[(j, (z + j) % 4, other) for j in range(4)])
    jobs.run(2)
    own.wait()
    share(0)
    jobs.run(2)
    onward(1)
    arrive(2)
    received(0)
    jobs.run(2)
    arrive(3)
    share(1)
    received(1)
    jobs.run(1)
    onward(2)
    jobs.run(2)
    share(2)
    received(2)
    jobs.run(1)
    onward(3)
    jobs.run(2)
    share(3)
    received(3)
    jobs.run(16)
    for i in range(4):
        level = order[i]
        along(level, sources[i], gone)
        for h in range(2):
            for k in range(3):
                _sent(part(u, level, h), p_send.at[level, h, k], here)
        for k in range(4):
            _sent(block(u, level), c_send.at[level, k], here)
    _sent(other_here, h_send, here)
    for k in range(4):
        _sent(other_g.at[k], g_send.at[k], here)
    for copy in sent.values():
        copy.wait()


def gather_pick(x, here_g, g, slot, router, slots, collective_id):
    T, D = x.shape
    groups, EL, group = slot.shape
    picked = jax.ShapeDtypeStruct((EL, groups, slots, D), BF16)
    outs = [
        jax.ShapeDtypeStruct((32, T, D), BF16),
        picked,
        picked,
        jax.ShapeDtypeStruct((EL, groups, slots, 128), F32),
        jax.ShapeDtypeStruct((4, T, D), BF16),
        jax.ShapeDtypeStruct((4, 3, T, D), BF16),
    ]
    scratch = [
        pltpu.VMEM((groups, EL * slots, group), BF16),
        pltpu.VMEM((2, group, D), BF16),
        pltpu.VMEM((2, EL, slots, D), BF16),
        DMA((2, 4)),
        DMA((2,)),
        DMA,
        DMA((2, 4)),
        DMA((4,)),
        DMA((4, 2, 3)),
        DMA((4, 2, 3)),
        DMA((4, 4)),
        DMA((4, 4)),
        DMA((4,)),
        DMA((4,)),
        DMA,
        DMA,
    ]
    specs = ([IN_VMEM] + [ANY_SPACE] * 5 + [IN_VMEM] * 2, [ANY_SPACE] * 3 + [IN_VMEM] + [ANY_SPACE] * 2)
    kernel = functools.partial(_gather_pick_kernel, width=PICK_WIDTH)
    out, xr, gr, gates, *_ = _comm(kernel, outs, scratch, collective_id, specs)(x, here_g, *g, slot, router)
    return out.reshape(32 * T, D), xr, gr, gates


def _tree_sum_steps(u, z, own, bufs, sems, T, count):
    c_buf, p_buf, q_buf = bufs
    c_send, c_recv, p_send, p_recv, q_send, q_recv = sems
    here = (u, z)
    half = T // 2
    halves = (pl.ds(0, half), pl.ds(half, half))

    def to_sibling(i, k, ref):
        _send(ref, c_buf.at[i, k], c_send.at[i, k], c_recv.at[i, k], (u ^ 1, z))

    def add_core(i):
        for k in (3, 2, 1, 0):
            _expect(c_buf.at[i, k], c_recv.at[i, k], here)
            _accumulate(own(i, k), c_buf.at[i, k], T)
            for h in range(2):
                if k and (k == 3 or CHIPS[k] == THEN[h]):
                    j = 1 if k == 3 else 0
                    part = own(i, k).at[halves[h]]
                    _send(part, p_buf.at[i, h, j], p_send.at[i, h, j], p_recv.at[i, h, j], (u ^ THEN[h], z))

    def add_far(i):
        for h in range(2):
            part = own(i, CHIPS.index(FIRST[h])).at[halves[h]]
            _expect(p_buf.at[i, h, 1], p_recv.at[i, h, 1], here)
            _accumulate(part, p_buf.at[i, h, 1], half)
            _send(part, q_buf.at[i, h], q_send.at[i, h], q_recv.at[i, h], (u ^ FIRST[h], z))

    def add_near(i):
        for h in range(2):
            _expect(p_buf.at[i, h, 0], p_recv.at[i, h, 0], here)
            _accumulate(own(i, 0).at[halves[h]], p_buf.at[i, h, 0], half)

    def add_then(i):
        for h in range(2):
            _expect(q_buf.at[i, h], q_recv.at[i, h], here)
            _accumulate(own(i, 0).at[halves[h]], q_buf.at[i, h], half)

    def finish():
        for i in range(count):
            for k in range(4):
                _sent(c_buf.at[i, k], c_send.at[i, k], here)
            for h in range(2):
                for j in range(2):
                    _sent(p_buf.at[i, h, j], p_send.at[i, h, j], here)
                _sent(q_buf.at[i, h], q_send.at[i, h], here)

    return to_sibling, add_core, add_far, add_near, add_then, finish


def _line_end(u, z, level, i, part, z_buf, sems, rows):
    z_send, z_recv = sems
    here = (u, z)

    @pl.when((level >= z) & (z > 0))
    def _():
        _expect(z_buf.at[0, level], z_recv.at[0, level], here)
        _accumulate(part, z_buf.at[0, level], rows)

    @pl.when((level <= z) & (z < DEPTH - 1))
    def _():
        _expect(z_buf.at[1, level], z_recv.at[1, level], here)
        _accumulate(part, z_buf.at[1, level], rows)

    if i < 3:

        @pl.when(level > z)
        def _():
            _send(part, z_buf.at[0, level], z_send.at[i], z_recv.at[0, level], (u, z + 1))

        @pl.when(level < z)
        def _():
            _send(part, z_buf.at[1, level], z_send.at[i], z_recv.at[1, level], (u, z - 1))


def _place(chip, k, T):
    return pl.ds(pl.multiple_of((chip ^ (CHIPS[k] // 2)) * T, T), T)


def _tree_part(u, z, ready, refs, T, then_do):
    work, c_buf, p_buf, q_buf, sem = refs[:5]
    core, chip = u % 2, u // 2
    to_sibling, add_core, add_far, add_near, add_then, finish = _tree_sum_steps(
        u, z, lambda i, k: work.at[_place(chip, k, T)], (c_buf, p_buf, q_buf), refs[5:], T, 1
    )
    for k in (3, 2, 1, 0):
        to_sibling(0, k, ready.at[1 - core, _place(chip, k, T)])
    copy = pltpu.make_async_copy(ready.at[core], work, sem)
    copy.start()
    yield
    copy.wait()
    add_core(0)
    yield
    add_far(0)
    yield
    add_near(0)
    add_then(0)
    then_do(work.at[_place(chip, 0, T)])
    yield
    finish()


def _tree_scratch(T, D):
    half = T // 2
    return [
        pltpu.VMEM((4 * T, D), BF16),
        pltpu.VMEM((1, 4, T, D), BF16),
        pltpu.VMEM((1, 2, 2, half, D), BF16),
        pltpu.VMEM((1, 2, half, D), BF16),
        DMA,
        DMA((1, 4)),
        DMA((1, 4)),
        DMA((1, 2, 2)),
        DMA((1, 2, 2)),
        DMA((1, 2)),
        DMA((1, 2)),
    ]


def _spread_part(u, z, slot_ref, source, gg_ref, order, refs, level_done, later=lambda i: None, extra=None):
    work, c_buf, p_buf, q_buf, side, in_buf, in_sem = refs[:7]
    core, chip = u % 2, u // 2
    other = 1 - core
    _, group, experts = slot_ref.shape
    slots, D = source.shape[2:]
    total = experts * slots
    T = group // 4
    count = len(order)

    def place(k):
        return _place(chip, k, T)

    def own(i, k):
        return work.at[i, place(k)]

    to_sibling, add_core, add_far, add_near, add_then, finish = _tree_sum_steps(
        u, z, own, (c_buf, p_buf, q_buf), refs[7:], T, count
    )
    lane = lax.broadcasted_iota(jnp.int32, (experts, total), 1)
    which = lax.broadcasted_iota(jnp.int32, (experts, total), 0)
    choose = jnp.where((lane >= which * slots) & (lane < (which + 1) * slots), 1.0, 0.0).astype(BF16)
    offset = lane[:1] - jnp.sum(jnp.where(lane >= (which + 1) * slots, slots, 0), axis=0, keepdims=True)
    offset = offset.astype(F32)
    column = lax.broadcasted_iota(jnp.int32, (slots, 128), 1)

    def load(n, job, start):
        i, c = job
        level = z if i is None else order[i]
        copy = pltpu.make_async_copy(source.at[:, 2 * level + c], in_buf.at[n % 2], in_sem.at[n % 2])
        copy.start() if start else copy.wait()

    def compute(n, job):
        i, c = job
        at = 2 * (z if i is None else order[i]) + c
        mine = dot(slot_ref[at].astype(BF16), choose)
        pick = jnp.where(mine == offset, 1.0, 0.0).astype(BF16)
        rows_in = in_buf.at[n % 2]
        if i is None:
            target = extra[0].at[c]
        else:
            target = work.at[i] if c is core else side.at[i]
        if gg_ref is not None:
            grads = [jnp.where(column == u * experts + e, gg_ref[e, at], 0.0).astype(BF16) for e in range(experts)]
            target[:, pl.ds(D, 128)] = dot(pick, jnp.concatenate(grads, axis=0)).astype(BF16)

        def step(j, _):
            cols = pl.ds(pl.multiple_of(j * SPREAD_WIDTH, SPREAD_WIDTH), SPREAD_WIDTH)
            rows = jnp.concatenate([rows_in[e, :, cols] for e in range(experts)], axis=0)
            target[:, cols] = dot(pick, rows).astype(BF16)
            return 0

        lax.fori_loop(0, D // SPREAD_WIDTH, step, 0)
        if i is None:
            extra_copy(c).start()
        elif c is not core:
            for k in (3, 2, 1, 0):
                to_sibling(i, k, side.at[i, place(k)])

    def extra_copy(c):
        return pltpu.make_async_copy(extra[0].at[c], extra[1].at[c], extra[2].at[c])

    def end(i):
        add_then(i)
        level_done(i, own(i, 0))

    jobs = _Jobs(load, compute)
    for i in range(count):
        jobs.add((i, other), (i, core))
    if extra is not None:
        jobs.add((None, 0), (None, 1))
    for step in range(count + 3):
        if step >= 3:
            end(step - 3)
            later(step - 3)
        if 0 <= step - 2 < count:
            add_near(step - 2)
        jobs.run(2 if step < count else 1)
        if 0 <= step - 1 < count:
            add_far(step - 1)
        if step < count:
            add_core(step)
        yield
    if extra is not None:
        extra_copy(0).wait()
        extra_copy(1).wait()
    yield
    finish()


def _spread_scratch(T, W, rows_shape, count=4):
    half = T // 2
    return [
        pltpu.VMEM((count, 4 * T, W), BF16),
        pltpu.VMEM((count, 4, T, W), BF16),
        pltpu.VMEM((count, 2, 2, half, W), BF16),
        pltpu.VMEM((count, 2, half, W), BF16),
        pltpu.VMEM((count, 4 * T, W), BF16),
        pltpu.VMEM((2,) + rows_shape, BF16),
        DMA((2,)),
        DMA((count, 4)),
        DMA((count, 4)),
        DMA((count, 2, 2)),
        DMA((count, 2, 2)),
        DMA((count, 2)),
        DMA((count, 2)),
    ]


def spread_scatter(slot, gate_grads, entry_rows, collective_id):
    groups, group, EL = slot.shape
    slots, D = entry_rows.shape[2:]
    T, W = group // 4, D + 128

    def kernel(slot_ref, gg_ref, entry_ref, o_ref, z_buf, z_send, z_recv, *refs):
        u, z = lax.axis_index("uly"), lax.axis_index("blk")
        order = tuple(reversed(_line_order(z)))
        parts = []

        def done(i, part):
            parts.append(part)

        def line(i):
            _line_end(u, z, order[i], i, parts[i], z_buf, (z_send, z_recv), T)

        _greet(u, z, (1, 2, 4), line=True)
        _run(_spread_part(u, z, slot_ref, entry_ref, gg_ref, order, refs, done, line))
        o_ref[...] = parts[3][...]
        for i in range(3):
            _sent(parts[i], z_send.at[i], (u, z))

    scratch = [pltpu.VMEM((2, 4, T, W), BF16), DMA((4,)), DMA((2, 4))] + _spread_scratch(T, W, (EL, slots, D))
    specs = ([IN_VMEM, IN_VMEM, ANY_SPACE], IN_VMEM)
    out = jax.ShapeDtypeStruct((T, W), BF16)
    return _comm(kernel, out, scratch, collective_id, specs)(slot, gate_grads, entry_rows)


def slots_of(chosen):
    count = chosen.shape[-1]
    before = (jnp.arange(count)[:, None] < jnp.arange(count)[None, :]).astype(BF16)
    earlier = jnp.einsum("abs,st->abt", chosen.astype(BF16), before, preferred_element_type=F32)
    return jnp.where(chosen, earlier.astype(jnp.int32), -1)


class Slice:
    def __init__(self, U, Z, T, D):
        self.U, self.Z, self.T, self.D = U, Z, T, D
        self.u, self.z = lax.axis_index("uly"), lax.axis_index("blk")
        self.C = D // 8
        self.L = 8 * T
        self.group = 2 * self.z + self.u % 2
        self.first_block, self.block_step = 8 * (self.u // 2), 1
        self.rows = ATTEND_ROWS

    def enter(self, hidden, weights, gains, out_weight, router, routes, out_grad):
        rows, weights, packs, routes, self.here = enter(hidden, weights, gains, router, routes, out_grad, 1)
        there = [((2 * ((z + u // 2) % 4) + u % 2), u // 2) for u in range(8) for z in range(4)]
        self.forth = [(i, 4 * u + z) for i, (u, z) in enumerate(there)]
        rows, mine = lax.optimization_barrier((rows, self.permute(out_weight, self.forth)))
        self.out_parts = [mine] + [self.permute(mine, self.across(bit)) for bit in (2, 4, 6)]
        self.parts = [((self.u // 2) ^ k) - self.z + 4 for k in range(4)]
        self.parts = [p % 4 for p in self.parts]
        return (
            rows.reshape(self.L, self.D),
            weights.reshape(self.D, 3 * self.C),
            packs.reshape(self.D, -1),
            routes,
        )

    def permute(self, x, pairs):
        return lax.ppermute(x, ALL, pairs)

    def across(self, bit):
        return [(i, i ^ (4 * bit)) for i in range(32)]

    def sequence(self, key, value, squares, upstream):
        keys, values, own, stats, k_stat = plane_pair(key, value, upstream, squares.reshape(-1, 128), 4)
        own, *self.out_parts = lax.optimization_barrier((own, *self.out_parts))
        first = [(i, i ^ (8 if i // 4 % 2 == 0 else 16)) for i in range(32)]
        self.then = [(i, i ^ (16 if i // 4 % 2 == 0 else 8)) for i in range(32)]
        self.upstream = (own, self.permute(own, first))
        return keys.reshape(-1, self.C), values.reshape(-1, self.C), stats.reshape(2, -1, 128), k_stat.reshape(-1, 128)

    def heads_to_rows(self, x):
        x, own, near, *self.prepared = lax.optimization_barrier((x, *self.upstream, *self.prepared))
        self.upstream = (own, near, self.permute(own, self.then), self.permute(near, self.then))
        return column_scatter(x.reshape(2, 4, self.T, self.D), 5)

    def prepare(self, routes, EL, router):
        T = self.T
        chosen = jnp.any(routes[None] == (self.u * EL + jnp.arange(EL, dtype=jnp.int32))[:, None, None, None, None], axis=3)
        chosen = chosen.reshape(EL, 4, 2, 4, T).transpose(3, 2, 0, 1, 4).reshape(8, EL, 4 * T)
        slot = slots_of(chosen)
        self.prepared = (slot, slot.transpose(0, 2, 1), router)

    def experts(self, second_low, weights):
        EL, D = weights.shape[0], self.D
        slots = -(-4 * CAP // 16) * 16
        slot, self.slot, router = self.prepared
        second_all, xr, gr, gates = gather_pick(second_low, self.here, self.upstream, slot, router, slots, 7)
        flat, cut = (EL, 8 * slots, -1), (EL, 8, slots, -1)
        out_rows, entry_rows, self.expert_grads, gate_grads = run_experts(
            xr.reshape(flat), gr.reshape(flat), gates.reshape(flat), weights, 8 * slots
        )
        self.out_rows = out_rows.reshape(cut)
        return second_all, spread_scatter(self.slot, gate_grads.reshape(cut), entry_rows.reshape(cut), 8)

    def rows_to_heads(self, x):
        rows, self.out_line, self.out_here = column_gather(x, self.slot, self.out_rows, 6)
        return rows.reshape(self.L, self.D), self.expert_grads

    def sequence_sums(self, dk, dv, out_part, q_inner, k_inner):
        cut = (4, self.L, self.C)
        inner = jnp.concatenate([q_inner, k_inner.reshape(-1, 128)], axis=0)
        dk, dv, out_sum, inner = key_value_sums(dk.reshape(cut), dv.reshape(cut), self.out_line, inner, 10)
        parts = out_part.reshape(4, -1, self.D)
        mine, *others = [lax.dynamic_index_in_dim(parts, p, 0, False) for p in self.parts]
        dk, *others = lax.optimization_barrier((dk, *others))
        self.out_terms = [mine] + [self.permute(x, self.across(bit)) for x, bit in zip(others, (2, 4, 6))]
        return dk, dv, out_sum, inner.reshape(2, -1, 128)

    def leave(self, first_part, weight_part, logit_grad, ffn_part, head_parts):
        T, R = self.T, self.D // 32
        first_part, *terms = lax.optimization_barrier((first_part, *self.out_terms))
        out_grad = sum(x.astype(F32) for x in terms).astype(BF16)
        out_grad = self.permute(out_grad, [(b, a) for a, b in self.forth])
        thin = jnp.concatenate([ffn_part.reshape(-1, 128), head_parts.reshape(-1, 128)], axis=0)
        wide = self.D // 128
        used = thin.shape[0]
        thin = jnp.pad(thin, ((0, -used % 8), (0, 0)))
        first, weights, self.out_own, logit_all, thin = leave(
            first_part.reshape(2, 4, T, self.D),
            weight_part.reshape(4, 2, 4 * R, 3 * self.C),
            [logit_grad.reshape(T // 2, 2 * EXPERTS), thin],
            self.out_here,
            11,
        )
        ffn = lax.dynamic_slice_in_dim(
            jnp.sum(thin[:, :, :wide], axis=(0, 1)).reshape(self.D), (self.u * 4 + self.z) * R, R, 0
        )
        mine = lax.dynamic_index_in_dim(thin.reshape(4, 2, 4, -1, 128), self.u % 2, 1, False)
        mine = lax.dynamic_index_in_dim(mine, self.u // 2, 1, False)
        heads = jnp.sum(mine[:, wide:used], axis=0).reshape(2, self.C)
        heads = lax.dynamic_slice_in_dim(heads, self.z * R, R, 1)
        return first, weights, out_grad, logit_all.reshape(32 * T, EXPERTS), ffn, heads


class General:
    def __init__(self, U, Z, T, D):
        self.U, self.Z, self.T, self.D = U, Z, T, D
        self.u, self.z = lax.axis_index("uly"), lax.axis_index("blk")
        self.C = D // U
        self.L = U * T
        self.group = self.u
        self.parts = range(4)
        self.first_block, self.block_step = self.z, Z
        self.rows = T

    def gather(self, x):
        return lax.all_gather(x, ALL, axis=0, tiled=True)

    def scatter_wide(self, x):
        return lax.psum_scatter(x, ALL, scatter_dimension=0, tiled=True)

    def enter(self, hidden, weights, gains, out_weight, router, routes, out_grad):
        U, R = self.U, router.shape[0]
        gains, hidden = gains.astype(F32), hidden.astype(F32)
        scaled = jnp.stack([(w.astype(F32) * gains[:, :1]).astype(BF16) for w in weights])
        pack = jnp.concatenate(_packed(router, gains), axis=1)
        rows = (hidden * norm_scale(hidden)).astype(BF16)
        self.out_parts = jnp.split(lax.all_gather(out_weight, "blk", axis=0, tiled=True), 4)
        swapped = lax.all_to_all(scaled.transpose(1, 0, 2).reshape(R, 3, U, self.C), "uly", split_axis=2, concat_axis=0, tiled=True)
        weights = lax.all_gather(swapped.reshape(U, R, 3 * self.C), "blk", axis=1, tiled=True)
        return (
            self.rows_all(rows),
            weights.reshape(self.D, 3 * self.C),
            self.gather(pack),
            self.gather(routes[None]).reshape((U, self.Z) + routes.shape),
        )

    def sequence(self, key, value, squares, upstream):
        self.upstream = upstream
        pair = jnp.stack([key, value]).reshape(2, self.U, self.T, self.C)
        pair = lax.all_gather(pair, "blk", axis=2, tiled=False).reshape(2, -1, self.C)
        stats = lax.psum(squares, "uly")
        k_stat = lax.all_gather(stats[1].reshape(self.U, -1, 128), "blk", axis=1, tiled=False).reshape(-1, 128)
        return pair[0], pair[1], stats, k_stat

    def heads_to_rows(self, x):
        return self.rows_sum(x)

    def rows_sum(self, x):
        return lax.psum_scatter(x, "uly", scatter_dimension=0, tiled=True)

    def rows_all(self, x):
        return lax.all_gather(x, "uly", axis=0, tiled=True)

    def prepare(self, routes, EL, router):
        self.prepared = (routes, router)

    def experts(self, second_low, weights):
        EL, D = weights.shape[0], self.D
        routes, router = self.prepared
        second_all, upstream_all = self.gather(second_low), self.gather(self.upstream)
        N = upstream_all.shape[0]
        group = min(512, N)
        groups = N // group
        slots = -(-(group // self.T * CAP) // 16) * 16
        rows = groups * slots
        own_first = self.u * EL
        chosen = jnp.any(routes[None] == (own_first + jnp.arange(EL, dtype=jnp.int32))[:, None, None, None, None], axis=3)
        slot = slots_of(chosen.reshape(EL, groups, group)).reshape(EL, N)
        entry_in, upstream_in, gates = pick_rows(slot, router, second_all, upstream_all, group, slots)
        flat, split = (EL, rows, -1), (EL, groups, slots, -1)
        out_rows, entry_rows, self.expert_grads, gate_grads = run_experts(
            entry_in.reshape(flat), upstream_in.reshape(flat), gates.reshape(flat), weights, min(8, groups) * slots
        )
        out_part, entry_part = spread_rows(
            own_first.astype(jnp.int32)[None],
            slot.T,
            gate_grads.reshape(split),
            out_rows.reshape(split),
            entry_rows.reshape(split),
            group,
        )
        self.out_sum = self.scatter_wide(out_part)
        self.out_own = jnp.zeros_like(self.out_sum)
        return second_all, self.scatter_wide(entry_part)

    def rows_to_heads(self, x):
        return self.rows_all(x), self.expert_grads

    def sequence_sums(self, dk, dv, out_part, q_inner, k_inner):
        pair = jnp.stack([dk, dv]).reshape(2, self.U, self.Z, self.T, self.C)
        pair = lax.psum_scatter(pair, "blk", scatter_dimension=2, tiled=True).reshape(2, self.L, self.C)
        k_inner = lax.psum_scatter(
            k_inner.reshape(self.U, self.Z, -1, 128), "blk", scatter_dimension=1, tiled=True
        ).reshape(-1, 128)
        inner = lax.psum(jnp.stack([q_inner, k_inner]), "uly")
        self.out_grad = lax.psum_scatter(out_part, "blk", scatter_dimension=0, tiled=True)
        return pair[0], pair[1], self.out_sum, inner

    def leave(self, first_part, weight_part, logit_grad, ffn_part, head_parts):
        U, R = self.U, self.D // (self.U * self.Z)
        part = weight_part.reshape(U, self.Z * R, 3 * self.C)
        part = lax.psum_scatter(part, "blk", scatter_dimension=1, tiled=True)
        part = lax.all_to_all(part, "uly", split_axis=0, concat_axis=0, tiled=True)
        weights = part.reshape(U, R, 3, self.C).transpose(2, 1, 0, 3).reshape(3, R, self.D)
        heads = lax.psum_scatter(head_parts, "blk", scatter_dimension=1, tiled=True)
        first = self.rows_sum(first_part)
        return first, weights, self.out_grad, self.gather(logit_grad), self.scatter_wide(ffn_part), heads


def _row_limits(doc_ref, first, rows):
    position = first + lax.broadcasted_iota(jnp.int32, (rows, 1), 0)
    start = jnp.zeros_like(position)
    lowest = jnp.int32(0)
    for d in range(doc_ref.shape[0]):
        begin = doc_ref[d]
        start = jnp.where(begin <= position, jnp.maximum(start, begin), start)
        lowest = jnp.where(begin <= first, jnp.maximum(lowest, begin), lowest)
    return position, start, lowest


def _norm_row(squares, width):
    return lax.rsqrt(squares * (1.0 / width) + EPS)


def _as_column(row):
    return jnp.broadcast_to(row, (128, 128)).T


def _row_sums(values):
    ones = jnp.ones((8, values.shape[1]), F32)
    return lax.dot_general(ones, values, LAST_DIM, precision=lax.Precision.HIGHEST, preferred_element_type=F32)[:1]


def _key_scales(stat_ref, at, chunk, width):
    rows = stat_ref[pl.ds(pl.multiple_of(at // 128, chunk // 128), chunk // 128), :]
    return _norm_row(jnp.concatenate([rows[r : r + 1] for r in range(chunk // 128)], axis=1), width)


def _scores(query, key, factor, position, start, key_first):
    raw = dot(query, key, LAST_DIM) * factor
    key_position = key_first + lax.broadcasted_iota(jnp.int32, raw.shape, 1)
    return jnp.where((key_position <= position) & (key_position >= start), raw, NEG)


def _scaled_query(q_ref, stat_ref, width):
    heads, units = q_ref.shape[1] // HEAD_DIM, q_ref.shape[0] // 128
    scale = jnp.concatenate(
        [_as_column(_norm_row(stat_ref[pl.ds(pl.program_id(0) * units + r, 1), :], width)) for r in range(units)], axis=0
    )
    cols = [pl.ds(h * HEAD_DIM, HEAD_DIM) for h in range(heads)]
    return [(q_ref[:, at].astype(F32) * scale).astype(BF16) for at in cols], cols


def _lay_parts(index_ref, parts, whole):
    @pl.when(pl.program_id(0) == 0)
    def _():
        for i, part in enumerate(parts):
            height = part.shape[0]
            whole[pl.ds(pl.multiple_of(index_ref[2 + i] * height, height), height), :] = part[...]


def _attend_kernel(
    index_ref, doc_ref, q_stat, k_stat, q_ref, k_ref, v_ref, w0, w1, w2, w3, o_ref, log_ref, mix_ref, whole, *, chunk, scaling, width
):
    rows = q_ref.shape[0]
    _lay_parts(index_ref, (w0, w1, w2, w3), whole)
    heads = q_ref.shape[1] // HEAD_DIM
    first = (pl.program_id(0) * index_ref[1] + index_ref[0]) * rows
    position, start, lowest = _row_limits(doc_ref, first, rows)
    queries, cols = _scaled_query(q_ref, q_stat, width)

    def step(i, state):
        at = pl.multiple_of(i * chunk, chunk)
        factor = _key_scales(k_stat, at, chunk, width) * scaling
        new = []
        for h in range(heads):
            top, total, out = state[h]
            scores = _scores(queries[h], k_ref[pl.ds(at, chunk), cols[h]], factor, position, start, at)
            now = jnp.maximum(top, jnp.max(scores, axis=1, keepdims=True))
            weights = jnp.exp(scores - now)
            fade = jnp.exp(top - now)
            total = total * fade + jnp.sum(weights, axis=1, keepdims=True)
            out = out * fade + dot(weights.astype(BF16), v_ref[pl.ds(at, chunk), cols[h]])
            new.append((now, total, out))
        return tuple(new)

    zero = (
        jnp.full((rows, 1), NEG, F32),
        jnp.zeros((rows, 1), F32),
        jnp.zeros((rows, HEAD_DIM), F32),
    )
    last = first + rows
    state = lax.fori_loop(lowest // chunk, (last + chunk - 1) // chunk, step, (zero,) * heads)
    for h in range(heads):
        top, total, out = state[h]
        o_ref[:, cols[h]] = out / total
        log_ref[:, cols[h]] = jnp.broadcast_to(top + jnp.log(total), (rows, HEAD_DIM))
    mix_ref[...] = dot(o_ref[...].astype(BF16), whole[...]).astype(BF16)


def _attend_back_kernel(
    index_ref,
    doc_ref,
    q_stat,
    k_stat,
    q_ref,
    r_ref,
    o_ref,
    log_ref,
    k_ref,
    v_ref,
    w0,
    w1,
    w2,
    w3,
    dq_ref,
    dk_ref,
    dv_ref,
    dw_ref,
    mq_ref,
    mk_ref,
    dk_sum,
    dv_sum,
    dw_sum,
    whole,
    *,
    chunk,
    scaling,
    width,
):
    rows = q_ref.shape[0]
    _lay_parts(index_ref, (w0, w1, w2, w3), whole)
    heads = q_ref.shape[1] // HEAD_DIM
    first = (pl.program_id(0) * index_ref[1] + index_ref[0]) * rows
    position, start, lowest = _row_limits(doc_ref, first, rows)
    queries, cols = _scaled_query(q_ref, q_stat, width)

    @pl.when(pl.program_id(0) == 0)
    def _():
        dk_sum[...] = jnp.zeros_like(dk_sum)
        dv_sum[...] = jnp.zeros_like(dv_sum)
        dw_sum[...] = jnp.zeros_like(dw_sum)
        mk_ref[...] = jnp.zeros_like(mk_ref)

    upstream = r_ref[...]
    dw_sum[...] += dot(o_ref[...].astype(BF16), upstream, FIRST_DIM)
    all_grads = dot(upstream, whole[...], LAST_DIM).astype(BF16)
    grads = [all_grads[:, h * HEAD_DIM : (h + 1) * HEAD_DIM] for h in range(heads)]
    deltas = [jnp.sum(grads[h].astype(F32) * o_ref[:, cols[h]], axis=1, keepdims=True) for h in range(heads)]
    logs = [log_ref[:, at][:, :1] for at in cols]

    def step(i, state):
        at = pl.multiple_of(i * chunk, chunk)
        scale = _key_scales(k_stat, at, chunk, width)
        new = []
        key_inner = jnp.zeros((1, chunk), F32)
        query_inner = state[-1]
        for h in range(heads):
            grad = grads[h]
            key = k_ref[pl.ds(at, chunk), cols[h]]
            scores = _scores(queries[h], key, scale * scaling, position, start, at)
            weights = jnp.exp(scores - logs[h])
            weight_grad = dot(grad, v_ref[pl.ds(at, chunk), cols[h]], LAST_DIM)
            score_grad = weights * (weight_grad - deltas[h])
            inner = score_grad * scores
            key_inner = key_inner + jnp.sum(inner, axis=0, keepdims=True)
            query_inner = query_inner + jnp.sum(inner, axis=1, keepdims=True)
            dv_sum[pl.ds(at, chunk), cols[h]] += dot(weights.astype(BF16), grad, FIRST_DIM)
            dk_sum[pl.ds(at, chunk), cols[h]] += dot(score_grad.astype(BF16), queries[h], FIRST_DIM)
            new.append(state[h] + dot((score_grad * scale).astype(BF16), key))
        mk_ref[pl.ds(i, 1), :] += key_inner
        return tuple(new) + (query_inner,)

    last = first + rows
    zeros = (jnp.zeros((rows, HEAD_DIM), F32),) * heads + (jnp.zeros((rows, 1), F32),)
    state = lax.fori_loop(lowest // chunk, (last + chunk - 1) // chunk, step, zeros)
    for h in range(heads):
        dq_ref[:, cols[h]] = (state[h] * scaling).astype(BF16)
    for r in range(rows // 128):
        inner = jnp.broadcast_to(state[-1][r * 128 : (r + 1) * 128], (128, 128)).T[:1]
        mq_ref[pl.ds(pl.program_id(0) * (rows // 128) + r, 1), :] = inner

    @pl.when(pl.program_id(0) == pl.num_programs(0) - 1)
    def _():
        dk_ref[...] = (dk_sum[...] * scaling).astype(BF16)
        dv_ref[...] = dv_sum[...].astype(BF16)
        dw_ref[...] = dw_sum[...].astype(BF16)


def _resident(*shape):
    return pl.BlockSpec(shape, lambda i, *_: (0,) * len(shape), pipeline_mode=pl.Buffered(1))


def attention_forward(index, docs, q_stat, k_stat, query, key_all, value_all, out_parts, rows, chunk):
    (L, C), N = query.shape, key_all.shape[0]
    D = out_parts[0].shape[1]
    block = pl.BlockSpec((rows, C), lambda i, *_: (i, 0))
    stats = [_resident(*q_stat.shape), _resident(*k_stat.shape)]
    return pl.pallas_call(
        functools.partial(_attend_kernel, chunk=chunk, scaling=HEAD_DIM ** (-0.5), width=HEADS * HEAD_DIM),
        out_shape=[jax.ShapeDtypeStruct((L, C), F32)] * 2 + [jax.ShapeDtypeStruct((L, D), BF16)],
        grid_spec=pltpu.PrefetchScalarGridSpec(
            num_scalar_prefetch=2,
            grid=(L // rows,),
            in_specs=stats + [block, _resident(N, C), _resident(N, C)] + [_resident(C // 4, D)] * 4,
            out_specs=[block, block, pl.BlockSpec((rows, D), lambda i, *_: (i, 0))],
            scratch_shapes=[pltpu.VMEM((C, D), BF16)],
        ),
        compiler_params=pltpu.CompilerParams(vmem_limit_bytes=VMEM_BYTES),
        cost_estimate=pl.CostEstimate(flops=4 * L * C * 1024, bytes_accessed=4 * N * C, transcendentals=L * 1024),
    )(index, docs, q_stat, k_stat, query, key_all, value_all, *out_parts)


def attention_backward(
    index, docs, q_stat, k_stat, query, residual_grad, attended, logs, key_all, value_all, out_parts, rows, chunk
):
    (L, C), N = query.shape, key_all.shape[0]
    D = residual_grad.shape[1]
    block = pl.BlockSpec((rows, C), lambda i, *_: (i, 0))
    whole = _resident(N, C)
    stats = [_resident(*q_stat.shape), _resident(*k_stat.shape)]
    return pl.pallas_call(
        functools.partial(_attend_back_kernel, chunk=chunk, scaling=HEAD_DIM ** (-0.5), width=HEADS * HEAD_DIM),
        out_shape=[jax.ShapeDtypeStruct((L, C), BF16)]
        + [jax.ShapeDtypeStruct((N, C), BF16)] * 2
        + [jax.ShapeDtypeStruct((C, D), BF16)]
        + [jax.ShapeDtypeStruct(q_stat.shape, F32), jax.ShapeDtypeStruct((N // chunk, chunk), F32)],
        grid_spec=pltpu.PrefetchScalarGridSpec(
            num_scalar_prefetch=2,
            grid=(L // rows,),
            in_specs=stats
            + [block, pl.BlockSpec((rows, D), lambda i, *_: (i, 0)), block, block, whole, whole]
            + [_resident(C // 4, D)] * 4,
            out_specs=[block, whole, whole, _resident(C, D), stats[0], _resident(N // chunk, chunk)],
            scratch_shapes=[pltpu.VMEM((N, C), F32)] * 2 + [pltpu.VMEM((C, D), F32), pltpu.VMEM((C, D), BF16)],
        ),
        compiler_params=pltpu.CompilerParams(vmem_limit_bytes=VMEM_BYTES),
        cost_estimate=pl.CostEstimate(flops=10 * L * C * 1024, bytes_accessed=8 * N * C, transcendentals=L * 1024),
    )(index, docs, q_stat, k_stat, query, residual_grad, attended, logs, key_all, value_all, *out_parts)


def _project_kernel(x_ref, w_ref, gain_ref, cos_ref, sin_ref, pre_ref, q_ref, k_ref, v_ref, stat_ref):
    rows = x_ref.shape[0]
    C = q_ref.shape[1]
    pre = dot(x_ref[...], w_ref[...])
    pre_ref[...] = pre[:, : 2 * C]
    v_ref[...] = pre[:, 2 * C :].astype(BF16)
    cosine, sine = cos_ref[...], sin_ref[...]
    for j, out in enumerate((q_ref, k_ref)):
        part = pre[:, j * C : (j + 1) * C]
        sums = _row_sums(part * part)
        for r in range(rows // 128):
            stat_ref[j, pl.ds(pl.program_id(0) * (rows // 128) + r, 1), :] = sums[:, r * 128 : (r + 1) * 128]
        scaled = part * gain_ref[j : j + 1, :]
        for h in range(C // HEAD_DIM):
            one = scaled[:, h * HEAD_DIM : (h + 1) * HEAD_DIM]
            turned = pltpu.roll(one, HEAD_DIM // 2, 1)
            out[:, pl.ds(h * HEAD_DIM, HEAD_DIM)] = (one * cosine + turned * sine).astype(BF16)


def project(x, weights, gains, cosine, sine):
    L, D = x.shape
    C = weights.shape[1] // 3
    rows = min(PROJECT_ROWS, L)

    def block(width):
        return pl.BlockSpec((rows, width), lambda i: (i, 0))

    return pl.pallas_call(
        _project_kernel,
        out_shape=[jax.ShapeDtypeStruct((L, 2 * C), F32)]
        + [jax.ShapeDtypeStruct((L, C), BF16)] * 3
        + [jax.ShapeDtypeStruct((2, L // 128, 128), F32)],
        grid=(L // rows,),
        in_specs=[block(D), _resident(D, 3 * C), _resident(8, C), block(HEAD_DIM), block(HEAD_DIM)],
        out_specs=[block(2 * C), block(C), block(C), block(C), _resident(2, L // 128, 128)],
        compiler_params=pltpu.CompilerParams(vmem_limit_bytes=VMEM_BYTES),
        cost_estimate=pl.CostEstimate(flops=6 * L * D * C, bytes_accessed=2 * L * D + 6 * D * C, transcendentals=0),
    )(x, weights, gains, cosine, sine)


def _project_back_kernel(
    dq_ref, dk_ref, dv_ref, pre_ref, stat_ref, inner_ref, gain_ref, cos_ref, sin_ref, x_ref, w_ref, dw_ref, first_ref, dg_ref, total, *, width
):
    rows, C = dq_ref.shape
    cosine, sine = cos_ref[...], sin_ref[...]
    start = pl.program_id(0) == 0

    @pl.when(start)
    def _():
        dg_ref[...] = jnp.zeros_like(dg_ref)

    grads = []
    for j, ref in enumerate((dq_ref, dk_ref)):
        scales, means = [], []
        for r in range(rows // 128):
            at = pl.ds(pl.program_id(0) * (rows // 128) + r, 1)
            scale = _norm_row(stat_ref[j, at, :], width)
            scales.append(_as_column(scale))
            means.append(_as_column(inner_ref[j, at, :] * scale * scale * (1.0 / width)))
        scale, mean = jnp.concatenate(scales, axis=0), jnp.concatenate(means, axis=0)
        for h in range(C // HEAD_DIM):
            at = pl.ds(h * HEAD_DIM, HEAD_DIM)
            up = ref[:, at].astype(F32)
            up = up * cosine + pltpu.roll(up * sine, HEAD_DIM // 2, 1)
            pre = pre_ref[:, pl.ds(j * C + h * HEAD_DIM, HEAD_DIM)]
            grads.append((scale * up * gain_ref[j : j + 1, at] - pre * mean).astype(BF16))
            dg_ref[j : j + 1, at] += jnp.sum(up * pre * scale, axis=0, keepdims=True)
    grads.append(dv_ref[...])
    both = jnp.concatenate(grads, axis=1)
    first_ref[...] = dot(both, w_ref[...], LAST_DIM).astype(BF16)
    part = dot(x_ref[...], both, FIRST_DIM)

    @pl.when(start)
    def _():
        total[...] = part

    @pl.when(jnp.logical_not(start))
    def _():
        total[...] += part

    @pl.when(pl.program_id(0) == pl.num_programs(0) - 1)
    def _():
        dw_ref[...] = total[...].astype(BF16)


def project_back(dq, dk, dv, pre, stats, inner, gains, cosine, sine, x, weights):
    L, D = x.shape
    C = weights.shape[1] // 3
    rows = min(BACK_ROWS, L)

    def block(width):
        return pl.BlockSpec((rows, width), lambda i: (i, 0))

    return pl.pallas_call(
        functools.partial(_project_back_kernel, width=D),
        out_shape=[
            jax.ShapeDtypeStruct((D, 3 * C), BF16),
            jax.ShapeDtypeStruct((L, D), BF16),
            jax.ShapeDtypeStruct((8, C), F32),
        ],
        grid=(L // rows,),
        in_specs=[block(C)] * 3
        + [block(2 * C), _resident(*stats.shape), _resident(*inner.shape), _resident(8, C)]
        + [block(HEAD_DIM), block(HEAD_DIM), block(D), _resident(D, 3 * C)],
        out_specs=[_resident(D, 3 * C), block(D), _resident(8, C)],
        scratch_shapes=[pltpu.VMEM((D, 3 * C), F32)],
        compiler_params=pltpu.CompilerParams(vmem_limit_bytes=VMEM_BYTES),
        cost_estimate=pl.CostEstimate(flops=12 * L * D * C, bytes_accessed=4 * L * D + 12 * D * C, transcendentals=0),
    )(dq, dk, dv, pre, stats, inner, gains, cosine, sine, x, weights)


def _pick_kernel(slot_ref, router_ref, x_ref, g_ref, xr_ref, gr_ref, gate_ref, *, slots, width):
    experts, group = slot_ref.shape
    logits = lax.dot_general(router_ref[...], x_ref[...], (((0,), (1,)), ((), ())), preferred_element_type=F32)
    powers = jnp.exp(logits - jnp.max(logits, axis=0, keepdims=True))
    chances = powers / jnp.sum(powers, axis=0, keepdims=True)
    row = lax.broadcasted_iota(jnp.int32, (slots, group), 0)
    picks = []
    for e in range(experts):
        hit = slot_ref[e : e + 1, :] == row
        gate = jnp.sum(jnp.where(hit, chances[e : e + 1, :], 0.0), axis=1, keepdims=True)
        lane = lax.broadcasted_iota(jnp.int32, (slots, 128), 1)
        gate_ref[e, 0] = jnp.where(lane == e, gate, 0.0)
        picks.append(jnp.where(hit, 1.0, 0.0).astype(BF16))
    pick = jnp.concatenate(picks, axis=0)
    for source, target in ((x_ref, xr_ref), (g_ref, gr_ref)):

        def step(i, _, source=source, target=target):
            cols = pl.ds(pl.multiple_of(i * width, width), width)
            rows = dot(pick, source[:, cols]).astype(BF16)
            for e in range(experts):
                target[e, 0, :, cols] = rows[e * slots : (e + 1) * slots]
            return 0

        lax.fori_loop(0, source.shape[1] // width, step, 0)


def pick_rows(slot, router, x, g, group, slots):
    EL, N = slot.shape
    D = x.shape[1]
    groups = N // group
    tokens = pl.BlockSpec((group, D), lambda i: (i, 0))
    picked = pl.BlockSpec((EL, 1, slots, D), lambda i: (0, i, 0, 0))
    rows = jax.ShapeDtypeStruct((EL, groups, slots, D), BF16)
    return pl.pallas_call(
        functools.partial(_pick_kernel, slots=slots, width=512),
        out_shape=[rows, rows, jax.ShapeDtypeStruct((EL, groups, slots, 128), F32)],
        grid=(groups,),
        in_specs=[
            pl.BlockSpec((EL, group), lambda i: (0, i)),
            pl.BlockSpec(router.shape, lambda i: (0, 0)),
            tokens,
            tokens,
        ],
        out_specs=[picked, picked, pl.BlockSpec((EL, 1, slots, 128), lambda i: (0, i, 0, 0))],
        compiler_params=pltpu.CompilerParams(vmem_limit_bytes=VMEM_BYTES),
        cost_estimate=pl.CostEstimate(
            flops=4 * EL * slots * N * D, bytes_accessed=8 * N * D, transcendentals=N * EXPERTS
        ),
    )(slot, router, x, g)


def _expert_kernel(x_ref, g_ref, gate_ref, w_ref, out_ref, entry_ref, dw_ref, gg_ref):
    x, g = x_ref[0], g_ref[0]
    lane = lax.broadcasted_iota(jnp.int32, gate_ref.shape[1:], 1)
    gate = jnp.where(lane % EXPERTS == pl.program_id(0), gate_ref[0], 0.0)
    gate = jnp.sum(gate, axis=1, keepdims=True)
    gate_pre = dot(x, w_ref[0, 0])
    up = dot(x, w_ref[0, 1])
    back = dot(g, w_ref[0, 2])
    sig = jax.nn.sigmoid(gate_pre)
    act = gate_pre * sig
    inner = act * up
    gg_ref[0] = jnp.broadcast_to(jnp.sum(inner * back, axis=1, keepdims=True), gg_ref.shape[1:])
    inner_grad = back * gate
    gate_pre_grad = (inner_grad * up * sig * (1.0 + gate_pre * (1.0 - sig))).astype(BF16)
    up_grad = (inner_grad * act).astype(BF16)
    gated = (inner * gate).astype(BF16)
    both = jnp.concatenate([gate_pre_grad, up_grad], axis=1)
    out_ref[0] = dot(gated, w_ref[0, 2], LAST_DIM).astype(BF16)
    entry_ref[0] = dot(both, jnp.concatenate([w_ref[0, 0], w_ref[0, 1]], axis=1), LAST_DIM).astype(BF16)
    FL = w_ref.shape[3]
    pair = dot(x, both, FIRST_DIM)
    parts = (pair[:, :FL], pair[:, FL:], dot(g, gated, FIRST_DIM))
    first = pl.program_id(1) == 0
    for k in range(3):

        @pl.when(first)
        def _(k=k):
            dw_ref[0, k] = parts[k]

        @pl.when(jnp.logical_not(first))
        def _(k=k):
            dw_ref[0, k] += parts[k]


def run_experts(x, g, gate, weights, chunk):
    EL, rows, D = x.shape
    FL = weights.shape[3]
    row_block = pl.BlockSpec((1, chunk, D), lambda e, c: (e, c, 0))
    thin = pl.BlockSpec((1, chunk, 128), lambda e, c: (e, c, 0))
    matrices = pl.BlockSpec((1, 3, D, FL), lambda e, c: (e, 0, 0, 0))
    return pl.pallas_call(
        _expert_kernel,
        out_shape=[
            jax.ShapeDtypeStruct(x.shape, BF16),
            jax.ShapeDtypeStruct(x.shape, BF16),
            jax.ShapeDtypeStruct(weights.shape, F32),
            jax.ShapeDtypeStruct((EL, rows, 128), F32),
        ],
        grid=(EL, rows // chunk),
        in_specs=[row_block, row_block, thin, matrices],
        out_specs=[row_block, row_block, matrices, thin],
        compiler_params=pltpu.CompilerParams(vmem_limit_bytes=VMEM_BYTES),
        cost_estimate=pl.CostEstimate(
            flops=18 * EL * rows * D * FL, bytes_accessed=8 * EL * rows * D + 18 * EL * D * FL, transcendentals=EL * rows * FL
        ),
    )(x, g, gate, weights)


def _spread_kernel(own_ref, slot_ref, gg_ref, out_ref, entry_ref, o_ref, e_ref, *, width):
    group, experts = slot_ref.shape
    slots = out_ref.shape[2]
    total = experts * slots
    D = out_ref.shape[3]
    lane = lax.broadcasted_iota(jnp.int32, (experts, total), 1)
    which = lax.broadcasted_iota(jnp.int32, (experts, total), 0)
    choose = jnp.where((lane >= which * slots) & (lane < (which + 1) * slots), 1.0, 0.0).astype(BF16)
    offset = lane[:1] - jnp.sum(jnp.where(lane >= (which + 1) * slots, slots, 0), axis=0, keepdims=True)
    mine = dot(slot_ref[...].astype(BF16), choose)
    pick = jnp.where(mine == offset.astype(F32), 1.0, 0.0).astype(BF16)
    column = lax.broadcasted_iota(jnp.int32, (slots, 128), 1)
    grads = [jnp.where(column == own_ref[0] + e, gg_ref[e, 0], 0.0).astype(BF16) for e in range(experts)]
    e_ref[:, pl.ds(D, 128)] = dot(pick, jnp.concatenate(grads, axis=0)).astype(BF16)

    def step(i, _):
        cols = pl.ds(pl.multiple_of(i * width, width), width)
        for source, target in ((out_ref, o_ref), (entry_ref, e_ref)):
            rows = jnp.concatenate([source[e, 0, :, cols] for e in range(experts)], axis=0)
            target[:, cols] = dot(pick, rows).astype(BF16)
        return 0

    lax.fori_loop(0, D // width, step, 0)


def spread_rows(own, slot, gate_grads, out_rows, entry_rows, group):
    N, EL = slot.shape
    _, groups, slots, D = out_rows.shape
    picked = pl.BlockSpec((EL, 1, slots, D), lambda i, *_: (0, i, 0, 0))
    return pl.pallas_call(
        functools.partial(_spread_kernel, width=512),
        out_shape=[jax.ShapeDtypeStruct((N, D), BF16), jax.ShapeDtypeStruct((N, D + 128), BF16)],
        grid_spec=pltpu.PrefetchScalarGridSpec(
            num_scalar_prefetch=1,
            grid=(groups,),
            in_specs=[
                pl.BlockSpec((group, EL), lambda i, *_: (i, 0)),
                pl.BlockSpec((EL, 1, slots, 128), lambda i, *_: (0, i, 0, 0)),
                picked,
                picked,
            ],
            out_specs=[
                pl.BlockSpec((group, D), lambda i, *_: (i, 0)),
                pl.BlockSpec((group, D + 128), lambda i, *_: (i, 0)),
            ],
        ),
        compiler_params=pltpu.CompilerParams(vmem_limit_bytes=VMEM_BYTES),
        cost_estimate=pl.CostEstimate(flops=4 * EL * slots * N * D, bytes_accessed=8 * N * D, transcendentals=0),
    )(own, slot, gate_grads, out_rows, entry_rows)


def body(
    hidden_in,
    out_grad,
    attn_gain,
    query_weight,
    key_weight,
    value_weight,
    out_weight,
    query_gain,
    key_gain,
    ffn_gain,
    router_weight,
    expert_weights,
    routes,
    doc_starts,
):
    U = lax.axis_size("uly")
    Z = lax.axis_size("blk")
    u = lax.axis_index("uly")
    z = lax.axis_index("blk")
    T, D = hidden_in.shape
    EL = expert_weights.shape[0]
    N = U * Z * T
    RW = query_weight.shape[0]
    move = (Slice if (U, Z, T, D) == (8, 4, 128, 2048) else General)(U, Z, T, D)
    C, L = move.C, move.L

    own_weights = (query_weight, key_weight, value_weight)
    gains = jnp.stack([attn_gain, ffn_gain, query_gain, key_gain], axis=1)
    first_rows, qkv_weight, packed, routes_all = move.enter(
        hidden_in, own_weights, gains, out_weight, router_weight, routes.T, out_grad
    )
    hidden = hidden_in.astype(F32)
    weight_router = packed[:, :EXPERTS]
    gain_ffn = packed[:, EXPERTS].astype(F32)
    head_gains = lax.dynamic_slice_in_dim(packed[:, EXPERTS + 1 : EXPERTS + 3], move.group * C, C, 0).astype(F32)
    head_gains = jnp.pad(head_gains.T, ((0, 6), (0, 0)))
    local = jnp.arange(L, dtype=jnp.int32)
    cosine, sine = rotary_tables((local // T * move.block_step + move.first_block) * T + local % T)
    pre, query_rot, key_rot, value, squares = project(first_rows, qkv_weight, head_gains, cosine, sine)
    key_all, value_all, stats, k_stat = move.sequence(key_rot, value, squares, out_grad)
    index = jnp.stack([jnp.int32(i) for i in (move.first_block * T // move.rows, move.block_step, *move.parts)])
    chunk = min(ATTEND_CHUNK, N)
    attended, logs, mixed = attention_forward(
        index, doc_starts, stats[0], k_stat, query_rot, key_all, value_all, move.out_parts, move.rows, chunk
    )
    move.prepare(routes_all, EL, jnp.roll(weight_router, -u * EL, axis=1))
    residual = hidden + move.heads_to_rows(mixed).astype(F32)

    second_scale = norm_scale(residual)
    second_low = (residual * second_scale * gain_ffn).astype(BF16)
    probabilities = jax.nn.softmax(dot(second_low, weight_router), axis=-1)
    second_all, entry_sum = move.experts(second_low, expert_weights)
    entry_sum = entry_sum.astype(F32)

    second_grad, prob_grad = entry_sum[:, :D], entry_sum[:, D : D + EXPERTS]
    logit_grad = (
        probabilities * (prob_grad - jnp.sum(probabilities * prob_grad, axis=1, keepdims=True))
    ).astype(BF16)
    second_grad = second_grad + dot(logit_grad, weight_router, LAST_DIM)
    upstream = out_grad.astype(F32)
    weighted = second_grad * gain_ffn
    inner_mean = jnp.mean(weighted * residual, axis=-1, keepdims=True)
    residual_grad = upstream + second_scale * weighted - residual * (second_scale**3) * inner_mean
    ffn_gain_part = jnp.sum(second_grad * residual * second_scale, axis=0)

    residual_rows, expert_grads = move.rows_to_heads(residual_grad.astype(BF16))
    dq, dk_part, dv_part, out_weight_part, q_inner, k_inner = attention_backward(
        index,
        doc_starts,
        stats[0],
        k_stat,
        query_rot,
        residual_rows,
        attended,
        logs,
        key_all,
        value_all,
        move.out_parts,
        move.rows,
        chunk,
    )
    dk, dv, out_sum, inner = move.sequence_sums(dk_part, dv_part, out_weight_part, q_inner, k_inner)
    weight_part, first_part, gain_parts = project_back(
        dq, dk, dv, pre, stats, inner, head_gains, cosine, sine, first_rows, qkv_weight
    )
    gain_parts = gain_parts[:2]
    first_weighted, weight_sum, out_weight_grad, logit_grad_all, ffn_gain_grad, head_gain_grads = move.leave(
        first_part, weight_part, logit_grad, ffn_gain_part, gain_parts
    )
    own_columns = lax.dynamic_slice_in_dim(second_all, (u * Z + z) * RW, RW, 1)
    router_grad = dot(own_columns, logit_grad_all, FIRST_DIM)
    output, hidden_grad, attn_gain_grad, *weight_grads = finish(
        hidden_in, residual, residual_grad, first_weighted, out_sum, move.out_own, own_weights, weight_sum, out_weight_grad, gains
    )
    return (
        output,
        hidden_grad,
        attn_gain_grad[:, 0],
        weight_grads[0],
        weight_grads[1],
        weight_grads[2],
        weight_grads[3],
        head_gain_grads[0],
        head_gain_grads[1],
        ffn_gain_grad,
        router_grad,
        expert_grads,
    )


def solution(mesh):
    rows = P(ALL, None)
    flat = P(ALL)
    experts = P("uly", None, None, "blk")
    return jax.shard_map(
        body,
        mesh=mesh,
        in_specs=(rows, rows, flat, rows, rows, rows, rows, flat, flat, flat, rows, experts, rows, P()),
        out_specs=(rows, rows, flat, rows, rows, rows, rows, flat, flat, flat, rows, experts),
        check_vma=False,
    )
```

```python
import functools

import jax
import jax.numpy as jnp
from jax import lax
from jax.experimental import pallas as pl
from jax.experimental.pallas import tpu as pltpu
from jax.sharding import PartitionSpec as P

HEADS = 16
HEAD_DIM = 128
EXPERTS = 64
CAP = 17

EPS = 1e-05
THETA = 10000.0
NEG = -1e30
FIRST_DIM = (((0,), (0,)), ((), ()))
LAST_DIM = (((1,), (1,)), ((), ()))
ALL = ("uly", "blk")
F32 = jnp.float32
BF16 = jnp.bfloat16
VMEM_BYTES = 56 * 1024 * 1024
PICK_WIDTH = 512
ATTEND_CHUNK = 512
ATTEND_ROWS = 512
BACK_ROWS = 1024
PROJECT_ROWS = 512
SPREAD_WIDTH = 2048


def dot(a, b, dims=(((1,), (0,)), ((), ()))):
    return lax.dot_general(a, b, dims, preferred_element_type=F32)


def rotary_tables(position):
    halfway = HEAD_DIM // 2
    frequency = THETA ** (-(jnp.arange(halfway).astype(F32) * 2.0 / HEAD_DIM))
    angles = position.astype(F32)[:, None] * frequency[None, :]
    cosine, sine = jnp.cos(angles), jnp.sin(angles)
    return jnp.concatenate([cosine, cosine], axis=1), jnp.concatenate([-sine, sine], axis=1)


def norm_scale(values):
    return lax.rsqrt(jnp.mean(values * values, axis=-1, keepdims=True) + EPS)


MESH = pl.DeviceIdType.MESH
DMA = pltpu.SemaphoreType.DMA
ANY_SPACE = pl.BlockSpec(memory_space=pl.ANY)
IN_VMEM = pl.BlockSpec(memory_space=pltpu.VMEM)
DEPTH = 4
CHIPS = (0, 2, 4, 6)
FIRST, THEN = (2, 4), (4, 2)


def _send(src, dst, send_sem, recv_sem, to):
    pltpu.make_async_remote_copy(
        src_ref=src, dst_ref=dst, send_sem=send_sem, recv_sem=recv_sem, device_id=to, device_id_type=MESH
    ).start()


def _expect(ref, sem, here):
    pltpu.make_async_remote_copy(
        src_ref=ref, dst_ref=ref, send_sem=sem, recv_sem=sem, device_id=here, device_id_type=MESH
    ).wait_recv()


def _sent(ref, sem, here):
    pltpu.make_async_remote_copy(
        src_ref=ref, dst_ref=ref, send_sem=sem, recv_sem=sem, device_id=here, device_id_type=MESH
    ).wait_send()


def _greet(u, z, planes, line=False, others=(), meanwhile=lambda: None):
    barrier = pltpu.get_barrier_semaphore()
    for bit in planes:
        pl.semaphore_signal(barrier, inc=1, device_id=(u ^ bit, z), device_id_type=MESH)
    for to in others:
        pl.semaphore_signal(barrier, inc=1, device_id=to, device_id_type=MESH)
    count = len(planes) + len(others)
    if line:

        @pl.when(z > 0)
        def _():
            pl.semaphore_signal(barrier, inc=1, device_id=(u, z - 1), device_id_type=MESH)

        @pl.when(z < DEPTH - 1)
        def _():
            pl.semaphore_signal(barrier, inc=1, device_id=(u, z + 1), device_id_type=MESH)

        count = count + jnp.where((z == 0) | (z == DEPTH - 1), 1, 2)
    meanwhile()
    pl.semaphore_wait(barrier, count)


def _line_order(z):
    second = jnp.where(z == 0, 1, z - 1)
    third = jnp.where(z == 0, 2, jnp.where(z == 3, 1, z + 1))
    fourth = jnp.where(z < 2, 3, 0)
    return (z, second, third, fourth)


def _accumulate(target, source, rows):
    strip = 16

    def step(i, _):
        at = pl.ds(pl.multiple_of(i * strip, strip), strip)
        target[at, :] = target[at, :] + source[at, :]
        return 0

    lax.fori_loop(0, rows // strip, step, 0)


def _run(*parts, order=()):
    for i in order:
        next(parts[i])
    live = list(parts)
    while live:
        for part in list(live):
            try:
                next(part)
            except StopIteration:
                live.remove(part)


def _line_part(u, z, source, block, sems, share=True, place=None):
    z_send, z_recv, c_send, c_recv, own_sem = sems
    here, core = (u, z), u % 2
    if place is None:
        own = pltpu.make_async_copy(source, block(core, z), own_sem)
        own.start()
    else:
        def block(_, level):
            return place(level, z)

    order = _line_order(z)

    def along(level, ref, step):
        @pl.when((z > 0) & (level >= z))
        def _():
            step(ref, 0, level, (u, z - 1))

        @pl.when((z < DEPTH - 1) & (level <= z))
        def _():
            step(ref, 1, level, (u, z + 1))

    def go(ref, way, level, to):
        there = block(core, level) if place is None else place(level, to[1])
        _send(ref, there, z_send.at[way, level], z_recv.at[level], to)

    def gone(ref, way, level, to):
        _sent(ref, z_send.at[way, level], here)

    for i in range(4):
        level = order[i]
        ref = source if i == 0 else block(core, level)
        if i > 0:
            yield
            _expect(ref, z_recv.at[level], here)
        along(level, ref, go)
        if share:
            _send(ref, block(core, level), c_send.at[level], c_recv.at[level], (u ^ 1, z))
    yield
    if share:
        for i in range(4):
            _expect(block(1 - core, order[i]), c_recv.at[order[i]], here)
    yield
    for i in range(4):
        along(order[i], source, gone)
        if share:
            _sent(source, c_send.at[order[i]], here)
    if place is None:
        own.wait()


def _plane_part(u, z, own, block, sems):
    p_send, p_recv, o_sem = sems
    here = (u, z)
    for way, bits in enumerate((FIRST, THEN)):
        for h in range(2):
            _send(own(h), block(h, u), p_send.at[h, way], p_recv.at[h, way], (u ^ bits[h], z))
    for h in range(2):
        pltpu.make_async_copy(own(h), block(h, u), o_sem.at[h]).start()
    for h in range(2):
        yield
        _expect(block(h, u ^ FIRST[h]), p_recv.at[h, 0], here)
        near = block(h, u ^ FIRST[h])
        _send(near, near, p_send.at[h, 2], p_recv.at[h, 2], (u ^ THEN[h], z))
    yield
    for h in range(2):
        _expect(block(h, u ^ THEN[h]), p_recv.at[h, 1], here)
        _expect(block(h, u ^ 6), p_recv.at[h, 2], here)
    yield
    for h in range(2):
        for k in range(3):
            _sent(block(h, u), p_send.at[h, k], here)
        pltpu.make_async_copy(own(h), block(h, u), o_sem.at[h]).wait()


def _plane_sum_part(u, z, source, work, bufs, sems, rows, then_do):
    p_buf, q_buf = bufs
    load, p_send, p_recv, q_send, q_recv = sems
    here = (u, z)
    for j in (1, 0):
        for h in range(2):
            bit = (THEN[h], 6)[j]
            _send(source(h, u ^ bit), p_buf.at[h, j], p_send.at[h, j], p_recv.at[h, j], (u ^ THEN[h], z))
    for h in range(2):
        for j, bit in enumerate((0, FIRST[h])):
            pltpu.make_async_copy(source(h, u ^ bit), work.at[h, j], load.at[h, j]).start()
    for h in range(2):
        yield
        for j, bit in enumerate((0, FIRST[h])):
            pltpu.make_async_copy(source(h, u ^ bit), work.at[h, j], load.at[h, j]).wait()
        _expect(p_buf.at[h, 1], p_recv.at[h, 1], here)
        _accumulate(work.at[h, 1], p_buf.at[h, 1], rows)
        _send(work.at[h, 1], q_buf.at[h], q_send.at[h], q_recv.at[h], (u ^ FIRST[h], z))
    yield
    for h in range(2):
        _expect(p_buf.at[h, 0], p_recv.at[h, 0], here)
        _accumulate(work.at[h, 0], p_buf.at[h, 0], rows)
    for h in range(2):
        _expect(q_buf.at[h], q_recv.at[h], here)
        _accumulate(work.at[h, 0], q_buf.at[h], rows)
    then_do()
    yield
    for h in range(2):
        for j in range(2):
            _sent(p_buf.at[h, j], p_send.at[h, j], here)
        _sent(q_buf.at[h], q_send.at[h], here)


def _line_sum_part(u, z, source, work, bufs, sems, rows, then_do):
    c_buf, z_buf = bufs
    load, c_send, c_recv, z_send, z_recv = sems
    here, core = (u, z), u % 2
    order = tuple(reversed(_line_order(z)))
    for i in range(4):
        _send(source(1 - core, order[i]), c_buf.at[i], c_send.at[i], c_recv.at[i], (u ^ 1, z))
        pltpu.make_async_copy(source(core, order[i]), work.at[i], load.at[i]).start()
    for i in range(4):
        yield
        pltpu.make_async_copy(source(core, order[i]), work.at[i], load.at[i]).wait()
        _expect(c_buf.at[i], c_recv.at[i], here)
        _accumulate(work.at[i], c_buf.at[i], rows)
        if i == 3:
            yield
        _line_end(u, z, order[i], i, work.at[i], z_buf, (z_send, z_recv), rows)
    then_do()
    yield
    for i in range(4):
        _sent(c_buf.at[i], c_send.at[i], here)
        if i < 3:
            _sent(work.at[i], z_send.at[i], here)


def _column_peers(u, z):
    return [((u ^ c, z ^ k), c, k) for c in range(2) for k in range(4) if c or k]


def _comm(kernel, outs, scratch, collective_id, specs, flops=0, moved=100_000_000):
    return pl.pallas_call(
        kernel,
        out_shape=outs,
        in_specs=specs[0],
        out_specs=specs[1],
        scratch_shapes=scratch,
        compiler_params=pltpu.CompilerParams(
            collective_id=collective_id, has_side_effects=True, vmem_limit_bytes=VMEM_BYTES
        ),
        cost_estimate=pl.CostEstimate(flops=flops, bytes_accessed=moved, transcendentals=0),
    )


ENTER_ORDER = (0, 2, 3, 1, 3, 3, 0, 2, 1, 0, 2, 0, 2)
KV_ORDER = (2, 0, 1, 0, 0, 1, 2, 1, 0, 1)
PAIR_ORDER = (1, 0, 2, 1, 0, 0, 1, 2, 1, 0)
LEAVE_ORDER = (0, 1, 2, 1, 2, 1, 0, 0, 1, 3, 3, 0, 1, 3, 3, 1)
LINE_SEMS = [DMA((2, 4)), DMA((4,)), DMA((4,)), DMA((4,)), DMA]
PLANE_SEMS = [DMA((2, 3)), DMA((2, 3)), DMA((2,))]
PLANE_SUM_SEMS = [DMA((2, 2)), DMA((2, 2)), DMA((2, 2)), DMA((2,)), DMA((2,))]
LINE_SUM_SEMS = [DMA((4,)), DMA((4,)), DMA((4,)), DMA((4,)), DMA((2, 4))]


def _small_part(u, z, xs, outs, sems):
    own_sem, z_send, z_recv, u_send, u_recv = sems
    here = (u, z)
    for a, (x, o) in enumerate(zip(xs, outs)):
        pltpu.make_async_copy(x, o.at[u, z], own_sem.at[a]).start()
        for k in range(1, 4):
            _send(x, o.at[u, z], z_send.at[a, k], z_recv.at[a, k], (u, z ^ k))
    yield
    for a, (x, o) in enumerate(zip(xs, outs)):
        pltpu.make_async_copy(x, o.at[u, z], own_sem.at[a]).wait()
        for k in range(1, 4):
            _expect(o.at[u, z ^ k], z_recv.at[a, k], here)
        for k in range(1, 8):
            _send(o.at[u], o.at[u], u_send.at[a, k], u_recv.at[a, k], (u ^ k, z))
    yield
    yield
    for a, (x, o) in enumerate(zip(xs, outs)):
        for k in range(1, 4):
            _sent(x, z_send.at[a, k], here)
        for k in range(1, 8):
            _sent(o.at[u], u_send.at[a, k], here)
            _expect(o.at[u ^ k], u_recv.at[a, k], here)


def _small_sems(n):
    return [DMA((n,)), DMA((n, 4)), DMA((n, 4)), DMA((n, 8)), DMA((n, 8))]


def _packed(router, gains):
    lane = lax.broadcasted_iota(jnp.int32, (router.shape[0], 128 - EXPERTS), 1)
    tail = jnp.zeros(lane.shape, F32)
    for j in range(1, 4):
        tail = jnp.where(lane == j - 1, gains[:, j : j + 1], tail)
    return router, tail.astype(BF16)


def enter(hidden, weights, gains, router, routes, out_grad, collective_id):
    T, D = hidden.shape
    R, C = weights[0].shape[0], weights[0].shape[1] // 8
    held = (2, 4, R, 3 * C)
    strip = 16

    def kernel(h_ref, wq_ref, wk_ref, wv_ref, gain_ref, router_ref, route_ref, g_ref, x_out, w_out, p_out, r_out, g_out, *refs):
        x_ref, w_ref, pack_ref, w_buf, w_send, w_recv = refs[:6]
        half = [pl.ds(h * (T // 2), T // 2) for h in range(2)]
        sems = refs[6:]
        u, z = lax.axis_index("uly"), lax.axis_index("blk")
        here, core, chip = (u, z), u % 2, u // 2
        column = _column_peers(u, z)

        def weight_part():
            def cut(j, c, level):
                return w_ref.at[j, :, pl.ds(pl.multiple_of((2 * level + c) * C, C), C)]

            def slot(j, c, level):
                return w_buf.at[c, level, :, pl.ds(j * C, C)]

            for i, (to, c, k) in enumerate(column):
                for j in range(3):
                    _send(cut(j, core ^ c, z ^ k), slot(j, core, z), w_send.at[i, j], w_recv.at[i, j], to)
            for j in range(3):
                slot(j, core, z)[...] = cut(j, core, z)[...]
            yield
            for i, (to, c, k) in enumerate(column):
                for j in range(3):
                    _expect(slot(j, core ^ c, z ^ k), w_recv.at[i, j], here)
            yield from _plane_part(u, z, lambda h: w_buf.at[h], lambda h, v: w_out.at[v // 2, h], sems[:3])
            for i, (to, c, k) in enumerate(column):
                for j in range(3):
                    _sent(cut(j, core ^ c, z ^ k), w_send.at[i, j], here)

        def prepare():
            gains = gain_ref[...].astype(F32)
            for j, ref in enumerate((wq_ref, wk_ref, wv_ref)):
                w_ref[j] = (ref[...].astype(F32) * gains[:, :1]).astype(BF16)

            def norm(i, _):
                at = pl.ds(pl.multiple_of(i * strip, strip), strip)
                value = h_ref[at, :].astype(F32)
                x_ref[at, :] = (value * norm_scale(value)).astype(BF16)
                return 0

            lax.fori_loop(0, T // strip, norm, 0)
            pack_ref[:, pl.ds(0, EXPERTS)], pack_ref[:, pl.ds(EXPERTS, 128 - EXPERTS)] = _packed(router_ref[...], gains)

        _greet(u, z, range(1, 8), others=[to for to, c, k in column if k], meanwhile=prepare)
        _run(
            weight_part(),
            _small_part(u, z, (pack_ref, route_ref), (p_out, r_out), sems[11:]),
            _line_part(u, z, x_ref, lambda c, level: x_out.at[c, level], sems[3:8]),
            _plane_part(u, z, lambda h: g_ref.at[half[h]], lambda h, v: g_out.at[v // 2, half[h]], sems[8:11]),
            order=ENTER_ORDER,
        )

    outs = [
        jax.ShapeDtypeStruct((2, 4, T, D), BF16),
        jax.ShapeDtypeStruct((4,) + held, BF16),
        jax.ShapeDtypeStruct((8, 4, R, 128), BF16),
        jax.ShapeDtypeStruct((8, 4) + routes.shape, routes.dtype),
        jax.ShapeDtypeStruct((4, T, D), BF16),
    ]
    scratch = [pltpu.VMEM((T, D), BF16), pltpu.VMEM((3, R, D), BF16), pltpu.VMEM((R, 128), BF16)]
    scratch += [pltpu.VMEM(held, BF16), DMA((7, 3)), DMA((7, 3))] + PLANE_SEMS + LINE_SEMS + PLANE_SEMS + _small_sems(2)
    specs = ([IN_VMEM] * 7 + [ANY_SPACE], [ANY_SPACE] * 5)
    return _comm(kernel, outs, scratch, collective_id, specs)(hidden, *weights, gains, router, routes, out_grad)


def _column_sum_part(u, z, x_ref, total, buf, sems, then_do):
    send, recv = sems
    here = (u, z)
    column = _column_peers(u, z)
    for i, (to, c, k) in enumerate(column):
        _send(x_ref, buf.at[i], send.at[i], recv.at[i], to)
    yield
    value = x_ref[...]
    for i in range(7):
        _expect(buf.at[i], recv.at[i], here)
        value = value + buf[i]
    total[...] = value
    then_do()
    yield
    for i in range(7):
        _sent(x_ref, send.at[i], here)


def plane_pair(first, second, rows, squares, collective_id):
    R = squares.shape[0] // 2

    def kernel(a_ref, b_ref, x_ref, s_ref, a_out, b_out, x_out, s_out, k_out, buf, *sems):
        u, z = lax.axis_index("uly"), lax.axis_index("blk")
        here, chip = (u, z), u // 2
        k_send, k_recv = sems[10:]
        _greet(u, z, (2, 4, 6), others=[to for to, c, k in _column_peers(u, z)])
        own, outs = (a_ref, b_ref), (a_out, b_out)
        keys = s_out.at[pl.ds(R, R)]

        def tell():
            k_out[chip] = keys[...]
            for i, bit in enumerate((2, 4, 6)):
                _send(keys, k_out.at[chip], k_send.at[i], k_recv.at[i], (u ^ bit, z))

        _run(
            _plane_part(u, z, lambda h: own[h], lambda h, v: outs[h].at[v // 2], sems[:3]),
            _line_part(
                u, z, x_ref, None, sems[3:8], share=False, place=lambda level, at: x_out.at[(level - at + 3) % 4]
            ),
            _column_sum_part(u, z, s_ref, s_out, buf, sems[8:10], tell),
            order=PAIR_ORDER,
        )
        for i, bit in enumerate((2, 4, 6)):
            _expect(k_out.at[(u ^ bit) // 2], k_recv.at[i], here)
            _sent(keys, k_send.at[i], here)

    outs = [jax.ShapeDtypeStruct((4,) + x.shape, x.dtype) for x in (first, second)]
    outs += [jax.ShapeDtypeStruct((3,) + rows.shape, rows.dtype)]
    outs += [jax.ShapeDtypeStruct(squares.shape, F32), jax.ShapeDtypeStruct((4, R, 128), F32)]
    specs = ([IN_VMEM] * 2 + [ANY_SPACE, IN_VMEM], [ANY_SPACE] * 3 + [IN_VMEM] * 2)
    scratch = [pltpu.VMEM((7,) + squares.shape, F32)] + PLANE_SEMS + LINE_SEMS + [DMA((7,)), DMA((7,)), DMA((3,)), DMA((3,))]
    return _comm(kernel, outs, scratch, collective_id, specs)(first, second, rows, squares)


def column_gather(rows, slot, out_rows, collective_id):
    T, D = rows.shape
    EL, _, slots, _ = out_rows.shape

    def kernel(r_ref, slot_ref, rows_ref, r_out, x_out, part_out, stage, stage_sem, *refs):
        u, z = lax.axis_index("uly"), lax.axis_index("blk")
        _greet(u, z, (1, 2, 4), line=True)
        order = _line_order(z)[1:]

        def keep(i, part):
            x_out[(order[i] - z + 3) % 4] = part[...]

        extra = (stage, part_out, stage_sem)
        _run(
            _line_part(u, z, r_ref, lambda c, level: r_out.at[c, level], refs[-5:]),
            _spread_part(u, z, slot_ref, rows_ref, None, order, refs[:-5], keep, extra=extra),
        )

    outs = [
        jax.ShapeDtypeStruct((2, 4, T, D), BF16),
        jax.ShapeDtypeStruct((3, T, D), BF16),
        jax.ShapeDtypeStruct((2, 4 * T, D), BF16),
    ]
    specs = ([IN_VMEM, IN_VMEM, ANY_SPACE], [ANY_SPACE, IN_VMEM, ANY_SPACE])
    scratch = [pltpu.VMEM((2, 4 * T, D), BF16), DMA((2,))] + _spread_scratch(T, D, (EL, slots, D), 3) + LINE_SEMS
    return _comm(kernel, outs, scratch, collective_id, specs)(rows, slot, out_rows)


def _line_sum_scratch(T, D):
    return [pltpu.VMEM((4, T, D), BF16), pltpu.VMEM((4, T, D), BF16), pltpu.VMEM((2, 4, T, D), BF16)]


def column_scatter(x, collective_id):
    T, D = x.shape[2:]

    def kernel(x_ref, o_ref, work, c_buf, z_buf, *sems):
        u, z = lax.axis_index("uly"), lax.axis_index("blk")
        _greet(u, z, (1,), line=True)

        def finish():
            o_ref[...] = work[3]

        _run(_line_sum_part(u, z, lambda c, level: x_ref.at[c, level], work, (c_buf, z_buf), sems, T, finish))

    scratch = _line_sum_scratch(T, D) + LINE_SUM_SEMS
    return _comm(kernel, jax.ShapeDtypeStruct((T, D), BF16), scratch, collective_id, ([ANY_SPACE], IN_VMEM))(x)


def _plane_sum_scratch(rows, cols):
    return [pltpu.VMEM((2, 2, rows, cols), BF16), pltpu.VMEM((2, 2, rows, cols), BF16), pltpu.VMEM((2, rows, cols), BF16)]


def key_value_sums(dk, dv, x, inner, collective_id):
    T, D = x.shape[1:]
    L, C = dk.shape[1:]
    R = inner.shape[0] // 5

    def kernel(
        k_ref, v_ref, x_ref, s_ref, k_out, v_out, x_out, s_out, work, p_buf, q_buf, x_work, z_buf, buf, total, k_buf, *sems
    ):
        u, z = lax.axis_index("uly"), lax.axis_index("blk")
        here, chip = (u, z), u // 2
        _greet(u, z, (2, 4, 6), others=[to for to, c, k in _column_peers(u, z)])
        load, z_send, z_recv, k_send, k_recv = sems[7:]
        order = tuple(reversed(_line_order(z)))

        def keys(v):
            return total.at[pl.ds(pl.multiple_of((v // 2 + 1) * R, R), R)]

        def tell():
            for i, bit in enumerate((2, 4, 6)):
                _send(keys(u ^ bit), k_buf.at[i], k_send.at[i], k_recv.at[i], (u ^ bit, z))

        def finish():
            k_out[...] = work[0, 0]
            v_out[...] = work[1, 0]

        def line():
            copies = [
                pltpu.make_async_copy(x_ref.at[(order[i] - z + 3) % 4], x_work.at[i], load.at[i]) for i in range(3)
            ]
            for copy in copies:
                copy.start()
            x_work[3] = jnp.zeros((T, D), BF16)
            for copy in copies:
                copy.wait()
            for i in range(4):
                _line_end(u, z, order[i], i, x_work.at[i], z_buf, (z_send, z_recv), T)
                yield
            x_out[...] = x_work[3]
            for i in range(3):
                _sent(x_work.at[i], z_send.at[i], (u, z))

        _run(
            _plane_sum_part(
                u, z, lambda h, v: (k_ref, v_ref)[h].at[v // 2], work, (p_buf, q_buf), sems[:5], L, finish
            ),
            line(),
            _column_sum_part(u, z, s_ref, total, buf, sems[5:7], tell),
            order=KV_ORDER,
        )
        value = keys(u)[...]
        for i, bit in enumerate((2, 4, 6)):
            _expect(k_buf.at[i], k_recv.at[i], here)
            value = value + k_buf[i]
            _sent(k_buf.at[i], k_send.at[i], here)
        s_out[pl.ds(0, R), :] = total[pl.ds(0, R), :]
        s_out[pl.ds(R, R), :] = value

    outs = [jax.ShapeDtypeStruct((L, C), BF16)] * 2 + [jax.ShapeDtypeStruct((T, D), BF16)]
    outs += [jax.ShapeDtypeStruct((2 * R, 128), F32)]
    scratch = _plane_sum_scratch(L, C) + [pltpu.VMEM((4, T, D), BF16), pltpu.VMEM((2, 4, T, D), BF16)]
    scratch += [pltpu.VMEM((7,) + inner.shape, F32), pltpu.VMEM(inner.shape, F32), pltpu.VMEM((3, R, 128), F32)]
    scratch += PLANE_SUM_SEMS + [DMA((7,)), DMA((7,)), DMA((4,)), DMA((4,)), DMA((2, 4)), DMA((3,)), DMA((3,))]
    specs = ([ANY_SPACE] * 3 + [IN_VMEM], [IN_VMEM] * 4)
    return _comm(kernel, outs, scratch, collective_id, specs)(dk, dv, x, inner)


def leave(x, weights, smalls, ready, collective_id):
    n = len(smalls)
    T, D = x.shape[2:]
    rows, W = weights.shape[2:]
    R, C = rows // 4, W // 3

    def kernel(x_ref, w_ref, ready_ref, *refs):
        small_in, (o_ref, w_out, own_ref), small_out = refs[:n], refs[n : n + 3], refs[n + 3 : 2 * n + 3]
        work, c_buf, z_buf, w_work, wp_buf, wq_buf = refs[2 * n + 3 : 2 * n + 9]
        tree = refs[2 * n + 9 : 2 * n + 20]
        sems = refs[2 * n + 20 :]

        def keep(part):
            own_ref[...] = part[...]

        u, z = lax.axis_index("uly"), lax.axis_index("blk")
        here, core, chip = (u, z), u % 2, u // 2
        column = _column_peers(u, z)
        _greet(u, z, range(1, 8), others=[to for to, c, k in column if k])
        t_send, t_recv = sems[10:12]
        group = 2 * z + core

        def finish():
            o_ref[...] = work[3]

        def cut(j, c, level):
            return w_work.at[c, 0, pl.ds(pl.multiple_of(level * R, R), R), pl.ds(j * C, C)]

        def slot(j, g):
            return w_out.at[j, :, pl.ds(pl.multiple_of(g * C, C), C)]

        def deal():
            for i, (to, c, k) in enumerate(column):
                for j in range(3):
                    _send(cut(j, core ^ c, z ^ k), slot(j, group), t_send.at[i, j], t_recv.at[i, j], to)
            for j in range(3):
                slot(j, group)[...] = cut(j, core, z)[...]

        _run(
            _plane_sum_part(u, z, lambda h, v: w_ref.at[v // 2, h], w_work, (wp_buf, wq_buf), sems[5:10], rows, deal),
            _line_sum_part(u, z, lambda c, level: x_ref.at[c, level], work, (c_buf, z_buf), sems[:5], T, finish),
            _small_part(u, z, small_in, small_out, sems[12:]),
            _tree_part(u, z, ready_ref, tree, T, keep),
            order=LEAVE_ORDER,
        )
        for i, (to, c, k) in enumerate(column):
            for j in range(3):
                _expect(slot(j, 2 * (z ^ k) + (core ^ c)), t_recv.at[i, j], here)
                _sent(cut(j, core ^ c, z ^ k), t_send.at[i, j], here)

    outs = [jax.ShapeDtypeStruct((T, D), BF16), jax.ShapeDtypeStruct((3, R, 8 * C), BF16), jax.ShapeDtypeStruct((T, D), BF16)]
    outs += [jax.ShapeDtypeStruct((8, 4) + x.shape, x.dtype) for x in smalls]
    scratch = _line_sum_scratch(T, D) + _plane_sum_scratch(rows, W) + _tree_scratch(T, D) + LINE_SUM_SEMS + PLANE_SUM_SEMS
    scratch += [DMA((7, 3)), DMA((7, 3))] + _small_sems(n)
    specs = ([ANY_SPACE] * 3 + [IN_VMEM] * n, [IN_VMEM] * 3 + [ANY_SPACE] * n)
    return _comm(kernel, outs, scratch, collective_id, specs)(x, weights, ready, *smalls)


def _finish_kernel(
    h_ref, r_ref, rg_ref, first_ref, sum_ref, own_ref, wq_ref, wk_ref, wv_ref, dw_ref, do_ref, gain_ref, out_ref, hg_ref, ag_ref, *dws
):
    out_ref[...] = (r_ref[...] + (sum_ref[...].astype(F32) + own_ref[...].astype(F32))).astype(BF16)
    hidden, weighted = h_ref[...].astype(F32), first_ref[...].astype(F32)
    scale = norm_scale(hidden)
    mean = jnp.mean(weighted * hidden, axis=-1, keepdims=True)
    hg_ref[...] = rg_ref[...] + scale * weighted - hidden * (scale * scale * scale) * mean
    gain = gain_ref[...].astype(F32)[:, :1]
    total = jnp.zeros(dws[0].shape, F32)
    for j, ref in enumerate((wq_ref, wk_ref, wv_ref)):
        grad = dw_ref[j].astype(F32)
        total = total + grad * ref[...].astype(F32)
        dws[j][...] = grad * gain
    ag_ref[...] = jnp.sum(total, axis=1, keepdims=True)
    dws[3][...] = do_ref[...].astype(F32)


def finish(hidden, residual, residual_grad, first_weighted, out_sum, out_own, weights, weight_sum, out_weight_grad, gains):
    T, D = hidden.shape
    R = gains.shape[0]
    steps = 4 if R % 64 == 0 else 1

    def rows(count, width):
        return pl.BlockSpec((count // steps, width), lambda i: (i, 0))

    tokens, dense = rows(T, D), rows(R, D)
    return pl.pallas_call(
        _finish_kernel,
        out_shape=[
            jax.ShapeDtypeStruct((T, D), BF16),
            jax.ShapeDtypeStruct((T, D), F32),
            jax.ShapeDtypeStruct((R, 1), F32),
        ]
        + [jax.ShapeDtypeStruct((R, D), F32)] * 4,
        grid=(steps,),
        in_specs=[tokens] * 6
        + [dense] * 3
        + [pl.BlockSpec((3, R // steps, D), lambda i: (0, i, 0)), dense, rows(R, 4)],
        out_specs=[tokens, tokens, rows(R, 1)] + [dense] * 4,
        compiler_params=pltpu.CompilerParams(vmem_limit_bytes=VMEM_BYTES),
        cost_estimate=pl.CostEstimate(flops=20 * T * D, bytes_accessed=24 * T * D, transcendentals=0),
    )(hidden, residual, residual_grad, first_weighted, out_sum, out_own, *weights, weight_sum, out_weight_grad, gains)


class _Jobs:
    def __init__(self, load, compute):
        self.load, self.compute = load, compute
        self.queue, self.count, self.ready = [], 0, None

    def add(self, *jobs):
        self.queue += jobs

    def _next(self):
        if not self.queue:
            return None
        job = (self.count, self.queue.pop(0))
        self.count += 1
        self.load(*job, True)
        return job

    def run(self, number=1):
        for _ in range(number):
            now = self.ready or self._next()
            if now is None:
                return
            self.ready = self._next()
            self.load(*now, False)
            self.compute(*now)


def _gather_pick_kernel(
    x_ref, here_g, g0, g1, g2, g3, slot_ref, router_ref, o_ref, xr_ref, gr_ref, gate_ref, other_here, other_g, pick, in_buf, out_buf, in_sem, out_sem, *sems, width
):
    own_sem, z_send, z_recv, p_send, p_recv, c_send, c_recv, g_send, g_recv, h_send, h_recv = sems
    own_g = (g0, g1, g2, g3)
    u, z = lax.axis_index("uly"), lax.axis_index("blk")
    core, chip = u % 2, u // 2
    other = 1 - core
    T, D = x_ref.shape
    experts, group = slot_ref.shape[1:]
    slots = out_buf.shape[2]
    half = T // 2
    halves = (pl.ds(0, half), pl.ds(half, half))
    here = (u, z)
    _greet(u, z, (1, 2, 4), line=True)
    own = pltpu.make_async_copy(x_ref, o_ref.at[u * DEPTH + z], own_sem)
    own.start()
    order = _line_order(z)

    def block(who, level):
        return o_ref.at[who * DEPTH + level]

    def part(who, level, h):
        return o_ref.at[who * DEPTH + level, halves[h]]

    def load(n, job, start):
        source, level, which = job
        steps = (0, jnp.where(which == 0, 1, 2), jnp.where(which == 0, 2, 1), 3)
        for k in range(4):
            p = chip ^ steps[k]
            if source == "x":
                ref = o_ref.at[(2 * p + which) * DEPTH + level]
            elif source == 0:
                ref = (here_g if which is core else other_here).at[p]
            else:
                ref = (own_g[k] if which is core else other_g.at[k]).at[source - 1]
            rows = pl.ds(pl.multiple_of(p * T, T), T)
            copy = pltpu.make_async_copy(ref, in_buf.at[n % 2, rows], in_sem.at[n % 2, k])
            copy.start() if start else copy.wait()

    def out_copy(n, target, at):
        return pltpu.make_async_copy(out_buf.at[n % 2], target.at[:, at], out_sem.at[n % 2])

    sent = {}

    def compute(n, job):
        source, level, which = job
        at = 2 * level + which
        rows_in, rows_out = in_buf.at[n % 2], out_buf.at[n % 2]
        row = lax.broadcasted_iota(jnp.int32, (slots, group), 0)
        if source != "x":
            picks = [jnp.where(slot_ref[at, e : e + 1, :] == row, 1.0, 0.0).astype(BF16) for e in range(experts)]
            pick[at] = jnp.concatenate(picks, axis=0)
        if n >= 2:
            sent.pop(n - 2).wait()

        def step(i, _):
            cols = pl.ds(pl.multiple_of(i * width, width), width)
            rows = dot(pick[at], rows_in[:, cols]).astype(BF16)
            for e in range(experts):
                rows_out[e, :, cols] = rows[e * slots : (e + 1) * slots]
            return 0

        lax.fori_loop(0, D // width, step, 0)
        sent[n] = out_copy(n, xr_ref if source == "x" else gr_ref, at)
        sent[n].start()
        if source == "x":
            logits = dot(rows_in[...], router_ref[...])
            powers = jnp.exp(logits - jnp.max(logits, axis=1, keepdims=True))
            chances = powers / jnp.sum(powers, axis=1, keepdims=True)
            high = chances.astype(BF16)
            low = (chances - high.astype(F32)).astype(BF16)
            gates = dot(pick[at], jnp.concatenate([high, low], axis=1))
            for e in range(experts):
                gate_ref[e, at] = gates[e * slots : (e + 1) * slots]

    jobs = _Jobs(load, compute)
    jobs.add(*[(j, (z + j) % 4, core) for j in range(4)])

    def along(level, source, step):
        @pl.when((z > 0) & (level >= z))
        def _():
            step(source, 0, level, (u, z - 1))

        @pl.when((z < DEPTH - 1) & (level <= z))
        def _():
            step(source, 1, level, (u, z + 1))

    def go(source, way, level, to):
        _send(source, block(u, level), z_send.at[way, level], z_recv.at[level], to)

    def gone(source, way, level, to):
        _sent(source, z_send.at[way, level], here)

    sources = [x_ref] + [block(u, order[i]) for i in range(1, 4)]

    def arrive(i):
        level = order[i]
        if i:
            _expect(block(u, level), z_recv.at[level], here)
        along(level, sources[i], go)
        for way, bits in enumerate((FIRST, THEN)):
            for h in range(2):
                cut = sources[i].at[halves[h]]
                _send(cut, part(u, level, h), p_send.at[level, h, way], p_recv.at[level, h, way], (u ^ bits[h], z))
        _send(sources[i], block(u, level), c_send.at[level, 0], c_recv.at[level, 0], (u ^ 1, z))

    def onward(i):
        level = order[i]
        for h in range(2):
            near = part(u ^ FIRST[h], level, h)
            _expect(near, p_recv.at[level, h, 0], here)
            _send(near, near, p_send.at[level, h, 2], p_recv.at[level, h, 2], (u ^ THEN[h], z))

    def share(i):
        level = order[i]
        for h in range(2):
            _expect(part(u ^ THEN[h], level, h), p_recv.at[level, h, 1], here)
            _expect(part(u ^ 6, level, h), p_recv.at[level, h, 2], here)
        for k, bit in enumerate((2, 4, 6)):
            ref = block(u ^ bit, level)
            _send(ref, ref, c_send.at[level, k + 1], c_recv.at[level, k + 1], (u ^ 1, z))
        jobs.add(("x", level, core))

    def received(i):
        level = order[i]
        for k, bit in enumerate((0, 2, 4, 6)):
            _expect(block(u ^ 1 ^ bit, level), c_recv.at[level, k], here)
        jobs.add(("x", level, other))

    arrive(0)
    _send(here_g, other_here, h_send, h_recv, (u ^ 1, z))
    for k in range(4):
        _send(own_g[k], other_g.at[k], g_send.at[k], g_recv.at[k], (u ^ 1, z))
    jobs.run(2)
    onward(0)
    jobs.run(1)
    arrive(1)
    _expect(other_here, h_recv, here)
    for k in range(4):
        _expect(other_g.at[k], g_recv.at[k], here)
    jobs.add(*[(j, (z + j) % 4, other) for j in range(4)])
    jobs.run(2)
    own.wait()
    share(0)
    jobs.run(2)
    onward(1)
    arrive(2)
    received(0)
    jobs.run(2)
    arrive(3)
    share(1)
    received(1)
    jobs.run(1)
    onward(2)
    jobs.run(2)
    share(2)
    received(2)
    jobs.run(1)
    onward(3)
    jobs.run(2)
    share(3)
    received(3)
    jobs.run(16)
    for i in range(4):
        level = order[i]
        along(level, sources[i], gone)
        for h in range(2):
            for k in range(3):
                _sent(part(u, level, h), p_send.at[level, h, k], here)
        for k in range(4):
            _sent(block(u, level), c_send.at[level, k], here)
    _sent(other_here, h_send, here)
    for k in range(4):
        _sent(other_g.at[k], g_send.at[k], here)
    for copy in sent.values():
        copy.wait()


def gather_pick(x, here_g, g, slot, router, slots, collective_id):
    T, D = x.shape
    groups, EL, group = slot.shape
    picked = jax.ShapeDtypeStruct((EL, groups, slots, D), BF16)
    outs = [
        jax.ShapeDtypeStruct((32, T, D), BF16),
        picked,
        picked,
        jax.ShapeDtypeStruct((EL, groups, slots, 128), F32),
        jax.ShapeDtypeStruct((4, T, D), BF16),
        jax.ShapeDtypeStruct((4, 3, T, D), BF16),
    ]
    scratch = [
        pltpu.VMEM((groups, EL * slots, group), BF16),
        pltpu.VMEM((2, group, D), BF16),
        pltpu.VMEM((2, EL, slots, D), BF16),
        DMA((2, 4)),
        DMA((2,)),
        DMA,
        DMA((2, 4)),
        DMA((4,)),
        DMA((4, 2, 3)),
        DMA((4, 2, 3)),
        DMA((4, 4)),
        DMA((4, 4)),
        DMA((4,)),
        DMA((4,)),
        DMA,
        DMA,
    ]
    specs = ([IN_VMEM] + [ANY_SPACE] * 5 + [IN_VMEM] * 2, [ANY_SPACE] * 3 + [IN_VMEM] + [ANY_SPACE] * 2)
    kernel = functools.partial(_gather_pick_kernel, width=PICK_WIDTH)
    out, xr, gr, gates, *_ = _comm(kernel, outs, scratch, collective_id, specs)(x, here_g, *g, slot, router)
    return out.reshape(32 * T, D), xr, gr, gates


def _tree_sum_steps(u, z, own, bufs, sems, T, count):
    c_buf, p_buf, q_buf = bufs
    c_send, c_recv, p_send, p_recv, q_send, q_recv = sems
    here = (u, z)
    half = T // 2
    halves = (pl.ds(0, half), pl.ds(half, half))

    def to_sibling(i, k, ref):
        _send(ref, c_buf.at[i, k], c_send.at[i, k], c_recv.at[i, k], (u ^ 1, z))

    def add_core(i):
        for k in (3, 2, 1, 0):
            _expect(c_buf.at[i, k], c_recv.at[i, k], here)
            _accumulate(own(i, k), c_buf.at[i, k], T)
            for h in range(2):
                if k and (k == 3 or CHIPS[k] == THEN[h]):
                    j = 1 if k == 3 else 0
                    part = own(i, k).at[halves[h]]
                    _send(part, p_buf.at[i, h, j], p_send.at[i, h, j], p_recv.at[i, h, j], (u ^ THEN[h], z))

    def add_far(i):
        for h in range(2):
            part = own(i, CHIPS.index(FIRST[h])).at[halves[h]]
            _expect(p_buf.at[i, h, 1], p_recv.at[i, h, 1], here)
            _accumulate(part, p_buf.at[i, h, 1], half)
            _send(part, q_buf.at[i, h], q_send.at[i, h], q_recv.at[i, h], (u ^ FIRST[h], z))

    def add_near(i):
        for h in range(2):
            _expect(p_buf.at[i, h, 0], p_recv.at[i, h, 0], here)
            _accumulate(own(i, 0).at[halves[h]], p_buf.at[i, h, 0], half)

    def add_then(i):
        for h in range(2):
            _expect(q_buf.at[i, h], q_recv.at[i, h], here)
            _accumulate(own(i, 0).at[halves[h]], q_buf.at[i, h], half)

    def finish():
        for i in range(count):
            for k in range(4):
                _sent(c_buf.at[i, k], c_send.at[i, k], here)
            for h in range(2):
                for j in range(2):
                    _sent(p_buf.at[i, h, j], p_send.at[i, h, j], here)
                _sent(q_buf.at[i, h], q_send.at[i, h], here)

    return to_sibling, add_core, add_far, add_near, add_then, finish


def _line_end(u, z, level, i, part, z_buf, sems, rows):
    z_send, z_recv = sems
    here = (u, z)

    @pl.when((level >= z) & (z > 0))
    def _():
        _expect(z_buf.at[0, level], z_recv.at[0, level], here)
        _accumulate(part, z_buf.at[0, level], rows)

    @pl.when((level <= z) & (z < DEPTH - 1))
    def _():
        _expect(z_buf.at[1, level], z_recv.at[1, level], here)
        _accumulate(part, z_buf.at[1, level], rows)

    if i < 3:

        @pl.when(level > z)
        def _():
            _send(part, z_buf.at[0, level], z_send.at[i], z_recv.at[0, level], (u, z + 1))

        @pl.when(level < z)
        def _():
            _send(part, z_buf.at[1, level], z_send.at[i], z_recv.at[1, level], (u, z - 1))


def _place(chip, k, T):
    return pl.ds(pl.multiple_of((chip ^ (CHIPS[k] // 2)) * T, T), T)


def _tree_part(u, z, ready, refs, T, then_do):
    work, c_buf, p_buf, q_buf, sem = refs[:5]
    core, chip = u % 2, u // 2
    to_sibling, add_core, add_far, add_near, add_then, finish = _tree_sum_steps(
        u, z, lambda i, k: work.at[_place(chip, k, T)], (c_buf, p_buf, q_buf), refs[5:], T, 1
    )
    for k in (3, 2, 1, 0):
        to_sibling(0, k, ready.at[1 - core, _place(chip, k, T)])
    copy = pltpu.make_async_copy(ready.at[core], work, sem)
    copy.start()
    yield
    copy.wait()
    add_core(0)
    yield
    add_far(0)
    yield
    add_near(0)
    add_then(0)
    then_do(work.at[_place(chip, 0, T)])
    yield
    finish()


def _tree_scratch(T, D):
    half = T // 2
    return [
        pltpu.VMEM((4 * T, D), BF16),
        pltpu.VMEM((1, 4, T, D), BF16),
        pltpu.VMEM((1, 2, 2, half, D), BF16),
        pltpu.VMEM((1, 2, half, D), BF16),
        DMA,
        DMA((1, 4)),
        DMA((1, 4)),
        DMA((1, 2, 2)),
        DMA((1, 2, 2)),
        DMA((1, 2)),
        DMA((1, 2)),
    ]


def _spread_part(u, z, slot_ref, source, gg_ref, order, refs, level_done, later=lambda i: None, extra=None):
    work, c_buf, p_buf, q_buf, side, in_buf, in_sem = refs[:7]
    core, chip = u % 2, u // 2
    other = 1 - core
    _, group, experts = slot_ref.shape
    slots, D = source.shape[2:]
    total = experts * slots
    T = group // 4
    count = len(order)

    def place(k):
        return _place(chip, k, T)

    def own(i, k):
        return work.at[i, place(k)]

    to_sibling, add_core, add_far, add_near, add_then, finish = _tree_sum_steps(
        u, z, own, (c_buf, p_buf, q_buf), refs[7:], T, count
    )
    lane = lax.broadcasted_iota(jnp.int32, (experts, total), 1)
    which = lax.broadcasted_iota(jnp.int32, (experts, total), 0)
    choose = jnp.where((lane >= which * slots) & (lane < (which + 1) * slots), 1.0, 0.0).astype(BF16)
    offset = lane[:1] - jnp.sum(jnp.where(lane >= (which + 1) * slots, slots, 0), axis=0, keepdims=True)
    offset = offset.astype(F32)
    column = lax.broadcasted_iota(jnp.int32, (slots, 128), 1)

    def load(n, job, start):
        i, c = job
        level = z if i is None else order[i]
        copy = pltpu.make_async_copy(source.at[:, 2 * level + c], in_buf.at[n % 2], in_sem.at[n % 2])
        copy.start() if start else copy.wait()

    def compute(n, job):
        i, c = job
        at = 2 * (z if i is None else order[i]) + c
        mine = dot(slot_ref[at].astype(BF16), choose)
        pick = jnp.where(mine == offset, 1.0, 0.0).astype(BF16)
        rows_in = in_buf.at[n % 2]
        if i is None:
            target = extra[0].at[c]
        else:
            target = work.at[i] if c is core else side.at[i]
        if gg_ref is not None:
            grads = [jnp.where(column == u * experts + e, gg_ref[e, at], 0.0).astype(BF16) for e in range(experts)]
            target[:, pl.ds(D, 128)] = dot(pick, jnp.concatenate(grads, axis=0)).astype(BF16)

        def step(j, _):
            cols = pl.ds(pl.multiple_of(j * SPREAD_WIDTH, SPREAD_WIDTH), SPREAD_WIDTH)
            rows = jnp.concatenate([rows_in[e, :, cols] for e in range(experts)], axis=0)
            target[:, cols] = dot(pick, rows).astype(BF16)
            return 0

        lax.fori_loop(0, D // SPREAD_WIDTH, step, 0)
        if i is None:
            extra_copy(c).start()
        elif c is not core:
            for k in (3, 2, 1, 0):
                to_sibling(i, k, side.at[i, place(k)])

    def extra_copy(c):
        return pltpu.make_async_copy(extra[0].at[c], extra[1].at[c], extra[2].at[c])

    def end(i):
        add_then(i)
        level_done(i, own(i, 0))

    jobs = _Jobs(load, compute)
    for i in range(count):
        jobs.add((i, other), (i, core))
    if extra is not None:
        jobs.add((None, 0), (None, 1))
    for step in range(count + 3):
        if step >= 3:
            end(step - 3)
            later(step - 3)
        if 0 <= step - 2 < count:
            add_near(step - 2)
        jobs.run(2 if step < count else 1)
        if 0 <= step - 1 < count:
            add_far(step - 1)
        if step < count:
            add_core(step)
        yield
    if extra is not None:
        extra_copy(0).wait()
        extra_copy(1).wait()
    yield
    finish()


def _spread_scratch(T, W, rows_shape, count=4):
    half = T // 2
    return [
        pltpu.VMEM((count, 4 * T, W), BF16),
        pltpu.VMEM((count, 4, T, W), BF16),
        pltpu.VMEM((count, 2, 2, half, W), BF16),
        pltpu.VMEM((count, 2, half, W), BF16),
        pltpu.VMEM((count, 4 * T, W), BF16),
        pltpu.VMEM((2,) + rows_shape, BF16),
        DMA((2,)),
        DMA((count, 4)),
        DMA((count, 4)),
        DMA((count, 2, 2)),
        DMA((count, 2, 2)),
        DMA((count, 2)),
        DMA((count, 2)),
    ]


def spread_scatter(slot, gate_grads, entry_rows, collective_id):
    groups, group, EL = slot.shape
    slots, D = entry_rows.shape[2:]
    T, W = group // 4, D + 128

    def kernel(slot_ref, gg_ref, entry_ref, o_ref, z_buf, z_send, z_recv, *refs):
        u, z = lax.axis_index("uly"), lax.axis_index("blk")
        order = tuple(reversed(_line_order(z)))
        parts = []

        def done(i, part):
            parts.append(part)

        def line(i):
            _line_end(u, z, order[i], i, parts[i], z_buf, (z_send, z_recv), T)

        _greet(u, z, (1, 2, 4), line=True)
        _run(_spread_part(u, z, slot_ref, entry_ref, gg_ref, order, refs, done, line))
        o_ref[...] = parts[3][...]
        for i in range(3):
            _sent(parts[i], z_send.at[i], (u, z))

    scratch = [pltpu.VMEM((2, 4, T, W), BF16), DMA((4,)), DMA((2, 4))] + _spread_scratch(T, W, (EL, slots, D))
    specs = ([IN_VMEM, IN_VMEM, ANY_SPACE], IN_VMEM)
    out = jax.ShapeDtypeStruct((T, W), BF16)
    return _comm(kernel, out, scratch, collective_id, specs)(slot, gate_grads, entry_rows)


def slots_of(chosen):
    count = chosen.shape[-1]
    before = (jnp.arange(count)[:, None] < jnp.arange(count)[None, :]).astype(BF16)
    earlier = jnp.einsum("abs,st->abt", chosen.astype(BF16), before, preferred_element_type=F32)
    return jnp.where(chosen, earlier.astype(jnp.int32), -1)


class Slice:
    def __init__(self, U, Z, T, D):
        self.U, self.Z, self.T, self.D = U, Z, T, D
        self.u, self.z = lax.axis_index("uly"), lax.axis_index("blk")
        self.C = D // 8
        self.L = 8 * T
        self.group = 2 * self.z + self.u % 2
        self.first_block, self.block_step = 8 * (self.u // 2), 1
        self.rows = ATTEND_ROWS

    def enter(self, hidden, weights, gains, out_weight, router, routes, out_grad):
        rows, weights, packs, routes, self.here = enter(hidden, weights, gains, router, routes, out_grad, 1)
        there = [((2 * ((z + u // 2) % 4) + u % 2), u // 2) for u in range(8) for z in range(4)]
        self.forth = [(i, 4 * u + z) for i, (u, z) in enumerate(there)]
        rows, mine = lax.optimization_barrier((rows, self.permute(out_weight, self.forth)))
        self.out_parts = [mine] + [self.permute(mine, self.across(bit)) for bit in (2, 4, 6)]
        self.parts = [((self.u // 2) ^ k) - self.z + 4 for k in range(4)]
        self.parts = [p % 4 for p in self.parts]
        return (
            rows.reshape(self.L, self.D),
            weights.reshape(self.D, 3 * self.C),
            packs.reshape(self.D, -1),
            routes,
        )

    def permute(self, x, pairs):
        return lax.ppermute(x, ALL, pairs)

    def across(self, bit):
        return [(i, i ^ (4 * bit)) for i in range(32)]

    def sequence(self, key, value, squares, upstream):
        keys, values, own, stats, k_stat = plane_pair(key, value, upstream, squares.reshape(-1, 128), 4)
        own, *self.out_parts = lax.optimization_barrier((own, *self.out_parts))
        first = [(i, i ^ (8 if i // 4 % 2 == 0 else 16)) for i in range(32)]
        self.then = [(i, i ^ (16 if i // 4 % 2 == 0 else 8)) for i in range(32)]
        self.upstream = (own, self.permute(own, first))
        return keys.reshape(-1, self.C), values.reshape(-1, self.C), stats.reshape(2, -1, 128), k_stat.reshape(-1, 128)

    def heads_to_rows(self, x):
        x, own, near, *self.prepared = lax.optimization_barrier((x, *self.upstream, *self.prepared))
        self.upstream = (own, near, self.permute(own, self.then), self.permute(near, self.then))
        return column_scatter(x.reshape(2, 4, self.T, self.D), 5)

    def prepare(self, routes, EL, router):
        T = self.T
        chosen = jnp.any(routes[None] == (self.u * EL + jnp.arange(EL, dtype=jnp.int32))[:, None, None, None, None], axis=3)
        chosen = chosen.reshape(EL, 4, 2, 4, T).transpose(3, 2, 0, 1, 4).reshape(8, EL, 4 * T)
        slot = slots_of(chosen)
        self.prepared = (slot, slot.transpose(0, 2, 1), router)

    def experts(self, second_low, weights):
        EL, D = weights.shape[0], self.D
        slots = -(-4 * CAP // 16) * 16
        slot, self.slot, router = self.prepared
        second_all, xr, gr, gates = gather_pick(second_low, self.here, self.upstream, slot, router, slots, 7)
        flat, cut = (EL, 8 * slots, -1), (EL, 8, slots, -1)
        out_rows, entry_rows, self.expert_grads, gate_grads = run_experts(
            xr.reshape(flat), gr.reshape(flat), gates.reshape(flat), weights, 8 * slots
        )
        self.out_rows = out_rows.reshape(cut)
        return second_all, spread_scatter(self.slot, gate_grads.reshape(cut), entry_rows.reshape(cut), 8)

    def rows_to_heads(self, x):
        rows, self.out_line, self.out_here = column_gather(x, self.slot, self.out_rows, 6)
        return rows.reshape(self.L, self.D), self.expert_grads

    def sequence_sums(self, dk, dv, out_part, q_inner, k_inner):
        cut = (4, self.L, self.C)
        inner = jnp.concatenate([q_inner, k_inner.reshape(-1, 128)], axis=0)
        dk, dv, out_sum, inner = key_value_sums(dk.reshape(cut), dv.reshape(cut), self.out_line, inner, 10)
        parts = out_part.reshape(4, -1, self.D)
        mine, *others = [lax.dynamic_index_in_dim(parts, p, 0, False) for p in self.parts]
        dk, *others = lax.optimization_barrier((dk, *others))
        self.out_terms = [mine] + [self.permute(x, self.across(bit)) for x, bit in zip(others, (2, 4, 6))]
        return dk, dv, out_sum, inner.reshape(2, -1, 128)

    def leave(self, first_part, weight_part, logit_grad, ffn_part, head_parts):
        T, R = self.T, self.D // 32
        first_part, *terms = lax.optimization_barrier((first_part, *self.out_terms))
        out_grad = sum(x.astype(F32) for x in terms).astype(BF16)
        out_grad = self.permute(out_grad, [(b, a) for a, b in self.forth])
        thin = jnp.concatenate([ffn_part.reshape(-1, 128), head_parts.reshape(-1, 128)], axis=0)
        wide = self.D // 128
        used = thin.shape[0]
        thin = jnp.pad(thin, ((0, -used % 8), (0, 0)))
        first, weights, self.out_own, logit_all, thin = leave(
            first_part.reshape(2, 4, T, self.D),
            weight_part.reshape(4, 2, 4 * R, 3 * self.C),
            [logit_grad.reshape(T // 2, 2 * EXPERTS), thin],
            self.out_here,
            11,
        )
        ffn = lax.dynamic_slice_in_dim(
            jnp.sum(thin[:, :, :wide], axis=(0, 1)).reshape(self.D), (self.u * 4 + self.z) * R, R, 0
        )
        mine = lax.dynamic_index_in_dim(thin.reshape(4, 2, 4, -1, 128), self.u % 2, 1, False)
        mine = lax.dynamic_index_in_dim(mine, self.u // 2, 1, False)
        heads = jnp.sum(mine[:, wide:used], axis=0).reshape(2, self.C)
        heads = lax.dynamic_slice_in_dim(heads, self.z * R, R, 1)
        return first, weights, out_grad, logit_all.reshape(32 * T, EXPERTS), ffn, heads


class General:
    def __init__(self, U, Z, T, D):
        self.U, self.Z, self.T, self.D = U, Z, T, D
        self.u, self.z = lax.axis_index("uly"), lax.axis_index("blk")
        self.C = D // U
        self.L = U * T
        self.group = self.u
        self.parts = range(4)
        self.first_block, self.block_step = self.z, Z
        self.rows = T

    def gather(self, x):
        return lax.all_gather(x, ALL, axis=0, tiled=True)

    def scatter_wide(self, x):
        return lax.psum_scatter(x, ALL, scatter_dimension=0, tiled=True)

    def enter(self, hidden, weights, gains, out_weight, router, routes, out_grad):
        U, R = self.U, router.shape[0]
        gains, hidden = gains.astype(F32), hidden.astype(F32)
        scaled = jnp.stack([(w.astype(F32) * gains[:, :1]).astype(BF16) for w in weights])
        pack = jnp.concatenate(_packed(router, gains), axis=1)
        rows = (hidden * norm_scale(hidden)).astype(BF16)
        self.out_parts = jnp.split(lax.all_gather(out_weight, "blk", axis=0, tiled=True), 4)
        swapped = lax.all_to_all(scaled.transpose(1, 0, 2).reshape(R, 3, U, self.C), "uly", split_axis=2, concat_axis=0, tiled=True)
        weights = lax.all_gather(swapped.reshape(U, R, 3 * self.C), "blk", axis=1, tiled=True)
        return (
            self.rows_all(rows),
            weights.reshape(self.D, 3 * self.C),
            self.gather(pack),
            self.gather(routes[None]).reshape((U, self.Z) + routes.shape),
        )

    def sequence(self, key, value, squares, upstream):
        self.upstream = upstream
        pair = jnp.stack([key, value]).reshape(2, self.U, self.T, self.C)
        pair = lax.all_gather(pair, "blk", axis=2, tiled=False).reshape(2, -1, self.C)
        stats = lax.psum(squares, "uly")
        k_stat = lax.all_gather(stats[1].reshape(self.U, -1, 128), "blk", axis=1, tiled=False).reshape(-1, 128)
        return pair[0], pair[1], stats, k_stat

    def heads_to_rows(self, x):
        return self.rows_sum(x)

    def rows_sum(self, x):
        return lax.psum_scatter(x, "uly", scatter_dimension=0, tiled=True)

    def rows_all(self, x):
        return lax.all_gather(x, "uly", axis=0, tiled=True)

    def prepare(self, routes, EL, router):
        self.prepared = (routes, router)

    def experts(self, second_low, weights):
        EL, D = weights.shape[0], self.D
        routes, router = self.prepared
        second_all, upstream_all = self.gather(second_low), self.gather(self.upstream)
        N = upstream_all.shape[0]
        group = min(512, N)
        groups = N // group
        slots = -(-(group // self.T * CAP) // 16) * 16
        rows = groups * slots
        own_first = self.u * EL
        chosen = jnp.any(routes[None] == (own_first + jnp.arange(EL, dtype=jnp.int32))[:, None, None, None, None], axis=3)
        slot = slots_of(chosen.reshape(EL, groups, group)).reshape(EL, N)
        entry_in, upstream_in, gates = pick_rows(slot, router, second_all, upstream_all, group, slots)
        flat, split = (EL, rows, -1), (EL, groups, slots, -1)
        out_rows, entry_rows, self.expert_grads, gate_grads = run_experts(
            entry_in.reshape(flat), upstream_in.reshape(flat), gates.reshape(flat), weights, min(8, groups) * slots
        )
        out_part, entry_part = spread_rows(
            own_first.astype(jnp.int32)[None],
            slot.T,
            gate_grads.reshape(split),
            out_rows.reshape(split),
            entry_rows.reshape(split),
            group,
        )
        self.out_sum = self.scatter_wide(out_part)
        self.out_own = jnp.zeros_like(self.out_sum)
        return second_all, self.scatter_wide(entry_part)

    def rows_to_heads(self, x):
        return self.rows_all(x), self.expert_grads

    def sequence_sums(self, dk, dv, out_part, q_inner, k_inner):
        pair = jnp.stack([dk, dv]).reshape(2, self.U, self.Z, self.T, self.C)
        pair = lax.psum_scatter(pair, "blk", scatter_dimension=2, tiled=True).reshape(2, self.L, self.C)
        k_inner = lax.psum_scatter(
            k_inner.reshape(self.U, self.Z, -1, 128), "blk", scatter_dimension=1, tiled=True
        ).reshape(-1, 128)
        inner = lax.psum(jnp.stack([q_inner, k_inner]), "uly")
        self.out_grad = lax.psum_scatter(out_part, "blk", scatter_dimension=0, tiled=True)
        return pair[0], pair[1], self.out_sum, inner

    def leave(self, first_part, weight_part, logit_grad, ffn_part, head_parts):
        U, R = self.U, self.D // (self.U * self.Z)
        part = weight_part.reshape(U, self.Z * R, 3 * self.C)
        part = lax.psum_scatter(part, "blk", scatter_dimension=1, tiled=True)
        part = lax.all_to_all(part, "uly", split_axis=0, concat_axis=0, tiled=True)
        weights = part.reshape(U, R, 3, self.C).transpose(2, 1, 0, 3).reshape(3, R, self.D)
        heads = lax.psum_scatter(head_parts, "blk", scatter_dimension=1, tiled=True)
        first = self.rows_sum(first_part)
        return first, weights, self.out_grad, self.gather(logit_grad), self.scatter_wide(ffn_part), heads


def _row_limits(doc_ref, first, rows):
    position = first + lax.broadcasted_iota(jnp.int32, (rows, 1), 0)
    start = jnp.zeros_like(position)
    lowest = jnp.int32(0)
    for d in range(doc_ref.shape[0]):
        begin = doc_ref[d]
        start = jnp.where(begin <= position, jnp.maximum(start, begin), start)
        lowest = jnp.where(begin <= first, jnp.maximum(lowest, begin), lowest)
    return position, start, lowest


def _norm_row(squares, width):
    return lax.rsqrt(squares * (1.0 / width) + EPS)


def _as_column(row):
    return jnp.broadcast_to(row, (128, 128)).T


def _row_sums(values):
    ones = jnp.ones((8, values.shape[1]), F32)
    return lax.dot_general(ones, values, LAST_DIM, precision=lax.Precision.HIGHEST, preferred_element_type=F32)[:1]


def _key_scales(stat_ref, at, chunk, width):
    rows = stat_ref[pl.ds(pl.multiple_of(at // 128, chunk // 128), chunk // 128), :]
    return _norm_row(jnp.concatenate([rows[r : r + 1] for r in range(chunk // 128)], axis=1), width)


def _scores(query, key, factor, position, start, key_first):
    raw = dot(query, key, LAST_DIM) * factor
    key_position = key_first + lax.broadcasted_iota(jnp.int32, raw.shape, 1)
    return jnp.where((key_position <= position) & (key_position >= start), raw, NEG)


def _scaled_query(q_ref, stat_ref, width):
    heads, units = q_ref.shape[1] // HEAD_DIM, q_ref.shape[0] // 128
    scale = jnp.concatenate(
        [_as_column(_norm_row(stat_ref[pl.ds(pl.program_id(0) * units + r, 1), :], width)) for r in range(units)], axis=0
    )
    cols = [pl.ds(h * HEAD_DIM, HEAD_DIM) for h in range(heads)]
    return [(q_ref[:, at].astype(F32) * scale).astype(BF16) for at in cols], cols


def _lay_parts(index_ref, parts, whole):
    @pl.when(pl.program_id(0) == 0)
    def _():
        for i, part in enumerate(parts):
            height = part.shape[0]
            whole[pl.ds(pl.multiple_of(index_ref[2 + i] * height, height), height), :] = part[...]


def _attend_kernel(
    index_ref, doc_ref, q_stat, k_stat, q_ref, k_ref, v_ref, w0, w1, w2, w3, o_ref, log_ref, mix_ref, whole, *, chunk, scaling, width
):
    rows = q_ref.shape[0]
    _lay_parts(index_ref, (w0, w1, w2, w3), whole)
    heads = q_ref.shape[1] // HEAD_DIM
    first = (pl.program_id(0) * index_ref[1] + index_ref[0]) * rows
    position, start, lowest = _row_limits(doc_ref, first, rows)
    queries, cols = _scaled_query(q_ref, q_stat, width)

    def step(i, state):
        at = pl.multiple_of(i * chunk, chunk)
        factor = _key_scales(k_stat, at, chunk, width) * scaling
        new = []
        for h in range(heads):
            top, total, out = state[h]
            scores = _scores(queries[h], k_ref[pl.ds(at, chunk), cols[h]], factor, position, start, at)
            now = jnp.maximum(top, jnp.max(scores, axis=1, keepdims=True))
            weights = jnp.exp(scores - now)
            fade = jnp.exp(top - now)
            total = total * fade + jnp.sum(weights, axis=1, keepdims=True)
            out = out * fade + dot(weights.astype(BF16), v_ref[pl.ds(at, chunk), cols[h]])
            new.append((now, total, out))
        return tuple(new)

    zero = (
        jnp.full((rows, 1), NEG, F32),
        jnp.zeros((rows, 1), F32),
        jnp.zeros((rows, HEAD_DIM), F32),
    )
    last = first + rows
    state = lax.fori_loop(lowest // chunk, (last + chunk - 1) // chunk, step, (zero,) * heads)
    for h in range(heads):
        top, total, out = state[h]
        o_ref[:, cols[h]] = out / total
        log_ref[:, cols[h]] = jnp.broadcast_to(top + jnp.log(total), (rows, HEAD_DIM))
    mix_ref[...] = dot(o_ref[...].astype(BF16), whole[...]).astype(BF16)


def _attend_back_kernel(
    index_ref,
    doc_ref,
    q_stat,
    k_stat,
    q_ref,
    r_ref,
    o_ref,
    log_ref,
    k_ref,
    v_ref,
    w0,
    w1,
    w2,
    w3,
    dq_ref,
    dk_ref,
    dv_ref,
    dw_ref,
    mq_ref,
    mk_ref,
    dk_sum,
    dv_sum,
    dw_sum,
    whole,
    *,
    chunk,
    scaling,
    width,
):
    rows = q_ref.shape[0]
    _lay_parts(index_ref, (w0, w1, w2, w3), whole)
    heads = q_ref.shape[1] // HEAD_DIM
    first = (pl.program_id(0) * index_ref[1] + index_ref[0]) * rows
    position, start, lowest = _row_limits(doc_ref, first, rows)
    queries, cols = _scaled_query(q_ref, q_stat, width)

    @pl.when(pl.program_id(0) == 0)
    def _():
        dk_sum[...] = jnp.zeros_like(dk_sum)
        dv_sum[...] = jnp.zeros_like(dv_sum)
        dw_sum[...] = jnp.zeros_like(dw_sum)
        mk_ref[...] = jnp.zeros_like(mk_ref)

    upstream = r_ref[...]
    dw_sum[...] += dot(o_ref[...].astype(BF16), upstream, FIRST_DIM)
    all_grads = dot(upstream, whole[...], LAST_DIM).astype(BF16)
    grads = [all_grads[:, h * HEAD_DIM : (h + 1) * HEAD_DIM] for h in range(heads)]
    deltas = [jnp.sum(grads[h].astype(F32) * o_ref[:, cols[h]], axis=1, keepdims=True) for h in range(heads)]
    logs = [log_ref[:, at][:, :1] for at in cols]

    def step(i, state):
        at = pl.multiple_of(i * chunk, chunk)
        scale = _key_scales(k_stat, at, chunk, width)
        new = []
        key_inner = jnp.zeros((1, chunk), F32)
        query_inner = state[-1]
        for h in range(heads):
            grad = grads[h]
            key = k_ref[pl.ds(at, chunk), cols[h]]
            scores = _scores(queries[h], key, scale * scaling, position, start, at)
            weights = jnp.exp(scores - logs[h])
            weight_grad = dot(grad, v_ref[pl.ds(at, chunk), cols[h]], LAST_DIM)
            score_grad = weights * (weight_grad - deltas[h])
            inner = score_grad * scores
            key_inner = key_inner + jnp.sum(inner, axis=0, keepdims=True)
            query_inner = query_inner + jnp.sum(inner, axis=1, keepdims=True)
            dv_sum[pl.ds(at, chunk), cols[h]] += dot(weights.astype(BF16), grad, FIRST_DIM)
            dk_sum[pl.ds(at, chunk), cols[h]] += dot(score_grad.astype(BF16), queries[h], FIRST_DIM)
            new.append(state[h] + dot((score_grad * scale).astype(BF16), key))
        mk_ref[pl.ds(i, 1), :] += key_inner
        return tuple(new) + (query_inner,)

    last = first + rows
    zeros = (jnp.zeros((rows, HEAD_DIM), F32),) * heads + (jnp.zeros((rows, 1), F32),)
    state = lax.fori_loop(lowest // chunk, (last + chunk - 1) // chunk, step, zeros)
    for h in range(heads):
        dq_ref[:, cols[h]] = (state[h] * scaling).astype(BF16)
    for r in range(rows // 128):
        inner = jnp.broadcast_to(state[-1][r * 128 : (r + 1) * 128], (128, 128)).T[:1]
        mq_ref[pl.ds(pl.program_id(0) * (rows // 128) + r, 1), :] = inner

    @pl.when(pl.program_id(0) == pl.num_programs(0) - 1)
    def _():
        dk_ref[...] = (dk_sum[...] * scaling).astype(BF16)
        dv_ref[...] = dv_sum[...].astype(BF16)
        dw_ref[...] = dw_sum[...].astype(BF16)


def _resident(*shape):
    return pl.BlockSpec(shape, lambda i, *_: (0,) * len(shape), pipeline_mode=pl.Buffered(1))


def attention_forward(index, docs, q_stat, k_stat, query, key_all, value_all, out_parts, rows, chunk):
    (L, C), N = query.shape, key_all.shape[0]
    D = out_parts[0].shape[1]
    block = pl.BlockSpec((rows, C), lambda i, *_: (i, 0))
    stats = [_resident(*q_stat.shape), _resident(*k_stat.shape)]
    return pl.pallas_call(
        functools.partial(_attend_kernel, chunk=chunk, scaling=HEAD_DIM ** (-0.5), width=HEADS * HEAD_DIM),
        out_shape=[jax.ShapeDtypeStruct((L, C), F32)] * 2 + [jax.ShapeDtypeStruct((L, D), BF16)],
        grid_spec=pltpu.PrefetchScalarGridSpec(
            num_scalar_prefetch=2,
            grid=(L // rows,),
            in_specs=stats + [block, _resident(N, C), _resident(N, C)] + [_resident(C // 4, D)] * 4,
            out_specs=[block, block, pl.BlockSpec((rows, D), lambda i, *_: (i, 0))],
            scratch_shapes=[pltpu.VMEM((C, D), BF16)],
        ),
        compiler_params=pltpu.CompilerParams(vmem_limit_bytes=VMEM_BYTES),
        cost_estimate=pl.CostEstimate(flops=4 * L * C * 1024, bytes_accessed=4 * N * C, transcendentals=L * 1024),
    )(index, docs, q_stat, k_stat, query, key_all, value_all, *out_parts)


def attention_backward(
    index, docs, q_stat, k_stat, query, residual_grad, attended, logs, key_all, value_all, out_parts, rows, chunk
):
    (L, C), N = query.shape, key_all.shape[0]
    D = residual_grad.shape[1]
    block = pl.BlockSpec((rows, C), lambda i, *_: (i, 0))
    whole = _resident(N, C)
    stats = [_resident(*q_stat.shape), _resident(*k_stat.shape)]
    return pl.pallas_call(
        functools.partial(_attend_back_kernel, chunk=chunk, scaling=HEAD_DIM ** (-0.5), width=HEADS * HEAD_DIM),
        out_shape=[jax.ShapeDtypeStruct((L, C), BF16)]
        + [jax.ShapeDtypeStruct((N, C), BF16)] * 2
        + [jax.ShapeDtypeStruct((C, D), BF16)]
        + [jax.ShapeDtypeStruct(q_stat.shape, F32), jax.ShapeDtypeStruct((N // chunk, chunk), F32)],
        grid_spec=pltpu.PrefetchScalarGridSpec(
            num_scalar_prefetch=2,
            grid=(L // rows,),
            in_specs=stats
            + [block, pl.BlockSpec((rows, D), lambda i, *_: (i, 0)), block, block, whole, whole]
            + [_resident(C // 4, D)] * 4,
            out_specs=[block, whole, whole, _resident(C, D), stats[0], _resident(N // chunk, chunk)],
            scratch_shapes=[pltpu.VMEM((N, C), F32)] * 2 + [pltpu.VMEM((C, D), F32), pltpu.VMEM((C, D), BF16)],
        ),
        compiler_params=pltpu.CompilerParams(vmem_limit_bytes=VMEM_BYTES),
        cost_estimate=pl.CostEstimate(flops=10 * L * C * 1024, bytes_accessed=8 * N * C, transcendentals=L * 1024),
    )(index, docs, q_stat, k_stat, query, residual_grad, attended, logs, key_all, value_all, *out_parts)


def _project_kernel(x_ref, w_ref, gain_ref, cos_ref, sin_ref, pre_ref, q_ref, k_ref, v_ref, stat_ref):
    rows = x_ref.shape[0]
    C = q_ref.shape[1]
    pre = dot(x_ref[...], w_ref[...])
    pre_ref[...] = pre[:, : 2 * C]
    v_ref[...] = pre[:, 2 * C :].astype(BF16)
    cosine, sine = cos_ref[...], sin_ref[...]
    for j, out in enumerate((q_ref, k_ref)):
        part = pre[:, j * C : (j + 1) * C]
        sums = _row_sums(part * part)
        for r in range(rows // 128):
            stat_ref[j, pl.ds(pl.program_id(0) * (rows // 128) + r, 1), :] = sums[:, r * 128 : (r + 1) * 128]
        scaled = part * gain_ref[j : j + 1, :]
        for h in range(C // HEAD_DIM):
            one = scaled[:, h * HEAD_DIM : (h + 1) * HEAD_DIM]
            turned = pltpu.roll(one, HEAD_DIM // 2, 1)
            out[:, pl.ds(h * HEAD_DIM, HEAD_DIM)] = (one * cosine + turned * sine).astype(BF16)


def project(x, weights, gains, cosine, sine):
    L, D = x.shape
    C = weights.shape[1] // 3
    rows = min(PROJECT_ROWS, L)

    def block(width):
        return pl.BlockSpec((rows, width), lambda i: (i, 0))

    return pl.pallas_call(
        _project_kernel,
        out_shape=[jax.ShapeDtypeStruct((L, 2 * C), F32)]
        + [jax.ShapeDtypeStruct((L, C), BF16)] * 3
        + [jax.ShapeDtypeStruct((2, L // 128, 128), F32)],
        grid=(L // rows,),
        in_specs=[block(D), _resident(D, 3 * C), _resident(8, C), block(HEAD_DIM), block(HEAD_DIM)],
        out_specs=[block(2 * C), block(C), block(C), block(C), _resident(2, L // 128, 128)],
        compiler_params=pltpu.CompilerParams(vmem_limit_bytes=VMEM_BYTES),
        cost_estimate=pl.CostEstimate(flops=6 * L * D * C, bytes_accessed=2 * L * D + 6 * D * C, transcendentals=0),
    )(x, weights, gains, cosine, sine)


def _project_back_kernel(
    dq_ref, dk_ref, dv_ref, pre_ref, stat_ref, inner_ref, gain_ref, cos_ref, sin_ref, x_ref, w_ref, dw_ref, first_ref, dg_ref, total, *, width
):
    rows, C = dq_ref.shape
    cosine, sine = cos_ref[...], sin_ref[...]
    start = pl.program_id(0) == 0

    @pl.when(start)
    def _():
        dg_ref[...] = jnp.zeros_like(dg_ref)

    grads = []
    for j, ref in enumerate((dq_ref, dk_ref)):
        scales, means = [], []
        for r in range(rows // 128):
            at = pl.ds(pl.program_id(0) * (rows // 128) + r, 1)
            scale = _norm_row(stat_ref[j, at, :], width)
            scales.append(_as_column(scale))
            means.append(_as_column(inner_ref[j, at, :] * scale * scale * (1.0 / width)))
        scale, mean = jnp.concatenate(scales, axis=0), jnp.concatenate(means, axis=0)
        for h in range(C // HEAD_DIM):
            at = pl.ds(h * HEAD_DIM, HEAD_DIM)
            up = ref[:, at].astype(F32)
            up = up * cosine + pltpu.roll(up * sine, HEAD_DIM // 2, 1)
            pre = pre_ref[:, pl.ds(j * C + h * HEAD_DIM, HEAD_DIM)]
            grads.append((scale * up * gain_ref[j : j + 1, at] - pre * mean).astype(BF16))
            dg_ref[j : j + 1, at] += jnp.sum(up * pre * scale, axis=0, keepdims=True)
    grads.append(dv_ref[...])
    both = jnp.concatenate(grads, axis=1)
    first_ref[...] = dot(both, w_ref[...], LAST_DIM).astype(BF16)
    part = dot(x_ref[...], both, FIRST_DIM)

    @pl.when(start)
    def _():
        total[...] = part

    @pl.when(jnp.logical_not(start))
    def _():
        total[...] += part

    @pl.when(pl.program_id(0) == pl.num_programs(0) - 1)
    def _():
        dw_ref[...] = total[...].astype(BF16)


def project_back(dq, dk, dv, pre, stats, inner, gains, cosine, sine, x, weights):
    L, D = x.shape
    C = weights.shape[1] // 3
    rows = min(BACK_ROWS, L)

    def block(width):
        return pl.BlockSpec((rows, width), lambda i: (i, 0))

    return pl.pallas_call(
        functools.partial(_project_back_kernel, width=D),
        out_shape=[
            jax.ShapeDtypeStruct((D, 3 * C), BF16),
            jax.ShapeDtypeStruct((L, D), BF16),
            jax.ShapeDtypeStruct((8, C), F32),
        ],
        grid=(L // rows,),
        in_specs=[block(C)] * 3
        + [block(2 * C), _resident(*stats.shape), _resident(*inner.shape), _resident(8, C)]
        + [block(HEAD_DIM), block(HEAD_DIM), block(D), _resident(D, 3 * C)],
        out_specs=[_resident(D, 3 * C), block(D), _resident(8, C)],
        scratch_shapes=[pltpu.VMEM((D, 3 * C), F32)],
        compiler_params=pltpu.CompilerParams(vmem_limit_bytes=VMEM_BYTES),
        cost_estimate=pl.CostEstimate(flops=12 * L * D * C, bytes_accessed=4 * L * D + 12 * D * C, transcendentals=0),
    )(dq, dk, dv, pre, stats, inner, gains, cosine, sine, x, weights)


def _pick_kernel(slot_ref, router_ref, x_ref, g_ref, xr_ref, gr_ref, gate_ref, *, slots, width):
    experts, group = slot_ref.shape
    logits = lax.dot_general(router_ref[...], x_ref[...], (((0,), (1,)), ((), ())), preferred_element_type=F32)
    powers = jnp.exp(logits - jnp.max(logits, axis=0, keepdims=True))
    chances = powers / jnp.sum(powers, axis=0, keepdims=True)
    row = lax.broadcasted_iota(jnp.int32, (slots, group), 0)
    picks = []
    for e in range(experts):
        hit = slot_ref[e : e + 1, :] == row
        gate = jnp.sum(jnp.where(hit, chances[e : e + 1, :], 0.0), axis=1, keepdims=True)
        lane = lax.broadcasted_iota(jnp.int32, (slots, 128), 1)
        gate_ref[e, 0] = jnp.where(lane == e, gate, 0.0)
        picks.append(jnp.where(hit, 1.0, 0.0).astype(BF16))
    pick = jnp.concatenate(picks, axis=0)
    for source, target in ((x_ref, xr_ref), (g_ref, gr_ref)):

        def step(i, _, source=source, target=target):
            cols = pl.ds(pl.multiple_of(i * width, width), width)
            rows = dot(pick, source[:, cols]).astype(BF16)
            for e in range(experts):
                target[e, 0, :, cols] = rows[e * slots : (e + 1) * slots]
            return 0

        lax.fori_loop(0, source.shape[1] // width, step, 0)


def pick_rows(slot, router, x, g, group, slots):
    EL, N = slot.shape
    D = x.shape[1]
    groups = N // group
    tokens = pl.BlockSpec((group, D), lambda i: (i, 0))
    picked = pl.BlockSpec((EL, 1, slots, D), lambda i: (0, i, 0, 0))
    rows = jax.ShapeDtypeStruct((EL, groups, slots, D), BF16)
    return pl.pallas_call(
        functools.partial(_pick_kernel, slots=slots, width=512),
        out_shape=[rows, rows, jax.ShapeDtypeStruct((EL, groups, slots, 128), F32)],
        grid=(groups,),
        in_specs=[
            pl.BlockSpec((EL, group), lambda i: (0, i)),
            pl.BlockSpec(router.shape, lambda i: (0, 0)),
            tokens,
            tokens,
        ],
        out_specs=[picked, picked, pl.BlockSpec((EL, 1, slots, 128), lambda i: (0, i, 0, 0))],
        compiler_params=pltpu.CompilerParams(vmem_limit_bytes=VMEM_BYTES),
        cost_estimate=pl.CostEstimate(
            flops=4 * EL * slots * N * D, bytes_accessed=8 * N * D, transcendentals=N * EXPERTS
        ),
    )(slot, router, x, g)


def _expert_kernel(x_ref, g_ref, gate_ref, w_ref, out_ref, entry_ref, dw_ref, gg_ref):
    x, g = x_ref[0], g_ref[0]
    lane = lax.broadcasted_iota(jnp.int32, gate_ref.shape[1:], 1)
    gate = jnp.where(lane % EXPERTS == pl.program_id(0), gate_ref[0], 0.0)
    gate = jnp.sum(gate, axis=1, keepdims=True)
    gate_pre = dot(x, w_ref[0, 0])
    up = dot(x, w_ref[0, 1])
    back = dot(g, w_ref[0, 2])
    sig = jax.nn.sigmoid(gate_pre)
    act = gate_pre * sig
    inner = act * up
    gg_ref[0] = jnp.broadcast_to(jnp.sum(inner * back, axis=1, keepdims=True), gg_ref.shape[1:])
    inner_grad = back * gate
    gate_pre_grad = (inner_grad * up * sig * (1.0 + gate_pre * (1.0 - sig))).astype(BF16)
    up_grad = (inner_grad * act).astype(BF16)
    gated = (inner * gate).astype(BF16)
    both = jnp.concatenate([gate_pre_grad, up_grad], axis=1)
    out_ref[0] = dot(gated, w_ref[0, 2], LAST_DIM).astype(BF16)
    entry_ref[0] = dot(both, jnp.concatenate([w_ref[0, 0], w_ref[0, 1]], axis=1), LAST_DIM).astype(BF16)
    FL = w_ref.shape[3]
    pair = dot(x, both, FIRST_DIM)
    parts = (pair[:, :FL], pair[:, FL:], dot(g, gated, FIRST_DIM))
    first = pl.program_id(1) == 0
    for k in range(3):

        @pl.when(first)
        def _(k=k):
            dw_ref[0, k] = parts[k]

        @pl.when(jnp.logical_not(first))
        def _(k=k):
            dw_ref[0, k] += parts[k]


def run_experts(x, g, gate, weights, chunk):
    EL, rows, D = x.shape
    FL = weights.shape[3]
    row_block = pl.BlockSpec((1, chunk, D), lambda e, c: (e, c, 0))
    thin = pl.BlockSpec((1, chunk, 128), lambda e, c: (e, c, 0))
    matrices = pl.BlockSpec((1, 3, D, FL), lambda e, c: (e, 0, 0, 0))
    return pl.pallas_call(
        _expert_kernel,
        out_shape=[
            jax.ShapeDtypeStruct(x.shape, BF16),
            jax.ShapeDtypeStruct(x.shape, BF16),
            jax.ShapeDtypeStruct(weights.shape, F32),
            jax.ShapeDtypeStruct((EL, rows, 128), F32),
        ],
        grid=(EL, rows // chunk),
        in_specs=[row_block, row_block, thin, matrices],
        out_specs=[row_block, row_block, matrices, thin],
        compiler_params=pltpu.CompilerParams(vmem_limit_bytes=VMEM_BYTES),
        cost_estimate=pl.CostEstimate(
            flops=18 * EL * rows * D * FL, bytes_accessed=8 * EL * rows * D + 18 * EL * D * FL, transcendentals=EL * rows * FL
        ),
    )(x, g, gate, weights)


def _spread_kernel(own_ref, slot_ref, gg_ref, out_ref, entry_ref, o_ref, e_ref, *, width):
    group, experts = slot_ref.shape
    slots = out_ref.shape[2]
    total = experts * slots
    D = out_ref.shape[3]
    lane = lax.broadcasted_iota(jnp.int32, (experts, total), 1)
    which = lax.broadcasted_iota(jnp.int32, (experts, total), 0)
    choose = jnp.where((lane >= which * slots) & (lane < (which + 1) * slots), 1.0, 0.0).astype(BF16)
    offset = lane[:1] - jnp.sum(jnp.where(lane >= (which + 1) * slots, slots, 0), axis=0, keepdims=True)
    mine = dot(slot_ref[...].astype(BF16), choose)
    pick = jnp.where(mine == offset.astype(F32), 1.0, 0.0).astype(BF16)
    column = lax.broadcasted_iota(jnp.int32, (slots, 128), 1)
    grads = [jnp.where(column == own_ref[0] + e, gg_ref[e, 0], 0.0).astype(BF16) for e in range(experts)]
    e_ref[:, pl.ds(D, 128)] = dot(pick, jnp.concatenate(grads, axis=0)).astype(BF16)

    def step(i, _):
        cols = pl.ds(pl.multiple_of(i * width, width), width)
        for source, target in ((out_ref, o_ref), (entry_ref, e_ref)):
            rows = jnp.concatenate([source[e, 0, :, cols] for e in range(experts)], axis=0)
            target[:, cols] = dot(pick, rows).astype(BF16)
        return 0

    lax.fori_loop(0, D // width, step, 0)


def spread_rows(own, slot, gate_grads, out_rows, entry_rows, group):
    N, EL = slot.shape
    _, groups, slots, D = out_rows.shape
    picked = pl.BlockSpec((EL, 1, slots, D), lambda i, *_: (0, i, 0, 0))
    return pl.pallas_call(
        functools.partial(_spread_kernel, width=512),
        out_shape=[jax.ShapeDtypeStruct((N, D), BF16), jax.ShapeDtypeStruct((N, D + 128), BF16)],
        grid_spec=pltpu.PrefetchScalarGridSpec(
            num_scalar_prefetch=1,
            grid=(groups,),
            in_specs=[
                pl.BlockSpec((group, EL), lambda i, *_: (i, 0)),
                pl.BlockSpec((EL, 1, slots, 128), lambda i, *_: (0, i, 0, 0)),
                picked,
                picked,
            ],
            out_specs=[
                pl.BlockSpec((group, D), lambda i, *_: (i, 0)),
                pl.BlockSpec((group, D + 128), lambda i, *_: (i, 0)),
            ],
        ),
        compiler_params=pltpu.CompilerParams(vmem_limit_bytes=VMEM_BYTES),
        cost_estimate=pl.CostEstimate(flops=4 * EL * slots * N * D, bytes_accessed=8 * N * D, transcendentals=0),
    )(own, slot, gate_grads, out_rows, entry_rows)


def body(
    hidden_in,
    out_grad,
    attn_gain,
    query_weight,
    key_weight,
    value_weight,
    out_weight,
    query_gain,
    key_gain,
    ffn_gain,
    router_weight,
    expert_weights,
    routes,
    doc_starts,
):
    U = lax.axis_size("uly")
    Z = lax.axis_size("blk")
    u = lax.axis_index("uly")
    z = lax.axis_index("blk")
    T, D = hidden_in.shape
    EL = expert_weights.shape[0]
    N = U * Z * T
    RW = query_weight.shape[0]
    move = (Slice if (U, Z, T, D) == (8, 4, 128, 2048) else General)(U, Z, T, D)
    C, L = move.C, move.L

    own_weights = (query_weight, key_weight, value_weight)
    gains = jnp.stack([attn_gain, ffn_gain, query_gain, key_gain], axis=1)
    first_rows, qkv_weight, packed, routes_all = move.enter(
        hidden_in, own_weights, gains, out_weight, router_weight, routes.T, out_grad
    )
    hidden = hidden_in.astype(F32)
    weight_router = packed[:, :EXPERTS]
    gain_ffn = packed[:, EXPERTS].astype(F32)
    head_gains = lax.dynamic_slice_in_dim(packed[:, EXPERTS + 1 : EXPERTS + 3], move.group * C, C, 0).astype(F32)
    head_gains = jnp.pad(head_gains.T, ((0, 6), (0, 0)))
    local = jnp.arange(L, dtype=jnp.int32)
    cosine, sine = rotary_tables((local // T * move.block_step + move.first_block) * T + local % T)
    pre, query_rot, key_rot, value, squares = project(first_rows, qkv_weight, head_gains, cosine, sine)
    key_all, value_all, stats, k_stat = move.sequence(key_rot, value, squares, out_grad)
    index = jnp.stack([jnp.int32(i) for i in (move.first_block * T // move.rows, move.block_step, *move.parts)])
    chunk = min(ATTEND_CHUNK, N)
    attended, logs, mixed = attention_forward(
        index, doc_starts, stats[0], k_stat, query_rot, key_all, value_all, move.out_parts, move.rows, chunk
    )
    move.prepare(routes_all, EL, jnp.roll(weight_router, -u * EL, axis=1))
    residual = hidden + move.heads_to_rows(mixed).astype(F32)

    second_scale = norm_scale(residual)
    second_low = (residual * second_scale * gain_ffn).astype(BF16)
    probabilities = jax.nn.softmax(dot(second_low, weight_router), axis=-1)
    second_all, entry_sum = move.experts(second_low, expert_weights)
    entry_sum = entry_sum.astype(F32)

    second_grad, prob_grad = entry_sum[:, :D], entry_sum[:, D : D + EXPERTS]
    logit_grad = (
        probabilities * (prob_grad - jnp.sum(probabilities * prob_grad, axis=1, keepdims=True))
    ).astype(BF16)
    second_grad = second_grad + dot(logit_grad, weight_router, LAST_DIM)
    upstream = out_grad.astype(F32)
    weighted = second_grad * gain_ffn
    inner_mean = jnp.mean(weighted * residual, axis=-1, keepdims=True)
    residual_grad = upstream + second_scale * weighted - residual * (second_scale**3) * inner_mean
    ffn_gain_part = jnp.sum(second_grad * residual * second_scale, axis=0)

    residual_rows, expert_grads = move.rows_to_heads(residual_grad.astype(BF16))
    dq, dk_part, dv_part, out_weight_part, q_inner, k_inner = attention_backward(
        index,
        doc_starts,
        stats[0],
        k_stat,
        query_rot,
        residual_rows,
        attended,
        logs,
        key_all,
        value_all,
        move.out_parts,
        move.rows,
        chunk,
    )
    dk, dv, out_sum, inner = move.sequence_sums(dk_part, dv_part, out_weight_part, q_inner, k_inner)
    weight_part, first_part, gain_parts = project_back(
        dq, dk, dv, pre, stats, inner, head_gains, cosine, sine, first_rows, qkv_weight
    )
    gain_parts = gain_parts[:2]
    first_weighted, weight_sum, out_weight_grad, logit_grad_all, ffn_gain_grad, head_gain_grads = move.leave(
        first_part, weight_part, logit_grad, ffn_gain_part, gain_parts
    )
    own_columns = lax.dynamic_slice_in_dim(second_all, (u * Z + z) * RW, RW, 1)
    router_grad = dot(own_columns, logit_grad_all, FIRST_DIM)
    output, hidden_grad, attn_gain_grad, *weight_grads = finish(
        hidden_in, residual, residual_grad, first_weighted, out_sum, move.out_own, own_weights, weight_sum, out_weight_grad, gains
    )
    return (
        output,
        hidden_grad,
        attn_gain_grad[:, 0],
        weight_grads[0],
        weight_grads[1],
        weight_grads[2],
        weight_grads[3],
        head_gain_grads[0],
        head_gain_grads[1],
        ffn_gain_grad,
        router_grad,
        expert_grads,
    )


def solution(mesh):
    rows = P(ALL, None)
    flat = P(ALL)
    experts = P("uly", None, None, "blk")
    return jax.shard_map(
        body,
        mesh=mesh,
        in_specs=(rows, rows, flat, rows, rows, rows, rows, flat, flat, flat, rows, experts, rows, P()),
        out_specs=(rows, rows, flat, rows, rows, rows, rows, flat, flat, flat, rows, experts),
        check_vma=False,
    )
```
